32 devices in a mesh: section: 4 (over y, core), table: 8 (over z, x).
Axes of the slice: x: 2, y: 2, z: 4, core: 2. Of those that a mesh axis runs over, the one named last changes fastest.
Arguments:
- emb_table: bfloat16 [131072, 128], P(('section', 'table')), may hold values from -6 to 6
- lcb_weight: bfloat16 [8, 512], replicated, may hold values from -0.25 to 0.25
- fm_proj: bfloat16 [4, 8, 128], P('section'), may hold values from -2 to 2
- norm_gain: bfloat16 [4, 1024], P('section'), may hold values from 0.25 to 1.75
- w_up: bfloat16 [4, 1024, 4096], P('section'), may hold values from -0.1875 to 0.1875
- w_down: bfloat16 [4, 4096, 1024], P('section'), may hold values from -0.09375 to 0.09375
- top_grad: bfloat16 [8, 4, 64, 1024], P('table'), may hold values from -12 to 12
- lookup_slot: int32 [8, 256, 512], P('table', 'section'), may hold values from 0 to 4095, as said below
- wanted_rows: int32 [32, 32, 128], P(('section', 'table')), may hold values from 0 to 4095, as said below
- row_counts: int32 [32, 32], P(('section', 'table')), may hold values from 32 to 128, as said below
Outputs:
- table_grad: float32 [131072, 128], P(('section', 'table'))
The draws below stay inside these ranges and needn't reach their ends.
Inputs may be any that keep to these rules, and one draw needn't show every extreme that they name: The first row_counts[o, q] entries of wanted_rows[o, q] are distinct rows; the others are also rows of the owner. `row_counts`: some owners have 128 live slots for every asking device. `lookup_slot`: A lookup of asking device q names slot o * 128 + c with c below row_counts[o, q].
All inputs are finite; a program needn't handle non-finite values.
Results may differ from the reference program's by a relative error of at most 0.025.
Values may be sent and summed in bfloat16 or wider, within the bound.
No kernel may reach another device: no remote copies, remote signals or barrier semaphores. Data moves between devices by JAX's collectives and lax.ppermute only.
A program may use at most 128 MiB of HBM per device.

```python
import jax
import jax.numpy as jnp
from jax import lax

E = 128
K = 8
R = 128
D = 1024
H = 4096
F = 512
M = 4
B_DEV = 64
ROWS_DEV = 4096
CAP = 128
LAYERS = 4
SHARDS = 8
OWNERS = 32
LOOK_DEV = 64
N_SECTION = 4


def routing(key):
    base_key = jax.random.fold_in(key, 11)
    k_hot, k_load, k_jit, k_own, k_col = jax.random.split(base_key, 5)
    hot_count = max(1, OWNERS // 32)
    hot_ids = jax.random.permutation(k_hot, OWNERS)[:hot_count]
    is_hot = jnp.any(jnp.arange(OWNERS)[:, None] == hot_ids[None, :], axis=1)
    light_load = jax.random.randint(k_load, (OWNERS, OWNERS), max(1, CAP // 4), max(1, CAP // 2) + 1)
    counts = jnp.where(is_hot[:, None], CAP, light_load).astype(jnp.int32)
    stripe = ROWS_DEV // CAP
    jitter = jax.random.randint(k_jit, (OWNERS, OWNERS, CAP), 0, stripe)
    wanted = (jnp.arange(CAP)[None, None, :] * stripe + jitter).astype(jnp.int32)
    source = (jnp.arange(M * B_DEV) // LOOK_DEV)[None, :] * SHARDS + jnp.arange(SHARDS)[:, None]
    owner_ids = jax.random.randint(k_own, (SHARDS, M * B_DEV, F), 0, OWNERS)
    count_cap = counts[owner_ids, source[:, :, None]]
    column = jax.random.randint(k_col, (SHARDS, M * B_DEV, F), 0, 1 << 20) % count_cap
    slot_ids = (owner_ids * CAP + column).astype(jnp.int32)
    return (wanted, counts, slot_ids)


def draw_lookup_slot(key, part):
    return routing(key)[2]


def draw_wanted_rows(key, part):
    return routing(key)[0]


def draw_row_counts(key, part):
    return routing(key)[1]


def steps_of(own_key, extent, cuts, low, high):
    level, own = 1.0, jax.random.fold_in(own_key, 6)
    for axis_at, blocks in cuts:
        steps = jnp.exp(jax.random.uniform(jax.random.fold_in(own, axis_at), (blocks,), jnp.float32, low / len(cuts), high / len(cuts)))
        level = level * jnp.repeat(steps, extent[axis_at] // blocks).reshape([-1 if axis == axis_at else 1 for axis in range(len(extent))])
    return level


def bell_draw(stream_key, dims, spread, reach, cuts=(), kind=jnp.bfloat16):
    array = spread * jax.random.normal(stream_key, dims, jnp.float32)
    if cuts:
        array = array * steps_of(stream_key, dims, cuts, -0.22, 0.18)
    return jnp.clip(array, -reach, reach).astype(kind)


def setup_inputs(seed: int = 0) -> dict:
    streams_of = jax.random.split(jax.random.key(seed), 11)
    emb_table = bell_draw(streams_of[0], (OWNERS * ROWS_DEV, E), 1.0, 6.0, ((0, 32),))
    lcb_weight = bell_draw(streams_of[1], (K, F), F ** -0.5, 0.25)
    fm_proj = bell_draw(streams_of[2], (LAYERS, K, R), K ** -0.5, 2.0, ((0, 4),))
    norm_gain = jnp.clip(1.0 + 0.15 * jax.random.normal(streams_of[3], (LAYERS, D), jnp.float32), 0.25, 1.75).astype(jnp.bfloat16)
    w_up = bell_draw(streams_of[4], (LAYERS, D, H), D ** -0.5, 0.1875, ((0, 4),))
    w_down = bell_draw(streams_of[5], (LAYERS, H, D), H ** -0.5, 0.09375, ((0, 4),))
    top_grad = bell_draw(streams_of[6], (SHARDS, M, B_DEV, D), 2.0, 12.0, ((0, 8),))
    lookup_slot = draw_lookup_slot(jax.random.fold_in(streams_of[10], 71), 0)
    wanted_rows = draw_wanted_rows(jax.random.fold_in(streams_of[10], 71), 0)
    row_counts = draw_row_counts(jax.random.fold_in(streams_of[10], 71), 0)
    return {"emb_table": emb_table, "lcb_weight": lcb_weight, "fm_proj": fm_proj, "norm_gain": norm_gain, "w_up": w_up, "w_down": w_down, "top_grad": top_grad, "lookup_slot": lookup_slot, "wanted_rows": wanted_rows, "row_counts": row_counts}


EPSILON = 1e-05
DECAY_WEIGHT = 0.5

def fm_forward(inputs, proj, gain, w_up, w_down):
    batch_rows = inputs.shape[0]
    embed_count = proj.shape[0]
    features = inputs.reshape(batch_rows, embed_count, -1).astype(jnp.float32)
    mixed_cols = jnp.einsum('bke,kr->bre', features, proj.astype(jnp.float32)).astype(jnp.bfloat16)
    interact = jnp.einsum('bke,bre->bkr', features, mixed_cols.astype(jnp.float32)).reshape(batch_rows, -1)
    inv_scale = lax.rsqrt(lax.optimization_barrier(jnp.mean(interact * interact, axis=1, keepdims=True)) + EPSILON)
    normed = (interact * inv_scale * gain.astype(jnp.float32)).astype(jnp.bfloat16)
    before = jnp.dot(normed, w_up, preferred_element_type=jnp.float32)
    hidden = jnp.maximum(before, 0.0).astype(jnp.bfloat16)
    output = inputs.astype(jnp.float32) + jnp.dot(hidden, w_down, preferred_element_type=jnp.float32)
    return (output.astype(jnp.bfloat16), (features, mixed_cols, interact, inv_scale, before))

def fm_backward(inputs, grad_out, proj, gain, w_up, w_down):
    batch_rows = inputs.shape[0]
    embed_count = proj.shape[0]
    unused, saved = fm_forward(inputs, proj, gain, w_up, w_down)
    features, mixed_cols, interact, inv_scale, before = saved
    g_hidden = jnp.dot(grad_out, w_down.T, preferred_element_type=jnp.float32)
    g_before = jnp.where(before > 0.0, g_hidden, 0.0).astype(jnp.bfloat16)
    g_normed = jnp.dot(g_before, w_up.T, preferred_element_type=jnp.float32)
    weighted = g_normed * gain.astype(jnp.float32)
    g_interact = inv_scale * (weighted - interact * inv_scale * inv_scale * lax.optimization_barrier(jnp.mean(weighted * interact, axis=1, keepdims=True)))
    g_interact = g_interact.astype(jnp.bfloat16).reshape(batch_rows, embed_count, -1).astype(jnp.float32)
    g_features = jnp.einsum('bkr,bre->bke', g_interact, mixed_cols.astype(jnp.float32))
    g_mixed = jnp.einsum('bkr,bke->bre', g_interact, features).astype(jnp.bfloat16)
    g_features = g_features + jnp.einsum('bre,kr->bke', g_mixed.astype(jnp.float32), proj.astype(jnp.float32))
    return (grad_out.astype(jnp.float32) + g_features.reshape(batch_rows, -1)).astype(jnp.bfloat16)

def reference(emb_table, lcb_weight, fm_proj, norm_gain, w_up, w_down, top_grad, lookup_slot, wanted_rows, row_counts):
    look_dev = M * B_DEV // N_SECTION
    row_section = jnp.arange(M * B_DEV) // look_dev
    lcb_float = lcb_weight.astype(jnp.float32)

    def chain(pair):
        activ, grad_now = pair
        stash = []
        for layer in range(LAYERS):
            stash.append(activ)
            activ = fm_forward(activ, fm_proj[layer], norm_gain[layer], w_up[layer], w_down[layer])[0]
        for layer in reversed(range(LAYERS)):
            grad_now = fm_backward(stash[layer], grad_now, fm_proj[layer], norm_gain[layer], w_up[layer], w_down[layer])
        return grad_now

    def per_group(grads, group):
        source = row_section * SHARDS + group
        slots_here = lax.dynamic_index_in_dim(lookup_slot, group, 0, keepdims=False)
        owner_ids = slots_here // CAP
        column = slots_here % CAP
        row_id = owner_ids * ROWS_DEV + wanted_rows[owner_ids, source[:, None], column]
        embedded = emb_table[row_id].astype(jnp.float32)
        lead = jnp.einsum('kf,bfe->bke', lcb_float, embedded).astype(jnp.bfloat16).reshape(M, B_DEV, D)
        grads_top = lax.dynamic_index_in_dim(top_grad, group, 0, keepdims=False)
        lead_grad = lax.map(chain, (lead, grads_top))
        lead_grad = lead_grad.reshape(M * B_DEV, K, E).astype(jnp.float32)
        feature_grad = jnp.einsum('kf,bke->bfe', lcb_float, lead_grad)
        grads = grads.at[row_id.reshape(-1)].add(feature_grad.reshape(-1, E))
        return (grads, None)
    grads = jnp.zeros((OWNERS * ROWS_DEV, E), jnp.float32)
    grads, unused = lax.scan(per_group, grads, jnp.arange(SHARDS))

    def per_owner(grads, owner):
        local_rows = lax.dynamic_index_in_dim(wanted_rows, owner, 0, keepdims=False)
        counts_here = lax.dynamic_index_in_dim(row_counts, owner, 0, keepdims=False)
        live_slots = jnp.arange(CAP)[None, :] < counts_here[:, None]
        row_id = owner * ROWS_DEV + local_rows
        decay_term = jnp.where(live_slots[..., None], DECAY_WEIGHT * emb_table[row_id].astype(jnp.float32), 0.0)
        grads = grads.at[row_id.reshape(-1)].add(decay_term.reshape(-1, E))
        return (grads, None)
    grads, unused = lax.scan(per_owner, grads, jnp.arange(OWNERS))
    return grads
```

```python
import jax
import jax.numpy as jnp
from jax import lax
from jax.experimental import pallas as pl
from jax.experimental.pallas import tpu as pltpu
from jax.sharding import PartitionSpec as P

EPSILON = 1e-05
DECAY_WEIGHT = 0.5
VMEM_LIMIT = 40 * 1024 * 1024
UNROLL = 16


def whole(memory_space=pltpu.VMEM):
    return pl.BlockSpec(memory_space=memory_space)


def params():
    return pltpu.CompilerParams(vmem_limit_bytes=VMEM_LIMIT)


def tiles_of(count, most):
    return max(step for step in range(1, most + 1) if count % step == 0)


def pick_rows(emb_table, picked):
    rows, width = emb_table.shape
    count = picked.shape[0]
    chunk = min(count, 1024)

    def kernel(picked_ref, table_ref, out_ref, wide, lines):
        step = pl.program_id(0)

        @pl.when(step == 0)
        def _():
            wide[...] = table_ref[...].astype(jnp.float32)

        def body(group, carry):
            first = pl.multiple_of(group * UNROLL, UNROLL)
            for lane in range(UNROLL):
                row = picked_ref[step * chunk + first + lane]
                lines[pl.ds(first + lane, 1), :] = wide[pl.ds(row, 1), :]
            return carry

        lax.fori_loop(0, chunk // UNROLL, body, 0)
        out_ref[...] = lines[...].astype(out_ref.dtype)

    return pl.pallas_call(
        kernel,
        out_shape=jax.ShapeDtypeStruct((count, width), emb_table.dtype),
        grid_spec=pltpu.PrefetchScalarGridSpec(
            num_scalar_prefetch=1,
            grid=(count // chunk,),
            in_specs=[pl.BlockSpec((rows, width), lambda i, ids: (0, 0))],
            out_specs=pl.BlockSpec((chunk, width), lambda i, ids: (i, 0)),
            scratch_shapes=[
                pltpu.VMEM((rows, width), jnp.float32),
                pltpu.VMEM((chunk, width), jnp.float32),
            ],
        ),
        compiler_params=params(),
        name="pick_rows",
    )(picked, emb_table)


def spread_weights(lookup_slots, lcb_weight, owners, cap):
    samples, feature_count = lookup_slots.shape
    embed_count = lcb_weight.shape[0]
    group = tiles_of(samples, 8)

    def kernel(slots_ref, lcb_ref, out_ref):
        lcb = lcb_ref[...].astype(jnp.float32)
        owner_of = lax.broadcasted_iota(jnp.int32, (owners, embed_count, feature_count), 0)
        column_of = lax.broadcasted_iota(jnp.int32, (cap, feature_count), 0)
        for pair in range(0, group, 2):
            made = []
            for sample in (pair, pair + 1):
                slots = slots_ref[sample : sample + 1, :]
                owner = lax.div(slots, cap)
                column = slots - owner * cap
                left = jnp.where(owner_of == owner[None], lcb[None], 0.0)
                left = left.reshape(owners * embed_count, feature_count).astype(jnp.bfloat16)
                right = jnp.where(column_of == column, 1.0, 0.0).astype(jnp.bfloat16)
                both = lax.dot_general(
                    left, right, (((1,), (1,)), ((), ())), preferred_element_type=jnp.float32
                )
                made.append(both.reshape(owners, embed_count, cap))
            rows = pl.ds(pair * embed_count, 2 * embed_count)
            out_ref[:, rows, :] = jnp.concatenate(made, axis=1).astype(out_ref.dtype)

    return pl.pallas_call(
        kernel,
        out_shape=jax.ShapeDtypeStruct((owners, samples * embed_count, cap), jnp.bfloat16),
        grid=(samples // group,),
        in_specs=[
            pl.BlockSpec((group, feature_count), lambda i: (i, 0)),
            pl.BlockSpec((embed_count, feature_count), lambda i: (0, 0)),
        ],
        out_specs=pl.BlockSpec((owners, group * embed_count, cap), lambda i: (0, i, 0)),
        compiler_params=params(),
        cost_estimate=pl.CostEstimate(
            flops=2 * samples * owners * embed_count * feature_count * cap,
            bytes_accessed=2 * owners * samples * embed_count * cap,
            transcendentals=0,
        ),
        name="spread_weights",
    )(lookup_slots, lcb_weight)


def compress(spread, fetched, embed_count):
    owners, lines, cap = spread.shape
    width = fetched.shape[2]
    samples = lines // embed_count
    part = tiles_of(owners, 4)

    def kernel(spread_ref, rows_ref, out_ref, total):
        step = pl.program_id(0)
        left = jnp.concatenate([spread_ref[o] for o in range(part)], axis=1)
        right = rows_ref[...].reshape(part * cap, width)
        term = jnp.dot(left, right, preferred_element_type=jnp.float32)

        @pl.when(step == 0)
        def _():
            total[...] = term

        @pl.when(step > 0)
        def _():
            total[...] += term

        @pl.when(step == owners // part - 1)
        def _():
            for k in range(embed_count):
                piece = total[pl.ds(k, samples, stride=embed_count), :]
                out_ref[:, k * width : (k + 1) * width] = piece.astype(out_ref.dtype)

    return pl.pallas_call(
        kernel,
        out_shape=jax.ShapeDtypeStruct((samples, embed_count * width), jnp.bfloat16),
        grid=(owners // part,),
        in_specs=[
            pl.BlockSpec((part, lines, cap), lambda i: (i, 0, 0)),
            pl.BlockSpec((part, cap, width), lambda i: (i, 0, 0)),
        ],
        out_specs=pl.BlockSpec((samples, embed_count * width), lambda i: (0, 0)),
        scratch_shapes=[pltpu.VMEM((lines, width), jnp.float32)],
        compiler_params=params(),
        name="compress",
    )(spread, fetched)


def expand(spread, lead_share, embed_count):
    owners, lines, cap = spread.shape
    samples = lines // embed_count
    width = lead_share.shape[1] // embed_count
    part = tiles_of(owners, 4)

    def kernel(spread_ref, grad_ref, out_ref, tall, turned):
        @pl.when(pl.program_id(0) == 0)
        def _():
            for k in range(embed_count):
                piece = grad_ref[:, k * width : (k + 1) * width].astype(jnp.float32)
                tall[pl.ds(k, samples, stride=embed_count), :] = piece
            turned[...] = tall[...].T.astype(jnp.bfloat16)

        right = jnp.concatenate([spread_ref[o] for o in range(part)], axis=1)
        term = jnp.dot(turned[...], right, preferred_element_type=jnp.float32)
        out_ref[...] = term.T.astype(out_ref.dtype).reshape(part, cap, width)

    return pl.pallas_call(
        kernel,
        out_shape=jax.ShapeDtypeStruct((owners, cap, width), jnp.bfloat16),
        grid=(owners // part,),
        in_specs=[
            pl.BlockSpec((part, lines, cap), lambda i: (i, 0, 0)),
            pl.BlockSpec(lead_share.shape, lambda i: (0, 0)),
        ],
        out_specs=pl.BlockSpec((part, cap, width), lambda i: (i, 0, 0)),
        scratch_shapes=[
            pltpu.VMEM((lines, width), jnp.float32),
            pltpu.VMEM((width, lines), jnp.bfloat16),
        ],
        compiler_params=params(),
        name="expand",
    )(spread, lead_share)


def add_rows(targets, returned, outgoing, rows):
    count, width = returned.shape
    chunk = min(count, 1024)
    steps = count // chunk

    def kernel(targets_ref, back_ref, sent_ref, out_ref, total, terms, done):
        step = pl.program_id(0)

        @pl.when(step == 0)
        def _():
            total[...] = jnp.zeros_like(total)

        terms[...] = back_ref[...].astype(jnp.float32) + DECAY_WEIGHT * sent_ref[...].astype(
            jnp.float32
        )

        def body(group, carry):
            first = pl.multiple_of(group * UNROLL, UNROLL)
            places = [targets_ref[step * chunk + first + lane] for lane in range(UNROLL)]
            sums = [
                total[pl.ds(places[lane], 1), :] + terms[pl.ds(first + lane, 1), :]
                for lane in range(UNROLL)
            ]
            for lane in range(UNROLL):
                total[pl.ds(places[lane], 1), :] = sums[lane]
            return carry

        lax.fori_loop(0, chunk // UNROLL, body, 0)

        @pl.when(step == steps - 1)
        def _():
            copy = pltpu.make_async_copy(total.at[pl.ds(0, rows), :], out_ref, done)
            copy.start()
            copy.wait()

    return pl.pallas_call(
        kernel,
        out_shape=jax.ShapeDtypeStruct((rows, width), jnp.float32),
        grid_spec=pltpu.PrefetchScalarGridSpec(
            num_scalar_prefetch=1,
            grid=(steps,),
            in_specs=[
                pl.BlockSpec((chunk, width), lambda i, ids: (i, 0)),
                pl.BlockSpec((chunk, width), lambda i, ids: (i, 0)),
            ],
            out_specs=pl.BlockSpec(memory_space=pl.ANY),
            scratch_shapes=[
                pltpu.VMEM((rows + 8, width), jnp.float32),
                pltpu.VMEM((chunk, width), jnp.float32),
                pltpu.SemaphoreType.DMA,
            ],
        ),
        compiler_params=params(),
        name="add_rows",
    )(targets, returned, outgoing)


def shifted(value, axis, steps):
    count = lax.axis_size(axis)
    first, last = (max(0, -steps), min(count, count - steps))
    return lax.ppermute(value, axis, [(source, source + steps) for source in range(first, last)])


def fm_forward(inputs, proj, gain, w_up, w_down):
    batch_rows = inputs.shape[0]
    embed_count = proj.shape[0]
    features = inputs.reshape(batch_rows, embed_count, -1)
    mixed_cols = jnp.einsum(
        "bke,kr->bre", features, proj, preferred_element_type=jnp.float32
    ).astype(jnp.bfloat16)
    interact = jnp.einsum(
        "bke,bre->bkr", features, mixed_cols, preferred_element_type=jnp.float32
    ).reshape(batch_rows, -1)
    inv_scale = lax.rsqrt(jnp.mean(interact * interact, axis=1, keepdims=True) + EPSILON)
    normed = (interact * inv_scale * gain.astype(jnp.float32)).astype(jnp.bfloat16)
    before = jnp.dot(normed, w_up, preferred_element_type=jnp.float32)
    hidden = jnp.maximum(before, 0.0).astype(jnp.bfloat16)
    output = inputs.astype(jnp.float32) + jnp.dot(
        hidden, w_down, preferred_element_type=jnp.float32
    )
    return (output.astype(jnp.bfloat16), (features, mixed_cols, interact, inv_scale, before))


def fm_backward(inputs, grad_out, proj, gain, w_up, w_down):
    batch_rows = inputs.shape[0]
    embed_count = proj.shape[0]
    unused, saved = fm_forward(inputs, proj, gain, w_up, w_down)
    features, mixed_cols, interact, inv_scale, before = saved
    last_dims = (((1,), (1,)), ((), ()))
    g_hidden = lax.dot_general(grad_out, w_down, last_dims, preferred_element_type=jnp.float32)
    g_before = jnp.where(before > 0.0, g_hidden, 0.0).astype(jnp.bfloat16)
    g_normed = lax.dot_general(g_before, w_up, last_dims, preferred_element_type=jnp.float32)
    weighted = g_normed * gain.astype(jnp.float32)
    g_interact = inv_scale * (
        weighted
        - interact * inv_scale * inv_scale * jnp.mean(weighted * interact, axis=1, keepdims=True)
    )
    g_interact = g_interact.astype(jnp.bfloat16).reshape(batch_rows, embed_count, -1)
    g_features = jnp.einsum(
        "bkr,bre->bke", g_interact, mixed_cols, preferred_element_type=jnp.float32
    )
    g_mixed = jnp.einsum(
        "bkr,bke->bre", g_interact, features, preferred_element_type=jnp.float32
    ).astype(jnp.bfloat16)
    g_features = g_features + jnp.einsum(
        "bre,kr->bke", g_mixed, proj, preferred_element_type=jnp.float32
    )
    return (grad_out.astype(jnp.float32) + g_features.reshape(batch_rows, -1)).astype(jnp.bfloat16)


def pass_on(payload, offset):
    return shifted(payload, "section", offset)


def per_device(
    emb_table,
    lcb_weight,
    fm_proj,
    norm_gain,
    w_up,
    w_down,
    top_grad,
    lookup_slot,
    wanted_rows,
    row_counts,
):
    section_count = lax.axis_size("section")
    shard_count = lax.axis_size("table")
    my_section = lax.axis_index("section")
    owners = section_count * shard_count
    cap = wanted_rows.shape[2]
    embed_width = emb_table.shape[1]
    picked_rows = wanted_rows[0]
    look_dev = lookup_slot.shape[1]
    embed_count = lcb_weight.shape[0]
    outgoing = pick_rows(emb_table, picked_rows.reshape(-1))
    fetched = lax.all_to_all(
        outgoing.reshape(owners, cap, embed_width),
        ("section", "table"),
        split_axis=0,
        concat_axis=0,
        tiled=True,
    )
    spread = spread_weights(lookup_slot[0], lcb_weight, owners, cap)
    compressed = compress(spread, fetched, embed_count)
    leading = lax.all_gather(compressed, "section", axis=0, tiled=True)
    micro_count = top_grad.shape[1]
    batch_rows = top_grad.shape[2]
    model_width = top_grad.shape[3]
    leading = leading.reshape(micro_count, batch_rows, model_width)
    weights = (fm_proj[0], norm_gain[0], w_up[0], w_down[0])
    tick_count = micro_count + section_count - 1

    def forward_tick(tick, state):
        incoming, stash = state
        micro_idx = tick - my_section
        is_valid = (micro_idx >= 0) & (micro_idx < micro_count)
        clipped = jnp.clip(micro_idx, 0, micro_count - 1)
        inputs = jnp.where(
            my_section == 0, lax.dynamic_index_in_dim(leading, clipped, 0, keepdims=False), incoming
        )
        outputs = lax.cond(
            is_valid,
            lambda value: fm_forward(value, *weights)[0],
            lambda value: jnp.zeros_like(value),
            inputs,
        )
        kept_rows = jnp.where(
            is_valid, inputs, lax.dynamic_index_in_dim(stash, clipped, 0, keepdims=False)
        )
        stash = lax.dynamic_update_index_in_dim(stash, kept_rows, clipped, 0)
        return (pass_on(outputs, 1), stash)

    empty_rows = jnp.zeros((batch_rows, model_width), jnp.bfloat16)
    empty_stash = jnp.zeros((micro_count, batch_rows, model_width), jnp.bfloat16)
    unused, stash = lax.fori_loop(0, tick_count, forward_tick, (empty_rows, empty_stash))
    grads_top = top_grad[0]

    def backward_tick(tick, state):
        incoming, lead_grad = state
        micro_idx = tick - (section_count - 1 - my_section)
        is_valid = (micro_idx >= 0) & (micro_idx < micro_count)
        clipped = jnp.clip(micro_idx, 0, micro_count - 1)
        given = jnp.where(
            my_section == section_count - 1,
            lax.dynamic_index_in_dim(grads_top, clipped, 0, keepdims=False),
            incoming,
        )
        saved_rows = lax.dynamic_index_in_dim(stash, clipped, 0, keepdims=False)
        result = lax.cond(
            is_valid,
            lambda pair: fm_backward(pair[0], pair[1], *weights),
            lambda pair: jnp.zeros_like(pair[0]),
            (saved_rows, given),
        )
        record = jnp.where(
            is_valid & (my_section == 0),
            result,
            lax.dynamic_index_in_dim(lead_grad, clipped, 0, keepdims=False),
        )
        lead_grad = lax.dynamic_update_index_in_dim(lead_grad, record, clipped, 0)
        return (pass_on(result, -1), lead_grad)

    unused, lead_grad = lax.fori_loop(0, tick_count, backward_tick, (empty_rows, empty_stash))
    terms = jnp.where(my_section == 0, lead_grad.astype(jnp.float32), 0.0).reshape(
        micro_count * batch_rows, model_width
    )
    lead_share = lax.psum_scatter(
        terms.astype(jnp.bfloat16), "section", scatter_dimension=0, tiled=True
    )
    slot_grad = expand(spread, lead_share, embed_count)
    returned = lax.all_to_all(
        slot_grad, ("section", "table"), split_axis=0, concat_axis=0, tiled=True
    )
    live_slots = jnp.arange(cap)[None, :] < row_counts[0][:, None]
    targets = jnp.where(live_slots, picked_rows, emb_table.shape[0]).reshape(-1)
    return add_rows(targets, returned.reshape(-1, embed_width), outgoing, emb_table.shape[0])


def solution(mesh):
    in_specs = (
        P(("section", "table"), None),
        P(),
        P("section", None, None),
        P("section", None),
        P("section", None, None),
        P("section", None, None),
        P("table", None, None, None),
        P("table", "section", None),
        P(("section", "table"), None, None),
        P(("section", "table"), None),
    )
    out_specs = P(("section", "table"), None)
    return jax.shard_map(
        per_device, mesh=mesh, in_specs=in_specs, out_specs=out_specs, check_vma=False
    )
```

```python
import jax
import jax.numpy as jnp
from jax import lax
from jax.experimental import pallas as pl
from jax.experimental.pallas import tpu as pltpu
from jax.sharding import PartitionSpec as P

EPSILON = 1e-05
DECAY_WEIGHT = 0.5
VMEM_LIMIT = 20 * 1024 * 1024
UNROLL = 16


def whole(memory_space=pltpu.VMEM):
    return pl.BlockSpec(memory_space=memory_space)


def params():
    return pltpu.CompilerParams(vmem_limit_bytes=VMEM_LIMIT)


def tiles_of(count, most):
    return max(step for step in range(1, most + 1) if count % step == 0)


def pick_rows(emb_table, picked):
    rows, width = emb_table.shape
    count = picked.shape[0]
    chunk = min(count, 1024)

    def kernel(picked_ref, table_ref, out_ref, wide, lines):
        step = pl.program_id(0)

        @pl.when(step == 0)
        def _():
            wide[...] = table_ref[...].astype(jnp.float32)

        def body(group, carry):
            first = pl.multiple_of(group * UNROLL, UNROLL)
            for lane in range(UNROLL):
                row = picked_ref[step * chunk + first + lane]
                lines[pl.ds(first + lane, 1), :] = wide[pl.ds(row, 1), :]
            return carry

        lax.fori_loop(0, chunk // UNROLL, body, 0)
        out_ref[...] = lines[...].astype(out_ref.dtype)

    return pl.pallas_call(
        kernel,
        out_shape=jax.ShapeDtypeStruct((count, width), emb_table.dtype),
        grid_spec=pltpu.PrefetchScalarGridSpec(
            num_scalar_prefetch=1,
            grid=(count // chunk,),
            in_specs=[pl.BlockSpec((rows, width), lambda i, ids: (0, 0))],
            out_specs=pl.BlockSpec((chunk, width), lambda i, ids: (i, 0)),
            scratch_shapes=[
                pltpu.VMEM((rows, width), jnp.float32),
                pltpu.VMEM((chunk, width), jnp.float32),
            ],
        ),
        compiler_params=params(),
        name="pick_rows",
    )(picked, emb_table)


def spread_weights(lookup_slots, lcb_weight, owners, cap):
    samples, feature_count = lookup_slots.shape
    embed_count = lcb_weight.shape[0]
    group = tiles_of(samples, 8)

    def kernel(slots_ref, lcb_ref, out_ref):
        lcb = lcb_ref[...].astype(jnp.float32)
        owner_of = lax.broadcasted_iota(jnp.int32, (owners, embed_count, feature_count), 0)
        column_of = lax.broadcasted_iota(jnp.int32, (cap, feature_count), 0)
        for pair in range(0, group, 2):
            made = []
            for sample in (pair, pair + 1):
                slots = slots_ref[sample : sample + 1, :]
                owner = lax.div(slots, cap)
                column = slots - owner * cap
                left = jnp.where(owner_of == owner[None], lcb[None], 0.0)
                left = left.reshape(owners * embed_count, feature_count).astype(jnp.bfloat16)
                right = jnp.where(column_of == column, 1.0, 0.0).astype(jnp.bfloat16)
                both = lax.dot_general(
                    left, right, (((1,), (1,)), ((), ())), preferred_element_type=jnp.float32
                )
                made.append(both.reshape(owners, embed_count, cap))
            rows = pl.ds(pair * embed_count, 2 * embed_count)
            out_ref[:, rows, :] = jnp.concatenate(made, axis=1).astype(out_ref.dtype)

    return pl.pallas_call(
        kernel,
        out_shape=jax.ShapeDtypeStruct((owners, samples * embed_count, cap), jnp.bfloat16),
        grid=(samples // group,),
        in_specs=[
            pl.BlockSpec((group, feature_count), lambda i: (i, 0)),
            pl.BlockSpec((embed_count, feature_count), lambda i: (0, 0)),
        ],
        out_specs=pl.BlockSpec((owners, group * embed_count, cap), lambda i: (0, i, 0)),
        compiler_params=params(),
        cost_estimate=pl.CostEstimate(
            flops=2 * samples * owners * embed_count * feature_count * cap,
            bytes_accessed=2 * owners * samples * embed_count * cap,
            transcendentals=0,
        ),
        name="spread_weights",
    )(lookup_slots, lcb_weight)


def compress(spread, fetched, embed_count):
    owners, lines, cap = spread.shape
    width = fetched.shape[2]
    samples = lines // embed_count
    part = tiles_of(owners, 4)

    def kernel(spread_ref, rows_ref, out_ref, total):
        step = pl.program_id(0)
        left = jnp.concatenate([spread_ref[o] for o in range(part)], axis=1)
        right = rows_ref[...].reshape(part * cap, width)
        term = jnp.dot(left, right, preferred_element_type=jnp.float32)

        @pl.when(step == 0)
        def _():
            total[...] = term

        @pl.when(step > 0)
        def _():
            total[...] += term

        @pl.when(step == owners // part - 1)
        def _():
            for k in range(embed_count):
                piece = total[pl.ds(k, samples, stride=embed_count), :]
                out_ref[:, k * width : (k + 1) * width] = piece.astype(out_ref.dtype)

    return pl.pallas_call(
        kernel,
        out_shape=jax.ShapeDtypeStruct((samples, embed_count * width), jnp.bfloat16),
        grid=(owners // part,),
        in_specs=[
            pl.BlockSpec((part, lines, cap), lambda i: (i, 0, 0)),
            pl.BlockSpec((part, cap, width), lambda i: (i, 0, 0)),
        ],
        out_specs=pl.BlockSpec((samples, embed_count * width), lambda i: (0, 0)),
        scratch_shapes=[pltpu.VMEM((lines, width), jnp.float32)],
        compiler_params=params(),
        name="compress",
    )(spread, fetched)


def expand(spread, lead_share, embed_count):
    owners, lines, cap = spread.shape
    samples = lines // embed_count
    width = lead_share.shape[1] // embed_count
    part = tiles_of(owners, 4)

    def kernel(spread_ref, grad_ref, out_ref, tall, turned):
        @pl.when(pl.program_id(0) == 0)
        def _():
            for k in range(embed_count):
                piece = grad_ref[:, k * width : (k + 1) * width].astype(jnp.float32)
                tall[pl.ds(k, samples, stride=embed_count), :] = piece
            turned[...] = tall[...].T.astype(jnp.bfloat16)

        right = jnp.concatenate([spread_ref[o] for o in range(part)], axis=1)
        term = jnp.dot(turned[...], right, preferred_element_type=jnp.float32)
        out_ref[...] = term.T.astype(out_ref.dtype).reshape(part, cap, width)

    return pl.pallas_call(
        kernel,
        out_shape=jax.ShapeDtypeStruct((owners, cap, width), jnp.bfloat16),
        grid=(owners // part,),
        in_specs=[
            pl.BlockSpec((part, lines, cap), lambda i: (i, 0, 0)),
            pl.BlockSpec(lead_share.shape, lambda i: (0, 0)),
        ],
        out_specs=pl.BlockSpec((part, cap, width), lambda i: (i, 0, 0)),
        scratch_shapes=[
            pltpu.VMEM((lines, width), jnp.float32),
            pltpu.VMEM((width, lines), jnp.bfloat16),
        ],
        compiler_params=params(),
        name="expand",
    )(spread, lead_share)


def add_rows(targets, returned, outgoing, rows):
    count, width = returned.shape
    chunk = min(count, 1024)
    steps = count // chunk

    def kernel(targets_ref, back_ref, sent_ref, out_ref, total, terms, done):
        step = pl.program_id(0)

        @pl.when(step == 0)
        def _():
            total[...] = jnp.zeros_like(total)

        terms[...] = back_ref[...].astype(jnp.float32) + DECAY_WEIGHT * sent_ref[...].astype(
            jnp.float32
        )

        def body(group, carry):
            first = pl.multiple_of(group * UNROLL, UNROLL)
            places = [targets_ref[step * chunk + first + lane] for lane in range(UNROLL)]
            sums = [
                total[pl.ds(places[lane], 1), :] + terms[pl.ds(first + lane, 1), :]
                for lane in range(UNROLL)
            ]
            for lane in range(UNROLL):
                total[pl.ds(places[lane], 1), :] = sums[lane]
            return carry

        lax.fori_loop(0, chunk // UNROLL, body, 0)

        @pl.when(step == steps - 1)
        def _():
            copy = pltpu.make_async_copy(total.at[pl.ds(0, rows), :], out_ref, done)
            copy.start()
            copy.wait()

    return pl.pallas_call(
        kernel,
        out_shape=jax.ShapeDtypeStruct((rows, width), jnp.float32),
        grid_spec=pltpu.PrefetchScalarGridSpec(
            num_scalar_prefetch=1,
            grid=(steps,),
            in_specs=[
                pl.BlockSpec((chunk, width), lambda i, ids: (i, 0)),
                pl.BlockSpec((chunk, width), lambda i, ids: (i, 0)),
            ],
            out_specs=pl.BlockSpec(memory_space=pl.ANY),
            scratch_shapes=[
                pltpu.VMEM((rows + 8, width), jnp.float32),
                pltpu.VMEM((chunk, width), jnp.float32),
                pltpu.SemaphoreType.DMA,
            ],
        ),
        compiler_params=params(),
        name="add_rows",
    )(targets, returned, outgoing)


GROUP = 32
SMALL_LIMIT = 20 * 1024 * 1024
NT = (((1,), (1,)), ((), ()))


def dot_nt(left, right):
    return lax.dot_general(left, right, NT, preferred_element_type=jnp.float32)


def dot(left, right):
    return jnp.dot(left, right, preferred_element_type=jnp.float32)


def split_dot(left, right):
    high = left.astype(jnp.bfloat16)
    low = (left - high.astype(jnp.float32)).astype(jnp.bfloat16)
    return dot(high, right) + dot(low, right)


def same_sample(count):
    first = lax.broadcasted_iota(jnp.int32, (count * GROUP, count * GROUP), 0)
    second = lax.broadcasted_iota(jnp.int32, (count * GROUP, count * GROUP), 1)
    return (first & (GROUP - 1)) == (second & (GROUP - 1))


def stacked(ref, rows, count, width):
    return jnp.concatenate([ref[rows, k * width : (k + 1) * width] for k in range(count)], axis=0)


def repeated(proj):
    count, width = proj.shape
    lines = [jnp.broadcast_to(proj[k : k + 1, :], (GROUP, width)) for k in range(count)]
    return jnp.concatenate(lines, axis=0).astype(jnp.bfloat16)


def mix_forward(small, layer, acts, inter, scale, normed, count):
    batch, model_width = acts.shape
    width = model_width // count
    both = small[layer].astype(jnp.float32)
    proj = repeated(both[:count])
    keep = same_sample(count)
    for start in range(0, batch, GROUP):
        rows = pl.ds(start, GROUP)
        block = stacked(acts, rows, count, width)
        gram = jnp.where(keep, dot_nt(block, block), 0.0)
        mixed = split_dot(gram, proj)
        parts = [mixed[k * GROUP : (k + 1) * GROUP] for k in range(count)]
        squares = sum(part * part for part in parts)
        mean = jnp.sum(squares, axis=1, keepdims=True) * (1.0 / model_width)
        inv = lax.rsqrt(mean + EPSILON)
        scale[rows, :] = jnp.broadcast_to(inv, (GROUP, width))
        for k in range(count):
            columns = slice(k * width, (k + 1) * width)
            inter[rows, columns] = parts[k]
            gain = both[count + k : count + k + 1]
            normed[rows, columns] = (parts[k] * inv * gain).astype(jnp.bfloat16)


def up_product(normed, w_up, layer, hidden, tile=512):
    def body(step, carry):
        columns = pl.ds(pl.multiple_of(step * tile, tile), tile)
        before = dot(normed[...], w_up[layer, :, columns])
        hidden[:, columns] = jnp.maximum(before, 0.0).astype(jnp.bfloat16)
        return carry

    lax.fori_loop(0, hidden.shape[1] // tile, body, 0)


def down_product(hidden, w_down, layer, acts, out, tile=256):
    def body(step, carry):
        columns = pl.ds(pl.multiple_of(step * tile, tile), tile)
        term = dot(hidden[...], w_down[layer, :, columns])
        out[:, columns] = (acts[:, columns].astype(jnp.float32) + term).astype(jnp.bfloat16)
        return carry

    lax.fori_loop(0, out.shape[1] // tile, body, 0)


def layer_backward(small, layer, grad, acts, inter, scale, hidden, w_up, w_down, out, g_before, weighted, count):
    batch, model_width = acts.shape
    width = model_width // count
    tile = 512

    def masked(step, carry):
        columns = pl.ds(pl.multiple_of(step * tile, tile), tile)
        g_hidden = dot_nt(grad[...], w_down[layer, columns, :])
        is_open = hidden[:, columns].astype(jnp.float32) > 0.0
        g_before[:, columns] = jnp.where(is_open, g_hidden, 0.0).astype(jnp.bfloat16)
        return carry

    lax.fori_loop(0, hidden.shape[1] // tile, masked, 0)

    def to_normed(step, carry):
        columns = pl.ds(pl.multiple_of(step * 256, 256), 256)
        weighted[:, columns] = dot_nt(g_before[...], w_up[layer, columns, :])
        return carry

    lax.fori_loop(0, model_width // 256, to_normed, 0)
    both = small[layer].astype(jnp.float32)
    proj = repeated(both[:count])
    keep = same_sample(count)
    for start in range(0, batch, GROUP):
        rows = pl.ds(start, GROUP)
        columns = [slice(k * width, (k + 1) * width) for k in range(count)]
        gained = [weighted[rows, columns[k]] * both[count + k : count + k + 1] for k in range(count)]
        shared = sum(gained[k] * inter[rows, columns[k]] for k in range(count))
        mean = jnp.sum(shared, axis=1, keepdims=True) * (1.0 / model_width)
        inv = scale[rows, 0:1]
        pull = inv * inv * mean
        parts = [
            (inv * (gained[k] - inter[rows, columns[k]] * pull)).astype(jnp.bfloat16)
            for k in range(count)
        ]
        block = stacked(acts, rows, count, width)
        g_inter = jnp.concatenate(parts, axis=0)
        left = jnp.concatenate([g_inter, proj], axis=1)
        right = jnp.concatenate([proj, g_inter], axis=1)
        links = jnp.where(keep, dot_nt(left, right), 0.0)
        g_acts = split_dot(links, block)
        for k in range(count):
            piece = g_acts[k * GROUP : (k + 1) * GROUP] + grad[rows, columns[k]].astype(jnp.float32)
            out[rows, columns[k]] = piece.astype(jnp.bfloat16)


def in_vmem(shape, dtype):
    return pltpu.VMEM(shape, dtype)


def hold_weights(core, pairs):
    def kernel(core_ref, *refs):
        own, other = refs[0 : len(pairs)], refs[len(pairs) : 2 * len(pairs)]
        outs, sems = refs[2 * len(pairs) : 3 * len(pairs)], refs[3 * len(pairs)]
        here = core_ref[0]
        copies = []
        for i in range(len(pairs)):
            copies.append(pltpu.make_async_copy(own[i], outs[i].at[here], sems.at[2 * i]))
            copies.append(pltpu.make_async_copy(other[i], outs[i].at[1 - here], sems.at[2 * i + 1]))
        for copy in copies:
            copy.start()
        for copy in copies:
            copy.wait()

    return pl.pallas_call(
        kernel,
        out_shape=[in_vmem((2,) + own.shape, own.dtype) for own, other in pairs],
        in_specs=[pl.BlockSpec(memory_space=pltpu.SMEM)]
        + [pl.BlockSpec(memory_space=pl.ANY)] * (2 * len(pairs)),
        out_specs=[whole() for pair in pairs],
        scratch_shapes=[pltpu.SemaphoreType.DMA((2 * len(pairs),))],
        compiler_params=pltpu.CompilerParams(vmem_limit_bytes=SMALL_LIMIT),
        name="hold_weights",
    )(core, *[own for own, other in pairs], *[other for own, other in pairs])


def saved_shapes(batch, model_width, hidden_width, width):
    return [
        in_vmem((2, batch, hidden_width), jnp.bfloat16),
        in_vmem((2, batch, model_width), jnp.float32),
        in_vmem((2, batch, width), jnp.float32),
        in_vmem((2, batch, model_width), jnp.bfloat16),
    ]


def forward_stage(active, acts, weights, count):
    small, w_up, w_down = weights
    batch, model_width = acts.shape
    hidden_width = w_up.shape[2]
    width = model_width // count

    def kernel(active_ref, acts_ref, small_ref, up_ref, down_ref, out_ref, hid, inter, scale, kept, normed):
        @pl.when(active_ref[0] == 1)
        def _():
            kept[0] = acts_ref[...]
            for layer in (0, 1):
                mix_forward(
                    small_ref, layer, kept.at[layer], inter.at[layer], scale.at[layer], normed, count
                )
                up_product(normed, up_ref, layer, hid.at[layer])
                to = kept.at[1] if layer == 0 else out_ref
                down_product(hid.at[layer], down_ref, layer, kept.at[layer], to)

    out = pl.pallas_call(
        kernel,
        out_shape=[jax.ShapeDtypeStruct(acts.shape, jnp.bfloat16)]
        + saved_shapes(batch, model_width, hidden_width, width),
        in_specs=[pl.BlockSpec(memory_space=pltpu.SMEM)] + [whole()] * 4,
        out_specs=[whole()] * 5,
        scratch_shapes=[pltpu.VMEM((batch, model_width), jnp.bfloat16)],
        compiler_params=pltpu.CompilerParams(vmem_limit_bytes=SMALL_LIMIT),
        cost_estimate=stage_cost(4, batch, model_width, hidden_width),
        name="forward_stage",
    )(active, acts, small, w_up, w_down)
    return out[0], out[1:]


def stage_cost(products, batch, model_width, hidden_width):
    return pl.CostEstimate(
        flops=2 * products * batch * model_width * hidden_width, bytes_accessed=1 << 20, transcendentals=0
    )


def turn_stage(active, acts, top, weights, count):
    small, w_up, w_down = weights
    batch, model_width = acts.shape
    hidden_width = w_up.shape[2]
    width = model_width // count

    def kernel(active_ref, acts_ref, top_ref, small_ref, up_ref, down_ref, out_ref, hid, inter, scale, upper, grad, normed, weighted, g_before):
        @pl.when(active_ref[0] == 1)
        def _():
            mix_forward(small_ref, 0, acts_ref, inter.at[0], scale.at[0], normed, count)
            up_product(normed, up_ref, 0, hid.at[0])
            down_product(hid.at[0], down_ref, 0, acts_ref, upper)
            mix_forward(small_ref, 1, upper, inter.at[1], scale.at[1], normed, count)
            up_product(normed, up_ref, 1, hid.at[1])
            for layer, given, source, to in ((1, top_ref, upper, grad), (0, grad, acts_ref, out_ref)):
                layer_backward(
                    small_ref, layer, given, source, inter.at[layer], scale.at[layer], hid.at[layer],
                    up_ref, down_ref, to, g_before, weighted, count,
                )

    return pl.pallas_call(
        kernel,
        out_shape=jax.ShapeDtypeStruct(acts.shape, jnp.bfloat16),
        in_specs=[pl.BlockSpec(memory_space=pltpu.SMEM)] + [whole()] * 5,
        out_specs=whole(),
        scratch_shapes=[
            pltpu.VMEM((2, batch, hidden_width), jnp.bfloat16),
            pltpu.VMEM((2, batch, model_width), jnp.float32),
            pltpu.VMEM((2, batch, width), jnp.float32),
            pltpu.VMEM((batch, model_width), jnp.bfloat16),
            pltpu.VMEM((batch, model_width), jnp.bfloat16),
            pltpu.VMEM((batch, model_width), jnp.bfloat16),
            pltpu.VMEM((batch, model_width), jnp.float32),
            pltpu.VMEM((batch, hidden_width), jnp.bfloat16),
        ],
        compiler_params=pltpu.CompilerParams(vmem_limit_bytes=SMALL_LIMIT),
        cost_estimate=stage_cost(7, batch, model_width, hidden_width),
        name="turn_stage",
    )(active, acts, top, small, w_up, w_down)


def backward_stage(active, grad, saved, weights, count):
    small, w_up, w_down = weights
    batch, model_width = grad.shape
    hidden_width = w_up.shape[2]

    def kernel(active_ref, grad_ref, hid, inter, scale, kept, small_ref, up_ref, down_ref, out_ref, middle, weighted, g_before):
        @pl.when(active_ref[0] == 1)
        def _():
            for layer, given, to in ((1, grad_ref, middle), (0, middle, out_ref)):
                layer_backward(
                    small_ref, layer, given, kept.at[layer], inter.at[layer], scale.at[layer],
                    hid.at[layer], up_ref, down_ref, to, g_before, weighted, count,
                )

    return pl.pallas_call(
        kernel,
        out_shape=jax.ShapeDtypeStruct(grad.shape, jnp.bfloat16),
        in_specs=[pl.BlockSpec(memory_space=pltpu.SMEM)] + [whole()] * 8,
        out_specs=whole(),
        scratch_shapes=[
            pltpu.VMEM((batch, model_width), jnp.bfloat16),
            pltpu.VMEM((batch, model_width), jnp.float32),
            pltpu.VMEM((batch, hidden_width), jnp.bfloat16),
        ],
        compiler_params=pltpu.CompilerParams(vmem_limit_bytes=SMALL_LIMIT),
        cost_estimate=stage_cost(4, batch, model_width, hidden_width),
        name="backward_stage",
    )(active, grad, *saved, small, w_up, w_down)


def swapped(value, section_count):
    return lax.ppermute(value, "section", [(s, s ^ 1) for s in range(section_count)])


def moved(value, from_stage, to_stage):
    pairs = [(2 * from_stage + core, 2 * to_stage + core) for core in (0, 1)]
    return lax.ppermute(value, "section", pairs)


def per_device(
    emb_table,
    lcb_weight,
    fm_proj,
    norm_gain,
    w_up,
    w_down,
    top_grad,
    lookup_slot,
    wanted_rows,
    row_counts,
):
    section_count = lax.axis_size("section")
    owners = section_count * lax.axis_size("table")
    stages = section_count // 2
    stage = lax.axis_index("section") // 2
    core = lax.axis_index("section") % 2
    cap = wanted_rows.shape[2]
    rows, embed_width = emb_table.shape
    embed_count = lcb_weight.shape[0]
    look_dev = lookup_slot.shape[1]
    model_width = top_grad.shape[3]
    table_axes = ("section", "table")

    small = jnp.concatenate([fm_proj[0], norm_gain[0].reshape(embed_count, -1)], axis=0)
    other_up = swapped(w_up[0], section_count)
    other_down = swapped(w_down[0], section_count)
    other_small = swapped(small, section_count)

    picked = wanted_rows[0]
    outgoing = pick_rows(emb_table, picked.reshape(-1))
    fetched = lax.all_to_all(
        outgoing.reshape(owners, cap, embed_width), table_axes, split_axis=0, concat_axis=0, tiled=True
    )
    spread = spread_weights(lookup_slot[0], lcb_weight, owners, cap)
    smalls = jnp.stack(
        [jnp.where(core == 0, small, other_small), jnp.where(core == 0, other_small, small)]
    )
    core_id = core.astype(jnp.int32).reshape(1)
    weights = [smalls] + list(
        hold_weights(core_id, [(w_up[0], other_up), (w_down[0], other_down)])
    )
    lead = compress(spread, fetched, embed_count)

    acts = jnp.concatenate([lead] + [moved(lead, s, 0) for s in range(1, stages)], axis=0)
    top = top_grad.reshape(stages, 2, look_dev, model_width)
    top = lax.dynamic_index_in_dim(top, core, 1, keepdims=False).reshape(-1, model_width)

    def at(tick):
        return (stage == tick).astype(jnp.int32).reshape(1)

    saved = None
    for tick in range(stages - 1):
        out, fresh = forward_stage(at(tick), acts, weights, embed_count)
        if saved is None:
            saved = fresh
        else:
            saved = [jnp.where(stage == tick, new, old) for new, old in zip(fresh, saved)]
        acts = moved(out, tick, tick + 1)
    grad = turn_stage(at(stages - 1), acts, top, weights, embed_count)
    for tick in reversed(range(stages - 1)):
        grad = moved(grad, tick + 1, tick)
        grad = backward_stage(at(tick), grad, saved, weights, embed_count)

    lead_share = grad[:look_dev]
    for s in range(1, stages):
        arrived = moved(grad[s * look_dev : (s + 1) * look_dev], 0, s)
        lead_share = jnp.where(stage == s, arrived, lead_share)

    slot_grad = expand(spread, lead_share, embed_count)
    returned = lax.all_to_all(slot_grad, table_axes, split_axis=0, concat_axis=0, tiled=True)
    live_slots = jnp.arange(cap)[None, :] < row_counts[0][:, None]
    targets = jnp.where(live_slots, picked, rows).reshape(-1)
    return add_rows(targets, returned.reshape(-1, embed_width), outgoing, rows)


def solution(mesh):
    in_specs = (
        P(("section", "table"), None),
        P(),
        P("section", None, None),
        P("section", None),
        P("section", None, None),
        P("section", None, None),
        P("table", None, None, None),
        P("table", "section", None),
        P(("section", "table"), None, None),
        P(("section", "table"), None),
    )
    out_specs = P(("section", "table"), None)
    return jax.shard_map(
        per_device, mesh=mesh, in_specs=in_specs, out_specs=out_specs, check_vma=False
    )
```

```python
import jax
import jax.numpy as jnp
from jax import lax
from jax.experimental import pallas as pl
from jax.experimental.pallas import tpu as pltpu
from jax.sharding import PartitionSpec as P

EPSILON = 1e-05
DECAY_WEIGHT = 0.5
VMEM_LIMIT = 20 * 1024 * 1024
UNROLL = 16


def whole(memory_space=pltpu.VMEM):
    return pl.BlockSpec(memory_space=memory_space)


def params():
    return pltpu.CompilerParams(vmem_limit_bytes=VMEM_LIMIT)


def tiles_of(count, most):
    return max(step for step in range(1, most + 1) if count % step == 0)


def pick_rows(emb_table, picked):
    rows, width = emb_table.shape
    count = picked.shape[0]
    chunk = min(count, 1024)

    def kernel(picked_ref, table_ref, out_ref, wide, lines):
        step = pl.program_id(0)

        @pl.when(step == 0)
        def _():
            wide[...] = table_ref[...].astype(jnp.float32)

        def body(group, carry):
            first = pl.multiple_of(group * UNROLL, UNROLL)
            for lane in range(UNROLL):
                row = picked_ref[step * chunk + first + lane]
                lines[pl.ds(first + lane, 1), :] = wide[pl.ds(row, 1), :]
            return carry

        lax.fori_loop(0, chunk // UNROLL, body, 0)
        out_ref[...] = lines[...].astype(out_ref.dtype)

    return pl.pallas_call(
        kernel,
        out_shape=jax.ShapeDtypeStruct((count, width), emb_table.dtype),
        grid_spec=pltpu.PrefetchScalarGridSpec(
            num_scalar_prefetch=1,
            grid=(count // chunk,),
            in_specs=[pl.BlockSpec((rows, width), lambda i, ids: (0, 0))],
            out_specs=pl.BlockSpec((chunk, width), lambda i, ids: (i, 0)),
            scratch_shapes=[
                pltpu.VMEM((rows, width), jnp.float32),
                pltpu.VMEM((chunk, width), jnp.float32),
            ],
        ),
        compiler_params=params(),
        name="pick_rows",
    )(picked, emb_table)


def spread_weights(lookup_slots, lcb_weight, owners, cap):
    samples, feature_count = lookup_slots.shape
    embed_count = lcb_weight.shape[0]
    group = tiles_of(samples, 8)

    def kernel(slots_ref, lcb_ref, out_ref):
        lcb = lcb_ref[...].astype(jnp.float32)
        owner_of = lax.broadcasted_iota(jnp.int32, (owners, embed_count, feature_count), 0)
        column_of = lax.broadcasted_iota(jnp.int32, (cap, feature_count), 0)
        for pair in range(0, group, 2):
            made = []
            for sample in (pair, pair + 1):
                slots = slots_ref[sample : sample + 1, :]
                owner = lax.div(slots, cap)
                column = slots - owner * cap
                left = jnp.where(owner_of == owner[None], lcb[None], 0.0)
                left = left.reshape(owners * embed_count, feature_count).astype(jnp.bfloat16)
                right = jnp.where(column_of == column, 1.0, 0.0).astype(jnp.bfloat16)
                both = lax.dot_general(
                    left, right, (((1,), (1,)), ((), ())), preferred_element_type=jnp.float32
                )
                made.append(both.reshape(owners, embed_count, cap))
            rows = pl.ds(pair * embed_count, 2 * embed_count)
            out_ref[:, rows, :] = jnp.concatenate(made, axis=1).astype(out_ref.dtype)

    return pl.pallas_call(
        kernel,
        out_shape=pltpu.HBM((owners, samples * embed_count, cap), jnp.bfloat16),
        grid=(samples // group,),
        in_specs=[
            pl.BlockSpec((group, feature_count), lambda i: (i, 0)),
            pl.BlockSpec((embed_count, feature_count), lambda i: (0, 0)),
        ],
        out_specs=pl.BlockSpec((owners, group * embed_count, cap), lambda i: (0, i, 0)),
        compiler_params=params(),
        cost_estimate=pl.CostEstimate(
            flops=2 * samples * owners * embed_count * feature_count * cap,
            bytes_accessed=2 * owners * samples * embed_count * cap,
            transcendentals=0,
        ),
        name="spread_weights",
    )(lookup_slots, lcb_weight)


def compress(spread, fetched, embed_count):
    owners, lines, cap = spread.shape
    width = fetched.shape[2]
    samples = lines // embed_count
    part = tiles_of(owners, 4)

    def kernel(spread_ref, rows_ref, out_ref, total):
        step = pl.program_id(0)
        left = jnp.concatenate([spread_ref[o] for o in range(part)], axis=1)
        right = rows_ref[...].reshape(part * cap, width)
        term = jnp.dot(left, right, preferred_element_type=jnp.float32)

        @pl.when(step == 0)
        def _():
            total[...] = term

        @pl.when(step > 0)
        def _():
            total[...] += term

        @pl.when(step == owners // part - 1)
        def _():
            for k in range(embed_count):
                piece = total[pl.ds(k, samples, stride=embed_count), :]
                out_ref[:, k * width : (k + 1) * width] = piece.astype(out_ref.dtype)

    return pl.pallas_call(
        kernel,
        out_shape=jax.ShapeDtypeStruct((samples, embed_count * width), jnp.bfloat16),
        grid=(owners // part,),
        in_specs=[
            pl.BlockSpec((part, lines, cap), lambda i: (i, 0, 0)),
            pl.BlockSpec((part, cap, width), lambda i: (i, 0, 0)),
        ],
        out_specs=pl.BlockSpec((samples, embed_count * width), lambda i: (0, 0)),
        scratch_shapes=[pltpu.VMEM((lines, width), jnp.float32)],
        compiler_params=params(),
        name="compress",
    )(spread, fetched)


def expand(spread, lead_share, embed_count):
    owners, lines, cap = spread.shape
    samples = lines // embed_count
    width = lead_share.shape[1] // embed_count
    part = tiles_of(owners, 4)

    def kernel(spread_ref, grad_ref, out_ref, tall, turned):
        @pl.when(pl.program_id(0) == 0)
        def _():
            for k in range(embed_count):
                piece = grad_ref[:, k * width : (k + 1) * width].astype(jnp.float32)
                tall[pl.ds(k, samples, stride=embed_count), :] = piece
            turned[...] = tall[...].T.astype(jnp.bfloat16)

        right = jnp.concatenate([spread_ref[o] for o in range(part)], axis=1)
        term = jnp.dot(turned[...], right, preferred_element_type=jnp.float32)
        out_ref[...] = term.T.astype(out_ref.dtype).reshape(part, cap, width)

    return pl.pallas_call(
        kernel,
        out_shape=jax.ShapeDtypeStruct((owners, cap, width), jnp.bfloat16),
        grid=(owners // part,),
        in_specs=[
            pl.BlockSpec((part, lines, cap), lambda i: (i, 0, 0)),
            pl.BlockSpec(lead_share.shape, lambda i: (0, 0)),
        ],
        out_specs=pl.BlockSpec((part, cap, width), lambda i: (i, 0, 0)),
        scratch_shapes=[
            pltpu.VMEM((lines, width), jnp.float32),
            pltpu.VMEM((width, lines), jnp.bfloat16),
        ],
        compiler_params=params(),
        name="expand",
    )(spread, lead_share)


def add_rows(targets, returned, outgoing, rows):
    count, width = returned.shape
    chunk = min(count, 1024)
    steps = count // chunk

    def kernel(targets_ref, back_ref, sent_ref, out_ref, total, terms, done):
        step = pl.program_id(0)

        @pl.when(step == 0)
        def _():
            total[...] = jnp.zeros_like(total)

        terms[...] = back_ref[...].astype(jnp.float32) + DECAY_WEIGHT * sent_ref[...].astype(
            jnp.float32
        )

        def body(group, carry):
            first = pl.multiple_of(group * UNROLL, UNROLL)
            places = [targets_ref[step * chunk + first + lane] for lane in range(UNROLL)]
            sums = [
                total[pl.ds(places[lane], 1), :] + terms[pl.ds(first + lane, 1), :]
                for lane in range(UNROLL)
            ]
            for lane in range(UNROLL):
                total[pl.ds(places[lane], 1), :] = sums[lane]
            return carry

        lax.fori_loop(0, chunk // UNROLL, body, 0)

        @pl.when(step == steps - 1)
        def _():
            copy = pltpu.make_async_copy(total.at[pl.ds(0, rows), :], out_ref, done)
            copy.start()
            copy.wait()

    return pl.pallas_call(
        kernel,
        out_shape=jax.ShapeDtypeStruct((rows, width), jnp.float32),
        grid_spec=pltpu.PrefetchScalarGridSpec(
            num_scalar_prefetch=1,
            grid=(steps,),
            in_specs=[
                pl.BlockSpec((chunk, width), lambda i, ids: (i, 0)),
                pl.BlockSpec((chunk, width), lambda i, ids: (i, 0)),
            ],
            out_specs=pl.BlockSpec(memory_space=pl.ANY),
            scratch_shapes=[
                pltpu.VMEM((rows + 8, width), jnp.float32),
                pltpu.VMEM((chunk, width), jnp.float32),
                pltpu.SemaphoreType.DMA,
            ],
        ),
        compiler_params=params(),
        name="add_rows",
    )(targets, returned, outgoing)


GROUP = 32
STAGE_LIMIT = 44 * 1024 * 1024
NT = (((1,), (1,)), ((), ()))


def dot_nt(left, right):
    return lax.dot_general(left, right, NT, preferred_element_type=jnp.float32)


def dot(left, right):
    return jnp.dot(left, right, preferred_element_type=jnp.float32)


def split_dot(left, right):
    high = left.astype(jnp.bfloat16)
    low = (left - high.astype(jnp.float32)).astype(jnp.bfloat16)
    return dot(high, right) + dot(low, right)


def same_sample(count):
    first = lax.broadcasted_iota(jnp.int32, (count * GROUP, count * GROUP), 0)
    second = lax.broadcasted_iota(jnp.int32, (count * GROUP, count * GROUP), 1)
    return (first & (GROUP - 1)) == (second & (GROUP - 1))


def stacked(ref, rows, count, width):
    return jnp.concatenate([ref[rows, k * width : (k + 1) * width] for k in range(count)], axis=0)


def repeated(proj):
    count, width = proj.shape
    lines = [jnp.broadcast_to(proj[k : k + 1, :], (GROUP, width)) for k in range(count)]
    return jnp.concatenate(lines, axis=0).astype(jnp.bfloat16)


def mix_forward(small, layer, acts, inter, scale, normed, count):
    batch, model_width = acts.shape
    width = model_width // count
    both = small[layer].astype(jnp.float32)
    proj = repeated(both[:count])
    keep = same_sample(count)
    for start in range(0, batch, GROUP):
        rows = pl.ds(start, GROUP)
        block = stacked(acts, rows, count, width)
        gram = jnp.where(keep, dot_nt(block, block), 0.0)
        mixed = split_dot(gram, proj)
        parts = [mixed[k * GROUP : (k + 1) * GROUP] for k in range(count)]
        squares = sum(part * part for part in parts)
        mean = jnp.sum(squares, axis=1, keepdims=True) * (1.0 / model_width)
        inv = lax.rsqrt(mean + EPSILON)
        scale[rows, :] = jnp.broadcast_to(inv, (GROUP, width))
        for k in range(count):
            columns = slice(k * width, (k + 1) * width)
            inter[rows, columns] = parts[k]
            gain = both[count + k : count + k + 1]
            normed[rows, columns] = (parts[k] * inv * gain).astype(jnp.bfloat16)


def hidden_tile(hidden_width):
    return min(hidden_width, 512)


def model_tile(model_width):
    return min(model_width, 256)


def tile_at(step, size):
    return pl.ds(pl.multiple_of(step * size, size), size)


class Stream:
    def __init__(self, mine, own, other, held, sems, axis, size):
        self.mine, self.own, self.other, self.held, self.sems = mine, own, other, held, sems
        self.axis, self.size = axis, size
        self.tiles = own.shape[axis] // size

    def copy(self, source, step):
        cut = tile_at(step, self.size)
        index = (slice(None), cut) if self.axis == 1 else (cut, slice(None))
        return pltpu.make_async_copy(source.at[index], self.held.at[index], self.sems.at[step])

    def start(self):
        @pl.when(self.mine)
        def _():
            for step in range(self.tiles):
                self.copy(self.own, step).start()

        @pl.when(jnp.logical_not(self.mine))
        def _():
            for step in range(self.tiles):
                self.copy(self.other, step).start()

    def wait(self, step):
        self.copy(self.own, step).wait()


def no_wait(step):
    return None


def up_product(normed, w_up, hidden, wait):
    tile = hidden_tile(hidden.shape[1])

    def body(step, carry):
        wait(step)
        columns = tile_at(step, tile)
        before = dot(normed[...], w_up[:, columns])
        hidden[:, columns] = jnp.maximum(before, 0.0).astype(jnp.bfloat16)
        return carry

    lax.fori_loop(0, hidden.shape[1] // tile, body, 0)


def down_product(hidden, w_down, acts, out, wait):
    tile = model_tile(out.shape[1])

    def body(step, carry):
        wait(step)
        columns = tile_at(step, tile)
        term = dot(hidden[...], w_down[:, columns])
        out[:, columns] = (acts[:, columns].astype(jnp.float32) + term).astype(jnp.bfloat16)
        return carry

    lax.fori_loop(0, out.shape[1] // tile, body, 0)


def down_back(grad, w_down, hidden, out, wait):
    tile = hidden_tile(out.shape[1])

    def body(step, carry):
        wait(step)
        columns = tile_at(step, tile)
        g_hidden = dot_nt(grad[...], w_down[columns, :])
        if hidden is not None:
            is_open = hidden[:, columns].astype(jnp.float32) > 0.0
            g_hidden = jnp.where(is_open, g_hidden, 0.0)
        out[:, columns] = g_hidden.astype(jnp.bfloat16)
        return carry

    lax.fori_loop(0, out.shape[1] // tile, body, 0)


def up_back(g_before, w_up, weighted, wait):
    tile = model_tile(weighted.shape[1])

    def body(step, carry):
        wait(step)
        columns = tile_at(step, tile)
        weighted[:, columns] = dot_nt(g_before[...], w_up[columns, :])
        return carry

    lax.fori_loop(0, weighted.shape[1] // tile, body, 0)


def mix_backward(small, layer, grad, acts, inter, scale, weighted, out, count):
    batch, model_width = acts.shape
    width = model_width // count
    both = small[layer].astype(jnp.float32)
    proj = repeated(both[:count])
    keep = same_sample(count)
    for start in range(0, batch, GROUP):
        rows = pl.ds(start, GROUP)
        columns = [slice(k * width, (k + 1) * width) for k in range(count)]
        gained = [weighted[rows, columns[k]] * both[count + k : count + k + 1] for k in range(count)]
        shared = sum(gained[k] * inter[rows, columns[k]] for k in range(count))
        mean = jnp.sum(shared, axis=1, keepdims=True) * (1.0 / model_width)
        inv = scale[rows, 0:1]
        pull = inv * inv * mean
        parts = [
            (inv * (gained[k] - inter[rows, columns[k]] * pull)).astype(jnp.bfloat16)
            for k in range(count)
        ]
        block = stacked(acts, rows, count, width)
        g_inter = jnp.concatenate(parts, axis=0)
        left = jnp.concatenate([g_inter, proj], axis=1)
        right = jnp.concatenate([proj, g_inter], axis=1)
        links = jnp.where(keep, dot_nt(left, right), 0.0)
        g_acts = split_dot(links, block)
        for k in range(count):
            piece = g_acts[k * GROUP : (k + 1) * GROUP] + grad[rows, columns[k]].astype(jnp.float32)
            out[rows, columns[k]] = piece.astype(jnp.bfloat16)


def saved_shapes(batch, model_width, hidden_width, width):
    return [
        jax.ShapeDtypeStruct((2, batch, hidden_width), jnp.bfloat16),
        jax.ShapeDtypeStruct((2, batch, model_width), jnp.float32),
        jax.ShapeDtypeStruct((2, batch, width), jnp.float32),
        jax.ShapeDtypeStruct((2, batch, model_width), jnp.bfloat16),
    ]


def weight_specs():
    return [whole()] + [whole(pl.ANY)] * 4


def weight_scratch(model_width, hidden_width):
    tiles = max(hidden_width // hidden_tile(hidden_width), model_width // model_tile(model_width))
    return [
        pltpu.VMEM((2, model_width, hidden_width), jnp.bfloat16),
        pltpu.VMEM((2, hidden_width, model_width), jnp.bfloat16),
        pltpu.SemaphoreType.DMA((4, tiles)),
    ]


def streams_of(core, weights, held, forward):
    own_up, other_up, own_down, other_down = weights
    held_up, held_down, sems = held
    model_width, hidden_width = own_up.shape
    wide, narrow = hidden_tile(hidden_width), model_tile(model_width)
    made = []
    for layer in (0, 1):
        mine = core == layer
        up_forward, down_forward = forward[layer]
        up_cut = (1, wide) if up_forward else (0, narrow)
        down_cut = (1, narrow) if down_forward else (0, wide)
        made.append(
            (
                Stream(mine, own_up, other_up, held_up.at[layer], sems.at[2 * layer], *up_cut),
                Stream(mine, own_down, other_down, held_down.at[layer], sems.at[2 * layer + 1], *down_cut),
            )
        )
    return made


def stage_cost(products, batch, model_width, hidden_width):
    return pl.CostEstimate(
        flops=2 * products * batch * model_width * hidden_width, bytes_accessed=1 << 20, transcendentals=0
    )


def stage_params():
    return pltpu.CompilerParams(vmem_limit_bytes=STAGE_LIMIT)


def forward_stage(place, acts, top, weights, count):
    batch, model_width = acts.shape
    hidden_width = weights[1].shape[1]
    width = model_width // count

    def kernel(place_ref, acts_ref, top_ref, small_ref, *refs):
        matrices, refs = refs[:4], refs[4:]
        out_ref, hid, inter, scale, kept, g_hidden = refs[:6]
        held, normed = refs[6:9], refs[9]
        core = place_ref[0]

        @pl.when(place_ref[1] == 1)
        def _():
            layers = streams_of(core, matrices, held, [(True, True), (True, True)])
            for up, down in layers:
                up.start()
                down.start()
            kept[0] = acts_ref[...]
            for layer, (up, down) in enumerate(layers):
                mix_forward(
                    small_ref, layer, kept.at[layer], inter.at[layer], scale.at[layer], normed, count
                )
                up_product(normed, up.held, hid.at[layer], up.wait)
                to = kept.at[1] if layer == 0 else out_ref
                down_product(hid.at[layer], down.held, kept.at[layer], to, down.wait)

        @pl.when(place_ref[2] == 1)
        def _():
            layers = streams_of(core, matrices, held, [(True, True), (True, False)])
            down = layers[1][1]
            down.start()
            down_back(top_ref, down.held, None, g_hidden, down.wait)

    out = pl.pallas_call(
        kernel,
        out_shape=[jax.ShapeDtypeStruct(acts.shape, jnp.bfloat16)]
        + saved_shapes(batch, model_width, hidden_width, width)
        + [jax.ShapeDtypeStruct((batch, hidden_width), jnp.bfloat16)],
        in_specs=[whole(pltpu.SMEM), whole(), whole()] + weight_specs(),
        out_specs=[whole()] * 6,
        scratch_shapes=weight_scratch(model_width, hidden_width)
        + [pltpu.VMEM((batch, model_width), jnp.bfloat16)],
        compiler_params=stage_params(),
        cost_estimate=stage_cost(4, batch, model_width, hidden_width),
        name="forward_stage",
    )(place, acts, top, *weights)
    return out[0], out[1:5], out[5]


def turn_stage(place, acts, top, g_hidden, weights, count):
    batch, model_width = acts.shape
    hidden_width = weights[1].shape[1]
    width = model_width // count

    def kernel(place_ref, acts_ref, top_ref, ghid_ref, small_ref, *refs):
        matrices, refs = refs[:4], refs[4:]
        out_ref, held = refs[0], refs[1:4]
        hid, inter, scale, upper, grad, normed, weighted, g_before = refs[4:]

        @pl.when(place_ref[1] == 1)
        def _():
            layers = streams_of(place_ref[0], matrices, held, [(True, True), (True, True)])
            (up0, down0), (up1, down1) = layers
            for stream in (up0, down0, up1):
                stream.start()
            mix_forward(small_ref, 0, acts_ref, inter.at[0], scale.at[0], normed, count)
            up_product(normed, up0.held, hid, up0.wait)
            down_product(hid, down0.held, acts_ref, upper, down0.wait)
            mix_forward(small_ref, 1, upper, inter.at[1], scale.at[1], normed, count)
            tile = hidden_tile(hidden_width)

            def masked(step, carry):
                up1.wait(step)
                columns = tile_at(step, tile)
                before = dot(normed[...], up1.held[:, columns])
                g_open = jnp.where(before > 0.0, ghid_ref[:, columns].astype(jnp.float32), 0.0)
                g_before[:, columns] = g_open.astype(jnp.bfloat16)
                return carry

            lax.fori_loop(0, hidden_width // tile, masked, 0)
            up_back(g_before, up1.held, weighted, no_wait)
            mix_backward(small_ref, 1, top_ref, upper, inter.at[1], scale.at[1], weighted, grad, count)
            down_back(grad, down0.held, hid, g_before, no_wait)
            up_back(g_before, up0.held, weighted, no_wait)
            mix_backward(small_ref, 0, grad, acts_ref, inter.at[0], scale.at[0], weighted, out_ref, count)

    return pl.pallas_call(
        kernel,
        out_shape=jax.ShapeDtypeStruct(acts.shape, jnp.bfloat16),
        in_specs=[whole(pltpu.SMEM)] + [whole()] * 3 + weight_specs(),
        out_specs=whole(),
        scratch_shapes=weight_scratch(model_width, hidden_width)
        + [
            pltpu.VMEM((batch, hidden_width), jnp.bfloat16),
            pltpu.VMEM((2, batch, model_width), jnp.float32),
            pltpu.VMEM((2, batch, width), jnp.float32),
            pltpu.VMEM((batch, model_width), jnp.bfloat16),
            pltpu.VMEM((batch, model_width), jnp.bfloat16),
            pltpu.VMEM((batch, model_width), jnp.bfloat16),
            pltpu.VMEM((batch, model_width), jnp.float32),
            pltpu.VMEM((batch, hidden_width), jnp.bfloat16),
        ],
        compiler_params=stage_params(),
        cost_estimate=stage_cost(6, batch, model_width, hidden_width),
        name="turn_stage",
    )(place, acts, top, g_hidden, *weights)


def backward_stage(place, grad, saved, weights, count):
    batch, model_width = grad.shape
    hidden_width = weights[1].shape[1]

    def kernel(place_ref, grad_ref, hid, inter, scale, kept, small_ref, *refs):
        matrices, refs = refs[:4], refs[4:]
        out_ref, held = refs[0], refs[1:4]
        middle, weighted, g_before = refs[4:]

        @pl.when(place_ref[1] == 1)
        def _():
            layers = streams_of(place_ref[0], matrices, held, [(False, False), (False, False)])
            for up, down in reversed(layers):
                down.start()
                up.start()
            for layer, given, to in ((1, grad_ref, middle), (0, middle, out_ref)):
                up, down = layers[layer]
                down_back(given, down.held, hid.at[layer], g_before, down.wait)
                up_back(g_before, up.held, weighted, up.wait)
                mix_backward(
                    small_ref, layer, given, kept.at[layer], inter.at[layer], scale.at[layer],
                    weighted, to, count,
                )

    return pl.pallas_call(
        kernel,
        out_shape=jax.ShapeDtypeStruct(grad.shape, jnp.bfloat16),
        in_specs=[whole(pltpu.SMEM)] + [whole()] * 5 + weight_specs(),
        out_specs=whole(),
        scratch_shapes=weight_scratch(model_width, hidden_width)
        + [
            pltpu.VMEM((batch, model_width), jnp.bfloat16),
            pltpu.VMEM((batch, model_width), jnp.float32),
            pltpu.VMEM((batch, hidden_width), jnp.bfloat16),
        ],
        compiler_params=stage_params(),
        cost_estimate=stage_cost(4, batch, model_width, hidden_width),
        name="backward_stage",
    )(place, grad, *saved, *weights)


def swapped(value, section_count):
    return lax.ppermute(value, "section", [(s, s ^ 1) for s in range(section_count)])


def moved(value, from_stage, to_stage):
    pairs = [(2 * from_stage + core, 2 * to_stage + core) for core in (0, 1)]
    return lax.ppermute(value, "section", pairs)


def per_device(
    emb_table,
    lcb_weight,
    fm_proj,
    norm_gain,
    w_up,
    w_down,
    top_grad,
    lookup_slot,
    wanted_rows,
    row_counts,
):
    section_count = lax.axis_size("section")
    owners = section_count * lax.axis_size("table")
    stages = section_count // 2
    stage = lax.axis_index("section") // 2
    core = lax.axis_index("section") % 2
    cap = wanted_rows.shape[2]
    rows, embed_width = emb_table.shape
    embed_count = lcb_weight.shape[0]
    look_dev = lookup_slot.shape[1]
    model_width = top_grad.shape[3]
    table_axes = ("section", "table")

    small = jnp.concatenate([fm_proj[0], norm_gain[0].reshape(embed_count, -1)], axis=0)
    other_up = swapped(w_up[0], section_count)
    other_down = swapped(w_down[0], section_count)
    other_small = swapped(small, section_count)

    picked = wanted_rows[0]
    outgoing = pick_rows(emb_table, picked.reshape(-1))
    fetched = lax.all_to_all(
        outgoing.reshape(owners, cap, embed_width), table_axes, split_axis=0, concat_axis=0, tiled=True
    )
    spread = spread_weights(lookup_slot[0], lcb_weight, owners, cap)
    smalls = jnp.stack(
        [jnp.where(core == 0, small, other_small), jnp.where(core == 0, other_small, small)]
    )
    weights = [smalls, w_up[0], other_up, w_down[0], other_down]
    lead = compress(spread, fetched, embed_count)

    acts = jnp.concatenate([lead] + [moved(lead, s, 0) for s in range(1, stages)], axis=0)
    top = top_grad.reshape(stages, 2, look_dev, model_width)
    top = lax.dynamic_index_in_dim(top, core, 1, keepdims=False).reshape(-1, model_width)

    def at(tick):
        is_last = (stage == stages - 1) & (tick == 0)
        return jnp.stack([core, stage == tick, is_last]).astype(jnp.int32)

    saved = None
    for tick in range(stages - 1):
        out, fresh, product = forward_stage(at(tick), acts, top, weights, embed_count)
        if saved is None:
            saved, g_hidden = fresh, product
        else:
            saved = [jnp.where(stage == tick, new, old) for new, old in zip(fresh, saved)]
        acts = moved(out, tick, tick + 1)
    grad = turn_stage(at(stages - 1), acts, top, g_hidden, weights, embed_count)
    for tick in reversed(range(stages - 1)):
        grad = moved(grad, tick + 1, tick)
        grad = backward_stage(at(tick), grad, saved, weights, embed_count)

    lead_share = grad[:look_dev]
    for s in range(1, stages):
        arrived = moved(grad[s * look_dev : (s + 1) * look_dev], 0, s)
        lead_share = jnp.where(stage == s, arrived, lead_share)

    slot_grad = expand(spread, lead_share, embed_count)
    returned = lax.all_to_all(slot_grad, table_axes, split_axis=0, concat_axis=0, tiled=True)
    live_slots = jnp.arange(cap)[None, :] < row_counts[0][:, None]
    targets = jnp.where(live_slots, picked, rows).reshape(-1)
    return add_rows(targets, returned.reshape(-1, embed_width), outgoing, rows)


def solution(mesh):
    in_specs = (
        P(("section", "table"), None),
        P(),
        P("section", None, None),
        P("section", None),
        P("section", None, None),
        P("section", None, None),
        P("table", None, None, None),
        P("table", "section", None),
        P(("section", "table"), None, None),
        P(("section", "table"), None),
    )
    out_specs = P(("section", "table"), None)
    return jax.shard_map(
        per_device, mesh=mesh, in_specs=in_specs, out_specs=out_specs, check_vma=False
    )
```

```python
import jax
import jax.numpy as jnp
from jax import lax
from jax.experimental import pallas as pl
from jax.experimental.pallas import tpu as pltpu
from jax.sharding import PartitionSpec as P

EPSILON = 1e-05
DECAY_WEIGHT = 0.5
VMEM_LIMIT = 28 * 1024 * 1024
UNROLL = 32


def whole(memory_space=pltpu.VMEM):
    return pl.BlockSpec(memory_space=memory_space)


def params():
    return pltpu.CompilerParams(vmem_limit_bytes=VMEM_LIMIT)


def tiles_of(count, most):
    return max(step for step in range(1, most + 1) if count % step == 0)


def pick_rows(emb_table, picked):
    rows, width = emb_table.shape
    count = picked.shape[0]
    chunk = min(count, 1024)

    def kernel(picked_ref, table_ref, out_ref, wide, lines):
        wide[...] = table_ref[...].astype(jnp.float32)

        def fill(part, carry):
            base = pl.multiple_of(part * chunk, chunk)

            def body(group, inner):
                first = pl.multiple_of(group * UNROLL, UNROLL)
                for lane in range(UNROLL):
                    row = picked_ref[base + first + lane]
                    lines[pl.ds(first + lane, 1), :] = wide[pl.ds(row, 1), :]
                return inner

            lax.fori_loop(0, chunk // UNROLL, body, 0)
            out_ref[pl.ds(base, chunk), :] = lines[...].astype(out_ref.dtype)
            return carry

        lax.fori_loop(0, count // chunk, fill, 0)

    return pl.pallas_call(
        kernel,
        out_shape=jax.ShapeDtypeStruct((count, width), emb_table.dtype),
        in_specs=[whole(pltpu.SMEM), whole()],
        out_specs=whole(),
        scratch_shapes=[
            pltpu.VMEM((rows, width), jnp.float32),
            pltpu.VMEM((chunk, width), jnp.float32),
        ],
        compiler_params=params(),
        name="pick_rows",
    )(picked, emb_table)


def spread_weights(lookup_slots, lcb_weight, owners, cap):
    samples, feature_count = lookup_slots.shape
    embed_count = lcb_weight.shape[0]
    group = tiles_of(samples, 8)

    def kernel(slots_ref, lcb_ref, out_ref):
        lcb = lcb_ref[...].astype(jnp.float32)
        owner_of = lax.broadcasted_iota(jnp.int32, (owners, embed_count, feature_count), 0)
        column_of = lax.broadcasted_iota(jnp.int32, (cap, feature_count), 0)
        for pair in range(0, group, 2):
            made = []
            for sample in (pair, pair + 1):
                slots = slots_ref[sample : sample + 1, :]
                owner = lax.div(slots, cap)
                column = slots - owner * cap
                left = jnp.where(owner_of == owner[None], lcb[None], 0.0)
                left = left.reshape(owners * embed_count, feature_count).astype(jnp.bfloat16)
                right = jnp.where(column_of == column, 1.0, 0.0).astype(jnp.bfloat16)
                both = lax.dot_general(
                    left, right, (((1,), (1,)), ((), ())), preferred_element_type=jnp.float32
                )
                made.append(both.reshape(owners, embed_count, cap))
            rows = pl.ds(pair * embed_count, 2 * embed_count)
            out_ref[:, rows, :] = jnp.concatenate(made, axis=1).astype(out_ref.dtype)

    return pl.pallas_call(
        kernel,
        out_shape=pltpu.HBM((owners, samples * embed_count, cap), jnp.bfloat16),
        grid=(samples // group,),
        in_specs=[
            pl.BlockSpec((group, feature_count), lambda i: (i, 0)),
            pl.BlockSpec((embed_count, feature_count), lambda i: (0, 0)),
        ],
        out_specs=pl.BlockSpec((owners, group * embed_count, cap), lambda i: (0, i, 0)),
        compiler_params=params(),
        cost_estimate=pl.CostEstimate(
            flops=2 * samples * owners * embed_count * feature_count * cap,
            bytes_accessed=2 * owners * samples * embed_count * cap,
            transcendentals=0,
        ),
        name="spread_weights",
    )(lookup_slots, lcb_weight)


def compress(spread, fetched, embed_count):
    owners, lines, cap = spread.shape
    width = fetched.shape[2]
    samples = lines // embed_count
    part = tiles_of(owners, 4)
    steps = owners // part

    def kernel(spread_ref, rows_ref, out_ref, held, total, sems):
        def copy(step):
            piece = tile_at(step, part)
            return pltpu.make_async_copy(spread_ref.at[piece], held.at[piece], sems.at[step])

        for step in range(steps):
            copy(step).start()
        total[...] = jnp.zeros_like(total)

        def body(step, carry):
            copy(step).wait()
            first = step * part
            left = jnp.concatenate([held[first + o] for o in range(part)], axis=1)
            right = rows_ref[tile_at(step, part)].reshape(part * cap, width)
            total[...] += jnp.dot(left, right, preferred_element_type=jnp.float32)
            return carry

        lax.fori_loop(0, steps, body, 0)
        for k in range(embed_count):
            piece = total[pl.ds(k, samples, stride=embed_count), :]
            out_ref[:, k * width : (k + 1) * width] = piece.astype(out_ref.dtype)

    return pl.pallas_call(
        kernel,
        out_shape=jax.ShapeDtypeStruct((samples, embed_count * width), jnp.bfloat16),
        in_specs=[whole(pltpu.HBM), whole()],
        out_specs=whole(),
        scratch_shapes=[
            pltpu.VMEM(spread.shape, jnp.bfloat16),
            pltpu.VMEM((lines, width), jnp.float32),
            pltpu.SemaphoreType.DMA((steps,)),
        ],
        compiler_params=params(),
        name="compress",
    )(spread, fetched)


def expand(spread, lead_share, embed_count):
    owners, lines, cap = spread.shape
    samples = lines // embed_count
    width = lead_share.shape[1] // embed_count
    part = tiles_of(owners, 4)

    def kernel(spread_ref, grad_ref, out_ref, tall, turned):
        for k in range(embed_count):
            piece = grad_ref[:, k * width : (k + 1) * width].astype(jnp.float32)
            tall[pl.ds(k, samples, stride=embed_count), :] = piece
        turned[...] = tall[...].T.astype(jnp.bfloat16)

        def body(step, carry):
            first = step * part
            right = jnp.concatenate([spread_ref[first + o] for o in range(part)], axis=1)
            term = jnp.dot(turned[...], right, preferred_element_type=jnp.float32)
            piece = term.T.astype(out_ref.dtype).reshape(part, cap, width)
            out_ref[tile_at(step, part)] = piece
            return carry

        lax.fori_loop(0, owners // part, body, 0)

    return pl.pallas_call(
        kernel,
        out_shape=jax.ShapeDtypeStruct((owners, cap, width), jnp.bfloat16),
        in_specs=[whole(), whole()],
        out_specs=whole(),
        scratch_shapes=[
            pltpu.VMEM((lines, width), jnp.float32),
            pltpu.VMEM((width, lines), jnp.bfloat16),
        ],
        compiler_params=params(),
        name="expand",
    )(spread, lead_share)


def add_rows(targets, returned, outgoing, rows):
    count, width = returned.shape
    chunk = min(count, 1024)

    def kernel(targets_ref, back_ref, sent_ref, out_ref, total, terms, done):
        total[...] = jnp.zeros_like(total)

        def fill(part, carry):
            base = pl.multiple_of(part * chunk, chunk)
            lines = pl.ds(base, chunk)
            terms[...] = back_ref[lines, :].astype(jnp.float32) + DECAY_WEIGHT * sent_ref[
                lines, :
            ].astype(jnp.float32)

            def body(group, inner):
                first = pl.multiple_of(group * UNROLL, UNROLL)
                places = [targets_ref[base + first + lane] for lane in range(UNROLL)]
                sums = [
                    total[pl.ds(places[lane], 1), :] + terms[pl.ds(first + lane, 1), :]
                    for lane in range(UNROLL)
                ]
                for lane in range(UNROLL):
                    total[pl.ds(places[lane], 1), :] = sums[lane]
                return inner

            lax.fori_loop(0, chunk // UNROLL, body, 0)
            return carry

        lax.fori_loop(0, count // chunk, fill, 0)
        copy = pltpu.make_async_copy(total.at[pl.ds(0, rows), :], out_ref, done)
        copy.start()
        copy.wait()

    return pl.pallas_call(
        kernel,
        out_shape=jax.ShapeDtypeStruct((rows, width), jnp.float32),
        in_specs=[whole(pltpu.SMEM), whole(), whole()],
        out_specs=whole(pl.ANY),
        scratch_shapes=[
            pltpu.VMEM((rows + 8, width), jnp.float32),
            pltpu.VMEM((chunk, width), jnp.float32),
            pltpu.SemaphoreType.DMA,
        ],
        compiler_params=params(),
        name="add_rows",
    )(targets, returned, outgoing)


GROUP = 32
STAGE_LIMIT = 44 * 1024 * 1024
NT = (((1,), (1,)), ((), ()))


def dot_nt(left, right):
    return lax.dot_general(left, right, NT, preferred_element_type=jnp.float32)


def dot(left, right):
    return jnp.dot(left, right, preferred_element_type=jnp.float32)


def split_dot(left, right):
    high = left.astype(jnp.bfloat16)
    low = (left - high.astype(jnp.float32)).astype(jnp.bfloat16)
    return dot(high, right) + dot(low, right)


def same_sample(count):
    first = lax.broadcasted_iota(jnp.int32, (count * GROUP, count * GROUP), 0)
    second = lax.broadcasted_iota(jnp.int32, (count * GROUP, count * GROUP), 1)
    return (first & (GROUP - 1)) == (second & (GROUP - 1))


def stacked(ref, rows, count, width):
    return jnp.concatenate([ref[rows, k * width : (k + 1) * width] for k in range(count)], axis=0)


def repeated(proj):
    count, width = proj.shape
    lines = [jnp.broadcast_to(proj[k : k + 1, :], (GROUP, width)) for k in range(count)]
    return jnp.concatenate(lines, axis=0).astype(jnp.bfloat16)


def mix_forward(small, layer, acts, inter, scale, normed, count):
    batch, model_width = acts.shape
    width = model_width // count
    both = small[layer].astype(jnp.float32)
    proj = repeated(both[:count])
    keep = same_sample(count)
    for start in range(0, batch, GROUP):
        rows = pl.ds(start, GROUP)
        block = stacked(acts, rows, count, width)
        gram = jnp.where(keep, dot_nt(block, block), 0.0)
        mixed = split_dot(gram, proj)
        parts = [mixed[k * GROUP : (k + 1) * GROUP] for k in range(count)]
        squares = sum(part * part for part in parts)
        mean = jnp.sum(squares, axis=1, keepdims=True) * (1.0 / model_width)
        inv = lax.rsqrt(mean + EPSILON)
        scale[rows, :] = jnp.broadcast_to(inv, (GROUP, width))
        for k in range(count):
            columns = slice(k * width, (k + 1) * width)
            inter[rows, columns] = parts[k]
            gain = both[count + k : count + k + 1]
            normed[rows, columns] = (parts[k] * inv * gain).astype(jnp.bfloat16)


def hidden_tile(hidden_width):
    return min(hidden_width, 512)


def model_tile(model_width):
    return min(model_width, 256)


def tile_at(step, size):
    return pl.ds(pl.multiple_of(step * size, size), size)


class Stream:
    def __init__(self, mine, own, other, held, sems, axis, size):
        self.mine, self.own, self.other, self.held, self.sems = mine, own, other, held, sems
        self.axis, self.size = axis, size
        self.tiles = own.shape[axis] // size

    def copy(self, source, step):
        cut = tile_at(step, self.size)
        index = (slice(None), cut) if self.axis == 1 else (cut, slice(None))
        return pltpu.make_async_copy(source.at[index], self.held.at[index], self.sems.at[step])

    def start(self):
        @pl.when(self.mine)
        def _():
            for step in range(self.tiles):
                self.copy(self.own, step).start()

        @pl.when(jnp.logical_not(self.mine))
        def _():
            for step in range(self.tiles):
                self.copy(self.other, step).start()

    def wait(self, step):
        self.copy(self.own, step).wait()


def no_wait(step):
    return None


def up_product(normed, w_up, hidden, turned, wait):
    tile = hidden_tile(hidden.shape[1])

    def body(step, carry):
        wait(step)
        columns = tile_at(step, tile)
        before = dot(normed[...], w_up[:, columns])
        opened = jnp.maximum(before, 0.0)
        hidden[:, columns] = opened.astype(jnp.bfloat16)
        turned[columns, :] = opened.T.astype(jnp.bfloat16)
        return carry

    lax.fori_loop(0, hidden.shape[1] // tile, body, 0)


def down_product(hidden, w_down, acts, out, wait):
    tile = model_tile(out.shape[1])

    def body(step, carry):
        wait(step)
        columns = tile_at(step, tile)
        term = dot(hidden[...], w_down[:, columns])
        out[:, columns] = (acts[:, columns].astype(jnp.float32) + term).astype(jnp.bfloat16)
        return carry

    lax.fori_loop(0, out.shape[1] // tile, body, 0)


def turn(rows, turned):
    turned[...] = rows[...].astype(jnp.float32).T.astype(jnp.bfloat16)


def opened_only(hidden, grad):
    return jnp.where(hidden.astype(jnp.float32) > 0.0, grad, 0.0).astype(jnp.bfloat16)


def down_back(grad, w_down, hidden, out, wait):
    tile = hidden_tile(out.shape[0])

    def body(step, carry):
        wait(step)
        lines = tile_at(step, tile)
        g_hidden = dot(w_down[lines, :], grad[...])
        if hidden is not None:
            out[lines, :] = opened_only(hidden[lines, :], g_hidden)
        else:
            out[lines, :] = g_hidden.astype(jnp.bfloat16)
        return carry

    lax.fori_loop(0, out.shape[0] // tile, body, 0)


def up_back(g_before, w_up, weighted, wait):
    tile = model_tile(weighted.shape[1])

    def body(step, carry):
        wait(step)
        columns = tile_at(step, tile)
        weighted[:, columns] = dot(w_up[columns, :], g_before[...]).T
        return carry

    lax.fori_loop(0, weighted.shape[1] // tile, body, 0)


def mix_backward(small, layer, grad, acts, inter, scale, weighted, out, count):
    batch, model_width = acts.shape
    width = model_width // count
    both = small[layer].astype(jnp.float32)
    proj = repeated(both[:count])
    keep = same_sample(count)
    for start in range(0, batch, GROUP):
        rows = pl.ds(start, GROUP)
        columns = [slice(k * width, (k + 1) * width) for k in range(count)]
        gained = [weighted[rows, columns[k]] * both[count + k : count + k + 1] for k in range(count)]
        shared = sum(gained[k] * inter[rows, columns[k]] for k in range(count))
        mean = jnp.sum(shared, axis=1, keepdims=True) * (1.0 / model_width)
        inv = scale[rows, 0:1]
        pull = inv * inv * mean
        parts = [
            (inv * (gained[k] - inter[rows, columns[k]] * pull)).astype(jnp.bfloat16)
            for k in range(count)
        ]
        block = stacked(acts, rows, count, width)
        g_inter = jnp.concatenate(parts, axis=0)
        left = jnp.concatenate([g_inter, proj], axis=1)
        right = jnp.concatenate([proj, g_inter], axis=1)
        links = jnp.where(keep, dot_nt(left, right), 0.0)
        g_acts = split_dot(links, block)
        for k in range(count):
            piece = g_acts[k * GROUP : (k + 1) * GROUP] + grad[rows, columns[k]].astype(jnp.float32)
            out[rows, columns[k]] = piece.astype(jnp.bfloat16)


def saved_shapes(batch, model_width, hidden_width, width):
    return [
        jax.ShapeDtypeStruct((2, hidden_width, batch), jnp.bfloat16),
        jax.ShapeDtypeStruct((2, batch, model_width), jnp.float32),
        jax.ShapeDtypeStruct((2, batch, width), jnp.float32),
        jax.ShapeDtypeStruct((2, batch, model_width), jnp.bfloat16),
    ]


def weight_specs():
    return [whole()] + [whole(pltpu.HBM)] * 4


def weight_scratch(model_width, hidden_width):
    tiles = max(hidden_width // hidden_tile(hidden_width), model_width // model_tile(model_width))
    return [
        pltpu.VMEM((2, model_width, hidden_width), jnp.bfloat16),
        pltpu.VMEM((2, hidden_width, model_width), jnp.bfloat16),
        pltpu.SemaphoreType.DMA((4, tiles)),
    ]


def streams_of(core, weights, held, forward):
    own_up, other_up, own_down, other_down = weights
    held_up, held_down, sems = held
    model_width, hidden_width = own_up.shape
    wide, narrow = hidden_tile(hidden_width), model_tile(model_width)
    made = []
    for layer in (0, 1):
        mine = core == layer
        up_forward, down_forward = forward[layer]
        up_cut = (1, wide) if up_forward else (0, narrow)
        down_cut = (1, narrow) if down_forward else (0, wide)
        made.append(
            (
                Stream(mine, own_up, other_up, held_up.at[layer], sems.at[2 * layer], *up_cut),
                Stream(mine, own_down, other_down, held_down.at[layer], sems.at[2 * layer + 1], *down_cut),
            )
        )
    return made


def stage_cost(products, batch, model_width, hidden_width):
    return pl.CostEstimate(
        flops=2 * products * batch * model_width * hidden_width, bytes_accessed=1 << 20, transcendentals=0
    )


def stage_params():
    return pltpu.CompilerParams(vmem_limit_bytes=STAGE_LIMIT)


def forward_stage(place, acts, top, weights, count):
    batch, model_width = acts.shape
    hidden_width = weights[1].shape[1]
    width = model_width // count

    def kernel(place_ref, acts_ref, top_ref, small_ref, *refs):
        matrices, refs = refs[:4], refs[4:]
        out_ref, hid, inter, scale, kept, g_hidden = refs[:6]
        held, (normed, hidden, top_turned) = refs[6:9], refs[9:]
        core = place_ref[0]

        @pl.when(place_ref[1] == 1)
        def _():
            layers = streams_of(core, matrices, held, [(True, True), (True, True)])
            for up, down in layers:
                up.start()
                down.start()
            kept[0] = acts_ref[...]
            for layer, (up, down) in enumerate(layers):
                mix_forward(
                    small_ref, layer, kept.at[layer], inter.at[layer], scale.at[layer], normed, count
                )
                up_product(normed, up.held, hidden, hid.at[layer], up.wait)
                to = kept.at[1] if layer == 0 else out_ref
                down_product(hidden, down.held, kept.at[layer], to, down.wait)

        @pl.when(place_ref[2] == 1)
        def _():
            layers = streams_of(core, matrices, held, [(True, True), (True, False)])
            down = layers[1][1]
            down.start()
            turn(top_ref, top_turned)
            down_back(top_turned, down.held, None, g_hidden, down.wait)

    out = pl.pallas_call(
        kernel,
        out_shape=[jax.ShapeDtypeStruct(acts.shape, jnp.bfloat16)]
        + saved_shapes(batch, model_width, hidden_width, width)
        + [jax.ShapeDtypeStruct((hidden_width, batch), jnp.bfloat16)],
        in_specs=[whole(pltpu.SMEM), whole(), whole()] + weight_specs(),
        out_specs=[whole()] * 6,
        scratch_shapes=weight_scratch(model_width, hidden_width)
        + [
            pltpu.VMEM((batch, model_width), jnp.bfloat16),
            pltpu.VMEM((batch, hidden_width), jnp.bfloat16),
            pltpu.VMEM((model_width, batch), jnp.bfloat16),
        ],
        compiler_params=stage_params(),
        cost_estimate=stage_cost(4, batch, model_width, hidden_width),
        name="forward_stage",
    )(place, acts, top, *weights)
    return out[0], out[1:5], out[5]


def turn_stage(place, acts, top, g_hidden, weights, count):
    batch, model_width = acts.shape
    hidden_width = weights[1].shape[1]
    width = model_width // count

    def kernel(place_ref, acts_ref, top_ref, ghid_ref, small_ref, *refs):
        matrices, refs = refs[:4], refs[4:]
        out_ref, held = refs[0], refs[1:4]
        hid, hidden, inter, scale, upper, grad, turned, normed, weighted, g_before = refs[4:]

        @pl.when(place_ref[1] == 1)
        def _():
            layers = streams_of(place_ref[0], matrices, held, [(True, True), (True, True)])
            (up0, down0), (up1, down1) = layers
            for stream in (up0, down0, up1):
                stream.start()
            mix_forward(small_ref, 0, acts_ref, inter.at[0], scale.at[0], normed, count)
            up_product(normed, up0.held, hidden, hid, up0.wait)
            down_product(hidden, down0.held, acts_ref, upper, down0.wait)
            mix_forward(small_ref, 1, upper, inter.at[1], scale.at[1], normed, count)
            tile = hidden_tile(hidden_width)

            def masked(step, carry):
                up1.wait(step)
                columns = tile_at(step, tile)
                before = dot(normed[...], up1.held[:, columns])
                opened = jnp.maximum(before, 0.0).T
                g_before[columns, :] = opened_only(opened, ghid_ref[columns, :].astype(jnp.float32))
                return carry

            lax.fori_loop(0, hidden_width // tile, masked, 0)
            up_back(g_before, up1.held, weighted, no_wait)
            mix_backward(small_ref, 1, top_ref, upper, inter.at[1], scale.at[1], weighted, grad, count)
            turn(grad, turned)
            down_back(turned, down0.held, hid, g_before, no_wait)
            up_back(g_before, up0.held, weighted, no_wait)
            mix_backward(small_ref, 0, grad, acts_ref, inter.at[0], scale.at[0], weighted, out_ref, count)

    return pl.pallas_call(
        kernel,
        out_shape=jax.ShapeDtypeStruct(acts.shape, jnp.bfloat16),
        in_specs=[whole(pltpu.SMEM)] + [whole()] * 3 + weight_specs(),
        out_specs=whole(),
        scratch_shapes=weight_scratch(model_width, hidden_width)
        + [
            pltpu.VMEM((hidden_width, batch), jnp.bfloat16),
            pltpu.VMEM((batch, hidden_width), jnp.bfloat16),
            pltpu.VMEM((2, batch, model_width), jnp.float32),
            pltpu.VMEM((2, batch, width), jnp.float32),
            pltpu.VMEM((batch, model_width), jnp.bfloat16),
            pltpu.VMEM((batch, model_width), jnp.bfloat16),
            pltpu.VMEM((model_width, batch), jnp.bfloat16),
            pltpu.VMEM((batch, model_width), jnp.bfloat16),
            pltpu.VMEM((batch, model_width), jnp.float32),
            pltpu.VMEM((hidden_width, batch), jnp.bfloat16),
        ],
        compiler_params=stage_params(),
        cost_estimate=stage_cost(6, batch, model_width, hidden_width),
        name="turn_stage",
    )(place, acts, top, g_hidden, *weights)


def backward_stage(place, grad, saved, weights, count):
    batch, model_width = grad.shape
    hidden_width = weights[1].shape[1]

    def kernel(place_ref, grad_ref, hid, inter, scale, kept, small_ref, *refs):
        matrices, refs = refs[:4], refs[4:]
        out_ref, held = refs[0], refs[1:4]
        middle, turned, weighted, g_before = refs[4:]

        @pl.when(place_ref[1] == 1)
        def _():
            layers = streams_of(place_ref[0], matrices, held, [(False, False), (False, False)])
            for up, down in reversed(layers):
                down.start()
                up.start()
            for layer, given, to in ((1, grad_ref, middle), (0, middle, out_ref)):
                up, down = layers[layer]
                turn(given, turned)
                down_back(turned, down.held, hid.at[layer], g_before, down.wait)
                up_back(g_before, up.held, weighted, up.wait)
                mix_backward(
                    small_ref, layer, given, kept.at[layer], inter.at[layer], scale.at[layer],
                    weighted, to, count,
                )

    return pl.pallas_call(
        kernel,
        out_shape=jax.ShapeDtypeStruct(grad.shape, jnp.bfloat16),
        in_specs=[whole(pltpu.SMEM)] + [whole()] * 5 + weight_specs(),
        out_specs=whole(),
        scratch_shapes=weight_scratch(model_width, hidden_width)
        + [
            pltpu.VMEM((batch, model_width), jnp.bfloat16),
            pltpu.VMEM((model_width, batch), jnp.bfloat16),
            pltpu.VMEM((batch, model_width), jnp.float32),
            pltpu.VMEM((hidden_width, batch), jnp.bfloat16),
        ],
        compiler_params=stage_params(),
        cost_estimate=stage_cost(4, batch, model_width, hidden_width),
        name="backward_stage",
    )(place, grad, *saved, *weights)


def swapped(value, section_count):
    return lax.ppermute(value, "section", [(s, s ^ 1) for s in range(section_count)])


def moved(value, from_stage, to_stage):
    pairs = [(2 * from_stage + core, 2 * to_stage + core) for core in (0, 1)]
    return lax.ppermute(value, "section", pairs)


def per_device(
    emb_table,
    lcb_weight,
    fm_proj,
    norm_gain,
    w_up,
    w_down,
    top_grad,
    lookup_slot,
    wanted_rows,
    row_counts,
):
    section_count = lax.axis_size("section")
    owners = section_count * lax.axis_size("table")
    stages = section_count // 2
    stage = lax.axis_index("section") // 2
    core = lax.axis_index("section") % 2
    cap = wanted_rows.shape[2]
    rows, embed_width = emb_table.shape
    embed_count = lcb_weight.shape[0]
    look_dev = lookup_slot.shape[1]
    model_width = top_grad.shape[3]
    table_axes = ("section", "table")

    small = jnp.concatenate([fm_proj[0], norm_gain[0].reshape(embed_count, -1)], axis=0)
    other_up = swapped(w_up[0], section_count)
    other_down = swapped(w_down[0], section_count)
    other_small = swapped(small, section_count)

    picked = wanted_rows[0]
    outgoing = pick_rows(emb_table, picked.reshape(-1))
    fetched = lax.all_to_all(
        outgoing.reshape(owners, cap, embed_width), table_axes, split_axis=0, concat_axis=0, tiled=True
    )
    spread = spread_weights(lookup_slot[0], lcb_weight, owners, cap)
    smalls = jnp.stack(
        [jnp.where(core == 0, small, other_small), jnp.where(core == 0, other_small, small)]
    )
    weights = [smalls, w_up[0], other_up, w_down[0], other_down]
    lead = compress(spread, fetched, embed_count)

    acts = jnp.concatenate([lead] + [moved(lead, s, 0) for s in range(1, stages)], axis=0)
    top = top_grad.reshape(stages, 2, look_dev, model_width)
    top = lax.dynamic_index_in_dim(top, core, 1, keepdims=False).reshape(-1, model_width)

    def at(tick):
        is_last = (stage == stages - 1) & (tick == 0)
        return jnp.stack([core, stage == tick, is_last]).astype(jnp.int32)

    saved = None
    for tick in range(stages - 1):
        out, fresh, product = forward_stage(at(tick), acts, top, weights, embed_count)
        if saved is None:
            saved, g_hidden = fresh, product
        else:
            saved = [jnp.where(stage == tick, new, old) for new, old in zip(fresh, saved)]
        acts = moved(out, tick, tick + 1)
    grad = turn_stage(at(stages - 1), acts, top, g_hidden, weights, embed_count)
    for tick in reversed(range(stages - 1)):
        grad = moved(grad, tick + 1, tick)
        grad = backward_stage(at(tick), grad, saved, weights, embed_count)

    lead_share = grad[:look_dev]
    for s in range(1, stages):
        arrived = moved(grad[s * look_dev : (s + 1) * look_dev], 0, s)
        lead_share = jnp.where(stage == s, arrived, lead_share)

    slot_grad = expand(spread, lead_share, embed_count)
    returned = lax.all_to_all(slot_grad, table_axes, split_axis=0, concat_axis=0, tiled=True)
    live_slots = jnp.arange(cap)[None, :] < row_counts[0][:, None]
    targets = jnp.where(live_slots, picked, rows).reshape(-1)
    return add_rows(targets, returned.reshape(-1, embed_width), outgoing, rows)


def solution(mesh):
    in_specs = (
        P(("section", "table"), None),
        P(),
        P("section", None, None),
        P("section", None),
        P("section", None, None),
        P("section", None, None),
        P("table", None, None, None),
        P("table", "section", None),
        P(("section", "table"), None, None),
        P(("section", "table"), None),
    )
    out_specs = P(("section", "table"), None)
    return jax.shard_map(
        per_device, mesh=mesh, in_specs=in_specs, out_specs=out_specs, check_vma=False
    )
```

```python
import jax
import jax.numpy as jnp
from jax import lax
from jax.experimental import pallas as pl
from jax.experimental.pallas import tpu as pltpu
from jax.sharding import PartitionSpec as P

EPSILON = 1e-05
DECAY_WEIGHT = 0.5
VMEM_LIMIT = 28 * 1024 * 1024
UNROLL = 32


def whole(memory_space=pltpu.VMEM):
    return pl.BlockSpec(memory_space=memory_space)


def in_hbm(value):
    return pltpu.with_memory_space_constraint(value, pltpu.HBM)


def params():
    return pltpu.CompilerParams(vmem_limit_bytes=VMEM_LIMIT)


def tiles_of(count, most):
    return max(step for step in range(1, most + 1) if count % step == 0)


def pick_rows(emb_table, picked):
    rows, width = emb_table.shape
    count = picked.shape[0]
    chunk = min(count, 1024)

    def kernel(picked_ref, table_ref, out_ref, wide, lines):
        wide[...] = table_ref[...].astype(jnp.float32)

        def fill(part, carry):
            base = pl.multiple_of(part * chunk, chunk)

            def body(group, inner):
                first = pl.multiple_of(group * UNROLL, UNROLL)
                for lane in range(UNROLL):
                    row = picked_ref[base + first + lane]
                    lines[pl.ds(first + lane, 1), :] = wide[pl.ds(row, 1), :]
                return inner

            lax.fori_loop(0, chunk // UNROLL, body, 0)
            out_ref[pl.ds(base, chunk), :] = lines[...].astype(out_ref.dtype)
            return carry

        lax.fori_loop(0, count // chunk, fill, 0)

    return pl.pallas_call(
        kernel,
        out_shape=jax.ShapeDtypeStruct((count, width), emb_table.dtype),
        in_specs=[whole(pltpu.SMEM), whole()],
        out_specs=whole(),
        scratch_shapes=[
            pltpu.VMEM((rows, width), jnp.float32),
            pltpu.VMEM((chunk, width), jnp.float32),
        ],
        compiler_params=params(),
        name="pick_rows",
    )(picked, emb_table)


def spread_weights(codes, lcb_weight, owners, cap):
    views, samples, feature_count = codes.shape
    embed_count = lcb_weight.shape[0]
    group = tiles_of(samples, 16)

    def kernel(codes_ref, lcb_ref, out_ref):
        lcb = lcb_ref[...].astype(jnp.float32)
        owner_of = lax.broadcasted_iota(jnp.int32, (owners, embed_count, feature_count), 0)
        column_of = lax.broadcasted_iota(jnp.int32, (cap, feature_count), 0)
        for pair in range(0, group, 2):
            made = []
            for sample in (pair, pair + 1):
                slots = codes_ref[0, sample : sample + 1, :]
                owner = lax.div(slots, cap)
                column = slots - owner * cap
                left = jnp.where(owner_of == owner[None], lcb[None], 0.0)
                left = left.reshape(owners * embed_count, feature_count).astype(jnp.bfloat16)
                right = jnp.where(column_of == column, 1.0, 0.0).astype(jnp.bfloat16)
                both = lax.dot_general(
                    left, right, (((1,), (1,)), ((), ())), preferred_element_type=jnp.float32
                )
                made.append(both.reshape(owners, embed_count, cap))
            rows = pl.ds(pair * embed_count, 2 * embed_count)
            out_ref[0, :, rows, :] = jnp.concatenate(made, axis=1).astype(out_ref.dtype)

    return pl.pallas_call(
        kernel,
        out_shape=pltpu.HBM((views, owners, samples * embed_count, cap), jnp.bfloat16),
        grid=(views, samples // group),
        in_specs=[
            pl.BlockSpec((1, group, feature_count), lambda v, i: (v, i, 0)),
            pl.BlockSpec((embed_count, feature_count), lambda v, i: (0, 0)),
        ],
        out_specs=pl.BlockSpec((1, owners, group * embed_count, cap), lambda v, i: (v, 0, i, 0)),
        compiler_params=params(),
        cost_estimate=pl.CostEstimate(
            flops=2 * views * samples * owners * embed_count * feature_count * cap,
            bytes_accessed=2 * views * owners * samples * embed_count * cap,
            transcendentals=0,
        ),
        name="spread_weights",
    )(codes, lcb_weight)


def compress(spread, fetched, embed_count):
    views, owners, lines, cap = spread.shape
    width = fetched.shape[3]
    samples = lines // embed_count
    part = tiles_of(owners, 4)
    steps = owners // part

    def kernel(spread_ref, rows_ref, out_ref, held, total, sems):
        def copy(view, step):
            piece = tile_at(step, part)
            return pltpu.make_async_copy(
                spread_ref.at[view, piece], held.at[view, piece], sems.at[view, step]
            )

        for view in range(views):
            for step in range(steps):
                copy(view, step).start()
        for view in range(views):
            total[...] = jnp.zeros_like(total)

            def body(step, carry):
                copy(view, step).wait()
                first = step * part
                left = jnp.concatenate([held[view, first + o] for o in range(part)], axis=1)
                right = jnp.concatenate([rows_ref[first + o, view] for o in range(part)], axis=0)
                total[...] += jnp.dot(left, right, preferred_element_type=jnp.float32)
                return carry

            lax.fori_loop(0, steps, body, 0)
            for k in range(embed_count):
                piece = total[pl.ds(k, samples, stride=embed_count), :]
                out_ref[view, :, k * width : (k + 1) * width] = piece.astype(out_ref.dtype)

    return pl.pallas_call(
        kernel,
        out_shape=jax.ShapeDtypeStruct((views, samples, embed_count * width), jnp.bfloat16),
        in_specs=[whole(pltpu.HBM), whole()],
        out_specs=whole(),
        scratch_shapes=[
            pltpu.VMEM(spread.shape, jnp.bfloat16),
            pltpu.VMEM((lines, width), jnp.float32),
            pltpu.SemaphoreType.DMA((views, steps)),
        ],
        compiler_params=params(),
        name="compress",
    )(in_hbm(spread), fetched)


def expand(spread, lead_grads, embed_count):
    views, owners, lines, cap = spread.shape
    samples = lines // embed_count
    width = lead_grads[0].shape[1] // embed_count
    part = tiles_of(owners, 4)

    def kernel(spread_ref, *refs):
        grad_refs, (out_ref, tall, turned) = refs[:views], refs[views:]
        for view in range(views):
            for k in range(embed_count):
                piece = grad_refs[view][:, k * width : (k + 1) * width].astype(jnp.float32)
                tall[pl.ds(k, samples, stride=embed_count), :] = piece
            turned[...] = tall[...].T.astype(jnp.bfloat16)

            def body(step, carry):
                first = step * part
                right = jnp.concatenate([spread_ref[view, first + o] for o in range(part)], axis=1)
                term = jnp.dot(turned[...], right, preferred_element_type=jnp.float32)
                piece = term.T.astype(out_ref.dtype).reshape(part, cap, width)
                for o in range(part):
                    out_ref[first + o, view] = piece[o]
                return carry

            lax.fori_loop(0, owners // part, body, 0)

    return pl.pallas_call(
        kernel,
        out_shape=jax.ShapeDtypeStruct((owners, views, cap, width), jnp.bfloat16),
        in_specs=[whole()] * (1 + views),
        out_specs=whole(),
        scratch_shapes=[
            pltpu.VMEM((lines, width), jnp.float32),
            pltpu.VMEM((width, lines), jnp.bfloat16),
        ],
        compiler_params=params(),
        name="expand",
    )(spread, *lead_grads)


def add_rows(targets, returned, outgoing, rows):
    count, width = returned.shape
    chunk = min(count, 1024)

    def kernel(targets_ref, back_ref, sent_ref, out_ref, total, terms, done):
        total[...] = jnp.zeros_like(total)

        def fill(part, carry):
            base = pl.multiple_of(part * chunk, chunk)
            lines = pl.ds(base, chunk)
            terms[...] = back_ref[lines, :].astype(jnp.float32) + DECAY_WEIGHT * sent_ref[
                lines, :
            ].astype(jnp.float32)

            def body(group, inner):
                first = pl.multiple_of(group * UNROLL, UNROLL)
                places = [targets_ref[base + first + lane] for lane in range(UNROLL)]
                sums = [
                    total[pl.ds(places[lane], 1), :] + terms[pl.ds(first + lane, 1), :]
                    for lane in range(UNROLL)
                ]
                for lane in range(UNROLL):
                    total[pl.ds(places[lane], 1), :] = sums[lane]
                return inner

            lax.fori_loop(0, chunk // UNROLL, body, 0)
            return carry

        lax.fori_loop(0, count // chunk, fill, 0)
        copy = pltpu.make_async_copy(total.at[pl.ds(0, rows), :], out_ref, done)
        copy.start()
        copy.wait()

    return pl.pallas_call(
        kernel,
        out_shape=jax.ShapeDtypeStruct((rows, width), jnp.float32),
        in_specs=[whole(pltpu.SMEM), whole(), whole()],
        out_specs=whole(pl.ANY),
        scratch_shapes=[
            pltpu.VMEM((rows + 8, width), jnp.float32),
            pltpu.VMEM((chunk, width), jnp.float32),
            pltpu.SemaphoreType.DMA,
        ],
        compiler_params=params(),
        name="add_rows",
    )(targets, returned, outgoing)


GROUP = 32
TABLE_AXES = ("section", "table")
STAGE_LIMIT = 44 * 1024 * 1024
NT = (((1,), (1,)), ((), ()))


def dot_nt(left, right):
    return lax.dot_general(left, right, NT, preferred_element_type=jnp.float32)


def dot(left, right):
    return jnp.dot(left, right, preferred_element_type=jnp.float32)


def split_dot(left, right):
    high = left.astype(jnp.bfloat16)
    low = (left - high.astype(jnp.float32)).astype(jnp.bfloat16)
    return dot(high, right) + dot(low, right)


def same_sample(count):
    first = lax.broadcasted_iota(jnp.int32, (count * GROUP, count * GROUP), 0)
    second = lax.broadcasted_iota(jnp.int32, (count * GROUP, count * GROUP), 1)
    return (first & (GROUP - 1)) == (second & (GROUP - 1))


def stacked(ref, rows, count, width):
    return jnp.concatenate([ref[rows, k * width : (k + 1) * width] for k in range(count)], axis=0)


def repeated(proj):
    count, width = proj.shape
    lines = [jnp.broadcast_to(proj[k : k + 1, :], (GROUP, width)) for k in range(count)]
    return jnp.concatenate(lines, axis=0).astype(jnp.bfloat16)


def mix_forward(small, layer, acts, inter, scale, normed, count):
    batch, model_width = acts.shape
    width = model_width // count
    both = small[layer].astype(jnp.float32)
    proj = repeated(both[:count])
    keep = same_sample(count)
    for start in range(0, batch, GROUP):
        rows = pl.ds(start, GROUP)
        block = stacked(acts, rows, count, width)
        gram = jnp.where(keep, dot_nt(block, block), 0.0)
        mixed = split_dot(gram, proj)
        parts = [mixed[k * GROUP : (k + 1) * GROUP] for k in range(count)]
        squares = sum(part * part for part in parts)
        mean = jnp.sum(squares, axis=1, keepdims=True) * (1.0 / model_width)
        inv = lax.rsqrt(mean + EPSILON)
        scale[rows, :] = jnp.broadcast_to(inv, (GROUP, width))
        for k in range(count):
            columns = slice(k * width, (k + 1) * width)
            inter[rows, columns] = parts[k]
            gain = both[count + k : count + k + 1]
            normed[rows, columns] = (parts[k] * inv * gain).astype(jnp.bfloat16)


def hidden_tile(hidden_width):
    return min(hidden_width, 1024)


def model_tile(model_width):
    return min(model_width, 512)


def tile_at(step, size):
    return pl.ds(pl.multiple_of(step * size, size), size)


class Stream:
    def __init__(self, mine, own, other, held, sems, axis, size):
        self.mine, self.own, self.other, self.held, self.sems = mine, own, other, held, sems
        self.axis, self.size = axis, size
        self.tiles = own.shape[axis] // size

    def copy(self, source, step):
        cut = tile_at(step, self.size)
        index = (slice(None), cut) if self.axis == 1 else (cut, slice(None))
        return pltpu.make_async_copy(source.at[index], self.held.at[index], self.sems.at[step])

    def start(self):
        @pl.when(self.mine)
        def _():
            for step in range(self.tiles):
                self.copy(self.own, step).start()

        @pl.when(jnp.logical_not(self.mine))
        def _():
            for step in range(self.tiles):
                self.copy(self.other, step).start()

    def wait(self, step):
        self.copy(self.own, step).wait()


def no_wait(step):
    return None


def up_product(normed, w_up, hidden, turned, wait):
    tile = hidden_tile(hidden.shape[1])

    def body(step, carry):
        wait(step)
        columns = tile_at(step, tile)
        before = dot(normed[...], w_up[:, columns])
        opened = jnp.maximum(before, 0.0)
        hidden[:, columns] = opened.astype(jnp.bfloat16)
        turned[columns, :] = opened.T.astype(jnp.bfloat16)
        return carry

    lax.fori_loop(0, hidden.shape[1] // tile, body, 0)


def down_product(hidden, w_down, acts, out, wait):
    tile = model_tile(out.shape[1])

    def body(step, carry):
        wait(step)
        columns = tile_at(step, tile)
        term = dot(hidden[...], w_down[:, columns])
        out[:, columns] = (acts[:, columns].astype(jnp.float32) + term).astype(jnp.bfloat16)
        return carry

    lax.fori_loop(0, out.shape[1] // tile, body, 0)


def turn(rows, turned):
    turned[...] = rows[...].astype(jnp.float32).T.astype(jnp.bfloat16)


def opened_only(hidden, grad):
    return jnp.where(hidden.astype(jnp.float32) > 0.0, grad, 0.0).astype(jnp.bfloat16)


def down_back(grad, w_down, hidden, out, wait):
    tile = hidden_tile(out.shape[0])

    def body(step, carry):
        wait(step)
        lines = tile_at(step, tile)
        g_hidden = dot(w_down[lines, :], grad[...])
        if hidden is not None:
            out[lines, :] = opened_only(hidden[lines, :], g_hidden)
        else:
            out[lines, :] = g_hidden.astype(jnp.bfloat16)
        return carry

    lax.fori_loop(0, out.shape[0] // tile, body, 0)


def up_back(g_before, w_up, weighted, wait):
    tile = model_tile(weighted.shape[1])

    def body(step, carry):
        wait(step)
        columns = tile_at(step, tile)
        weighted[:, columns] = dot(w_up[columns, :], g_before[...]).T
        return carry

    lax.fori_loop(0, weighted.shape[1] // tile, body, 0)


def mix_backward(small, layer, grad, acts, inter, scale, weighted, out, count):
    batch, model_width = acts.shape
    width = model_width // count
    both = small[layer].astype(jnp.float32)
    proj = repeated(both[:count])
    keep = same_sample(count)
    for start in range(0, batch, GROUP):
        rows = pl.ds(start, GROUP)
        columns = [slice(k * width, (k + 1) * width) for k in range(count)]
        gained = [weighted[rows, columns[k]] * both[count + k : count + k + 1] for k in range(count)]
        shared = sum(gained[k] * inter[rows, columns[k]] for k in range(count))
        mean = jnp.sum(shared, axis=1, keepdims=True) * (1.0 / model_width)
        inv = scale[rows, 0:1]
        pull = inv * inv * mean
        parts = [
            (inv * (gained[k] - inter[rows, columns[k]] * pull)).astype(jnp.bfloat16)
            for k in range(count)
        ]
        block = stacked(acts, rows, count, width)
        g_inter = jnp.concatenate(parts, axis=0)
        left = jnp.concatenate([g_inter, proj], axis=1)
        right = jnp.concatenate([proj, g_inter], axis=1)
        links = jnp.where(keep, dot_nt(left, right), 0.0)
        g_acts = split_dot(links, block)
        for k in range(count):
            piece = g_acts[k * GROUP : (k + 1) * GROUP] + grad[rows, columns[k]].astype(jnp.float32)
            out[rows, columns[k]] = piece.astype(jnp.bfloat16)


def saved_shapes(batch, model_width, hidden_width, width):
    return [
        jax.ShapeDtypeStruct((2, hidden_width, batch), jnp.bfloat16),
        jax.ShapeDtypeStruct((2, batch, model_width), jnp.float32),
        jax.ShapeDtypeStruct((2, batch, width), jnp.float32),
        jax.ShapeDtypeStruct((2, batch, model_width), jnp.bfloat16),
    ]


def weight_specs():
    return [whole()] + [whole(pltpu.HBM)] * 4


def weight_scratch(model_width, hidden_width):
    tiles = max(hidden_width // hidden_tile(hidden_width), model_width // model_tile(model_width))
    return [
        pltpu.VMEM((2, model_width, hidden_width), jnp.bfloat16),
        pltpu.VMEM((2, hidden_width, model_width), jnp.bfloat16),
        pltpu.SemaphoreType.DMA((4, tiles)),
    ]


def streams_of(core, weights, held, forward):
    own_up, other_up, own_down, other_down = weights
    held_up, held_down, sems = held
    model_width, hidden_width = own_up.shape
    wide, narrow = hidden_tile(hidden_width), model_tile(model_width)
    made = []
    for layer in (0, 1):
        mine = core == layer
        up_forward, down_forward = forward[layer]
        up_cut = (1, wide) if up_forward else (0, narrow)
        down_cut = (1, narrow) if down_forward else (0, wide)
        made.append(
            (
                Stream(mine, own_up, other_up, held_up.at[layer], sems.at[2 * layer], *up_cut),
                Stream(mine, own_down, other_down, held_down.at[layer], sems.at[2 * layer + 1], *down_cut),
            )
        )
    return made


def stage_cost(products, batch, model_width, hidden_width):
    return pl.CostEstimate(
        flops=2 * products * batch * model_width * hidden_width, bytes_accessed=1 << 20, transcendentals=0
    )


def stage_params():
    return pltpu.CompilerParams(vmem_limit_bytes=STAGE_LIMIT)


def forward_stage(place, acts, top, weights, count):
    batch, model_width = acts.shape
    hidden_width = weights[1].shape[1]
    width = model_width // count

    def kernel(place_ref, acts_ref, top_ref, small_ref, *refs):
        matrices, refs = refs[:4], refs[4:]
        out_ref, hid, inter, scale, kept, g_hidden = refs[:6]
        held, (normed, hidden, top_turned) = refs[6:9], refs[9:]
        core = place_ref[0]

        @pl.when(place_ref[1] == 1)
        def _():
            layers = streams_of(core, matrices, held, [(True, True), (True, True)])
            for up, down in layers:
                up.start()
                down.start()
            kept[0] = acts_ref[...]
            for layer, (up, down) in enumerate(layers):
                mix_forward(
                    small_ref, layer, kept.at[layer], inter.at[layer], scale.at[layer], normed, count
                )
                up_product(normed, up.held, hidden, hid.at[layer], up.wait)
                to = kept.at[1] if layer == 0 else out_ref
                down_product(hidden, down.held, kept.at[layer], to, down.wait)

        @pl.when(place_ref[2] == 1)
        def _():
            layers = streams_of(core, matrices, held, [(True, True), (True, False)])
            down = layers[1][1]
            down.start()
            turn(top_ref, top_turned)
            down_back(top_turned, down.held, None, g_hidden, down.wait)

    out = pl.pallas_call(
        kernel,
        out_shape=[jax.ShapeDtypeStruct(acts.shape, jnp.bfloat16)]
        + saved_shapes(batch, model_width, hidden_width, width)
        + [jax.ShapeDtypeStruct((hidden_width, batch), jnp.bfloat16)],
        in_specs=[whole(pltpu.SMEM), whole(), whole()] + weight_specs(),
        out_specs=[whole()] * 6,
        scratch_shapes=weight_scratch(model_width, hidden_width)
        + [
            pltpu.VMEM((batch, model_width), jnp.bfloat16),
            pltpu.VMEM((batch, hidden_width), jnp.bfloat16),
            pltpu.VMEM((model_width, batch), jnp.bfloat16),
        ],
        compiler_params=stage_params(),
        cost_estimate=stage_cost(4, batch, model_width, hidden_width),
        name="forward_stage",
    )(place, acts, top, weights[0], *map(in_hbm, weights[1:]))
    return out[0], out[1:5], out[5]


def turn_stage(place, acts, top, g_hidden, weights, count):
    batch, model_width = acts.shape
    hidden_width = weights[1].shape[1]
    width = model_width // count

    def kernel(place_ref, acts_ref, top_ref, ghid_ref, small_ref, *refs):
        matrices, refs = refs[:4], refs[4:]
        out_ref, held = refs[0], refs[1:4]
        hid, hidden, inter, scale, upper, grad, turned, normed, weighted, g_before = refs[4:]

        @pl.when(place_ref[1] == 1)
        def _():
            layers = streams_of(place_ref[0], matrices, held, [(True, True), (True, True)])
            (up0, down0), (up1, down1) = layers
            for stream in (up0, down0, up1):
                stream.start()
            mix_forward(small_ref, 0, acts_ref, inter.at[0], scale.at[0], normed, count)
            up_product(normed, up0.held, hidden, hid, up0.wait)
            down_product(hidden, down0.held, acts_ref, upper, down0.wait)
            mix_forward(small_ref, 1, upper, inter.at[1], scale.at[1], normed, count)
            tile = hidden_tile(hidden_width)

            def masked(step, carry):
                up1.wait(step)
                columns = tile_at(step, tile)
                before = dot(normed[...], up1.held[:, columns])
                opened = jnp.maximum(before, 0.0).T
                g_before[columns, :] = opened_only(opened, ghid_ref[columns, :].astype(jnp.float32))
                return carry

            lax.fori_loop(0, hidden_width // tile, masked, 0)
            up_back(g_before, up1.held, weighted, no_wait)
            mix_backward(small_ref, 1, top_ref, upper, inter.at[1], scale.at[1], weighted, grad, count)
            turn(grad, turned)
            down_back(turned, down0.held, hid, g_before, no_wait)
            up_back(g_before, up0.held, weighted, no_wait)
            mix_backward(small_ref, 0, grad, acts_ref, inter.at[0], scale.at[0], weighted, out_ref, count)

    return pl.pallas_call(
        kernel,
        out_shape=jax.ShapeDtypeStruct(acts.shape, jnp.bfloat16),
        in_specs=[whole(pltpu.SMEM)] + [whole()] * 3 + weight_specs(),
        out_specs=whole(),
        scratch_shapes=weight_scratch(model_width, hidden_width)
        + [
            pltpu.VMEM((hidden_width, batch), jnp.bfloat16),
            pltpu.VMEM((batch, hidden_width), jnp.bfloat16),
            pltpu.VMEM((2, batch, model_width), jnp.float32),
            pltpu.VMEM((2, batch, width), jnp.float32),
            pltpu.VMEM((batch, model_width), jnp.bfloat16),
            pltpu.VMEM((batch, model_width), jnp.bfloat16),
            pltpu.VMEM((model_width, batch), jnp.bfloat16),
            pltpu.VMEM((batch, model_width), jnp.bfloat16),
            pltpu.VMEM((batch, model_width), jnp.float32),
            pltpu.VMEM((hidden_width, batch), jnp.bfloat16),
        ],
        compiler_params=stage_params(),
        cost_estimate=stage_cost(6, batch, model_width, hidden_width),
        name="turn_stage",
    )(place, acts, top, g_hidden, weights[0], *map(in_hbm, weights[1:]))


def backward_stage(place, grad, saved, weights, count):
    batch, model_width = grad.shape
    hidden_width = weights[1].shape[1]

    def kernel(place_ref, grad_ref, hid, inter, scale, kept, small_ref, *refs):
        matrices, refs = refs[:4], refs[4:]
        out_ref, held = refs[0], refs[1:4]
        middle, turned, weighted, g_before = refs[4:]

        @pl.when(place_ref[1] == 1)
        def _():
            layers = streams_of(place_ref[0], matrices, held, [(False, False), (False, False)])
            for up, down in reversed(layers):
                down.start()
                up.start()
            for layer, given, to in ((1, grad_ref, middle), (0, middle, out_ref)):
                up, down = layers[layer]
                turn(given, turned)
                down_back(turned, down.held, hid.at[layer], g_before, down.wait)
                up_back(g_before, up.held, weighted, up.wait)
                mix_backward(
                    small_ref, layer, given, kept.at[layer], inter.at[layer], scale.at[layer],
                    weighted, to, count,
                )

    return pl.pallas_call(
        kernel,
        out_shape=jax.ShapeDtypeStruct(grad.shape, jnp.bfloat16),
        in_specs=[whole(pltpu.SMEM)] + [whole()] * 5 + weight_specs(),
        out_specs=whole(),
        scratch_shapes=weight_scratch(model_width, hidden_width)
        + [
            pltpu.VMEM((batch, model_width), jnp.bfloat16),
            pltpu.VMEM((model_width, batch), jnp.bfloat16),
            pltpu.VMEM((batch, model_width), jnp.float32),
            pltpu.VMEM((hidden_width, batch), jnp.bfloat16),
        ],
        compiler_params=stage_params(),
        cost_estimate=stage_cost(4, batch, model_width, hidden_width),
        name="backward_stage",
    )(place, grad, *saved, weights[0], *map(in_hbm, weights[1:]))


def swapped(value, section_count):
    return lax.ppermute(value, "section", [(s, s ^ 1) for s in range(section_count)])


def moved(value, from_stage, to_stage, mirrored=False):
    if not mirrored:
        pairs = [(2 * from_stage + core, 2 * to_stage + core) for core in (0, 1)]
        return lax.ppermute(value, "section", pairs)
    along = lax.axis_size("table")
    pairs = []
    for core in (0, 1):
        for t in range(along):
            other = (t + along // 2) % along
            pairs.append(((2 * from_stage + core) * along + t, (2 * to_stage + core) * along + other))
    return lax.ppermute(value, TABLE_AXES, pairs)


def mirror(value):
    along = lax.axis_size("table")
    return lax.ppermute(value, "table", [(t, (t + along // 2) % along) for t in range(along)])


def swap_in_half(value):
    along = lax.axis_size("table")
    half = along // 2
    groups = [
        [s * along + h * half + t for s in range(lax.axis_size("section")) for t in range(half)]
        for h in (0, 1)
    ]
    return lax.all_to_all(
        value, TABLE_AXES, split_axis=0, concat_axis=0, axis_index_groups=groups, tiled=True
    )


def near_first(per_asker, my_half):
    sections = lax.axis_size("section")
    half = lax.axis_size("table") // 2
    split = per_asker.reshape((sections, 2, half) + per_asker.shape[1:])
    near = lax.dynamic_index_in_dim(split, my_half, 1, keepdims=False)
    far = lax.dynamic_index_in_dim(split, 1 - my_half, 1, keepdims=False)
    return jnp.stack([near, far], axis=2).reshape((sections * half, 2) + per_asker.shape[1:])


def per_device(
    emb_table,
    lcb_weight,
    fm_proj,
    norm_gain,
    w_up,
    w_down,
    top_grad,
    lookup_slot,
    wanted_rows,
    row_counts,
):
    section_count = lax.axis_size("section")
    along = lax.axis_size("table")
    half = along // 2
    near_owners = section_count * half
    stages = section_count // 2
    stage = lax.axis_index("section") // 2
    core = lax.axis_index("section") % 2
    my_half = lax.axis_index("table") // half
    cap = wanted_rows.shape[2]
    rows, embed_width = emb_table.shape
    embed_count = lcb_weight.shape[0]
    look_dev = lookup_slot.shape[1]
    model_width = top_grad.shape[3]

    slots = jnp.concatenate([lookup_slot, mirror(lookup_slot)], axis=0)
    small = jnp.concatenate([fm_proj[0], norm_gain[0].reshape(embed_count, -1)], axis=0)
    other_up = swapped(w_up[0], section_count)
    other_down = swapped(w_down[0], section_count)
    other_small = swapped(small, section_count)

    picked = near_first(wanted_rows[0], my_half)
    outgoing = pick_rows(emb_table, picked.reshape(-1))
    fetched = swap_in_half(outgoing.reshape(near_owners, 2, cap, embed_width))
    owner, column = slots // cap, slots % cap
    place = owner % along
    is_near = place // half == my_half
    near_owner = jnp.where(is_near, owner // along * half + place % half, near_owners)
    spread = spread_weights(near_owner * cap + column, lcb_weight, near_owners, cap)
    smalls = jnp.stack(
        [jnp.where(core == 0, small, other_small), jnp.where(core == 0, other_small, small)]
    )
    weights = [smalls, w_up[0], other_up, w_down[0], other_down]
    parts = compress(spread, fetched, embed_count)

    def joined(near, far):
        return (near.astype(jnp.float32) + far.astype(jnp.float32)).astype(jnp.bfloat16)

    leads = [joined(parts[0], moved(parts[1], 0, 0, mirrored=True))]
    for s in range(1, stages):
        leads.append(joined(moved(parts[0], s, 0), moved(parts[1], s, 0, mirrored=True)))
    acts = jnp.concatenate(leads, axis=0)
    top = top_grad.reshape(stages, 2, look_dev, model_width)
    top = lax.dynamic_index_in_dim(top, core, 1, keepdims=False).reshape(-1, model_width)

    def at(tick):
        is_last = (stage == stages - 1) & (tick == 0)
        return jnp.stack([core, stage == tick, is_last]).astype(jnp.int32)

    saved = None
    for tick in range(stages - 1):
        out, fresh, product = forward_stage(at(tick), acts, top, weights, embed_count)
        if saved is None:
            saved, g_hidden = fresh, product
        else:
            saved = [jnp.where(stage == tick, new, old) for new, old in zip(fresh, saved)]
        acts = moved(out, tick, tick + 1)
    grad = turn_stage(at(stages - 1), acts, top, g_hidden, weights, embed_count)
    for tick in reversed(range(stages - 1)):
        grad = moved(grad, tick + 1, tick)
        grad = backward_stage(at(tick), grad, saved, weights, embed_count)

    own_grad = grad[:look_dev]
    mirror_grad = moved(own_grad, 0, 0, mirrored=True)
    for s in range(1, stages):
        piece = grad[s * look_dev : (s + 1) * look_dev]
        own_grad = jnp.where(stage == s, moved(piece, 0, s), own_grad)
        mirror_grad = jnp.where(stage == s, moved(piece, 0, s, mirrored=True), mirror_grad)

    slot_grad = expand(spread, [own_grad, mirror_grad], embed_count)
    returned = swap_in_half(slot_grad)
    live_slots = jnp.arange(cap) < near_first(row_counts[0], my_half)[..., None]
    targets = jnp.where(live_slots, picked, rows).reshape(-1)
    return add_rows(targets, returned.reshape(-1, embed_width), outgoing, rows)


def solution(mesh):
    in_specs = (
        P(("section", "table"), None),
        P(),
        P("section", None, None),
        P("section", None),
        P("section", None, None),
        P("section", None, None),
        P("table", None, None, None),
        P("table", "section", None),
        P(("section", "table"), None, None),
        P(("section", "table"), None),
    )
    out_specs = P(("section", "table"), None)
    return jax.shard_map(
        per_device, mesh=mesh, in_specs=in_specs, out_specs=out_specs, check_vma=False
    )
```

```python
import jax
import jax.numpy as jnp
from jax import lax
from jax.experimental import pallas as pl
from jax.experimental.pallas import tpu as pltpu
from jax.sharding import PartitionSpec as P

EPSILON = 1e-05
DECAY_WEIGHT = 0.5
VMEM_LIMIT = 28 * 1024 * 1024
UNROLL = 32


def whole(memory_space=pltpu.VMEM):
    return pl.BlockSpec(memory_space=memory_space)


def in_hbm(value):
    return pltpu.with_memory_space_constraint(value, pltpu.HBM)


def params():
    return pltpu.CompilerParams(vmem_limit_bytes=VMEM_LIMIT)


def tiles_of(count, most):
    return max(step for step in range(1, most + 1) if count % step == 0)


def pick_rows(emb_table, picked):
    rows, width = emb_table.shape
    count = picked.shape[0]
    chunk = min(count, 1024)

    def kernel(picked_ref, table_ref, out_ref, wide, lines):
        wide[...] = table_ref[...].astype(jnp.float32)

        def fill(part, carry):
            base = pl.multiple_of(part * chunk, chunk)

            def body(group, inner):
                first = pl.multiple_of(group * UNROLL, UNROLL)
                for lane in range(UNROLL):
                    row = picked_ref[base + first + lane]
                    lines[pl.ds(first + lane, 1), :] = wide[pl.ds(row, 1), :]
                return inner

            lax.fori_loop(0, chunk // UNROLL, body, 0)
            out_ref[pl.ds(base, chunk), :] = lines[...].astype(out_ref.dtype)
            return carry

        lax.fori_loop(0, count // chunk, fill, 0)

    return pl.pallas_call(
        kernel,
        out_shape=jax.ShapeDtypeStruct((count, width), emb_table.dtype),
        in_specs=[whole(pltpu.SMEM), whole()],
        out_specs=whole(),
        scratch_shapes=[
            pltpu.VMEM((rows, width), jnp.float32),
            pltpu.VMEM((chunk, width), jnp.float32),
        ],
        compiler_params=params(),
        name="pick_rows",
    )(picked, emb_table)


def spread_weights(codes, lcb_weight, owners, cap):
    samples, feature_count = codes.shape
    embed_count = lcb_weight.shape[0]
    group = tiles_of(samples, 16)

    def kernel(codes_ref, lcb_ref, out_ref):
        lcb = lcb_ref[...].astype(jnp.float32)
        owner_of = lax.broadcasted_iota(jnp.int32, (owners, embed_count, feature_count), 0)
        column_of = lax.broadcasted_iota(jnp.int32, (cap, feature_count), 0)
        for pair in range(0, group, 2):
            made = []
            for sample in (pair, pair + 1):
                slots = codes_ref[sample : sample + 1, :]
                owner = lax.div(slots, cap)
                column = slots - owner * cap
                left = jnp.where(owner_of == owner[None], lcb[None], 0.0)
                left = left.reshape(owners * embed_count, feature_count).astype(jnp.bfloat16)
                right = jnp.where(column_of == column, 1.0, 0.0).astype(jnp.bfloat16)
                both = lax.dot_general(
                    left, right, (((1,), (1,)), ((), ())), preferred_element_type=jnp.float32
                )
                made.append(both.reshape(owners, embed_count, cap))
            rows = pl.ds(pair * embed_count, 2 * embed_count)
            out_ref[:, rows, :] = jnp.concatenate(made, axis=1).astype(out_ref.dtype)

    return pl.pallas_call(
        kernel,
        out_shape=pltpu.HBM((owners, samples * embed_count, cap), jnp.bfloat16),
        grid=(samples // group,),
        in_specs=[
            pl.BlockSpec((group, feature_count), lambda i: (i, 0)),
            pl.BlockSpec((embed_count, feature_count), lambda i: (0, 0)),
        ],
        out_specs=pl.BlockSpec((owners, group * embed_count, cap), lambda i: (0, i, 0)),
        compiler_params=params(),
        cost_estimate=pl.CostEstimate(
            flops=2 * samples * owners * embed_count * feature_count * cap,
            bytes_accessed=2 * owners * samples * embed_count * cap,
            transcendentals=0,
        ),
        name="spread_weights",
    )(codes, lcb_weight)


def compress(spread, fetched, embed_count, others=None):
    owners, lines, cap = spread.shape
    width = fetched.shape[2]
    samples = lines // embed_count
    part = tiles_of(owners, 4)
    steps = owners // part
    extra = [] if others is None else [others]

    def kernel(spread_ref, rows_ref, *refs):
        other_refs, (out_ref, held, total, sems) = refs[: len(extra)], refs[len(extra) :]

        def copy(step):
            piece = tile_at(step, part)
            return pltpu.make_async_copy(spread_ref.at[piece], held.at[piece], sems.at[step])

        for step in range(steps):
            copy(step).start()
        total[...] = jnp.zeros_like(total)

        def body(step, carry):
            copy(step).wait()
            first = step * part
            left = jnp.concatenate([held[first + o] for o in range(part)], axis=1)
            right = rows_ref[tile_at(step, part)].reshape(part * cap, width)
            total[...] += jnp.dot(left, right, preferred_element_type=jnp.float32)
            return carry

        lax.fori_loop(0, steps, body, 0)
        for k in range(embed_count):
            columns = slice(k * width, (k + 1) * width)
            piece = total[pl.ds(k, samples, stride=embed_count), :]
            for other in other_refs:
                piece = piece + other[:, columns].astype(jnp.float32)
            out_ref[:, columns] = piece.astype(out_ref.dtype)

    return pl.pallas_call(
        kernel,
        out_shape=jax.ShapeDtypeStruct((samples, embed_count * width), jnp.bfloat16),
        in_specs=[whole(pltpu.HBM), whole()] + [whole()] * len(extra),
        out_specs=whole(),
        scratch_shapes=[
            pltpu.VMEM(spread.shape, jnp.bfloat16),
            pltpu.VMEM((lines, width), jnp.float32),
            pltpu.SemaphoreType.DMA((steps,)),
        ],
        compiler_params=params(),
        name="compress",
    )(in_hbm(spread), fetched, *extra)


def expand(spread, lead_grad, embed_count):
    owners, lines, cap = spread.shape
    samples = lines // embed_count
    width = lead_grad.shape[1] // embed_count
    part = tiles_of(owners, 4)

    def kernel(spread_ref, grad_ref, out_ref, tall, turned):
        for k in range(embed_count):
            piece = grad_ref[:, k * width : (k + 1) * width].astype(jnp.float32)
            tall[pl.ds(k, samples, stride=embed_count), :] = piece
        turned[...] = tall[...].T.astype(jnp.bfloat16)

        def body(step, carry):
            first = step * part
            right = jnp.concatenate([spread_ref[first + o] for o in range(part)], axis=1)
            term = jnp.dot(turned[...], right, preferred_element_type=jnp.float32)
            piece = term.T.astype(out_ref.dtype).reshape(part, cap, width)
            out_ref[tile_at(step, part)] = piece
            return carry

        lax.fori_loop(0, owners // part, body, 0)

    return pl.pallas_call(
        kernel,
        out_shape=jax.ShapeDtypeStruct((owners, cap, width), jnp.bfloat16),
        in_specs=[whole(), whole()],
        out_specs=whole(),
        scratch_shapes=[
            pltpu.VMEM((lines, width), jnp.float32),
            pltpu.VMEM((width, lines), jnp.bfloat16),
        ],
        compiler_params=params(),
        name="expand",
    )(spread, lead_grad)


def add_rows(targets, returned, outgoing, rows, base=None):
    count, width = returned.shape
    chunk = min(count, 1024)
    is_last = base is not None

    def kernel(targets_ref, back_ref, sent_ref, *refs):
        if is_last:
            base_ref, out_ref, terms, total, done = refs
            total[...] = base_ref[...]
        else:
            total, terms = refs
            total[...] = jnp.zeros_like(total)

        def fill(part, carry):
            first_line = pl.multiple_of(part * chunk, chunk)
            lines = pl.ds(first_line, chunk)
            terms[...] = back_ref[lines, :].astype(jnp.float32) + DECAY_WEIGHT * sent_ref[
                lines, :
            ].astype(jnp.float32)

            def body(group, inner):
                first = pl.multiple_of(group * UNROLL, UNROLL)
                places = [targets_ref[first_line + first + lane] for lane in range(UNROLL)]
                sums = [
                    total[pl.ds(places[lane], 1), :] + terms[pl.ds(first + lane, 1), :]
                    for lane in range(UNROLL)
                ]
                for lane in range(UNROLL):
                    total[pl.ds(places[lane], 1), :] = sums[lane]
                return inner

            lax.fori_loop(0, chunk // UNROLL, body, 0)
            return carry

        lax.fori_loop(0, count // chunk, fill, 0)
        if is_last:
            copy = pltpu.make_async_copy(total.at[pl.ds(0, rows), :], out_ref, done)
            copy.start()
            copy.wait()

    tall = (rows + 8, width)
    scratch = [pltpu.VMEM((chunk, width), jnp.float32)]
    if is_last:
        scratch += [pltpu.VMEM(tall, jnp.float32), pltpu.SemaphoreType.DMA]
    return pl.pallas_call(
        kernel,
        out_shape=jax.ShapeDtypeStruct((rows, width) if is_last else tall, jnp.float32),
        in_specs=[whole(pltpu.SMEM), whole(), whole()] + [whole()] * is_last,
        out_specs=whole(pl.ANY) if is_last else whole(),
        scratch_shapes=scratch,
        compiler_params=params(),
        name="add_rows",
    )(targets, returned, outgoing, *([base] if is_last else []))


GROUP = 32
TABLE_AXES = ("section", "table")
STAGE_LIMIT = 44 * 1024 * 1024
NT = (((1,), (1,)), ((), ()))


def dot_nt(left, right):
    return lax.dot_general(left, right, NT, preferred_element_type=jnp.float32)


def dot(left, right):
    return jnp.dot(left, right, preferred_element_type=jnp.float32)


def split_dot(left, right):
    high = left.astype(jnp.bfloat16)
    low = (left - high.astype(jnp.float32)).astype(jnp.bfloat16)
    return dot(high, right) + dot(low, right)


def same_sample(count):
    first = lax.broadcasted_iota(jnp.int32, (count * GROUP, count * GROUP), 0)
    second = lax.broadcasted_iota(jnp.int32, (count * GROUP, count * GROUP), 1)
    return (first & (GROUP - 1)) == (second & (GROUP - 1))


def stacked(ref, rows, count, width):
    return jnp.concatenate([ref[rows, k * width : (k + 1) * width] for k in range(count)], axis=0)


def repeated(proj):
    count, width = proj.shape
    lines = [jnp.broadcast_to(proj[k : k + 1, :], (GROUP, width)) for k in range(count)]
    return jnp.concatenate(lines, axis=0).astype(jnp.bfloat16)


def mix_forward(small, layer, acts, inter, scale, normed, count):
    batch, model_width = acts.shape
    width = model_width // count
    both = small[layer].astype(jnp.float32)
    proj = repeated(both[:count])
    keep = same_sample(count)
    for start in range(0, batch, GROUP):
        rows = pl.ds(start, GROUP)
        block = stacked(acts, rows, count, width)
        gram = jnp.where(keep, dot_nt(block, block), 0.0)
        mixed = split_dot(gram, proj)
        parts = [mixed[k * GROUP : (k + 1) * GROUP] for k in range(count)]
        squares = sum(part * part for part in parts)
        mean = jnp.sum(squares, axis=1, keepdims=True) * (1.0 / model_width)
        inv = lax.rsqrt(mean + EPSILON)
        scale[rows, :] = jnp.broadcast_to(inv, (GROUP, width))
        for k in range(count):
            columns = slice(k * width, (k + 1) * width)
            inter[rows, columns] = parts[k]
            gain = both[count + k : count + k + 1]
            normed[rows, columns] = (parts[k] * inv * gain).astype(jnp.bfloat16)


def hidden_tile(hidden_width):
    return min(hidden_width, 1024)


def model_tile(model_width):
    return min(model_width, 512)


def tile_at(step, size):
    return pl.ds(pl.multiple_of(step * size, size), size)


class Stream:
    def __init__(self, mine, own, other, held, sems, axis, size):
        self.mine, self.own, self.other, self.held, self.sems = mine, own, other, held, sems
        self.axis, self.size = axis, size
        self.tiles = own.shape[axis] // size

    def copy(self, source, step):
        cut = tile_at(step, self.size)
        index = (slice(None), cut) if self.axis == 1 else (cut, slice(None))
        return pltpu.make_async_copy(source.at[index], self.held.at[index], self.sems.at[step])

    def start(self):
        @pl.when(self.mine)
        def _():
            for step in range(self.tiles):
                self.copy(self.own, step).start()

        @pl.when(jnp.logical_not(self.mine))
        def _():
            for step in range(self.tiles):
                self.copy(self.other, step).start()

    def wait(self, step):
        self.copy(self.own, step).wait()


def no_wait(step):
    return None


def over_tiles(total, tile, many, wait, work):
    many = min(many, total // tile)

    def body(step, carry):
        for inner in range(many):
            wait(step * many + inner)
        work(tile_at(step, many * tile))
        return carry

    lax.fori_loop(0, total // (many * tile), body, 0)


def up_product(normed, w_up, hidden, turned, wait, many=1):
    def work(columns):
        opened = jnp.maximum(dot(normed[...], w_up[:, columns]), 0.0)
        hidden[:, columns] = opened.astype(jnp.bfloat16)
        turned[columns, :] = opened.T.astype(jnp.bfloat16)

    width = hidden.shape[1]
    over_tiles(width, hidden_tile(width), many, wait, work)


def down_product(hidden, w_down, acts, out, wait, many=1):
    def work(columns):
        term = dot(hidden[...], w_down[:, columns])
        out[:, columns] = (acts[:, columns].astype(jnp.float32) + term).astype(jnp.bfloat16)

    width = out.shape[1]
    over_tiles(width, model_tile(width), many, wait, work)


def turn(rows, turned):
    turned[...] = rows[...].astype(jnp.float32).T.astype(jnp.bfloat16)


def opened_only(hidden, grad):
    return jnp.where(hidden.astype(jnp.float32) > 0.0, grad, 0.0).astype(jnp.bfloat16)


def down_back(grad, w_down, hidden, out, wait, many=1):
    def work(lines):
        g_hidden = dot(w_down[lines, :], grad[...])
        if hidden is not None:
            out[lines, :] = opened_only(hidden[lines, :], g_hidden)
        else:
            out[lines, :] = g_hidden.astype(jnp.bfloat16)

    width = out.shape[0]
    over_tiles(width, hidden_tile(width), many, wait, work)


def up_back(g_before, w_up, weighted, wait, many=1):
    def work(columns):
        weighted[:, columns] = dot(w_up[columns, :], g_before[...]).T

    width = weighted.shape[1]
    over_tiles(width, model_tile(width), many, wait, work)


def mix_backward(small, layer, grad, acts, inter, scale, weighted, out, count):
    batch, model_width = acts.shape
    width = model_width // count
    both = small[layer].astype(jnp.float32)
    proj = repeated(both[:count])
    keep = same_sample(count)
    for start in range(0, batch, GROUP):
        rows = pl.ds(start, GROUP)
        columns = [slice(k * width, (k + 1) * width) for k in range(count)]
        gained = [weighted[rows, columns[k]] * both[count + k : count + k + 1] for k in range(count)]
        shared = sum(gained[k] * inter[rows, columns[k]] for k in range(count))
        mean = jnp.sum(shared, axis=1, keepdims=True) * (1.0 / model_width)
        inv = scale[rows, 0:1]
        pull = inv * inv * mean
        parts = [
            (inv * (gained[k] - inter[rows, columns[k]] * pull)).astype(jnp.bfloat16)
            for k in range(count)
        ]
        block = stacked(acts, rows, count, width)
        g_inter = jnp.concatenate(parts, axis=0)
        left = jnp.concatenate([g_inter, proj], axis=1)
        right = jnp.concatenate([proj, g_inter], axis=1)
        links = jnp.where(keep, dot_nt(left, right), 0.0)
        g_acts = split_dot(links, block)
        for k in range(count):
            piece = g_acts[k * GROUP : (k + 1) * GROUP] + grad[rows, columns[k]].astype(jnp.float32)
            out[rows, columns[k]] = piece.astype(jnp.bfloat16)


def saved_shapes(batch, model_width, hidden_width, width):
    return [
        jax.ShapeDtypeStruct((2, hidden_width, batch), jnp.bfloat16),
        jax.ShapeDtypeStruct((2, batch, model_width), jnp.float32),
        jax.ShapeDtypeStruct((2, batch, width), jnp.float32),
        jax.ShapeDtypeStruct((2, batch, model_width), jnp.bfloat16),
    ]


def weight_specs():
    return [whole()] + [whole(pltpu.HBM)] * 4


def weight_scratch(model_width, hidden_width):
    tiles = max(hidden_width // hidden_tile(hidden_width), model_width // model_tile(model_width))
    return [
        pltpu.VMEM((2, model_width, hidden_width), jnp.bfloat16),
        pltpu.VMEM((2, hidden_width, model_width), jnp.bfloat16),
        pltpu.SemaphoreType.DMA((4, tiles)),
    ]


def streams_of(core, weights, held, forward):
    own_up, other_up, own_down, other_down = weights
    held_up, held_down, sems = held
    model_width, hidden_width = own_up.shape
    wide, narrow = hidden_tile(hidden_width), model_tile(model_width)
    made = []
    for layer in (0, 1):
        mine = core == layer
        up_forward, down_forward = forward[layer]
        up_cut = (1, wide) if up_forward else (0, narrow)
        down_cut = (1, narrow) if down_forward else (0, wide)
        made.append(
            (
                Stream(mine, own_up, other_up, held_up.at[layer], sems.at[2 * layer], *up_cut),
                Stream(mine, own_down, other_down, held_down.at[layer], sems.at[2 * layer + 1], *down_cut),
            )
        )
    return made


def stage_cost(products, batch, model_width, hidden_width):
    return pl.CostEstimate(
        flops=2 * products * batch * model_width * hidden_width, bytes_accessed=1 << 20, transcendentals=0
    )


def stage_params():
    return pltpu.CompilerParams(vmem_limit_bytes=STAGE_LIMIT)


def forward_stage(place, pieces, top, weights, count):
    batch, model_width = top.shape
    hidden_width = weights[1].shape[1]
    width = model_width // count

    def kernel(place_ref, *refs):
        piece_refs, (top_ref, small_ref), refs = refs[: len(pieces)], refs[len(pieces) :][:2], refs[len(pieces) + 2 :]
        matrices, refs = refs[:4], refs[4:]
        out_ref, hid, inter, scale, kept, g_hidden = refs[:6]
        held, (normed, hidden, top_turned) = refs[6:9], refs[9:]
        core = place_ref[0]

        @pl.when(place_ref[1] == 1)
        def _():
            layers = streams_of(core, matrices, held, [(True, True), (True, True)])
            for up, down in layers:
                up.start()
                down.start()
            start = 0
            for piece in piece_refs:
                kept[0, start : start + piece.shape[0], :] = piece[...]
                start += piece.shape[0]
            for layer, (up, down) in enumerate(layers):
                mix_forward(
                    small_ref, layer, kept.at[layer], inter.at[layer], scale.at[layer], normed, count
                )
                up_product(normed, up.held, hidden, hid.at[layer], up.wait)
                to = kept.at[1] if layer == 0 else out_ref
                down_product(hidden, down.held, kept.at[layer], to, down.wait)

        @pl.when(place_ref[2] == 1)
        def _():
            layers = streams_of(core, matrices, held, [(True, True), (True, False)])
            down = layers[1][1]
            down.start()
            turn(top_ref, top_turned)
            down_back(top_turned, down.held, None, g_hidden, down.wait)

    out = pl.pallas_call(
        kernel,
        out_shape=[jax.ShapeDtypeStruct(top.shape, jnp.bfloat16)]
        + saved_shapes(batch, model_width, hidden_width, width)
        + [jax.ShapeDtypeStruct((hidden_width, batch), jnp.bfloat16)],
        in_specs=[whole(pltpu.SMEM)] + [whole()] * (len(pieces) + 1) + weight_specs(),
        out_specs=[whole()] * 6,
        scratch_shapes=weight_scratch(model_width, hidden_width)
        + [
            pltpu.VMEM((batch, model_width), jnp.bfloat16),
            pltpu.VMEM((batch, hidden_width), jnp.bfloat16),
            pltpu.VMEM((model_width, batch), jnp.bfloat16),
        ],
        compiler_params=stage_params(),
        cost_estimate=stage_cost(4, batch, model_width, hidden_width),
        name="forward_stage",
    )(place, *pieces, top, weights[0], *map(in_hbm, weights[1:]))
    return out[0], out[1:5], out[5]


def turn_stage(place, acts, top, g_hidden, weights, count):
    batch, model_width = acts.shape
    hidden_width = weights[1].shape[1]
    width = model_width // count

    def kernel(place_ref, acts_ref, top_ref, ghid_ref, small_ref, *refs):
        matrices, refs = refs[:4], refs[4:]
        out_ref, held = refs[0], refs[1:4]
        hid, hidden, inter, scale, upper, grad, turned, normed, weighted, g_before = refs[4:]

        @pl.when(place_ref[1] == 1)
        def _():
            layers = streams_of(place_ref[0], matrices, held, [(True, True), (True, True)])
            (up0, down0), (up1, down1) = layers
            for stream in (up0, down0, up1):
                stream.start()
            mix_forward(small_ref, 0, acts_ref, inter.at[0], scale.at[0], normed, count)
            up_product(normed, up0.held, hidden, hid, up0.wait)
            down_product(hidden, down0.held, acts_ref, upper, down0.wait, 2)
            mix_forward(small_ref, 1, upper, inter.at[1], scale.at[1], normed, count)

            def masked(columns):
                before = dot(normed[...], up1.held[:, columns])
                opened = jnp.maximum(before, 0.0).T
                g_before[columns, :] = opened_only(opened, ghid_ref[columns, :].astype(jnp.float32))

            over_tiles(hidden_width, hidden_tile(hidden_width), 2, up1.wait, masked)
            up_back(g_before, up1.held, weighted, no_wait, 2)
            mix_backward(small_ref, 1, top_ref, upper, inter.at[1], scale.at[1], weighted, grad, count)
            turn(grad, turned)
            down_back(turned, down0.held, hid, g_before, no_wait, 2)
            up_back(g_before, up0.held, weighted, no_wait, 2)
            mix_backward(small_ref, 0, grad, acts_ref, inter.at[0], scale.at[0], weighted, out_ref, count)

    return pl.pallas_call(
        kernel,
        out_shape=jax.ShapeDtypeStruct(acts.shape, jnp.bfloat16),
        in_specs=[whole(pltpu.SMEM)] + [whole()] * 3 + weight_specs(),
        out_specs=whole(),
        scratch_shapes=weight_scratch(model_width, hidden_width)
        + [
            pltpu.VMEM((hidden_width, batch), jnp.bfloat16),
            pltpu.VMEM((batch, hidden_width), jnp.bfloat16),
            pltpu.VMEM((2, batch, model_width), jnp.float32),
            pltpu.VMEM((2, batch, width), jnp.float32),
            pltpu.VMEM((batch, model_width), jnp.bfloat16),
            pltpu.VMEM((batch, model_width), jnp.bfloat16),
            pltpu.VMEM((model_width, batch), jnp.bfloat16),
            pltpu.VMEM((batch, model_width), jnp.bfloat16),
            pltpu.VMEM((batch, model_width), jnp.float32),
            pltpu.VMEM((hidden_width, batch), jnp.bfloat16),
        ],
        compiler_params=stage_params(),
        cost_estimate=stage_cost(6, batch, model_width, hidden_width),
        name="turn_stage",
    )(place, acts, top, g_hidden, weights[0], *map(in_hbm, weights[1:]))


def backward_stage(place, grad, saved, weights, count):
    batch, model_width = grad.shape
    hidden_width = weights[1].shape[1]

    def kernel(place_ref, grad_ref, hid, inter, scale, kept, small_ref, *refs):
        matrices, refs = refs[:4], refs[4:]
        out_ref, held = refs[0], refs[1:4]
        middle, turned, weighted, g_before = refs[4:]

        @pl.when(place_ref[1] == 1)
        def _():
            layers = streams_of(place_ref[0], matrices, held, [(False, False), (False, False)])
            for up, down in reversed(layers):
                down.start()
                up.start()
            for layer, given, to in ((1, grad_ref, middle), (0, middle, out_ref)):
                up, down = layers[layer]
                turn(given, turned)
                down_back(turned, down.held, hid.at[layer], g_before, down.wait, 2 - layer)
                up_back(g_before, up.held, weighted, up.wait, 2)
                mix_backward(
                    small_ref, layer, given, kept.at[layer], inter.at[layer], scale.at[layer],
                    weighted, to, count,
                )

    return pl.pallas_call(
        kernel,
        out_shape=jax.ShapeDtypeStruct(grad.shape, jnp.bfloat16),
        in_specs=[whole(pltpu.SMEM)] + [whole()] * 5 + weight_specs(),
        out_specs=whole(),
        scratch_shapes=weight_scratch(model_width, hidden_width)
        + [
            pltpu.VMEM((batch, model_width), jnp.bfloat16),
            pltpu.VMEM((model_width, batch), jnp.bfloat16),
            pltpu.VMEM((batch, model_width), jnp.float32),
            pltpu.VMEM((hidden_width, batch), jnp.bfloat16),
        ],
        compiler_params=stage_params(),
        cost_estimate=stage_cost(4, batch, model_width, hidden_width),
        name="backward_stage",
    )(place, grad, *saved, weights[0], *map(in_hbm, weights[1:]))


def swapped(value, section_count):
    return lax.ppermute(value, "section", [(s, s ^ 1) for s in range(section_count)])


def moved(value, from_stage, to_stage):
    pairs = [(2 * from_stage + core, 2 * to_stage + core) for core in (0, 1)]
    return lax.ppermute(value, "section", pairs)


def mirror(value):
    along = lax.axis_size("table")
    return lax.ppermute(value, "table", [(t, (t + along // 2) % along) for t in range(along)])


def swap_in_half(value):
    along = lax.axis_size("table")
    half = along // 2
    groups = [
        [s * along + h * half + t for s in range(lax.axis_size("section")) for t in range(half)]
        for h in (0, 1)
    ]
    return lax.all_to_all(
        value, TABLE_AXES, split_axis=0, concat_axis=0, axis_index_groups=groups, tiled=True
    )


def by_half(per_asker, half_at):
    sections = lax.axis_size("section")
    half = lax.axis_size("table") // 2
    split = per_asker.reshape((sections, 2, half) + per_asker.shape[1:])
    chosen = lax.dynamic_index_in_dim(split, half_at, 1, keepdims=False)
    return chosen.reshape((sections * half,) + per_asker.shape[1:])


def after(value, earlier):
    return lax.optimization_barrier((value, earlier))[0]


def per_device(
    emb_table,
    lcb_weight,
    fm_proj,
    norm_gain,
    w_up,
    w_down,
    top_grad,
    lookup_slot,
    wanted_rows,
    row_counts,
):
    section_count = lax.axis_size("section")
    along = lax.axis_size("table")
    half = along // 2
    near_owners = section_count * half
    stages = section_count // 2
    stage = lax.axis_index("section") // 2
    core = lax.axis_index("section") % 2
    my_half = lax.axis_index("table") // half
    cap = wanted_rows.shape[2]
    rows, embed_width = emb_table.shape
    embed_count = lcb_weight.shape[0]
    look_dev = lookup_slot.shape[1]
    model_width = top_grad.shape[3]

    own_slots = lookup_slot[0]
    mirror_slots = mirror(own_slots)
    small = jnp.concatenate([fm_proj[0], norm_gain[0].reshape(embed_count, -1)], axis=0)
    other_up = swapped(w_up[0], section_count)
    other_down = swapped(w_down[0], section_count)
    other_small = swapped(small, section_count)

    picked_far = by_half(wanted_rows[0], 1 - my_half)
    picked_near = by_half(wanted_rows[0], my_half)
    sent_far = pick_rows(emb_table, picked_far.reshape(-1))
    line_shape = (near_owners, cap, embed_width)
    fetched_far = swap_in_half(after(sent_far, mirror_slots).reshape(line_shape))
    sent_near = pick_rows(emb_table, after(picked_near, sent_far).reshape(-1))
    fetched_near = swap_in_half(after(sent_near, fetched_far).reshape(line_shape))

    def spread_of(slots):
        owner, column = slots // cap, slots % cap
        place = owner % along
        near = jnp.where(place // half == my_half, owner // along * half + place % half, near_owners)
        return spread_weights(near * cap + column, lcb_weight, near_owners, cap)

    spread_far = spread_of(mirror_slots)
    spread_near = spread_of(after(own_slots, fetched_far))
    smalls = jnp.stack(
        [jnp.where(core == 0, small, other_small), jnp.where(core == 0, other_small, small)]
    )
    weights = [smalls, w_up[0], other_up, w_down[0], other_down]
    far_part = mirror(compress(spread_far, fetched_far, embed_count))
    lead = compress(spread_near, fetched_near, embed_count, far_part)
    pieces = [lead] + [moved(lead, s, 0) for s in range(1, stages)]
    top = top_grad.reshape(stages, 2, look_dev, model_width)
    top = lax.dynamic_index_in_dim(top, core, 1, keepdims=False).reshape(-1, model_width)

    def at(tick):
        is_last = (stage == stages - 1) & (tick == 0)
        return jnp.stack([core, stage == tick, is_last]).astype(jnp.int32)

    saved = None
    for tick in range(stages - 1):
        out, fresh, product = forward_stage(at(tick), pieces, top, weights, embed_count)
        if saved is None:
            saved, g_hidden = fresh, product
        else:
            saved = [jnp.where(stage == tick, new, old) for new, old in zip(fresh, saved)]
        pieces = [moved(out, tick, tick + 1)]
    grad = turn_stage(at(stages - 1), pieces[0], top, g_hidden, weights, embed_count)
    for tick in reversed(range(stages - 1)):
        grad = moved(grad, tick + 1, tick)
        grad = backward_stage(at(tick), grad, saved, weights, embed_count)

    own_grad = grad[:look_dev]
    for s in range(1, stages):
        piece = grad[s * look_dev : (s + 1) * look_dev]
        own_grad = jnp.where(stage == s, moved(piece, 0, s), own_grad)
    mirror_grad = mirror(own_grad)

    def targets_of(picked, half_at):
        live_slots = jnp.arange(cap) < by_half(row_counts[0], half_at)[:, None]
        return jnp.where(live_slots, picked, rows).reshape(-1)

    near_grad = expand(spread_near, own_grad, embed_count)
    returned_near = swap_in_half(near_grad)
    far_grad = expand(spread_far, mirror_grad, embed_count)
    returned_far = swap_in_half(after(far_grad, returned_near))
    summed = add_rows(
        targets_of(picked_near, my_half),
        after(returned_near, far_grad).reshape(-1, embed_width),
        sent_near,
        rows,
    )
    return add_rows(
        targets_of(picked_far, 1 - my_half), returned_far.reshape(-1, embed_width), sent_far, rows, summed
    )


def solution(mesh):
    in_specs = (
        P(("section", "table"), None),
        P(),
        P("section", None, None),
        P("section", None),
        P("section", None, None),
        P("section", None, None),
        P("table", None, None, None),
        P("table", "section", None),
        P(("section", "table"), None, None),
        P(("section", "table"), None),
    )
    out_specs = P(("section", "table"), None)
    return jax.shard_map(
        per_device, mesh=mesh, in_specs=in_specs, out_specs=out_specs, check_vma=False
    )
```

```python
import jax
import jax.numpy as jnp
from jax import lax
from jax.experimental import pallas as pl
from jax.experimental.pallas import tpu as pltpu
from jax.sharding import PartitionSpec as P

EPSILON = 1e-05
DECAY_WEIGHT = 0.5
VMEM_LIMIT = 28 * 1024 * 1024
UNROLL = 32


def whole(memory_space=pltpu.VMEM):
    return pl.BlockSpec(memory_space=memory_space)


def in_hbm(value):
    return pltpu.with_memory_space_constraint(value, pltpu.HBM)


def params():
    return pltpu.CompilerParams(vmem_limit_bytes=VMEM_LIMIT)


def tiles_of(count, most):
    return max(step for step in range(1, most + 1) if count % step == 0)


def pick_rows(emb_table, picked):
    rows, width = emb_table.shape
    count = picked.shape[0]
    chunk = min(count, 1024)

    def kernel(picked_ref, table_ref, out_ref, wide, lines):
        wide[...] = table_ref[...].astype(jnp.float32)

        def fill(part, carry):
            base = pl.multiple_of(part * chunk, chunk)

            def body(group, inner):
                first = pl.multiple_of(group * UNROLL, UNROLL)
                for lane in range(UNROLL):
                    row = picked_ref[base + first + lane]
                    lines[pl.ds(first + lane, 1), :] = wide[pl.ds(row, 1), :]
                return inner

            lax.fori_loop(0, chunk // UNROLL, body, 0)
            out_ref[pl.ds(base, chunk), :] = lines[...].astype(out_ref.dtype)
            return carry

        lax.fori_loop(0, count // chunk, fill, 0)

    return pl.pallas_call(
        kernel,
        out_shape=jax.ShapeDtypeStruct((count, width), emb_table.dtype),
        in_specs=[whole(pltpu.SMEM), whole()],
        out_specs=whole(),
        scratch_shapes=[
            pltpu.VMEM((rows, width), jnp.float32),
            pltpu.VMEM((chunk, width), jnp.float32),
        ],
        compiler_params=params(),
        name="pick_rows",
    )(picked, emb_table)


def spread_weights(codes, lcb_weight, owners, cap):
    samples, feature_count = codes.shape
    embed_count = lcb_weight.shape[0]
    group = tiles_of(samples, 16)

    def kernel(codes_ref, lcb_ref, out_ref):
        lcb = lcb_ref[...].astype(jnp.float32)
        owner_of = lax.broadcasted_iota(jnp.int32, (owners, embed_count, feature_count), 0)
        column_of = lax.broadcasted_iota(jnp.int32, (cap, feature_count), 0)
        for pair in range(0, group, 2):
            made = []
            for sample in (pair, pair + 1):
                slots = codes_ref[sample : sample + 1, :]
                owner = lax.div(slots, cap)
                column = slots - owner * cap
                left = jnp.where(owner_of == owner[None], lcb[None], 0.0)
                left = left.reshape(owners * embed_count, feature_count).astype(jnp.bfloat16)
                right = jnp.where(column_of == column, 1.0, 0.0).astype(jnp.bfloat16)
                both = lax.dot_general(
                    left, right, (((1,), (1,)), ((), ())), preferred_element_type=jnp.float32
                )
                made.append(both.reshape(owners, embed_count, cap))
            rows = pl.ds(pair * embed_count, 2 * embed_count)
            out_ref[:, rows, :] = jnp.concatenate(made, axis=1).astype(out_ref.dtype)

    return pl.pallas_call(
        kernel,
        out_shape=pltpu.HBM((owners, samples * embed_count, cap), jnp.bfloat16),
        grid=(samples // group,),
        in_specs=[
            pl.BlockSpec((group, feature_count), lambda i: (i, 0)),
            pl.BlockSpec((embed_count, feature_count), lambda i: (0, 0)),
        ],
        out_specs=pl.BlockSpec((owners, group * embed_count, cap), lambda i: (0, i, 0)),
        compiler_params=params(),
        cost_estimate=pl.CostEstimate(
            flops=2 * samples * owners * embed_count * feature_count * cap,
            bytes_accessed=2 * owners * samples * embed_count * cap,
            transcendentals=0,
        ),
        name="spread_weights",
    )(codes, lcb_weight)


def compress(spread, fetched, view, embed_count, kind):
    owners, lines, cap = spread.shape
    width = fetched.shape[3]
    samples = lines // embed_count
    part = tiles_of(owners, 4)
    steps = owners // part

    def kernel(spread_ref, rows_ref, out_ref, held, total, sems):
        def copy(step):
            piece = tile_at(step, part)
            return pltpu.make_async_copy(spread_ref.at[piece], held.at[piece], sems.at[step])

        for step in range(steps):
            copy(step).start()
        total[...] = jnp.zeros_like(total)

        def body(step, carry):
            copy(step).wait()
            first = step * part
            left = jnp.concatenate([held[first + o] for o in range(part)], axis=1)
            right = jnp.concatenate([rows_ref[first + o, view] for o in range(part)], axis=0)
            total[...] += jnp.dot(left, right, preferred_element_type=jnp.float32)
            return carry

        lax.fori_loop(0, steps, body, 0)
        for k in range(embed_count):
            columns = slice(k * width, (k + 1) * width)
            piece = total[pl.ds(k, samples, stride=embed_count), :]
            out_ref[:, columns] = piece.astype(out_ref.dtype)

    return pl.pallas_call(
        kernel,
        out_shape=jax.ShapeDtypeStruct((samples, embed_count * width), kind),
        in_specs=[whole(pltpu.HBM), whole()],
        out_specs=whole(),
        scratch_shapes=[
            pltpu.VMEM(spread.shape, jnp.bfloat16),
            pltpu.VMEM((lines, width), jnp.float32),
            pltpu.SemaphoreType.DMA((steps,)),
        ],
        compiler_params=params(),
        name="compress",
    )(in_hbm(spread), fetched)


def expand(spread, lead_grad, embed_count, near=None):
    owners, lines, cap = spread.shape
    samples = lines // embed_count
    width = lead_grad.shape[1] // embed_count
    part = tiles_of(owners, 4)
    extra = [] if near is None else [near]

    def kernel(spread_ref, grad_ref, *refs):
        near_refs, (out_ref, tall, turned) = refs[: len(extra)], refs[len(extra) :]
        for k in range(embed_count):
            piece = grad_ref[:, k * width : (k + 1) * width].astype(jnp.float32)
            tall[pl.ds(k, samples, stride=embed_count), :] = piece
        turned[...] = tall[...].T.astype(jnp.bfloat16)

        def body(step, carry):
            first = step * part
            right = jnp.concatenate([spread_ref[first + o] for o in range(part)], axis=1)
            term = jnp.dot(turned[...], right, preferred_element_type=jnp.float32)
            piece = term.T.astype(out_ref.dtype).reshape(part, cap, width)
            if near_refs:
                for o in range(part):
                    out_ref[first + o, 0] = near_refs[0][first + o]
                    out_ref[first + o, 1] = piece[o]
            else:
                out_ref[tile_at(step, part)] = piece
            return carry

        lax.fori_loop(0, owners // part, body, 0)

    views = () if near is None else (2,)
    return pl.pallas_call(
        kernel,
        out_shape=jax.ShapeDtypeStruct((owners,) + views + (cap, width), jnp.bfloat16),
        in_specs=[whole()] * (2 + len(extra)),
        out_specs=whole(),
        scratch_shapes=[
            pltpu.VMEM((lines, width), jnp.float32),
            pltpu.VMEM((width, lines), jnp.bfloat16),
        ],
        compiler_params=params(),
        name="expand",
    )(spread, lead_grad, *extra)


def add_rows(targets, returned, outgoing, rows):
    count, width = returned.shape
    chunk = min(count, 1024)

    def kernel(targets_ref, back_ref, sent_ref, out_ref, total, terms, done):
        total[...] = jnp.zeros_like(total)

        def fill(part, carry):
            base = pl.multiple_of(part * chunk, chunk)
            lines = pl.ds(base, chunk)
            terms[...] = back_ref[lines, :].astype(jnp.float32) + DECAY_WEIGHT * sent_ref[
                lines, :
            ].astype(jnp.float32)

            def body(group, inner):
                first = pl.multiple_of(group * UNROLL, UNROLL)
                places = [targets_ref[base + first + lane] for lane in range(UNROLL)]
                sums = [
                    total[pl.ds(places[lane], 1), :] + terms[pl.ds(first + lane, 1), :]
                    for lane in range(UNROLL)
                ]
                for lane in range(UNROLL):
                    total[pl.ds(places[lane], 1), :] = sums[lane]
                return inner

            lax.fori_loop(0, chunk // UNROLL, body, 0)
            return carry

        lax.fori_loop(0, count // chunk, fill, 0)
        copy = pltpu.make_async_copy(total.at[pl.ds(0, rows), :], out_ref, done)
        copy.start()
        copy.wait()

    return pl.pallas_call(
        kernel,
        out_shape=jax.ShapeDtypeStruct((rows, width), jnp.float32),
        in_specs=[whole(pltpu.SMEM), whole(), whole()],
        out_specs=whole(pl.ANY),
        scratch_shapes=[
            pltpu.VMEM((rows + 8, width), jnp.float32),
            pltpu.VMEM((chunk, width), jnp.float32),
            pltpu.SemaphoreType.DMA,
        ],
        compiler_params=params(),
        name="add_rows",
    )(targets, returned, outgoing)


GROUP = 16
TABLE_AXES = ("section", "table")
STAGE_LIMIT = 44 * 1024 * 1024
NT = (((1,), (1,)), ((), ()))


def dot_nt(left, right):
    return lax.dot_general(left, right, NT, preferred_element_type=jnp.float32)


def dot(left, right):
    return jnp.dot(left, right, preferred_element_type=jnp.float32)


def split_dot(left, right):
    high = left.astype(jnp.bfloat16)
    low = (left - high.astype(jnp.float32)).astype(jnp.bfloat16)
    return dot(high, right) + dot(low, right)


def same_sample(count):
    first = lax.broadcasted_iota(jnp.int32, (count * GROUP, count * GROUP), 0)
    second = lax.broadcasted_iota(jnp.int32, (count * GROUP, count * GROUP), 1)
    return (first & (GROUP - 1)) == (second & (GROUP - 1))


def stacked(ref, rows, count, width):
    return jnp.concatenate([ref[rows, k * width : (k + 1) * width] for k in range(count)], axis=0)


def repeated(proj):
    count, width = proj.shape
    lines = [jnp.broadcast_to(proj[k : k + 1, :], (GROUP, width)) for k in range(count)]
    return jnp.concatenate(lines, axis=0).astype(jnp.bfloat16)


def mix_forward(small, layer, acts, inter, scale, normed, count):
    batch, model_width = acts.shape
    width = model_width // count
    both = small[layer].astype(jnp.float32)
    proj = repeated(both[:count])
    keep = same_sample(count)
    for start in range(0, batch, GROUP):
        rows = pl.ds(start, GROUP)
        block = stacked(acts, rows, count, width)
        gram = jnp.where(keep, dot_nt(block, block), 0.0)
        mixed = split_dot(gram, proj)
        parts = [mixed[k * GROUP : (k + 1) * GROUP] for k in range(count)]
        squares = sum(part * part for part in parts)
        mean = jnp.sum(squares, axis=1, keepdims=True) * (1.0 / model_width)
        inv = lax.rsqrt(mean + EPSILON)
        scale[rows, :] = jnp.broadcast_to(inv, (GROUP, width))
        for k in range(count):
            columns = slice(k * width, (k + 1) * width)
            inter[rows, columns] = parts[k]
            gain = both[count + k : count + k + 1]
            normed[rows, columns] = (parts[k] * inv * gain).astype(jnp.bfloat16)


def hidden_tile(hidden_width):
    return min(hidden_width, 1024)


def model_tile(model_width):
    return min(model_width, 512)


def tile_at(step, size):
    return pl.ds(pl.multiple_of(step * size, size), size)


class Stream:
    def __init__(self, mine, own, other, held, sems, axis, size):
        self.mine, self.own, self.other, self.held, self.sems = mine, own, other, held, sems
        self.axis, self.size = axis, size
        self.tiles = own.shape[axis] // size

    def copy(self, source, step):
        cut = tile_at(step, self.size)
        index = (slice(None), cut) if self.axis == 1 else (cut, slice(None))
        return pltpu.make_async_copy(source.at[index], self.held.at[index], self.sems.at[step])

    def start(self):
        @pl.when(self.mine)
        def _():
            for step in range(self.tiles):
                self.copy(self.own, step).start()

        @pl.when(jnp.logical_not(self.mine))
        def _():
            for step in range(self.tiles):
                self.copy(self.other, step).start()

    def wait(self, step):
        self.copy(self.own, step).wait()


def no_wait(step):
    return None


def over_tiles(total, tile, many, wait, work):
    many = min(many, total // tile)

    def body(step, carry):
        for inner in range(many):
            wait(step * many + inner)
        work(tile_at(step, many * tile))
        return carry

    lax.fori_loop(0, total // (many * tile), body, 0)


def up_product(normed, w_up, hidden, turned, wait, many=1):
    def work(columns):
        opened = jnp.maximum(dot(normed[...], w_up[:, columns]), 0.0)
        hidden[:, columns] = opened.astype(jnp.bfloat16)
        turned[columns, :] = opened.T.astype(jnp.bfloat16)

    width = hidden.shape[1]
    over_tiles(width, hidden_tile(width), many, wait, work)


def down_product(hidden, w_down, acts, out, wait, many=1):
    def work(columns):
        term = dot(hidden[...], w_down[:, columns])
        out[:, columns] = (acts[:, columns].astype(jnp.float32) + term).astype(jnp.bfloat16)

    width = out.shape[1]
    over_tiles(width, model_tile(width), many, wait, work)


def turn(rows, turned):
    turned[...] = rows[...].astype(jnp.float32).T.astype(jnp.bfloat16)


def opened_only(hidden, grad):
    return jnp.where(hidden.astype(jnp.float32) > 0.0, grad, 0.0).astype(jnp.bfloat16)


def down_back(grad, w_down, hidden, out, wait, many=1):
    def work(lines):
        g_hidden = dot(w_down[lines, :], grad[...])
        if hidden is not None:
            out[lines, :] = opened_only(hidden[lines, :], g_hidden)
        else:
            out[lines, :] = g_hidden.astype(jnp.bfloat16)

    width = out.shape[0]
    over_tiles(width, hidden_tile(width), many, wait, work)


def up_back(g_before, w_up, weighted, wait, many=1):
    def work(columns):
        weighted[:, columns] = dot(w_up[columns, :], g_before[...]).T

    width = weighted.shape[1]
    over_tiles(width, model_tile(width), many, wait, work)


def mix_backward(small, layer, grad, acts, inter, scale, weighted, out, count):
    batch, model_width = acts.shape
    width = model_width // count
    both = small[layer].astype(jnp.float32)
    proj = repeated(both[:count])
    keep = same_sample(count)
    for start in range(0, batch, GROUP):
        rows = pl.ds(start, GROUP)
        columns = [slice(k * width, (k + 1) * width) for k in range(count)]
        gained = [weighted[rows, columns[k]] * both[count + k : count + k + 1] for k in range(count)]
        shared = sum(gained[k] * inter[rows, columns[k]] for k in range(count))
        mean = jnp.sum(shared, axis=1, keepdims=True) * (1.0 / model_width)
        inv = scale[rows, 0:1]
        pull = inv * inv * mean
        parts = [
            (inv * (gained[k] - inter[rows, columns[k]] * pull)).astype(jnp.bfloat16)
            for k in range(count)
        ]
        block = stacked(acts, rows, count, width)
        g_inter = jnp.concatenate(parts, axis=0)
        left = jnp.concatenate([g_inter, proj], axis=1)
        right = jnp.concatenate([proj, g_inter], axis=1)
        links = jnp.where(keep, dot_nt(left, right), 0.0)
        g_acts = split_dot(links, block)
        for k in range(count):
            piece = g_acts[k * GROUP : (k + 1) * GROUP] + grad[rows, columns[k]].astype(jnp.float32)
            out[rows, columns[k]] = piece.astype(jnp.bfloat16)


def saved_shapes(batch, model_width, hidden_width, width):
    return [
        jax.ShapeDtypeStruct((2, hidden_width, batch), jnp.bfloat16),
        jax.ShapeDtypeStruct((2, batch, model_width), jnp.float32),
        jax.ShapeDtypeStruct((2, batch, width), jnp.float32),
        jax.ShapeDtypeStruct((2, batch, model_width), jnp.bfloat16),
    ]


def weight_specs():
    return [whole()] + [whole(pltpu.HBM)] * 4


def weight_scratch(model_width, hidden_width):
    tiles = max(hidden_width // hidden_tile(hidden_width), model_width // model_tile(model_width))
    return [
        pltpu.VMEM((2, model_width, hidden_width), jnp.bfloat16),
        pltpu.VMEM((2, hidden_width, model_width), jnp.bfloat16),
        pltpu.SemaphoreType.DMA((4, tiles)),
    ]


def streams_of(core, weights, held, forward):
    own_up, other_up, own_down, other_down = weights
    held_up, held_down, sems = held
    model_width, hidden_width = own_up.shape
    wide, narrow = hidden_tile(hidden_width), model_tile(model_width)
    made = []
    for layer in (0, 1):
        mine = core == layer
        up_forward, down_forward = forward[layer]
        up_cut = (1, wide) if up_forward else (0, narrow)
        down_cut = (1, narrow) if down_forward else (0, wide)
        made.append(
            (
                Stream(mine, own_up, other_up, held_up.at[layer], sems.at[2 * layer], *up_cut),
                Stream(mine, own_down, other_down, held_down.at[layer], sems.at[2 * layer + 1], *down_cut),
            )
        )
    return made


def stage_cost(products, batch, model_width, hidden_width):
    return pl.CostEstimate(
        flops=2 * products * batch * model_width * hidden_width, bytes_accessed=1 << 20, transcendentals=0
    )


def stage_params():
    return pltpu.CompilerParams(vmem_limit_bytes=STAGE_LIMIT)


def forward_stage(place, pieces, top, weights, count):
    batch, model_width = top.shape
    hidden_width = weights[1].shape[1]
    width = model_width // count

    def kernel(place_ref, *refs):
        piece_refs, (top_ref, small_ref), refs = refs[: len(pieces)], refs[len(pieces) :][:2], refs[len(pieces) + 2 :]
        matrices, refs = refs[:4], refs[4:]
        out_ref, hid, inter, scale, kept, g_hidden = refs[:6]
        held, (normed, hidden, top_turned) = refs[6:9], refs[9:]
        core = place_ref[0]

        @pl.when(place_ref[1] == 1)
        def _():
            layers = streams_of(core, matrices, held, [(True, True), (True, True)])
            for up, down in layers:
                up.start()
                down.start()
            start = 0
            for piece in piece_refs:
                kept[0, start : start + piece.shape[0], :] = piece[...]
                start += piece.shape[0]
            for layer, (up, down) in enumerate(layers):
                mix_forward(
                    small_ref, layer, kept.at[layer], inter.at[layer], scale.at[layer], normed, count
                )
                up_product(normed, up.held, hidden, hid.at[layer], up.wait)
                to = kept.at[1] if layer == 0 else out_ref
                down_product(hidden, down.held, kept.at[layer], to, down.wait)

        @pl.when(place_ref[2] == 1)
        def _():
            layers = streams_of(core, matrices, held, [(True, True), (True, False)])
            down = layers[1][1]
            down.start()
            turn(top_ref, top_turned)
            down_back(top_turned, down.held, None, g_hidden, down.wait)

    out = pl.pallas_call(
        kernel,
        out_shape=[jax.ShapeDtypeStruct(top.shape, jnp.bfloat16)]
        + saved_shapes(batch, model_width, hidden_width, width)
        + [jax.ShapeDtypeStruct((hidden_width, batch), jnp.bfloat16)],
        in_specs=[whole(pltpu.SMEM)] + [whole()] * (len(pieces) + 1) + weight_specs(),
        out_specs=[whole()] * 6,
        scratch_shapes=weight_scratch(model_width, hidden_width)
        + [
            pltpu.VMEM((batch, model_width), jnp.bfloat16),
            pltpu.VMEM((batch, hidden_width), jnp.bfloat16),
            pltpu.VMEM((model_width, batch), jnp.bfloat16),
        ],
        compiler_params=stage_params(),
        cost_estimate=stage_cost(4, batch, model_width, hidden_width),
        name="forward_stage",
    )(place, *pieces, top, weights[0], *map(in_hbm, weights[1:]))
    return out[0], out[1:5], out[5]


def turn_stage(place, acts, top, g_hidden, weights, count):
    batch, model_width = acts.shape
    hidden_width = weights[1].shape[1]
    width = model_width // count

    def kernel(place_ref, acts_ref, top_ref, ghid_ref, small_ref, *refs):
        matrices, refs = refs[:4], refs[4:]
        out_ref, held = refs[0], refs[1:4]
        hid, hidden, inter, scale, upper, grad, turned, normed, weighted, g_before = refs[4:]

        @pl.when(place_ref[1] == 1)
        def _():
            layers = streams_of(place_ref[0], matrices, held, [(True, True), (True, True)])
            (up0, down0), (up1, down1) = layers
            for stream in (up0, down0, up1):
                stream.start()
            mix_forward(small_ref, 0, acts_ref, inter.at[0], scale.at[0], normed, count)
            up_product(normed, up0.held, hidden, hid, up0.wait)
            down_product(hidden, down0.held, acts_ref, upper, down0.wait)
            mix_forward(small_ref, 1, upper, inter.at[1], scale.at[1], normed, count)

            def masked(columns):
                before = dot(normed[...], up1.held[:, columns])
                opened = jnp.maximum(before, 0.0).T
                g_before[columns, :] = opened_only(opened, ghid_ref[columns, :].astype(jnp.float32))

            over_tiles(hidden_width, hidden_tile(hidden_width), 1, up1.wait, masked)
            up_back(g_before, up1.held, weighted, no_wait)
            mix_backward(small_ref, 1, top_ref, upper, inter.at[1], scale.at[1], weighted, grad, count)
            turn(grad, turned)
            down_back(turned, down0.held, hid, g_before, no_wait)
            up_back(g_before, up0.held, weighted, no_wait)
            mix_backward(small_ref, 0, grad, acts_ref, inter.at[0], scale.at[0], weighted, out_ref, count)

    return pl.pallas_call(
        kernel,
        out_shape=jax.ShapeDtypeStruct(acts.shape, jnp.bfloat16),
        in_specs=[whole(pltpu.SMEM)] + [whole()] * 3 + weight_specs(),
        out_specs=whole(),
        scratch_shapes=weight_scratch(model_width, hidden_width)
        + [
            pltpu.VMEM((hidden_width, batch), jnp.bfloat16),
            pltpu.VMEM((batch, hidden_width), jnp.bfloat16),
            pltpu.VMEM((2, batch, model_width), jnp.float32),
            pltpu.VMEM((2, batch, width), jnp.float32),
            pltpu.VMEM((batch, model_width), jnp.bfloat16),
            pltpu.VMEM((batch, model_width), jnp.bfloat16),
            pltpu.VMEM((model_width, batch), jnp.bfloat16),
            pltpu.VMEM((batch, model_width), jnp.bfloat16),
            pltpu.VMEM((batch, model_width), jnp.float32),
            pltpu.VMEM((hidden_width, batch), jnp.bfloat16),
        ],
        compiler_params=stage_params(),
        cost_estimate=stage_cost(6, batch, model_width, hidden_width),
        name="turn_stage",
    )(place, acts, top, g_hidden, weights[0], *map(in_hbm, weights[1:]))


def backward_stage(place, grad, saved, weights, count):
    batch, model_width = grad.shape
    hidden_width = weights[1].shape[1]

    def kernel(place_ref, grad_ref, hid, inter, scale, kept, small_ref, *refs):
        matrices, refs = refs[:4], refs[4:]
        out_ref, held = refs[0], refs[1:4]
        middle, turned, weighted, g_before = refs[4:]

        @pl.when(place_ref[1] == 1)
        def _():
            layers = streams_of(place_ref[0], matrices, held, [(False, False), (False, False)])
            for up, down in reversed(layers):
                down.start()
                up.start()
            for layer, given, to in ((1, grad_ref, middle), (0, middle, out_ref)):
                up, down = layers[layer]
                turn(given, turned)
                down_back(turned, down.held, hid.at[layer], g_before, down.wait)
                up_back(g_before, up.held, weighted, up.wait)
                mix_backward(
                    small_ref, layer, given, kept.at[layer], inter.at[layer], scale.at[layer],
                    weighted, to, count,
                )

    return pl.pallas_call(
        kernel,
        out_shape=jax.ShapeDtypeStruct(grad.shape, jnp.bfloat16),
        in_specs=[whole(pltpu.SMEM)] + [whole()] * 5 + weight_specs(),
        out_specs=whole(),
        scratch_shapes=weight_scratch(model_width, hidden_width)
        + [
            pltpu.VMEM((batch, model_width), jnp.bfloat16),
            pltpu.VMEM((model_width, batch), jnp.bfloat16),
            pltpu.VMEM((batch, model_width), jnp.float32),
            pltpu.VMEM((hidden_width, batch), jnp.bfloat16),
        ],
        compiler_params=stage_params(),
        cost_estimate=stage_cost(4, batch, model_width, hidden_width),
        name="backward_stage",
    )(place, grad, *saved, weights[0], *map(in_hbm, weights[1:]))


def swapped(value, section_count):
    return lax.ppermute(value, "section", [(s, s ^ 1) for s in range(section_count)])


def moved(value, from_stage, to_stage):
    pairs = [(2 * from_stage + core, 2 * to_stage + core) for core in (0, 1)]
    return lax.ppermute(value, "section", pairs)


def mirror(value):
    along = lax.axis_size("table")
    return lax.ppermute(value, "table", [(t, (t + along // 2) % along) for t in range(along)])


def swap_in_half(value):
    along = lax.axis_size("table")
    half = along // 2
    groups = [
        [s * along + h * half + t for s in range(lax.axis_size("section")) for t in range(half)]
        for h in (0, 1)
    ]
    return lax.all_to_all(
        value, TABLE_AXES, split_axis=0, concat_axis=0, axis_index_groups=groups, tiled=True
    )


def near_first(per_asker, my_half):
    sections = lax.axis_size("section")
    half = lax.axis_size("table") // 2
    split = per_asker.reshape((sections, 2, half) + per_asker.shape[1:])
    near = lax.dynamic_index_in_dim(split, my_half, 1, keepdims=False)
    far = lax.dynamic_index_in_dim(split, 1 - my_half, 1, keepdims=False)
    return jnp.stack([near, far], axis=2).reshape((sections * half, 2) + per_asker.shape[1:])


def after(value, earlier):
    return lax.optimization_barrier((value, earlier))[0]


def per_device(
    emb_table,
    lcb_weight,
    fm_proj,
    norm_gain,
    w_up,
    w_down,
    top_grad,
    lookup_slot,
    wanted_rows,
    row_counts,
):
    section_count = lax.axis_size("section")
    along = lax.axis_size("table")
    half = along // 2
    near_owners = section_count * half
    stages = section_count // 2
    stage = lax.axis_index("section") // 2
    core = lax.axis_index("section") % 2
    my_half = lax.axis_index("table") // half
    cap = wanted_rows.shape[2]
    rows, embed_width = emb_table.shape
    embed_count = lcb_weight.shape[0]
    look_dev = lookup_slot.shape[1]
    model_width = top_grad.shape[3]

    own_slots = lookup_slot[0]
    mirror_slots = mirror(own_slots)
    small = jnp.concatenate([fm_proj[0], norm_gain[0].reshape(embed_count, -1)], axis=0)
    other_up = swapped(w_up[0], section_count)
    other_down = swapped(w_down[0], section_count)
    other_small = swapped(small, section_count)

    picked = near_first(wanted_rows[0], my_half)
    outgoing = pick_rows(emb_table, picked.reshape(-1))
    sent = after(outgoing, mirror_slots).reshape(near_owners, 2, cap, embed_width)
    fetched = swap_in_half(sent)

    def spread_of(slots):
        owner, column = slots // cap, slots % cap
        place = owner % along
        near = jnp.where(place // half == my_half, owner // along * half + place % half, near_owners)
        return spread_weights(near * cap + column, lcb_weight, near_owners, cap)

    spread_far = spread_of(mirror_slots)
    spread_near = spread_of(own_slots)
    smalls = jnp.stack(
        [jnp.where(core == 0, small, other_small), jnp.where(core == 0, other_small, small)]
    )
    weights = [smalls, w_up[0], other_up, w_down[0], other_down]
    spread_far, spread_near = lax.optimization_barrier((spread_far, spread_near))
    far_part = mirror(compress(spread_far, fetched, 1, embed_count, jnp.bfloat16))
    near_part = compress(spread_near, fetched, 0, embed_count, jnp.float32)
    lead = (near_part + far_part.astype(jnp.float32)).astype(jnp.bfloat16)
    pieces = [lead] + [moved(lead, s, 0) for s in range(1, stages)]
    top = top_grad.reshape(stages, 2, look_dev, model_width)
    top = lax.dynamic_index_in_dim(top, core, 1, keepdims=False).reshape(-1, model_width)

    def at(tick):
        is_last = (stage == stages - 1) & (tick == 0)
        return jnp.stack([core, stage == tick, is_last]).astype(jnp.int32)

    saved = None
    for tick in range(stages - 1):
        out, fresh, product = forward_stage(at(tick), pieces, top, weights, embed_count)
        if saved is None:
            saved, g_hidden = fresh, product
        else:
            saved = [jnp.where(stage == tick, new, old) for new, old in zip(fresh, saved)]
        pieces = [moved(out, tick, tick + 1)]
    grad = turn_stage(at(stages - 1), pieces[0], top, g_hidden, weights, embed_count)
    for tick in reversed(range(stages - 1)):
        grad = moved(grad, tick + 1, tick)
        grad = backward_stage(at(tick), grad, saved, weights, embed_count)

    own_grad = grad[:look_dev]
    for s in range(1, stages):
        piece = grad[s * look_dev : (s + 1) * look_dev]
        own_grad = jnp.where(stage == s, moved(piece, 0, s), own_grad)
    mirror_grad = mirror(own_grad)

    near_grad = expand(spread_near, own_grad, embed_count)
    slot_grad = expand(spread_far, mirror_grad, embed_count, near_grad)
    returned = swap_in_half(slot_grad)
    live_slots = jnp.arange(cap) < near_first(row_counts[0], my_half)[..., None]
    targets = jnp.where(live_slots, picked, rows).reshape(-1)
    return add_rows(targets, returned.reshape(-1, embed_width), outgoing, rows)


def solution(mesh):
    in_specs = (
        P(("section", "table"), None),
        P(),
        P("section", None, None),
        P("section", None),
        P("section", None, None),
        P("section", None, None),
        P("table", None, None, None),
        P("table", "section", None),
        P(("section", "table"), None, None),
        P(("section", "table"), None),
    )
    out_specs = P(("section", "table"), None)
    return jax.shard_map(
        per_device, mesh=mesh, in_specs=in_specs, out_specs=out_specs, check_vma=False
    )
```

```python
import jax
import jax.numpy as jnp
from jax import lax
from jax.experimental import pallas as pl
from jax.experimental.pallas import tpu as pltpu
from jax.sharding import PartitionSpec as P

EPSILON = 1e-05
DECAY_WEIGHT = 0.5
VMEM_LIMIT = 28 * 1024 * 1024
UNROLL = 32


def whole(memory_space=pltpu.VMEM):
    return pl.BlockSpec(memory_space=memory_space)


def in_hbm(value):
    return pltpu.with_memory_space_constraint(value, pltpu.HBM)


def params():
    return pltpu.CompilerParams(vmem_limit_bytes=VMEM_LIMIT)


def tiles_of(count, most):
    return max(step for step in range(1, most + 1) if count % step == 0)


def pick_rows(emb_table, picked):
    rows, width = emb_table.shape
    count = picked.shape[0]
    chunk = min(count, 1024)
    wide = emb_table.astype(jnp.float32).reshape(rows, 1, width)

    def kernel(picked_ref, wide_ref, out_ref, lines):
        def fill(part, carry):
            base = pl.multiple_of(part * chunk, chunk)

            def body(group, inner):
                first = pl.multiple_of(group * UNROLL, UNROLL)
                for lane in range(UNROLL):
                    lines[pl.ds(first + lane, 1), :] = wide_ref[picked_ref[base + first + lane]]
                return inner

            lax.fori_loop(0, chunk // UNROLL, body, 0)
            out_ref[pl.ds(base, chunk), :] = lines[...].astype(out_ref.dtype)
            return carry

        lax.fori_loop(0, count // chunk, fill, 0)

    return pl.pallas_call(
        kernel,
        out_shape=jax.ShapeDtypeStruct((count, width), emb_table.dtype),
        in_specs=[whole(pltpu.SMEM), whole()],
        out_specs=whole(),
        scratch_shapes=[pltpu.VMEM((chunk, width), jnp.float32)],
        compiler_params=params(),
        name="pick_rows",
    )(picked, wide)


def spread_weights(codes, lcb_weight, owners, cap):
    samples, feature_count = codes.shape
    embed_count = lcb_weight.shape[0]
    group = tiles_of(samples, 16)

    def kernel(codes_ref, lcb_ref, out_ref):
        lcb = lcb_ref[...].astype(jnp.float32)
        owner_of = lax.broadcasted_iota(jnp.int32, (owners, embed_count, feature_count), 0)
        column_of = lax.broadcasted_iota(jnp.int32, (cap, feature_count), 0)
        for pair in range(0, group, 2):
            made = []
            for sample in (pair, pair + 1):
                slots = codes_ref[sample : sample + 1, :]
                owner = lax.div(slots, cap)
                column = slots - owner * cap
                left = jnp.where(owner_of == owner[None], lcb[None], 0.0)
                left = left.reshape(owners * embed_count, feature_count).astype(jnp.bfloat16)
                right = jnp.where(column_of == column, 1.0, 0.0).astype(jnp.bfloat16)
                both = lax.dot_general(
                    left, right, (((1,), (1,)), ((), ())), preferred_element_type=jnp.float32
                )
                made.append(both.reshape(owners, embed_count, cap))
            rows = pl.ds(pair * embed_count, 2 * embed_count)
            out_ref[:, rows, :] = jnp.concatenate(made, axis=1).astype(out_ref.dtype)

    return pl.pallas_call(
        kernel,
        out_shape=pltpu.VMEM((owners, samples * embed_count, cap), jnp.bfloat16),
        grid=(samples // group,),
        in_specs=[
            pl.BlockSpec((group, feature_count), lambda i: (i, 0)),
            pl.BlockSpec((embed_count, feature_count), lambda i: (0, 0)),
        ],
        out_specs=pl.BlockSpec((owners, group * embed_count, cap), lambda i: (0, i, 0)),
        compiler_params=params(),
        cost_estimate=pl.CostEstimate(
            flops=2 * samples * owners * embed_count * feature_count * cap,
            bytes_accessed=2 * owners * samples * embed_count * cap,
            transcendentals=0,
        ),
        name="spread_weights",
    )(codes, lcb_weight)


def compress(spread, fetched, view, embed_count, kind):
    owners, lines, cap = spread.shape
    width = fetched.shape[3]
    samples = lines // embed_count
    part = tiles_of(owners, 8)
    steps = owners // part

    def kernel(spread_ref, rows_ref, out_ref, total):
        total[...] = jnp.zeros_like(total)

        def body(step, carry):
            first = step * part
            left = jnp.concatenate([spread_ref[first + o] for o in range(part)], axis=1)
            right = jnp.concatenate([rows_ref[first + o, view] for o in range(part)], axis=0)
            total[...] += jnp.dot(left, right, preferred_element_type=jnp.float32)
            return carry

        lax.fori_loop(0, steps, body, 0)
        for k in range(embed_count):
            columns = slice(k * width, (k + 1) * width)
            piece = total[pl.ds(k, samples, stride=embed_count), :]
            out_ref[:, columns] = piece.astype(out_ref.dtype)

    return pl.pallas_call(
        kernel,
        out_shape=jax.ShapeDtypeStruct((samples, embed_count * width), kind),
        in_specs=[whole(), whole()],
        out_specs=whole(),
        scratch_shapes=[pltpu.VMEM((lines, width), jnp.float32)],
        compiler_params=params(),
        name="compress",
    )(spread, fetched)


def expand(spread, lead_grad, embed_count, near=None):
    owners, lines, cap = spread.shape
    samples = lines // embed_count
    width = lead_grad.shape[1] // embed_count
    part = tiles_of(owners, 4)
    extra = [] if near is None else [near]

    def kernel(spread_ref, grad_ref, *refs):
        near_refs, (out_ref, tall, turned) = refs[: len(extra)], refs[len(extra) :]
        for k in range(embed_count):
            piece = grad_ref[:, k * width : (k + 1) * width].astype(jnp.float32)
            tall[pl.ds(k, samples, stride=embed_count), :] = piece
        turned[...] = tall[...].T.astype(jnp.bfloat16)

        def body(step, carry):
            first = step * part
            right = jnp.concatenate([spread_ref[first + o] for o in range(part)], axis=1)
            term = jnp.dot(turned[...], right, preferred_element_type=jnp.float32)
            piece = term.T.astype(out_ref.dtype).reshape(part, cap, width)
            if near_refs:
                for o in range(part):
                    out_ref[first + o, 0] = near_refs[0][first + o]
                    out_ref[first + o, 1] = piece[o]
            else:
                out_ref[tile_at(step, part)] = piece
            return carry

        lax.fori_loop(0, owners // part, body, 0)

    views = () if near is None else (2,)
    return pl.pallas_call(
        kernel,
        out_shape=jax.ShapeDtypeStruct((owners,) + views + (cap, width), jnp.bfloat16),
        in_specs=[whole()] * (2 + len(extra)),
        out_specs=whole(),
        scratch_shapes=[
            pltpu.VMEM((lines, width), jnp.float32),
            pltpu.VMEM((width, lines), jnp.bfloat16),
        ],
        compiler_params=params(),
        name="expand",
    )(spread, lead_grad, *extra)


def add_rows(targets, returned, outgoing, rows):
    count, width = returned.shape
    chunk = min(count, 1024)
    zeros = jnp.zeros((rows + 8, 1, width), jnp.float32)

    def kernel(targets_ref, back_ref, sent_ref, zeros_ref, out_ref, total, terms, sem):
        begin = pltpu.make_async_copy(zeros_ref, total, sem.at[0])
        begin.start()

        def fill(part, carry):
            base = pl.multiple_of(part * chunk, chunk)
            lines = pl.ds(base, chunk)
            terms[...] = back_ref[lines, :].astype(jnp.float32) + DECAY_WEIGHT * sent_ref[
                lines, :
            ].astype(jnp.float32)

            @pl.when(part == 0)
            def _():
                begin.wait()

            def body(group, inner):
                first = pl.multiple_of(group * UNROLL, UNROLL)
                places = [targets_ref[base + first + lane] for lane in range(UNROLL)]
                sums = [
                    total[places[lane]] + terms[pl.ds(first + lane, 1), :] for lane in range(UNROLL)
                ]
                for lane in range(UNROLL):
                    total[places[lane]] = sums[lane]
                return inner

            lax.fori_loop(0, chunk // UNROLL, body, 0)
            return carry

        lax.fori_loop(0, count // chunk, fill, 0)
        finish = pltpu.make_async_copy(total.at[pl.ds(0, rows)], out_ref, sem.at[1])
        finish.start()
        finish.wait()

    return pl.pallas_call(
        kernel,
        out_shape=jax.ShapeDtypeStruct((rows, 1, width), jnp.float32),
        in_specs=[whole(pltpu.SMEM), whole(), whole(), whole(pl.ANY)],
        out_specs=whole(pl.ANY),
        scratch_shapes=[
            pltpu.VMEM((rows + 8, 1, width), jnp.float32),
            pltpu.VMEM((chunk, width), jnp.float32),
            pltpu.SemaphoreType.DMA((2,)),
        ],
        compiler_params=params(),
        name="add_rows",
    )(targets, returned, outgoing, zeros).reshape(rows, width)


GROUP = 16
TABLE_AXES = ("section", "table")
STAGE_LIMIT = 44 * 1024 * 1024
NT = (((1,), (1,)), ((), ()))


def dot_nt(left, right):
    return lax.dot_general(left, right, NT, preferred_element_type=jnp.float32)


def dot(left, right):
    return jnp.dot(left, right, preferred_element_type=jnp.float32)


def halves(value):
    high = value.astype(jnp.bfloat16)
    low = (value - high.astype(jnp.float32)).astype(jnp.bfloat16)
    return jnp.concatenate([high, low], axis=1)


def same_sample(count):
    first = lax.broadcasted_iota(jnp.int32, (count * GROUP, count * GROUP), 0)
    second = lax.broadcasted_iota(jnp.int32, (count * GROUP, count * GROUP), 1)
    return (first & (GROUP - 1)) == (second & (GROUP - 1))


def stacked(ref, rows, count, width):
    return jnp.concatenate([ref[rows, k * width : (k + 1) * width] for k in range(count)], axis=0)


def repeated(proj):
    count, width = proj.shape
    lines = [jnp.broadcast_to(proj[k : k + 1, :], (GROUP, width)) for k in range(count)]
    return jnp.concatenate(lines, axis=0).astype(jnp.bfloat16)


def mix_forward(small, layer, acts, inter, scale, normed, grams, count):
    batch, model_width = acts.shape
    width = model_width // count
    both = small[layer].astype(jnp.float32)
    proj = repeated(both[:count])
    keep = same_sample(count)
    size = GROUP * count
    for group in range(batch // GROUP):
        block = stacked(acts, pl.ds(group * GROUP, GROUP), count, width)
        gram = jnp.where(keep, dot_nt(block, block), 0.0)
        grams[group * size : (group + 1) * size, :] = halves(gram)
    mixed = dot(grams[...], jnp.concatenate([proj, proj], axis=0))
    for group in range(batch // GROUP):
        rows = pl.ds(group * GROUP, GROUP)
        start = group * size
        parts = [mixed[start + k * GROUP : start + (k + 1) * GROUP] for k in range(count)]
        squares = sum(part * part for part in parts)
        mean = jnp.sum(squares, axis=1, keepdims=True) * (1.0 / model_width)
        inv = lax.rsqrt(mean + EPSILON)
        scale[rows, :] = jnp.broadcast_to(inv, (GROUP, width))
        for k in range(count):
            columns = slice(k * width, (k + 1) * width)
            inter[rows, columns] = parts[k]
            gain = both[count + k : count + k + 1]
            normed[rows, columns] = (parts[k] * inv * gain).astype(jnp.bfloat16)


def gram_scratch(batch, count):
    return pltpu.VMEM((batch * count, 2 * GROUP * count), jnp.bfloat16)


def hidden_tile(hidden_width):
    return min(hidden_width, 1024)


def model_tile(model_width):
    return min(model_width, 512)


def tile_at(step, size):
    return pl.ds(pl.multiple_of(step * size, size), size)


class Stream:
    def __init__(self, mine, own, other, held, sems, axis, size):
        self.mine, self.own, self.other, self.held, self.sems = mine, own, other, held, sems
        self.axis, self.size = axis, size
        self.tiles = own.shape[axis] // size

    def copy(self, source, step):
        cut = tile_at(step, self.size)
        index = (slice(None), cut) if self.axis == 1 else (cut, slice(None))
        return pltpu.make_async_copy(source.at[index], self.held.at[index], self.sems.at[step])

    def start(self):
        @pl.when(self.mine)
        def _():
            for step in range(self.tiles):
                self.copy(self.own, step).start()

        @pl.when(jnp.logical_not(self.mine))
        def _():
            for step in range(self.tiles):
                self.copy(self.other, step).start()

    def wait(self, step):
        self.copy(self.own, step).wait()


def no_wait(step):
    return None


def over_tiles(total, tile, many, wait, work):
    many = min(many, total // tile)

    def body(step, carry):
        for inner in range(many):
            wait(step * many + inner)
        work(tile_at(step, many * tile))
        return carry

    lax.fori_loop(0, total // (many * tile), body, 0)


def up_product(normed, w_up, hidden, turned, wait, many=1):
    def work(columns):
        opened = jnp.maximum(dot(normed[...], w_up[:, columns]), 0.0)
        hidden[:, columns] = opened.astype(jnp.bfloat16)
        turned[columns, :] = opened.T.astype(jnp.bfloat16)

    width = hidden.shape[1]
    over_tiles(width, hidden_tile(width), many, wait, work)


def down_product(hidden, w_down, acts, out, wait, many=1):
    def work(columns):
        term = dot(hidden[...], w_down[:, columns])
        out[:, columns] = (acts[:, columns].astype(jnp.float32) + term).astype(jnp.bfloat16)

    width = out.shape[1]
    over_tiles(width, model_tile(width), many, wait, work)


def turn(rows, turned):
    turned[...] = rows[...].astype(jnp.float32).T.astype(jnp.bfloat16)


def opened_only(hidden, grad):
    return jnp.where(hidden.astype(jnp.float32) > 0.0, grad, 0.0).astype(jnp.bfloat16)


def down_back(grad, w_down, hidden, out, wait, many=1):
    def work(lines):
        g_hidden = dot(w_down[lines, :], grad[...])
        if hidden is not None:
            out[lines, :] = opened_only(hidden[lines, :], g_hidden)
        else:
            out[lines, :] = g_hidden.astype(jnp.bfloat16)

    width = out.shape[0]
    over_tiles(width, hidden_tile(width), many, wait, work)


def up_back(g_before, w_up, weighted, wait, many=1):
    def work(columns):
        weighted[:, columns] = dot(w_up[columns, :], g_before[...]).T

    width = weighted.shape[1]
    over_tiles(width, model_tile(width), many, wait, work)


def mix_backward(small, layer, grad, acts, inter, scale, weighted, out, count):
    batch, model_width = acts.shape
    width = model_width // count
    both = small[layer].astype(jnp.float32)
    proj = repeated(both[:count])
    keep = same_sample(count)
    for start in range(0, batch, GROUP):
        rows = pl.ds(start, GROUP)
        columns = [slice(k * width, (k + 1) * width) for k in range(count)]
        gained = [weighted[rows, columns[k]] * both[count + k : count + k + 1] for k in range(count)]
        shared = sum(gained[k] * inter[rows, columns[k]] for k in range(count))
        mean = jnp.sum(shared, axis=1, keepdims=True) * (1.0 / model_width)
        inv = scale[rows, 0:1]
        pull = inv * inv * mean
        parts = [
            (inv * (gained[k] - inter[rows, columns[k]] * pull)).astype(jnp.bfloat16)
            for k in range(count)
        ]
        block = stacked(acts, rows, count, width)
        g_inter = jnp.concatenate(parts, axis=0)
        left = jnp.concatenate([g_inter, proj], axis=1)
        right = jnp.concatenate([proj, g_inter], axis=1)
        links = jnp.where(keep, dot_nt(left, right), 0.0)
        g_acts = dot(halves(links), jnp.concatenate([block, block], axis=0))
        for k in range(count):
            piece = g_acts[k * GROUP : (k + 1) * GROUP] + grad[rows, columns[k]].astype(jnp.float32)
            out[rows, columns[k]] = piece.astype(jnp.bfloat16)


def saved_shapes(batch, model_width, hidden_width, width):
    return [
        jax.ShapeDtypeStruct((2, hidden_width, batch), jnp.bfloat16),
        jax.ShapeDtypeStruct((2, batch, model_width), jnp.float32),
        jax.ShapeDtypeStruct((2, batch, width), jnp.float32),
        jax.ShapeDtypeStruct((2, batch, model_width), jnp.bfloat16),
    ]


def weight_specs():
    return [whole()] + [whole(pltpu.HBM)] * 4


def weight_scratch(model_width, hidden_width):
    tiles = max(hidden_width // hidden_tile(hidden_width), model_width // model_tile(model_width))
    return [
        pltpu.VMEM((2, model_width, hidden_width), jnp.bfloat16),
        pltpu.VMEM((2, hidden_width, model_width), jnp.bfloat16),
        pltpu.SemaphoreType.DMA((4, tiles)),
    ]


def streams_of(core, weights, held, forward):
    own_up, other_up, own_down, other_down = weights
    held_up, held_down, sems = held
    model_width, hidden_width = own_up.shape
    wide, narrow = hidden_tile(hidden_width), model_tile(model_width)
    made = []
    for layer in (0, 1):
        mine = core == layer
        up_forward, down_forward = forward[layer]
        up_cut = (1, wide) if up_forward else (0, narrow)
        down_cut = (1, narrow) if down_forward else (0, wide)
        made.append(
            (
                Stream(mine, own_up, other_up, held_up.at[layer], sems.at[2 * layer], *up_cut),
                Stream(mine, own_down, other_down, held_down.at[layer], sems.at[2 * layer + 1], *down_cut),
            )
        )
    return made


def stage_cost(products, batch, model_width, hidden_width):
    return pl.CostEstimate(
        flops=2 * products * batch * model_width * hidden_width, bytes_accessed=1 << 20, transcendentals=0
    )


def stage_params():
    return pltpu.CompilerParams(vmem_limit_bytes=STAGE_LIMIT)


def forward_stage(place, pieces, top, weights, count):
    batch, model_width = top.shape
    hidden_width = weights[1].shape[1]
    width = model_width // count

    def kernel(place_ref, *refs):
        piece_refs, (top_ref, small_ref), refs = refs[: len(pieces)], refs[len(pieces) :][:2], refs[len(pieces) + 2 :]
        matrices, refs = refs[:4], refs[4:]
        out_ref, hid, inter, scale, kept, g_hidden = refs[:6]
        held, (normed, hidden, top_turned, grams) = refs[6:9], refs[9:]
        core = place_ref[0]

        @pl.when(place_ref[1] == 1)
        def _():
            layers = streams_of(core, matrices, held, [(True, True), (True, True)])
            for up, down in layers:
                up.start()
                down.start()
            start = 0
            for piece in piece_refs:
                kept[0, start : start + piece.shape[0], :] = piece[...]
                start += piece.shape[0]
            for layer, (up, down) in enumerate(layers):
                mix_forward(
                    small_ref, layer, kept.at[layer], inter.at[layer], scale.at[layer], normed, grams, count
                )
                up_product(normed, up.held, hidden, hid.at[layer], up.wait)
                to = kept.at[1] if layer == 0 else out_ref
                down_product(hidden, down.held, kept.at[layer], to, down.wait)

        @pl.when(place_ref[2] == 1)
        def _():
            layers = streams_of(core, matrices, held, [(True, True), (True, False)])
            down = layers[1][1]
            down.start()
            turn(top_ref, top_turned)
            down_back(top_turned, down.held, None, g_hidden, down.wait)

    out = pl.pallas_call(
        kernel,
        out_shape=[jax.ShapeDtypeStruct(top.shape, jnp.bfloat16)]
        + saved_shapes(batch, model_width, hidden_width, width)
        + [jax.ShapeDtypeStruct((hidden_width, batch), jnp.bfloat16)],
        in_specs=[whole(pltpu.SMEM)] + [whole()] * (len(pieces) + 1) + weight_specs(),
        out_specs=[whole()] * 6,
        scratch_shapes=weight_scratch(model_width, hidden_width)
        + [
            pltpu.VMEM((batch, model_width), jnp.bfloat16),
            pltpu.VMEM((batch, hidden_width), jnp.bfloat16),
            pltpu.VMEM((model_width, batch), jnp.bfloat16),
            gram_scratch(batch, count),
        ],
        compiler_params=stage_params(),
        cost_estimate=stage_cost(4, batch, model_width, hidden_width),
        name="forward_stage",
    )(place, *pieces, top, weights[0], *map(in_hbm, weights[1:]))
    return out[0], out[1:5], out[5]


def turn_stage(place, acts, top, g_hidden, weights, count):
    batch, model_width = acts.shape
    hidden_width = weights[1].shape[1]
    width = model_width // count

    def kernel(place_ref, acts_ref, top_ref, ghid_ref, small_ref, *refs):
        matrices, refs = refs[:4], refs[4:]
        out_ref, held = refs[0], refs[1:4]
        hid, hidden, inter, scale, upper, grad, turned, normed, weighted, g_before, grams = refs[4:]

        @pl.when(place_ref[1] == 1)
        def _():
            layers = streams_of(place_ref[0], matrices, held, [(True, True), (True, True)])
            (up0, down0), (up1, down1) = layers
            for stream in (up0, down0, up1):
                stream.start()
            mix_forward(small_ref, 0, acts_ref, inter.at[0], scale.at[0], normed, grams, count)
            up_product(normed, up0.held, hidden, hid, up0.wait)
            down_product(hidden, down0.held, acts_ref, upper, down0.wait)
            mix_forward(small_ref, 1, upper, inter.at[1], scale.at[1], normed, grams, count)

            def masked(columns):
                before = dot(normed[...], up1.held[:, columns])
                opened = jnp.maximum(before, 0.0).T
                g_before[columns, :] = opened_only(opened, ghid_ref[columns, :].astype(jnp.float32))

            over_tiles(hidden_width, hidden_tile(hidden_width), 1, up1.wait, masked)
            up_back(g_before, up1.held, weighted, no_wait)
            mix_backward(small_ref, 1, top_ref, upper, inter.at[1], scale.at[1], weighted, grad, count)
            turn(grad, turned)
            down_back(turned, down0.held, hid, g_before, no_wait)
            up_back(g_before, up0.held, weighted, no_wait)
            mix_backward(small_ref, 0, grad, acts_ref, inter.at[0], scale.at[0], weighted, out_ref, count)

    return pl.pallas_call(
        kernel,
        out_shape=jax.ShapeDtypeStruct(acts.shape, jnp.bfloat16),
        in_specs=[whole(pltpu.SMEM)] + [whole()] * 3 + weight_specs(),
        out_specs=whole(),
        scratch_shapes=weight_scratch(model_width, hidden_width)
        + [
            pltpu.VMEM((hidden_width, batch), jnp.bfloat16),
            pltpu.VMEM((batch, hidden_width), jnp.bfloat16),
            pltpu.VMEM((2, batch, model_width), jnp.float32),
            pltpu.VMEM((2, batch, width), jnp.float32),
            pltpu.VMEM((batch, model_width), jnp.bfloat16),
            pltpu.VMEM((batch, model_width), jnp.bfloat16),
            pltpu.VMEM((model_width, batch), jnp.bfloat16),
            pltpu.VMEM((batch, model_width), jnp.bfloat16),
            pltpu.VMEM((batch, model_width), jnp.float32),
            pltpu.VMEM((hidden_width, batch), jnp.bfloat16),
            gram_scratch(batch, count),
        ],
        compiler_params=stage_params(),
        cost_estimate=stage_cost(6, batch, model_width, hidden_width),
        name="turn_stage",
    )(place, acts, top, g_hidden, weights[0], *map(in_hbm, weights[1:]))


def backward_stage(place, grad, saved, weights, count):
    batch, model_width = grad.shape
    hidden_width = weights[1].shape[1]

    def kernel(place_ref, grad_ref, hid, inter, scale, kept, small_ref, *refs):
        matrices, refs = refs[:4], refs[4:]
        out_ref, held = refs[0], refs[1:4]
        middle, turned, weighted, g_before = refs[4:]

        @pl.when(place_ref[1] == 1)
        def _():
            layers = streams_of(place_ref[0], matrices, held, [(False, False), (False, False)])
            for up, down in reversed(layers):
                down.start()
                up.start()
            for layer, given, to in ((1, grad_ref, middle), (0, middle, out_ref)):
                up, down = layers[layer]
                turn(given, turned)
                down_back(turned, down.held, hid.at[layer], g_before, down.wait)
                up_back(g_before, up.held, weighted, up.wait)
                mix_backward(
                    small_ref, layer, given, kept.at[layer], inter.at[layer], scale.at[layer],
                    weighted, to, count,
                )

    return pl.pallas_call(
        kernel,
        out_shape=jax.ShapeDtypeStruct(grad.shape, jnp.bfloat16),
        in_specs=[whole(pltpu.SMEM)] + [whole()] * 5 + weight_specs(),
        out_specs=whole(),
        scratch_shapes=weight_scratch(model_width, hidden_width)
        + [
            pltpu.VMEM((batch, model_width), jnp.bfloat16),
            pltpu.VMEM((model_width, batch), jnp.bfloat16),
            pltpu.VMEM((batch, model_width), jnp.float32),
            pltpu.VMEM((hidden_width, batch), jnp.bfloat16),
        ],
        compiler_params=stage_params(),
        cost_estimate=stage_cost(4, batch, model_width, hidden_width),
        name="backward_stage",
    )(place, grad, *saved, weights[0], *map(in_hbm, weights[1:]))


def swapped(value, section_count):
    return lax.ppermute(value, "section", [(s, s ^ 1) for s in range(section_count)])


def moved(value, from_stage, to_stage):
    pairs = [(2 * from_stage + core, 2 * to_stage + core) for core in (0, 1)]
    return lax.ppermute(value, "section", pairs)


def mirror(value):
    along = lax.axis_size("table")
    return lax.ppermute(value, "table", [(t, (t + along // 2) % along) for t in range(along)])


def swap_in_half(value):
    along = lax.axis_size("table")
    half = along // 2
    groups = [
        [s * along + h * half + t for s in range(lax.axis_size("section")) for t in range(half)]
        for h in (0, 1)
    ]
    return lax.all_to_all(
        value, TABLE_AXES, split_axis=0, concat_axis=0, axis_index_groups=groups, tiled=True
    )


def near_first(per_asker, my_half):
    sections = lax.axis_size("section")
    half = lax.axis_size("table") // 2
    split = per_asker.reshape((sections, 2, half) + per_asker.shape[1:])
    near = lax.dynamic_index_in_dim(split, my_half, 1, keepdims=False)
    far = lax.dynamic_index_in_dim(split, 1 - my_half, 1, keepdims=False)
    return jnp.stack([near, far], axis=2).reshape((sections * half, 2) + per_asker.shape[1:])


def after(value, earlier):
    return lax.optimization_barrier((value, earlier))[0]


def per_device(
    emb_table,
    lcb_weight,
    fm_proj,
    norm_gain,
    w_up,
    w_down,
    top_grad,
    lookup_slot,
    wanted_rows,
    row_counts,
):
    section_count = lax.axis_size("section")
    along = lax.axis_size("table")
    half = along // 2
    near_owners = section_count * half
    stages = section_count // 2
    stage = lax.axis_index("section") // 2
    core = lax.axis_index("section") % 2
    my_half = lax.axis_index("table") // half
    cap = wanted_rows.shape[2]
    rows, embed_width = emb_table.shape
    embed_count = lcb_weight.shape[0]
    look_dev = lookup_slot.shape[1]
    model_width = top_grad.shape[3]

    own_slots = lookup_slot[0]
    mirror_slots = mirror(own_slots)
    small = jnp.concatenate([fm_proj[0], norm_gain[0].reshape(embed_count, -1)], axis=0)
    other_up = swapped(w_up[0], section_count)
    other_down = swapped(w_down[0], section_count)
    other_small = swapped(small, section_count)

    picked = near_first(wanted_rows[0], my_half)
    outgoing = pick_rows(emb_table, picked.reshape(-1))
    sent = after(outgoing, mirror_slots).reshape(near_owners, 2, cap, embed_width)
    fetched = swap_in_half(sent)

    def spread_of(slots):
        owner, column = slots // cap, slots % cap
        place = owner % along
        near = jnp.where(place // half == my_half, owner // along * half + place % half, near_owners)
        return spread_weights(near * cap + column, lcb_weight, near_owners, cap)

    spread_far = spread_of(mirror_slots)
    spread_near = spread_of(own_slots)
    smalls = jnp.stack(
        [jnp.where(core == 0, small, other_small), jnp.where(core == 0, other_small, small)]
    )
    weights = [smalls, w_up[0], other_up, w_down[0], other_down]
    spread_far, spread_near = lax.optimization_barrier((spread_far, spread_near))
    far_part = mirror(compress(spread_far, fetched, 1, embed_count, jnp.bfloat16))
    near_part = compress(spread_near, fetched, 0, embed_count, jnp.float32)
    lead = (near_part + far_part.astype(jnp.float32)).astype(jnp.bfloat16)
    pieces = [lead] + [moved(lead, s, 0) for s in range(1, stages)]
    top = top_grad.reshape(stages, 2, look_dev, model_width)
    top = lax.dynamic_index_in_dim(top, core, 1, keepdims=False).reshape(-1, model_width)

    def at(tick):
        is_last = (stage == stages - 1) & (tick == 0)
        return jnp.stack([core, stage == tick, is_last]).astype(jnp.int32)

    saved = None
    for tick in range(stages - 1):
        out, fresh, product = forward_stage(at(tick), pieces, top, weights, embed_count)
        if saved is None:
            saved, g_hidden = fresh, product
        else:
            saved = [jnp.where(stage == tick, new, old) for new, old in zip(fresh, saved)]
        pieces = [moved(out, tick, tick + 1)]
    grad = turn_stage(at(stages - 1), pieces[0], top, g_hidden, weights, embed_count)
    for tick in reversed(range(stages - 1)):
        grad = moved(grad, tick + 1, tick)
        grad = backward_stage(at(tick), grad, saved, weights, embed_count)

    own_grad = grad[:look_dev]
    for s in range(1, stages):
        piece = grad[s * look_dev : (s + 1) * look_dev]
        own_grad = jnp.where(stage == s, moved(piece, 0, s), own_grad)
    mirror_grad = mirror(own_grad)

    near_grad = expand(spread_near, own_grad, embed_count)
    slot_grad = expand(spread_far, mirror_grad, embed_count, near_grad)
    returned = swap_in_half(slot_grad)
    live_slots = jnp.arange(cap) < near_first(row_counts[0], my_half)[..., None]
    targets = jnp.where(live_slots, picked, rows).reshape(-1)
    return add_rows(targets, returned.reshape(-1, embed_width), outgoing, rows)


def solution(mesh):
    in_specs = (
        P(("section", "table"), None),
        P(),
        P("section", None, None),
        P("section", None),
        P("section", None, None),
        P("section", None, None),
        P("table", None, None, None),
        P("table", "section", None),
        P(("section", "table"), None, None),
        P(("section", "table"), None),
    )
    out_specs = P(("section", "table"), None)
    return jax.shard_map(
        per_device, mesh=mesh, in_specs=in_specs, out_specs=out_specs, check_vma=False
    )
```

```python
import jax
import jax.numpy as jnp
from jax import lax
from jax.experimental import pallas as pl
from jax.experimental.pallas import tpu as pltpu
from jax.sharding import PartitionSpec as P

EPSILON = 1e-05
DECAY_WEIGHT = 0.5
VMEM_LIMIT = 28 * 1024 * 1024
UNROLL = 32
PICK_UNROLL = 128


def whole(memory_space=pltpu.VMEM):
    return pl.BlockSpec(memory_space=memory_space)


def in_hbm(value):
    return pltpu.with_memory_space_constraint(value, pltpu.HBM)


def params():
    return pltpu.CompilerParams(vmem_limit_bytes=VMEM_LIMIT)


def tiles_of(count, most):
    return max(step for step in range(1, most + 1) if count % step == 0)


def pick_rows(emb_table, picked):
    rows, width = emb_table.shape
    count = picked.shape[0]
    chunk = min(count, 1024)

    def kernel(picked_ref, table_ref, out_ref, wide, lines):
        wide[...] = table_ref[...].astype(jnp.float32)

        def fill(part, carry):
            base = pl.multiple_of(part * chunk, chunk)

            def body(group, inner):
                first = pl.multiple_of(group * PICK_UNROLL, PICK_UNROLL)
                for lane in range(PICK_UNROLL):
                    row = picked_ref[base + first + lane]
                    lines[pl.ds(first + lane, 1), :] = wide[pl.ds(row, 1), :]
                return inner

            lax.fori_loop(0, chunk // PICK_UNROLL, body, 0)
            out_ref[pl.ds(base, chunk), :] = lines[...].astype(out_ref.dtype)
            return carry

        lax.fori_loop(0, count // chunk, fill, 0)

    return pl.pallas_call(
        kernel,
        out_shape=jax.ShapeDtypeStruct((count, width), emb_table.dtype),
        in_specs=[whole(pltpu.SMEM), whole()],
        out_specs=whole(),
        scratch_shapes=[
            pltpu.VMEM((rows, width), jnp.float32),
            pltpu.VMEM((chunk, width), jnp.float32),
        ],
        compiler_params=params(),
        name="pick_rows",
    )(picked, emb_table)


def spread_weights(codes, lcb_weight, owners, cap):
    samples, feature_count = codes.shape
    embed_count = lcb_weight.shape[0]
    group = tiles_of(samples, 16)

    def kernel(codes_ref, lcb_ref, out_ref, kept_ref):
        lcb = lcb_ref[...].astype(jnp.float32)
        owner_of = lax.broadcasted_iota(jnp.int32, (owners, embed_count, feature_count), 0)
        column_of = lax.broadcasted_iota(jnp.int32, (cap, feature_count), 0)
        for pair in range(0, group, 2):
            made = []
            for sample in (pair, pair + 1):
                slots = codes_ref[sample : sample + 1, :]
                owner = lax.div(slots, cap)
                column = slots - owner * cap
                left = jnp.where(owner_of == owner[None], lcb[None], 0.0)
                left = left.reshape(owners * embed_count, feature_count).astype(jnp.bfloat16)
                right = jnp.where(column_of == column, 1.0, 0.0).astype(jnp.bfloat16)
                both = lax.dot_general(
                    left, right, (((1,), (1,)), ((), ())), preferred_element_type=jnp.float32
                )
                made.append(both.reshape(owners, embed_count, cap))
            rows = pl.ds(pair * embed_count, 2 * embed_count)
            joined = jnp.concatenate(made, axis=1).astype(out_ref.dtype)
            out_ref[:, rows, :] = joined
            kept_ref[:, rows, :] = joined

    return pl.pallas_call(
        kernel,
        out_shape=[
            pltpu.VMEM((owners, samples * embed_count, cap), jnp.bfloat16),
            pltpu.HBM((owners, samples * embed_count, cap), jnp.bfloat16),
        ],
        grid=(samples // group,),
        in_specs=[
            pl.BlockSpec((group, feature_count), lambda i: (i, 0)),
            pl.BlockSpec((embed_count, feature_count), lambda i: (0, 0)),
        ],
        out_specs=[pl.BlockSpec((owners, group * embed_count, cap), lambda i: (0, i, 0))] * 2,
        compiler_params=params(),
        cost_estimate=pl.CostEstimate(
            flops=2 * samples * owners * embed_count * feature_count * cap,
            bytes_accessed=2 * owners * samples * embed_count * cap,
            transcendentals=0,
        ),
        name="spread_weights",
    )(codes, lcb_weight)


def compress(spread, fetched, view, embed_count, kind):
    owners, lines, cap = spread.shape
    width = fetched.shape[3]
    samples = lines // embed_count
    part = tiles_of(owners, 8)
    steps = owners // part

    def kernel(spread_ref, rows_ref, out_ref, total):
        total[...] = jnp.zeros_like(total)

        def body(step, carry):
            first = step * part
            left = jnp.concatenate([spread_ref[first + o] for o in range(part)], axis=1)
            right = jnp.concatenate([rows_ref[first + o, view] for o in range(part)], axis=0)
            total[...] += jnp.dot(left, right, preferred_element_type=jnp.float32)
            return carry

        lax.fori_loop(0, steps, body, 0)
        for k in range(embed_count):
            columns = slice(k * width, (k + 1) * width)
            piece = total[pl.ds(k, samples, stride=embed_count), :]
            out_ref[:, columns] = piece.astype(out_ref.dtype)

    return pl.pallas_call(
        kernel,
        out_shape=jax.ShapeDtypeStruct((samples, embed_count * width), kind),
        in_specs=[whole(), whole()],
        out_specs=whole(),
        scratch_shapes=[pltpu.VMEM((lines, width), jnp.float32)],
        compiler_params=params(),
        name="compress",
    )(spread, fetched)


def expand(spread, lead_grad, embed_count, near=None):
    owners, lines, cap = spread.shape
    samples = lines // embed_count
    width = lead_grad.shape[1] // embed_count
    part = tiles_of(owners, 4)
    extra = [] if near is None else [near]

    def kernel(spread_ref, grad_ref, *refs):
        near_refs, (out_ref, tall, turned) = refs[: len(extra)], refs[len(extra) :]
        for k in range(embed_count):
            piece = grad_ref[:, k * width : (k + 1) * width].astype(jnp.float32)
            tall[pl.ds(k, samples, stride=embed_count), :] = piece
        turned[...] = tall[...].T.astype(jnp.bfloat16)

        def body(step, carry):
            first = step * part
            right = jnp.concatenate([spread_ref[first + o] for o in range(part)], axis=1)
            term = jnp.dot(turned[...], right, preferred_element_type=jnp.float32)
            piece = term.T.astype(out_ref.dtype).reshape(part, cap, width)
            if near_refs:
                for o in range(part):
                    out_ref[first + o, 0] = near_refs[0][first + o]
                    out_ref[first + o, 1] = piece[o]
            else:
                out_ref[tile_at(step, part)] = piece
            return carry

        lax.fori_loop(0, owners // part, body, 0)

    views = () if near is None else (2,)
    return pl.pallas_call(
        kernel,
        out_shape=jax.ShapeDtypeStruct((owners,) + views + (cap, width), jnp.bfloat16),
        in_specs=[whole()] * (2 + len(extra)),
        out_specs=whole(),
        scratch_shapes=[
            pltpu.VMEM((lines, width), jnp.float32),
            pltpu.VMEM((width, lines), jnp.bfloat16),
        ],
        compiler_params=params(),
        name="expand",
    )(spread, lead_grad, *extra)


def add_rows(targets, returned, outgoing, rows, cap):
    count, width = returned.shape
    pair = 2 * cap

    def kernel(targets_ref, back_ref, sent_ref, out_ref, total, second, terms, sem):
        total[...] = jnp.zeros_like(total)
        second[...] = jnp.zeros_like(second)

        def body(step, carry):
            base = pl.multiple_of(step * pair, pair)
            lines = pl.ds(base, pair)
            terms[...] = back_ref[lines, :].astype(jnp.float32) + DECAY_WEIGHT * sent_ref[
                lines, :
            ].astype(jnp.float32)
            for first in range(0, cap, UNROLL):
                lanes = range(first, first + UNROLL)
                places = [targets_ref[base + lane] for lane in lanes]
                others = [targets_ref[base + cap + lane] for lane in lanes]
                sums = [
                    total[pl.ds(place, 1), :] + terms[lane : lane + 1, :]
                    for place, lane in zip(places, lanes)
                ]
                other_sums = [
                    second[pl.ds(place, 1), :] + terms[cap + lane : cap + lane + 1, :]
                    for place, lane in zip(others, lanes)
                ]
                for place, value in zip(places, sums):
                    total[pl.ds(place, 1), :] = value
                for place, value in zip(others, other_sums):
                    second[pl.ds(place, 1), :] = value
            return carry

        lax.fori_loop(0, count // pair, body, 0)
        part = rows // 4
        copies = []
        for piece in range(4):
            cut = pl.ds(piece * part, part)
            total[cut, :] = total[cut, :] + second[cut, :]
            copies.append(pltpu.make_async_copy(total.at[cut, :], out_ref.at[cut, :], sem.at[piece]))
            copies[-1].start()
        for copy in copies:
            copy.wait()

    return pl.pallas_call(
        kernel,
        out_shape=jax.ShapeDtypeStruct((rows, width), jnp.float32),
        in_specs=[whole(pltpu.SMEM), whole(), whole()],
        out_specs=whole(pl.ANY),
        scratch_shapes=[
            pltpu.VMEM((rows + 8, width), jnp.float32),
            pltpu.VMEM((rows + 8, width), jnp.float32),
            pltpu.VMEM((pair, width), jnp.float32),
            pltpu.SemaphoreType.DMA((4,)),
        ],
        compiler_params=params(),
        name="add_rows",
    )(targets, returned, outgoing)


GROUP = 16
TABLE_AXES = ("section", "table")
STAGE_LIMIT = 44 * 1024 * 1024
NT = (((1,), (1,)), ((), ()))


def dot_nt(left, right):
    return lax.dot_general(left, right, NT, preferred_element_type=jnp.float32)


def dot(left, right):
    return jnp.dot(left, right, preferred_element_type=jnp.float32)


def halves(value):
    high = value.astype(jnp.bfloat16)
    low = (value - high.astype(jnp.float32)).astype(jnp.bfloat16)
    return jnp.concatenate([high, low], axis=1)


def same_sample(count):
    first = lax.broadcasted_iota(jnp.int32, (count * GROUP, count * GROUP), 0)
    second = lax.broadcasted_iota(jnp.int32, (count * GROUP, count * GROUP), 1)
    return (first & (GROUP - 1)) == (second & (GROUP - 1))


def stacked(ref, rows, count, width):
    return jnp.concatenate([ref[rows, k * width : (k + 1) * width] for k in range(count)], axis=0)


def repeated(proj):
    count, width = proj.shape
    lines = [jnp.broadcast_to(proj[k : k + 1, :], (GROUP, width)) for k in range(count)]
    return jnp.concatenate(lines, axis=0).astype(jnp.bfloat16)


def mix_forward(small, layer, acts, inter, scale, normed, grams, count):
    batch, model_width = acts.shape
    width = model_width // count
    both = small[layer].astype(jnp.float32)
    proj = repeated(both[:count])
    keep = same_sample(count)
    size = GROUP * count
    for group in range(batch // GROUP):
        block = stacked(acts, pl.ds(group * GROUP, GROUP), count, width)
        gram = jnp.where(keep, dot_nt(block, block), 0.0)
        grams[group * size : (group + 1) * size, :] = halves(gram)
    mixed = dot(grams[...], jnp.concatenate([proj, proj], axis=0))
    for group in range(batch // GROUP):
        rows = pl.ds(group * GROUP, GROUP)
        start = group * size
        parts = [mixed[start + k * GROUP : start + (k + 1) * GROUP] for k in range(count)]
        squares = sum(part * part for part in parts)
        mean = jnp.sum(squares, axis=1, keepdims=True) * (1.0 / model_width)
        inv = lax.rsqrt(mean + EPSILON)
        scale[rows, :] = jnp.broadcast_to(inv, (GROUP, width))
        for k in range(count):
            columns = slice(k * width, (k + 1) * width)
            inter[rows, columns] = parts[k]
            gain = both[count + k : count + k + 1]
            normed[rows, columns] = (parts[k] * inv * gain).astype(jnp.bfloat16)


def gram_scratch(batch, count):
    return pltpu.VMEM((batch * count, 2 * GROUP * count), jnp.bfloat16)


def hidden_tile(hidden_width):
    return min(hidden_width, 1024)


def model_tile(model_width):
    return min(model_width, 512)


def tile_at(step, size):
    return pl.ds(pl.multiple_of(step * size, size), size)


class Stream:
    def __init__(self, mine, own, other, held, sems, axis, size):
        self.mine, self.own, self.other, self.held, self.sems = mine, own, other, held, sems
        self.axis, self.size = axis, size
        self.tiles = own.shape[axis] // size

    def copy(self, source, step):
        cut = tile_at(step, self.size)
        index = (slice(None), cut) if self.axis == 1 else (cut, slice(None))
        return pltpu.make_async_copy(source.at[index], self.held.at[index], self.sems.at[step])

    def start(self):
        @pl.when(self.mine)
        def _():
            for step in range(self.tiles):
                self.copy(self.own, step).start()

        @pl.when(jnp.logical_not(self.mine))
        def _():
            for step in range(self.tiles):
                self.copy(self.other, step).start()

    def wait(self, step):
        self.copy(self.own, step).wait()


def no_wait(step):
    return None


def over_tiles(total, tile, many, wait, work):
    many = min(many, total // tile)

    def body(step, carry):
        for inner in range(many):
            wait(step * many + inner)
        work(tile_at(step, many * tile))
        return carry

    lax.fori_loop(0, total // (many * tile), body, 0)


def up_product(normed, w_up, hidden, turned, wait, many=1):
    def work(columns):
        opened = jnp.maximum(dot(normed[...], w_up[:, columns]), 0.0).astype(jnp.bfloat16)
        hidden[:, columns] = opened
        turned[columns, :] = opened.T

    width = hidden.shape[1]
    over_tiles(width, hidden_tile(width), many, wait, work)


def down_product(hidden, w_down, acts, out, wait, many=1):
    def work(columns):
        term = dot(hidden[...], w_down[:, columns])
        out[:, columns] = (acts[:, columns].astype(jnp.float32) + term).astype(jnp.bfloat16)

    width = out.shape[1]
    over_tiles(width, model_tile(width), many, wait, work)


def turn(rows, turned):
    turned[...] = rows[...].T


def opened_only(hidden, grad):
    return jnp.where(hidden.astype(jnp.float32) > 0.0, grad, 0.0).astype(jnp.bfloat16)


def down_back(grad, w_down, hidden, out, wait, many=1):
    def work(lines):
        g_hidden = dot(w_down[lines, :], grad[...])
        if hidden is not None:
            out[lines, :] = opened_only(hidden[lines, :], g_hidden)
        else:
            out[lines, :] = g_hidden.astype(jnp.bfloat16)

    width = out.shape[0]
    over_tiles(width, hidden_tile(width), many, wait, work)


def up_back(g_before, w_up, weighted, wait, many=1):
    def work(columns):
        weighted[:, columns] = dot(w_up[columns, :], g_before[...]).T

    width = weighted.shape[1]
    over_tiles(width, model_tile(width), many, wait, work)


def mix_backward(small, layer, grad, acts, inter, scale, weighted, out, count):
    batch, model_width = acts.shape
    width = model_width // count
    both = small[layer].astype(jnp.float32)
    proj = repeated(both[:count])
    keep = same_sample(count)
    for start in range(0, batch, GROUP):
        rows = pl.ds(start, GROUP)
        columns = [slice(k * width, (k + 1) * width) for k in range(count)]
        gained = [weighted[rows, columns[k]] * both[count + k : count + k + 1] for k in range(count)]
        shared = sum(gained[k] * inter[rows, columns[k]] for k in range(count))
        mean = jnp.sum(shared, axis=1, keepdims=True) * (1.0 / model_width)
        inv = scale[rows, 0:1]
        pull = inv * inv * mean
        parts = [
            (inv * (gained[k] - inter[rows, columns[k]] * pull)).astype(jnp.bfloat16)
            for k in range(count)
        ]
        block = stacked(acts, rows, count, width)
        g_inter = jnp.concatenate(parts, axis=0)
        left = jnp.concatenate([g_inter, proj], axis=1)
        right = jnp.concatenate([proj, g_inter], axis=1)
        links = jnp.where(keep, dot_nt(left, right), 0.0)
        g_acts = dot(halves(links), jnp.concatenate([block, block], axis=0))
        for k in range(count):
            piece = g_acts[k * GROUP : (k + 1) * GROUP] + grad[rows, columns[k]].astype(jnp.float32)
            out[rows, columns[k]] = piece.astype(jnp.bfloat16)


def saved_shapes(batch, model_width, hidden_width, width):
    return [
        jax.ShapeDtypeStruct((2, hidden_width, batch), jnp.bfloat16),
        jax.ShapeDtypeStruct((2, batch, model_width), jnp.float32),
        jax.ShapeDtypeStruct((2, batch, width), jnp.float32),
        jax.ShapeDtypeStruct((2, batch, model_width), jnp.bfloat16),
    ]


def weight_specs():
    return [whole()] + [whole(pltpu.HBM)] * 4


def weight_scratch(model_width, hidden_width):
    tiles = max(hidden_width // hidden_tile(hidden_width), model_width // model_tile(model_width))
    return [
        pltpu.VMEM((2, model_width, hidden_width), jnp.bfloat16),
        pltpu.VMEM((2, hidden_width, model_width), jnp.bfloat16),
        pltpu.SemaphoreType.DMA((4, tiles)),
    ]


def streams_of(core, weights, held, forward):
    own_up, other_up, own_down, other_down = weights
    held_up, held_down, sems = held
    model_width, hidden_width = own_up.shape
    wide, narrow = hidden_tile(hidden_width), model_tile(model_width)
    made = []
    for layer in (0, 1):
        mine = core == layer
        up_forward, down_forward = forward[layer]
        up_cut = (1, wide) if up_forward else (0, narrow)
        down_cut = (1, narrow) if down_forward else (0, wide)
        made.append(
            (
                Stream(mine, own_up, other_up, held_up.at[layer], sems.at[2 * layer], *up_cut),
                Stream(mine, own_down, other_down, held_down.at[layer], sems.at[2 * layer + 1], *down_cut),
            )
        )
    return made


def stage_cost(products, batch, model_width, hidden_width):
    return pl.CostEstimate(
        flops=2 * products * batch * model_width * hidden_width, bytes_accessed=1 << 20, transcendentals=0
    )


def stage_params():
    return pltpu.CompilerParams(vmem_limit_bytes=STAGE_LIMIT)


def forward_stage(place, pieces, top, weights, count):
    batch, model_width = top.shape
    hidden_width = weights[1].shape[1]
    width = model_width // count

    def kernel(place_ref, *refs):
        piece_refs, (top_ref, small_ref), refs = refs[: len(pieces)], refs[len(pieces) :][:2], refs[len(pieces) + 2 :]
        matrices, refs = refs[:4], refs[4:]
        out_ref, hid, inter, scale, kept, g_hidden = refs[:6]
        held, (normed, hidden, top_turned, grams) = refs[6:9], refs[9:]
        core = place_ref[0]

        @pl.when(place_ref[1] == 1)
        def _():
            layers = streams_of(core, matrices, held, [(True, True), (True, True)])
            for up, down in layers:
                up.start()
                down.start()
            start = 0
            for piece in piece_refs:
                kept[0, start : start + piece.shape[0], :] = piece[...]
                start += piece.shape[0]
            for layer, (up, down) in enumerate(layers):
                mix_forward(
                    small_ref, layer, kept.at[layer], inter.at[layer], scale.at[layer], normed, grams, count
                )
                up_product(normed, up.held, hidden, hid.at[layer], up.wait)
                to = kept.at[1] if layer == 0 else out_ref
                down_product(hidden, down.held, kept.at[layer], to, down.wait)

        @pl.when(place_ref[2] == 1)
        def _():
            layers = streams_of(core, matrices, held, [(True, True), (True, False)])
            down = layers[1][1]
            down.start()
            turn(top_ref, top_turned)
            down_back(top_turned, down.held, None, g_hidden, down.wait)

    out = pl.pallas_call(
        kernel,
        out_shape=[jax.ShapeDtypeStruct(top.shape, jnp.bfloat16)]
        + saved_shapes(batch, model_width, hidden_width, width)
        + [jax.ShapeDtypeStruct((hidden_width, batch), jnp.bfloat16)],
        in_specs=[whole(pltpu.SMEM)] + [whole()] * (len(pieces) + 1) + weight_specs(),
        out_specs=[whole()] * 6,
        scratch_shapes=weight_scratch(model_width, hidden_width)
        + [
            pltpu.VMEM((batch, model_width), jnp.bfloat16),
            pltpu.VMEM((batch, hidden_width), jnp.bfloat16),
            pltpu.VMEM((model_width, batch), jnp.bfloat16),
            gram_scratch(batch, count),
        ],
        compiler_params=stage_params(),
        cost_estimate=stage_cost(4, batch, model_width, hidden_width),
        name="forward_stage",
    )(place, *pieces, top, weights[0], *map(in_hbm, weights[1:]))
    return out[0], out[1:5], out[5]


def turn_stage(place, acts, top, g_hidden, weights, count):
    batch, model_width = acts.shape
    hidden_width = weights[1].shape[1]
    width = model_width // count

    def kernel(place_ref, acts_ref, top_ref, ghid_ref, small_ref, *refs):
        matrices, refs = refs[:4], refs[4:]
        out_ref, held = refs[0], refs[1:4]
        hid, hidden, inter, scale, upper, grad, turned, normed, weighted, g_before, grams = refs[4:]

        @pl.when(place_ref[1] == 1)
        def _():
            layers = streams_of(place_ref[0], matrices, held, [(True, True), (True, True)])
            (up0, down0), (up1, down1) = layers
            for stream in (up0, down0, up1):
                stream.start()
            mix_forward(small_ref, 0, acts_ref, inter.at[0], scale.at[0], normed, grams, count)
            up_product(normed, up0.held, hidden, hid, up0.wait)
            down_product(hidden, down0.held, acts_ref, upper, down0.wait)
            mix_forward(small_ref, 1, upper, inter.at[1], scale.at[1], normed, grams, count)

            def masked(columns):
                before = dot(normed[...], up1.held[:, columns])
                opened = jnp.maximum(before, 0.0).astype(jnp.bfloat16).T
                g_before[columns, :] = opened_only(opened, ghid_ref[columns, :].astype(jnp.float32))

            over_tiles(hidden_width, hidden_tile(hidden_width), 1, up1.wait, masked)
            up_back(g_before, up1.held, weighted, no_wait)
            mix_backward(small_ref, 1, top_ref, upper, inter.at[1], scale.at[1], weighted, grad, count)
            turn(grad, turned)
            down_back(turned, down0.held, hid, g_before, no_wait)
            up_back(g_before, up0.held, weighted, no_wait)
            mix_backward(small_ref, 0, grad, acts_ref, inter.at[0], scale.at[0], weighted, out_ref, count)

    return pl.pallas_call(
        kernel,
        out_shape=jax.ShapeDtypeStruct(acts.shape, jnp.bfloat16),
        in_specs=[whole(pltpu.SMEM)] + [whole()] * 3 + weight_specs(),
        out_specs=whole(),
        scratch_shapes=weight_scratch(model_width, hidden_width)
        + [
            pltpu.VMEM((hidden_width, batch), jnp.bfloat16),
            pltpu.VMEM((batch, hidden_width), jnp.bfloat16),
            pltpu.VMEM((2, batch, model_width), jnp.float32),
            pltpu.VMEM((2, batch, width), jnp.float32),
            pltpu.VMEM((batch, model_width), jnp.bfloat16),
            pltpu.VMEM((batch, model_width), jnp.bfloat16),
            pltpu.VMEM((model_width, batch), jnp.bfloat16),
            pltpu.VMEM((batch, model_width), jnp.bfloat16),
            pltpu.VMEM((batch, model_width), jnp.float32),
            pltpu.VMEM((hidden_width, batch), jnp.bfloat16),
            gram_scratch(batch, count),
        ],
        compiler_params=stage_params(),
        cost_estimate=stage_cost(6, batch, model_width, hidden_width),
        name="turn_stage",
    )(place, acts, top, g_hidden, weights[0], *map(in_hbm, weights[1:]))


def backward_stage(place, grad, saved, weights, count):
    batch, model_width = grad.shape
    hidden_width = weights[1].shape[1]

    def kernel(place_ref, grad_ref, hid, inter, scale, kept, small_ref, *refs):
        matrices, refs = refs[:4], refs[4:]
        out_ref, held = refs[0], refs[1:4]
        middle, turned, weighted, g_before = refs[4:]

        @pl.when(place_ref[1] == 1)
        def _():
            layers = streams_of(place_ref[0], matrices, held, [(False, False), (False, False)])
            for up, down in reversed(layers):
                down.start()
                up.start()
            for layer, given, to in ((1, grad_ref, middle), (0, middle, out_ref)):
                up, down = layers[layer]
                turn(given, turned)
                down_back(turned, down.held, hid.at[layer], g_before, down.wait)
                up_back(g_before, up.held, weighted, up.wait)
                mix_backward(
                    small_ref, layer, given, kept.at[layer], inter.at[layer], scale.at[layer],
                    weighted, to, count,
                )

    return pl.pallas_call(
        kernel,
        out_shape=jax.ShapeDtypeStruct(grad.shape, jnp.bfloat16),
        in_specs=[whole(pltpu.SMEM)] + [whole()] * 5 + weight_specs(),
        out_specs=whole(),
        scratch_shapes=weight_scratch(model_width, hidden_width)
        + [
            pltpu.VMEM((batch, model_width), jnp.bfloat16),
            pltpu.VMEM((model_width, batch), jnp.bfloat16),
            pltpu.VMEM((batch, model_width), jnp.float32),
            pltpu.VMEM((hidden_width, batch), jnp.bfloat16),
        ],
        compiler_params=stage_params(),
        cost_estimate=stage_cost(4, batch, model_width, hidden_width),
        name="backward_stage",
    )(place, grad, *saved, weights[0], *map(in_hbm, weights[1:]))


def swapped(value, section_count):
    return lax.ppermute(value, "section", [(s, s ^ 1) for s in range(section_count)])


def moved(value, from_stage, to_stage):
    pairs = [(2 * from_stage + core, 2 * to_stage + core) for core in (0, 1)]
    return lax.ppermute(value, "section", pairs)


def mirror(value):
    along = lax.axis_size("table")
    return lax.ppermute(value, "table", [(t, (t + along // 2) % along) for t in range(along)])


def swap_in_half(value):
    along = lax.axis_size("table")
    half = along // 2
    groups = [
        [s * along + h * half + t for s in range(lax.axis_size("section")) for t in range(half)]
        for h in (0, 1)
    ]
    return lax.all_to_all(
        value, TABLE_AXES, split_axis=0, concat_axis=0, axis_index_groups=groups, tiled=True
    )


def near_first(per_asker, my_half):
    sections = lax.axis_size("section")
    half = lax.axis_size("table") // 2
    split = per_asker.reshape((sections, 2, half) + per_asker.shape[1:])
    near = lax.dynamic_index_in_dim(split, my_half, 1, keepdims=False)
    far = lax.dynamic_index_in_dim(split, 1 - my_half, 1, keepdims=False)
    return jnp.stack([near, far], axis=2).reshape((sections * half, 2) + per_asker.shape[1:])


def after(value, earlier):
    return lax.optimization_barrier((value, earlier))[0]


def per_device(
    emb_table,
    lcb_weight,
    fm_proj,
    norm_gain,
    w_up,
    w_down,
    top_grad,
    lookup_slot,
    wanted_rows,
    row_counts,
):
    section_count = lax.axis_size("section")
    along = lax.axis_size("table")
    half = along // 2
    near_owners = section_count * half
    stages = section_count // 2
    stage = lax.axis_index("section") // 2
    core = lax.axis_index("section") % 2
    my_half = lax.axis_index("table") // half
    cap = wanted_rows.shape[2]
    rows, embed_width = emb_table.shape
    embed_count = lcb_weight.shape[0]
    look_dev = lookup_slot.shape[1]
    model_width = top_grad.shape[3]

    own_slots = lookup_slot[0]
    mirror_slots = mirror(own_slots)
    small = jnp.concatenate([fm_proj[0], norm_gain[0].reshape(embed_count, -1)], axis=0)
    other_up = swapped(w_up[0], section_count)
    other_down = swapped(w_down[0], section_count)
    other_small = swapped(small, section_count)

    picked = near_first(wanted_rows[0], my_half)
    outgoing = pick_rows(emb_table, picked.reshape(-1))
    sent = after(outgoing, mirror_slots).reshape(near_owners, 2, cap, embed_width)
    fetched = swap_in_half(sent)

    def spread_of(slots):
        owner, column = slots // cap, slots % cap
        place = owner % along
        near = jnp.where(place // half == my_half, owner // along * half + place % half, near_owners)
        return spread_weights(near * cap + column, lcb_weight, near_owners, cap)

    spread_far, kept_far = spread_of(mirror_slots)
    spread_near, kept_near = spread_of(own_slots)
    smalls = jnp.stack(
        [jnp.where(core == 0, small, other_small), jnp.where(core == 0, other_small, small)]
    )
    weights = [smalls, w_up[0], other_up, w_down[0], other_down]
    spread_far, spread_near = lax.optimization_barrier((spread_far, spread_near))
    far_part = mirror(compress(spread_far, fetched, 1, embed_count, jnp.bfloat16))
    near_part = compress(spread_near, fetched, 0, embed_count, jnp.float32)
    lead = (near_part + far_part.astype(jnp.float32)).astype(jnp.bfloat16)
    pieces = [lead] + [moved(lead, s, 0) for s in range(1, stages)]
    top = top_grad.reshape(stages, 2, look_dev, model_width)
    top = lax.dynamic_index_in_dim(top, core, 1, keepdims=False).reshape(-1, model_width)

    def at(tick):
        is_last = (stage == stages - 1) & (tick == 0)
        return jnp.stack([core, stage == tick, is_last]).astype(jnp.int32)

    saved = None
    for tick in range(stages - 1):
        out, fresh, product = forward_stage(at(tick), pieces, top, weights, embed_count)
        if saved is None:
            saved, g_hidden = fresh, product
        else:
            saved = [jnp.where(stage == tick, new, old) for new, old in zip(fresh, saved)]
        pieces = [moved(out, tick, tick + 1)]
    grad = turn_stage(at(stages - 1), pieces[0], top, g_hidden, weights, embed_count)
    for tick in reversed(range(stages - 1)):
        grad = moved(grad, tick + 1, tick)
        grad = backward_stage(at(tick), grad, saved, weights, embed_count)

    own_grad = grad[:look_dev]
    for s in range(1, stages):
        piece = grad[s * look_dev : (s + 1) * look_dev]
        own_grad = jnp.where(stage == s, moved(piece, 0, s), own_grad)
    mirror_grad = mirror(own_grad)

    near_grad = expand(kept_near, own_grad, embed_count)
    slot_grad = expand(kept_far, mirror_grad, embed_count, near_grad)
    returned = swap_in_half(slot_grad)
    live_slots = jnp.arange(cap) < near_first(row_counts[0], my_half)[..., None]
    targets = jnp.where(live_slots, picked, rows).reshape(-1)
    return add_rows(targets, returned.reshape(-1, embed_width), outgoing, rows, cap)


def solution(mesh):
    in_specs = (
        P(("section", "table"), None),
        P(),
        P("section", None, None),
        P("section", None),
        P("section", None, None),
        P("section", None, None),
        P("table", None, None, None),
        P("table", "section", None),
        P(("section", "table"), None, None),
        P(("section", "table"), None),
    )
    out_specs = P(("section", "table"), None)
    return jax.shard_map(
        per_device, mesh=mesh, in_specs=in_specs, out_specs=out_specs, check_vma=False
    )
```

```python
import jax
import jax.numpy as jnp
from jax import lax
from jax.experimental import pallas as pl
from jax.experimental.pallas import tpu as pltpu
from jax.sharding import PartitionSpec as P

EPSILON = 1e-05
DECAY_WEIGHT = 0.5
VMEM_LIMIT = 28 * 1024 * 1024
UNROLL = 32
PICK_UNROLL = 128


def whole(memory_space=pltpu.VMEM):
    return pl.BlockSpec(memory_space=memory_space)


def in_hbm(value):
    return pltpu.with_memory_space_constraint(value, pltpu.HBM)


def params():
    return pltpu.CompilerParams(vmem_limit_bytes=VMEM_LIMIT)


def tiles_of(count, most):
    return max(step for step in range(1, most + 1) if count % step == 0)


def pick_rows(emb_table, picked):
    rows, width = emb_table.shape
    count = picked.shape[0]
    chunk = min(count, 1024)

    def kernel(picked_ref, table_ref, out_ref, wide, lines):
        wide[...] = table_ref[...].astype(jnp.float32)

        def fill(part, carry):
            base = pl.multiple_of(part * chunk, chunk)

            def body(group, inner):
                first = pl.multiple_of(group * PICK_UNROLL, PICK_UNROLL)
                for lane in range(PICK_UNROLL):
                    row = picked_ref[base + first + lane]
                    lines[pl.ds(first + lane, 1), :] = wide[pl.ds(row, 1), :]
                return inner

            lax.fori_loop(0, chunk // PICK_UNROLL, body, 0)
            out_ref[pl.ds(base, chunk), :] = lines[...].astype(out_ref.dtype)
            return carry

        lax.fori_loop(0, count // chunk, fill, 0)

    return pl.pallas_call(
        kernel,
        out_shape=jax.ShapeDtypeStruct((count, width), emb_table.dtype),
        in_specs=[whole(pltpu.SMEM), whole()],
        out_specs=whole(),
        scratch_shapes=[
            pltpu.VMEM((rows, width), jnp.float32),
            pltpu.VMEM((chunk, width), jnp.float32),
        ],
        compiler_params=params(),
        name="pick_rows",
    )(picked, emb_table)


def spread_weights(codes, lcb_weight, owners, cap):
    samples, feature_count = codes.shape
    embed_count = lcb_weight.shape[0]
    group = tiles_of(samples, 16)

    def kernel(codes_ref, lcb_ref, out_ref):
        lcb = lcb_ref[...].astype(jnp.float32)
        owner_of = lax.broadcasted_iota(jnp.int32, (owners, embed_count, feature_count), 0)
        column_of = lax.broadcasted_iota(jnp.int32, (cap, feature_count), 0)
        for pair in range(0, group, 2):
            made = []
            for sample in (pair, pair + 1):
                slots = codes_ref[sample : sample + 1, :]
                owner = lax.div(slots, cap)
                column = slots - owner * cap
                left = jnp.where(owner_of == owner[None], lcb[None], 0.0)
                left = left.reshape(owners * embed_count, feature_count).astype(jnp.bfloat16)
                right = jnp.where(column_of == column, 1.0, 0.0).astype(jnp.bfloat16)
                both = lax.dot_general(
                    left, right, (((1,), (1,)), ((), ())), preferred_element_type=jnp.float32
                )
                made.append(both.reshape(owners, embed_count, cap))
            rows = pl.ds(pair * embed_count, 2 * embed_count)
            joined = jnp.concatenate(made, axis=1).astype(out_ref.dtype)
            out_ref[:, rows, :] = joined

    return pl.pallas_call(
        kernel,
        out_shape=pltpu.HBM((owners, samples * embed_count, cap), jnp.bfloat16),
        grid=(samples // group,),
        in_specs=[
            pl.BlockSpec((group, feature_count), lambda i: (i, 0)),
            pl.BlockSpec((embed_count, feature_count), lambda i: (0, 0)),
        ],
        out_specs=pl.BlockSpec((owners, group * embed_count, cap), lambda i: (0, i, 0)),
        compiler_params=params(),
        cost_estimate=pl.CostEstimate(
            flops=2 * samples * owners * embed_count * feature_count * cap,
            bytes_accessed=2 * owners * samples * embed_count * cap,
            transcendentals=0,
        ),
        name="spread_weights",
    )(codes, lcb_weight)


def compress(spread, fetched, view, embed_count, kind):
    owners, lines, cap = spread.shape
    width = fetched.shape[3]
    samples = lines // embed_count
    part = tiles_of(owners, 8)
    steps = owners // part

    def kernel(spread_ref, rows_ref, out_ref, held, total, sems):
        copies = []
        for step in range(steps):
            piece = pl.ds(step * part, part)
            copies.append(pltpu.make_async_copy(spread_ref.at[piece], held.at[piece], sems.at[step]))
            copies[-1].start()
        for step in range(steps):
            copies[step].wait()
            owners_here = range(step * part, (step + 1) * part)
            left = jnp.concatenate([held[o] for o in owners_here], axis=1)
            right = jnp.concatenate([rows_ref[o, view] for o in owners_here], axis=0)
            term = jnp.dot(left, right, preferred_element_type=jnp.float32)
            total[...] = term if step == 0 else total[...] + term
        for k in range(embed_count):
            columns = slice(k * width, (k + 1) * width)
            piece = total[pl.ds(k, samples, stride=embed_count), :]
            out_ref[:, columns] = piece.astype(out_ref.dtype)

    return pl.pallas_call(
        kernel,
        out_shape=jax.ShapeDtypeStruct((samples, embed_count * width), kind),
        in_specs=[whole(pltpu.HBM), whole()],
        out_specs=whole(),
        scratch_shapes=[
            pltpu.VMEM(spread.shape, jnp.bfloat16),
            pltpu.VMEM((lines, width), jnp.float32),
            pltpu.SemaphoreType.DMA((steps,)),
        ],
        compiler_params=params(),
        name="compress",
    )(in_hbm(spread), fetched)


def expand(spread, lead_grad, embed_count, near=None):
    owners, lines, cap = spread.shape
    samples = lines // embed_count
    width = lead_grad.shape[1] // embed_count
    part = tiles_of(owners, 8)
    extra = [] if near is None else [near]

    def kernel(spread_ref, grad_ref, *refs):
        near_refs, (out_ref, tall, turned) = refs[: len(extra)], refs[len(extra) :]
        for k in range(embed_count):
            piece = grad_ref[:, k * width : (k + 1) * width].astype(jnp.float32)
            tall[pl.ds(k, samples, stride=embed_count), :] = piece
        turned[...] = tall[...].T.astype(jnp.bfloat16)

        def body(step, carry):
            first = step * part
            right = jnp.concatenate([spread_ref[first + o] for o in range(part)], axis=1)
            term = jnp.dot(turned[...], right, preferred_element_type=jnp.float32)
            piece = term.T.astype(out_ref.dtype).reshape(part, cap, width)
            if near_refs:
                for o in range(part):
                    out_ref[first + o, 0] = near_refs[0][first + o]
                    out_ref[first + o, 1] = piece[o]
            else:
                out_ref[tile_at(step, part)] = piece
            return carry

        lax.fori_loop(0, owners // part, body, 0)

    views = () if near is None else (2,)
    return pl.pallas_call(
        kernel,
        out_shape=jax.ShapeDtypeStruct((owners,) + views + (cap, width), jnp.bfloat16),
        in_specs=[whole()] * (2 + len(extra)),
        out_specs=whole(),
        scratch_shapes=[
            pltpu.VMEM((lines, width), jnp.float32),
            pltpu.VMEM((width, lines), jnp.bfloat16),
        ],
        compiler_params=params(),
        name="expand",
    )(spread, lead_grad, *extra)


def add_rows(targets, returned, outgoing, rows, cap):
    count, width = returned.shape
    pair = 2 * cap

    def kernel(targets_ref, back_ref, sent_ref, out_ref, total, second, terms, sem):
        total[...] = jnp.zeros_like(total)
        second[...] = jnp.zeros_like(second)

        def body(step, carry):
            base = pl.multiple_of(step * pair, pair)
            lines = pl.ds(base, pair)
            terms[...] = back_ref[lines, :].astype(jnp.float32) + DECAY_WEIGHT * sent_ref[
                lines, :
            ].astype(jnp.float32)
            for first in range(0, cap, UNROLL):
                lanes = range(first, first + UNROLL)
                places = [targets_ref[base + lane] for lane in lanes]
                others = [targets_ref[base + cap + lane] for lane in lanes]
                sums = [
                    total[pl.ds(place, 1), :] + terms[lane : lane + 1, :]
                    for place, lane in zip(places, lanes)
                ]
                other_sums = [
                    second[pl.ds(place, 1), :] + terms[cap + lane : cap + lane + 1, :]
                    for place, lane in zip(others, lanes)
                ]
                for place, value in zip(places, sums):
                    total[pl.ds(place, 1), :] = value
                for place, value in zip(others, other_sums):
                    second[pl.ds(place, 1), :] = value
            return carry

        lax.fori_loop(0, count // pair, body, 0)
        part = rows // 4
        copies = []
        for piece in range(4):
            cut = pl.ds(piece * part, part)
            total[cut, :] = total[cut, :] + second[cut, :]
            copies.append(pltpu.make_async_copy(total.at[cut, :], out_ref.at[cut, :], sem.at[piece]))
            copies[-1].start()
        for copy in copies:
            copy.wait()

    return pl.pallas_call(
        kernel,
        out_shape=jax.ShapeDtypeStruct((rows, width), jnp.float32),
        in_specs=[whole(pltpu.SMEM), whole(), whole()],
        out_specs=whole(pl.ANY),
        scratch_shapes=[
            pltpu.VMEM((rows + 8, width), jnp.float32),
            pltpu.VMEM((rows + 8, width), jnp.float32),
            pltpu.VMEM((pair, width), jnp.float32),
            pltpu.SemaphoreType.DMA((4,)),
        ],
        compiler_params=params(),
        name="add_rows",
    )(targets, returned, outgoing)


GROUP = 16
TABLE_AXES = ("section", "table")
STAGE_LIMIT = 44 * 1024 * 1024
NT = (((1,), (1,)), ((), ()))


def dot_nt(left, right):
    return lax.dot_general(left, right, NT, preferred_element_type=jnp.float32)


def dot(left, right):
    return jnp.dot(left, right, preferred_element_type=jnp.float32)


def halves(value):
    high = value.astype(jnp.bfloat16)
    low = (value - high.astype(jnp.float32)).astype(jnp.bfloat16)
    return jnp.concatenate([high, low], axis=1)


def same_sample(count):
    first = lax.broadcasted_iota(jnp.int32, (count * GROUP, count * GROUP), 0)
    second = lax.broadcasted_iota(jnp.int32, (count * GROUP, count * GROUP), 1)
    return (first & (GROUP - 1)) == (second & (GROUP - 1))


def stacked(ref, rows, count, width):
    return jnp.concatenate([ref[rows, k * width : (k + 1) * width] for k in range(count)], axis=0)


def repeated(proj):
    count, width = proj.shape
    lines = [jnp.broadcast_to(proj[k : k + 1, :], (GROUP, width)) for k in range(count)]
    return jnp.concatenate(lines, axis=0).astype(jnp.bfloat16)


def mix_forward(small, layer, acts, inter, scale, normed, grams, count):
    batch, model_width = acts.shape
    width = model_width // count
    both = small[layer].astype(jnp.float32)
    proj = repeated(both[:count])
    keep = same_sample(count)
    size = GROUP * count
    for group in range(batch // GROUP):
        block = stacked(acts, pl.ds(group * GROUP, GROUP), count, width)
        gram = jnp.where(keep, dot_nt(block, block), 0.0)
        grams[group * size : (group + 1) * size, :] = halves(gram)
    mixed = dot(grams[...], jnp.concatenate([proj, proj], axis=0))
    for group in range(batch // GROUP):
        rows = pl.ds(group * GROUP, GROUP)
        start = group * size
        parts = [mixed[start + k * GROUP : start + (k + 1) * GROUP] for k in range(count)]
        squares = sum(part * part for part in parts)
        mean = jnp.sum(squares, axis=1, keepdims=True) * (1.0 / model_width)
        inv = lax.rsqrt(mean + EPSILON)
        scale[rows, :] = jnp.broadcast_to(inv, (GROUP, width))
        for k in range(count):
            columns = slice(k * width, (k + 1) * width)
            inter[rows, columns] = parts[k]
            gain = both[count + k : count + k + 1]
            normed[rows, columns] = (parts[k] * inv * gain).astype(jnp.bfloat16)


def gram_scratch(batch, count):
    return pltpu.VMEM((batch * count, 2 * GROUP * count), jnp.bfloat16)


def hidden_tile(hidden_width):
    return min(hidden_width, 1024)


def model_tile(model_width):
    return min(model_width, 512)


def tile_at(step, size):
    return pl.ds(pl.multiple_of(step * size, size), size)


class Stream:
    def __init__(self, mine, own, other, held, sems, axis, size):
        self.mine, self.own, self.other, self.held, self.sems = mine, own, other, held, sems
        self.axis, self.size = axis, size
        self.tiles = own.shape[axis] // size

    def copy(self, source, step):
        cut = tile_at(step, self.size)
        index = (slice(None), cut) if self.axis == 1 else (cut, slice(None))
        return pltpu.make_async_copy(source.at[index], self.held.at[index], self.sems.at[step])

    def start(self):
        @pl.when(self.mine)
        def _():
            for step in range(self.tiles):
                self.copy(self.own, step).start()

        @pl.when(jnp.logical_not(self.mine))
        def _():
            for step in range(self.tiles):
                self.copy(self.other, step).start()

    def wait(self, step):
        self.copy(self.own, step).wait()


def no_wait(step):
    return None


def over_tiles(total, tile, many, wait, work):
    many = min(many, total // tile)

    def body(step, carry):
        for inner in range(many):
            wait(step * many + inner)
        work(tile_at(step, many * tile))
        return carry

    lax.fori_loop(0, total // (many * tile), body, 0)


def up_product(normed, w_up, hidden, wait, many=1):
    def work(columns):
        before = dot(normed[...], w_up[:, columns])
        hidden[:, columns] = jnp.maximum(before, 0.0).astype(jnp.bfloat16)

    width = hidden.shape[1]
    over_tiles(width, hidden_tile(width), many, wait, work)


def down_product(hidden, w_down, acts, out, wait, many=1):
    def work(columns):
        term = dot(hidden[...], w_down[:, columns])
        out[:, columns] = (acts[:, columns].astype(jnp.float32) + term).astype(jnp.bfloat16)

    width = out.shape[1]
    over_tiles(width, model_tile(width), many, wait, work)


def opened_only(hidden, grad):
    return jnp.where(hidden.astype(jnp.float32) > 0.0, grad, 0.0).astype(jnp.bfloat16)


def down_back(grad, w_down, hidden, out, wait, many=1):
    def work(columns):
        g_hidden = dot_nt(grad[...], w_down[columns, :])
        if hidden is not None:
            out[:, columns] = opened_only(hidden[:, columns], g_hidden)
        else:
            out[:, columns] = g_hidden.astype(jnp.bfloat16)

    width = out.shape[1]
    over_tiles(width, hidden_tile(width), many, wait, work)


def up_back(g_before, w_up, weighted, wait, many=1):
    def work(columns):
        weighted[:, columns] = dot_nt(g_before[...], w_up[columns, :])

    width = weighted.shape[1]
    over_tiles(width, model_tile(width), many, wait, work)


def mix_backward(small, layer, grad, acts, inter, scale, weighted, out, count):
    batch, model_width = acts.shape
    width = model_width // count
    both = small[layer].astype(jnp.float32)
    proj = repeated(both[:count])
    keep = same_sample(count)
    for start in range(0, batch, GROUP):
        rows = pl.ds(start, GROUP)
        columns = [slice(k * width, (k + 1) * width) for k in range(count)]
        gained = [weighted[rows, columns[k]] * both[count + k : count + k + 1] for k in range(count)]
        shared = sum(gained[k] * inter[rows, columns[k]] for k in range(count))
        mean = jnp.sum(shared, axis=1, keepdims=True) * (1.0 / model_width)
        inv = scale[rows, 0:1]
        pull = inv * inv * mean
        parts = [
            (inv * (gained[k] - inter[rows, columns[k]] * pull)).astype(jnp.bfloat16)
            for k in range(count)
        ]
        block = stacked(acts, rows, count, width)
        g_inter = jnp.concatenate(parts, axis=0)
        left = jnp.concatenate([g_inter, proj], axis=1)
        right = jnp.concatenate([proj, g_inter], axis=1)
        links = jnp.where(keep, dot_nt(left, right), 0.0)
        g_acts = dot(halves(links), jnp.concatenate([block, block], axis=0))
        for k in range(count):
            piece = g_acts[k * GROUP : (k + 1) * GROUP] + grad[rows, columns[k]].astype(jnp.float32)
            out[rows, columns[k]] = piece.astype(jnp.bfloat16)


def saved_shapes(batch, model_width, hidden_width, width):
    return [
        jax.ShapeDtypeStruct((2, batch, hidden_width), jnp.bfloat16),
        jax.ShapeDtypeStruct((2, batch, model_width), jnp.float32),
        jax.ShapeDtypeStruct((2, batch, width), jnp.float32),
        jax.ShapeDtypeStruct((2, batch, model_width), jnp.bfloat16),
    ]


def weight_specs():
    return [whole()] + [whole(pltpu.HBM)] * 4


def weight_scratch(model_width, hidden_width):
    tiles = max(hidden_width // hidden_tile(hidden_width), model_width // model_tile(model_width))
    return [
        pltpu.VMEM((2, model_width, hidden_width), jnp.bfloat16),
        pltpu.VMEM((2, hidden_width, model_width), jnp.bfloat16),
        pltpu.SemaphoreType.DMA((4, tiles)),
    ]


def streams_of(core, weights, held, forward):
    own_up, other_up, own_down, other_down = weights
    held_up, held_down, sems = held
    model_width, hidden_width = own_up.shape
    wide, narrow = hidden_tile(hidden_width), model_tile(model_width)
    made = []
    for layer in (0, 1):
        mine = core == layer
        up_forward, down_forward = forward[layer]
        up_cut = (1, wide) if up_forward else (0, narrow)
        down_cut = (1, narrow) if down_forward else (0, wide)
        made.append(
            (
                Stream(mine, own_up, other_up, held_up.at[layer], sems.at[2 * layer], *up_cut),
                Stream(mine, own_down, other_down, held_down.at[layer], sems.at[2 * layer + 1], *down_cut),
            )
        )
    return made


def stage_cost(products, batch, model_width, hidden_width):
    return pl.CostEstimate(
        flops=2 * products * batch * model_width * hidden_width, bytes_accessed=1 << 20, transcendentals=0
    )


def stage_params():
    return pltpu.CompilerParams(vmem_limit_bytes=STAGE_LIMIT)


def forward_stage(place, pieces, top, weights, count):
    batch, model_width = top.shape
    hidden_width = weights[1].shape[1]
    width = model_width // count

    def kernel(place_ref, *refs):
        piece_refs, (top_ref, small_ref), refs = refs[: len(pieces)], refs[len(pieces) :][:2], refs[len(pieces) + 2 :]
        matrices, refs = refs[:4], refs[4:]
        out_ref, hid, inter, scale, kept, g_hidden = refs[:6]
        held, (normed, grams) = refs[6:9], refs[9:]
        core = place_ref[0]

        @pl.when(place_ref[1] == 1)
        def _():
            layers = streams_of(core, matrices, held, [(True, True), (True, True)])
            for up, down in layers:
                up.start()
                down.start()
            start = 0
            for piece in piece_refs:
                kept[0, start : start + piece.shape[0], :] = piece[...]
                start += piece.shape[0]
            for layer, (up, down) in enumerate(layers):
                mix_forward(
                    small_ref, layer, kept.at[layer], inter.at[layer], scale.at[layer], normed, grams, count
                )
                up_product(normed, up.held, hid.at[layer], up.wait)
                to = kept.at[1] if layer == 0 else out_ref
                down_product(hid.at[layer], down.held, kept.at[layer], to, down.wait)

        @pl.when(place_ref[2] == 1)
        def _():
            layers = streams_of(core, matrices, held, [(True, True), (True, False)])
            down = layers[1][1]
            down.start()
            down_back(top_ref, down.held, None, g_hidden, down.wait)

    out = pl.pallas_call(
        kernel,
        out_shape=[jax.ShapeDtypeStruct(top.shape, jnp.bfloat16)]
        + saved_shapes(batch, model_width, hidden_width, width)
        + [jax.ShapeDtypeStruct((batch, hidden_width), jnp.bfloat16)],
        in_specs=[whole(pltpu.SMEM)] + [whole()] * (len(pieces) + 1) + weight_specs(),
        out_specs=[whole()] * 6,
        scratch_shapes=weight_scratch(model_width, hidden_width)
        + [
            pltpu.VMEM((batch, model_width), jnp.bfloat16),
            gram_scratch(batch, count),
        ],
        compiler_params=stage_params(),
        cost_estimate=stage_cost(4, batch, model_width, hidden_width),
        name="forward_stage",
    )(place, *pieces, top, weights[0], *map(in_hbm, weights[1:]))
    return out[0], out[1:5], out[5]


def turn_stage(place, acts, top, g_hidden, weights, count):
    batch, model_width = acts.shape
    hidden_width = weights[1].shape[1]
    width = model_width // count

    def kernel(place_ref, acts_ref, top_ref, ghid_ref, small_ref, *refs):
        matrices, refs = refs[:4], refs[4:]
        out_ref, held = refs[0], refs[1:4]
        hid, inter, scale, upper, grad, normed, weighted, g_before, grams = refs[4:]

        @pl.when(place_ref[1] == 1)
        def _():
            layers = streams_of(place_ref[0], matrices, held, [(True, True), (True, True)])
            (up0, down0), (up1, down1) = layers
            for stream in (up0, down0, up1):
                stream.start()
            mix_forward(small_ref, 0, acts_ref, inter.at[0], scale.at[0], normed, grams, count)
            up_product(normed, up0.held, hid, up0.wait)
            down_product(hid, down0.held, acts_ref, upper, down0.wait)
            mix_forward(small_ref, 1, upper, inter.at[1], scale.at[1], normed, grams, count)

            def masked(columns):
                before = dot(normed[...], up1.held[:, columns])
                g_before[:, columns] = opened_only(before, ghid_ref[:, columns].astype(jnp.float32))

            over_tiles(hidden_width, hidden_tile(hidden_width), 1, up1.wait, masked)
            up_back(g_before, up1.held, weighted, no_wait)
            mix_backward(small_ref, 1, top_ref, upper, inter.at[1], scale.at[1], weighted, grad, count)
            down_back(grad, down0.held, hid, g_before, no_wait)
            up_back(g_before, up0.held, weighted, no_wait)
            mix_backward(small_ref, 0, grad, acts_ref, inter.at[0], scale.at[0], weighted, out_ref, count)

    return pl.pallas_call(
        kernel,
        out_shape=jax.ShapeDtypeStruct(acts.shape, jnp.bfloat16),
        in_specs=[whole(pltpu.SMEM)] + [whole()] * 3 + weight_specs(),
        out_specs=whole(),
        scratch_shapes=weight_scratch(model_width, hidden_width)
        + [
            pltpu.VMEM((batch, hidden_width), jnp.bfloat16),
            pltpu.VMEM((2, batch, model_width), jnp.float32),
            pltpu.VMEM((2, batch, width), jnp.float32),
            pltpu.VMEM((batch, model_width), jnp.bfloat16),
            pltpu.VMEM((batch, model_width), jnp.bfloat16),
            pltpu.VMEM((batch, model_width), jnp.bfloat16),
            pltpu.VMEM((batch, model_width), jnp.float32),
            pltpu.VMEM((batch, hidden_width), jnp.bfloat16),
            gram_scratch(batch, count),
        ],
        compiler_params=stage_params(),
        cost_estimate=stage_cost(6, batch, model_width, hidden_width),
        name="turn_stage",
    )(place, acts, top, g_hidden, weights[0], *map(in_hbm, weights[1:]))


def backward_stage(place, grad, saved, weights, count):
    batch, model_width = grad.shape
    hidden_width = weights[1].shape[1]

    def kernel(place_ref, grad_ref, hid, inter, scale, kept, small_ref, *refs):
        matrices, refs = refs[:4], refs[4:]
        out_ref, held = refs[0], refs[1:4]
        middle, weighted, g_before = refs[4:]

        @pl.when(place_ref[1] == 1)
        def _():
            layers = streams_of(place_ref[0], matrices, held, [(False, False), (False, False)])
            for up, down in reversed(layers):
                down.start()
                up.start()
            for layer, given, to in ((1, grad_ref, middle), (0, middle, out_ref)):
                up, down = layers[layer]
                down_back(given, down.held, hid.at[layer], g_before, down.wait)
                up_back(g_before, up.held, weighted, up.wait)
                mix_backward(
                    small_ref, layer, given, kept.at[layer], inter.at[layer], scale.at[layer],
                    weighted, to, count,
                )

    return pl.pallas_call(
        kernel,
        out_shape=jax.ShapeDtypeStruct(grad.shape, jnp.bfloat16),
        in_specs=[whole(pltpu.SMEM)] + [whole()] * 5 + weight_specs(),
        out_specs=whole(),
        scratch_shapes=weight_scratch(model_width, hidden_width)
        + [
            pltpu.VMEM((batch, model_width), jnp.bfloat16),
            pltpu.VMEM((batch, model_width), jnp.float32),
            pltpu.VMEM((batch, hidden_width), jnp.bfloat16),
        ],
        compiler_params=stage_params(),
        cost_estimate=stage_cost(4, batch, model_width, hidden_width),
        name="backward_stage",
    )(place, grad, *saved, weights[0], *map(in_hbm, weights[1:]))


def swapped(value, section_count):
    return lax.ppermute(value, "section", [(s, s ^ 1) for s in range(section_count)])


def moved(value, from_stage, to_stage):
    pairs = [(2 * from_stage + core, 2 * to_stage + core) for core in (0, 1)]
    return lax.ppermute(value, "section", pairs)


def mirror(value):
    along = lax.axis_size("table")
    return lax.ppermute(value, "table", [(t, (t + along // 2) % along) for t in range(along)])


def swap_in_half(value):
    along = lax.axis_size("table")
    half = along // 2
    groups = [
        [s * along + h * half + t for s in range(lax.axis_size("section")) for t in range(half)]
        for h in (0, 1)
    ]
    return lax.all_to_all(
        value, TABLE_AXES, split_axis=0, concat_axis=0, axis_index_groups=groups, tiled=True
    )


def near_first(per_asker, my_half):
    sections = lax.axis_size("section")
    half = lax.axis_size("table") // 2
    split = per_asker.reshape((sections, 2, half) + per_asker.shape[1:])
    near = lax.dynamic_index_in_dim(split, my_half, 1, keepdims=False)
    far = lax.dynamic_index_in_dim(split, 1 - my_half, 1, keepdims=False)
    return jnp.stack([near, far], axis=2).reshape((sections * half, 2) + per_asker.shape[1:])


def after(value, earlier):
    return lax.optimization_barrier((value, earlier))[0]


def per_device(
    emb_table,
    lcb_weight,
    fm_proj,
    norm_gain,
    w_up,
    w_down,
    top_grad,
    lookup_slot,
    wanted_rows,
    row_counts,
):
    section_count = lax.axis_size("section")
    along = lax.axis_size("table")
    half = along // 2
    near_owners = section_count * half
    stages = section_count // 2
    stage = lax.axis_index("section") // 2
    core = lax.axis_index("section") % 2
    my_half = lax.axis_index("table") // half
    cap = wanted_rows.shape[2]
    rows, embed_width = emb_table.shape
    embed_count = lcb_weight.shape[0]
    look_dev = lookup_slot.shape[1]
    model_width = top_grad.shape[3]

    own_slots = lookup_slot[0]
    mirror_slots = mirror(own_slots)
    small = jnp.concatenate([fm_proj[0], norm_gain[0].reshape(embed_count, -1)], axis=0)
    other_up = swapped(w_up[0], section_count)
    other_down = swapped(w_down[0], section_count)
    other_small = swapped(small, section_count)

    picked = near_first(wanted_rows[0], my_half)
    outgoing = pick_rows(emb_table, picked.reshape(-1))
    sent = after(outgoing, mirror_slots).reshape(near_owners, 2, cap, embed_width)
    fetched = swap_in_half(sent)

    def spread_of(slots):
        owner, column = slots // cap, slots % cap
        place = owner % along
        near = jnp.where(place // half == my_half, owner // along * half + place % half, near_owners)
        return spread_weights(near * cap + column, lcb_weight, near_owners, cap)

    spread_far = spread_of(mirror_slots)
    spread_near = spread_of(own_slots)
    smalls = jnp.stack(
        [jnp.where(core == 0, small, other_small), jnp.where(core == 0, other_small, small)]
    )
    weights = [smalls, w_up[0], other_up, w_down[0], other_down]
    spread_far, spread_near = lax.optimization_barrier((spread_far, spread_near))
    far_part = mirror(compress(spread_far, fetched, 1, embed_count, jnp.bfloat16))
    near_part = compress(spread_near, fetched, 0, embed_count, jnp.float32)
    lead = (near_part + far_part.astype(jnp.float32)).astype(jnp.bfloat16)
    pieces = [lead] + [moved(lead, s, 0) for s in range(1, stages)]
    top = top_grad.reshape(stages, 2, look_dev, model_width)
    top = lax.dynamic_index_in_dim(top, core, 1, keepdims=False).reshape(-1, model_width)

    def at(tick):
        is_last = (stage == stages - 1) & (tick == 0)
        return jnp.stack([core, stage == tick, is_last]).astype(jnp.int32)

    saved = None
    for tick in range(stages - 1):
        out, fresh, product = forward_stage(at(tick), pieces, top, weights, embed_count)
        if saved is None:
            saved, g_hidden = fresh, product
        else:
            saved = [jnp.where(stage == tick, new, old) for new, old in zip(fresh, saved)]
        pieces = [moved(out, tick, tick + 1)]
    grad = turn_stage(at(stages - 1), pieces[0], top, g_hidden, weights, embed_count)
    for tick in reversed(range(stages - 1)):
        grad = moved(grad, tick + 1, tick)
        grad = backward_stage(at(tick), grad, saved, weights, embed_count)

    own_grad = grad[:look_dev]
    for s in range(1, stages):
        piece = grad[s * look_dev : (s + 1) * look_dev]
        own_grad = jnp.where(stage == s, moved(piece, 0, s), own_grad)
    mirror_grad = mirror(own_grad)

    near_grad = expand(spread_near, own_grad, embed_count)
    slot_grad = expand(spread_far, mirror_grad, embed_count, near_grad)
    returned = swap_in_half(slot_grad)
    live_slots = jnp.arange(cap) < near_first(row_counts[0], my_half)[..., None]
    targets = jnp.where(live_slots, picked, rows).reshape(-1)
    return add_rows(targets, returned.reshape(-1, embed_width), outgoing, rows, cap)


def solution(mesh):
    in_specs = (
        P(("section", "table"), None),
        P(),
        P("section", None, None),
        P("section", None),
        P("section", None, None),
        P("section", None, None),
        P("table", None, None, None),
        P("table", "section", None),
        P(("section", "table"), None, None),
        P(("section", "table"), None),
    )
    out_specs = P(("section", "table"), None)
    return jax.shard_map(
        per_device, mesh=mesh, in_specs=in_specs, out_specs=out_specs, check_vma=False
    )
```

```python
import jax
import jax.numpy as jnp
from jax import lax
from jax.experimental import pallas as pl
from jax.experimental.pallas import tpu as pltpu
from jax.sharding import PartitionSpec as P

EPSILON = 1e-05
DECAY_WEIGHT = 0.5
VMEM_LIMIT = 28 * 1024 * 1024
UNROLL = 32


def whole(memory_space=pltpu.VMEM):
    return pl.BlockSpec(memory_space=memory_space)


def in_hbm(value):
    return pltpu.with_memory_space_constraint(value, pltpu.HBM)


def params():
    return pltpu.CompilerParams(vmem_limit_bytes=VMEM_LIMIT)


def tiles_of(count, most):
    return max(step for step in range(1, most + 1) if count % step == 0)


def pick_rows(emb_table, wanted, my_half):
    rows, width = emb_table.shape
    askers, cap = wanted.shape
    half = lax.axis_size("table") // 2
    together = tiles_of(askers, 8)
    pieces = 4

    def kernel(half_ref, wanted_ref, table_ref, out_ref, narrow, wide, lines, sems):
        copies = []
        for piece in range(pieces):
            cut = pl.ds(piece * (rows // pieces), rows // pieces)
            copies.append(pltpu.make_async_copy(table_ref.at[cut], narrow.at[cut], sems.at[piece]))
            copies[-1].start()
        for piece in range(pieces):
            cut = pl.ds(piece * (rows // pieces), rows // pieces)
            copies[piece].wait()
            wide[cut, :] = narrow[cut, :].astype(jnp.float32)

        def fill(part, carry):
            def one(line, inner):
                at = part * together + line
                device, is_mirror = at // 2, at % 2
                side = jnp.where(is_mirror == 0, half_ref[0], 1 - half_ref[0])
                asker = (device // half * 2 + side) * half + device % half
                first = pl.multiple_of(line * cap, cap)
                for lane in range(cap):
                    row = wanted_ref[asker * cap + lane]
                    lines[pl.ds(first + lane, 1), :] = wide[pl.ds(row, 1), :]
                return inner

            lax.fori_loop(0, together, one, 0)
            base = pl.multiple_of(part * (together * cap), together * cap)
            out_ref[pl.ds(base, together * cap), :] = lines[...].astype(out_ref.dtype)
            return carry

        lax.fori_loop(0, askers // together, fill, 0)

    return pl.pallas_call(
        kernel,
        out_shape=jax.ShapeDtypeStruct((askers * cap, width), emb_table.dtype),
        in_specs=[whole(pltpu.SMEM), whole(pltpu.SMEM), whole(pltpu.HBM)],
        out_specs=whole(),
        scratch_shapes=[
            pltpu.VMEM((rows, width), emb_table.dtype),
            pltpu.VMEM((rows, width), jnp.float32),
            pltpu.VMEM((together * cap, width), jnp.float32),
            pltpu.SemaphoreType.DMA((pieces,)),
        ],
        compiler_params=params(),
        name="pick_rows",
    )(my_half.astype(jnp.int32).reshape(1), wanted.reshape(-1), in_hbm(emb_table))


def spread_weights(codes, lcb_weight, owners, cap):
    samples, feature_count = codes.shape
    embed_count = lcb_weight.shape[0]
    group = tiles_of(samples, 16)

    def kernel(codes_ref, lcb_ref, out_ref, kept_ref):
        lcb = lcb_ref[...].astype(jnp.float32)
        owner_of = lax.broadcasted_iota(jnp.int32, (owners, embed_count, feature_count), 0)
        column_of = lax.broadcasted_iota(jnp.int32, (cap, feature_count), 0)
        for pair in range(0, group, 2):
            made = []
            for sample in (pair, pair + 1):
                slots = codes_ref[sample : sample + 1, :]
                owner = lax.div(slots, cap)
                column = slots - owner * cap
                left = jnp.where(owner_of == owner[None], lcb[None], 0.0)
                left = left.reshape(owners * embed_count, feature_count).astype(jnp.bfloat16)
                right = jnp.where(column_of == column, 1.0, 0.0).astype(jnp.bfloat16)
                both = lax.dot_general(
                    left, right, (((1,), (1,)), ((), ())), preferred_element_type=jnp.float32
                )
                made.append(both.reshape(owners, embed_count, cap))
            rows = pl.ds(pair * embed_count, 2 * embed_count)
            joined = jnp.concatenate(made, axis=1).astype(out_ref.dtype)
            out_ref[:, rows, :] = joined
            kept_ref[:, rows, :] = joined

    return pl.pallas_call(
        kernel,
        out_shape=[
            pltpu.VMEM((owners, samples * embed_count, cap), jnp.bfloat16),
            pltpu.HBM((owners, samples * embed_count, cap), jnp.bfloat16),
        ],
        grid=(samples // group,),
        in_specs=[
            pl.BlockSpec((group, feature_count), lambda i: (i, 0)),
            pl.BlockSpec((embed_count, feature_count), lambda i: (0, 0)),
        ],
        out_specs=[pl.BlockSpec((owners, group * embed_count, cap), lambda i: (0, i, 0))] * 2,
        compiler_params=params(),
        cost_estimate=pl.CostEstimate(
            flops=2 * samples * owners * embed_count * feature_count * cap,
            bytes_accessed=2 * owners * samples * embed_count * cap,
            transcendentals=0,
        ),
        name="spread_weights",
    )(codes, lcb_weight)


def compress(spread, fetched, view, embed_count, kind):
    owners, lines, cap = spread.shape
    width = fetched.shape[3]
    samples = lines // embed_count
    part = tiles_of(owners, 8)
    steps = owners // part

    def kernel(spread_ref, rows_ref, out_ref, total):
        total[...] = jnp.zeros_like(total)

        def body(step, carry):
            first = step * part
            left = jnp.concatenate([spread_ref[first + o] for o in range(part)], axis=1)
            right = jnp.concatenate([rows_ref[first + o, view] for o in range(part)], axis=0)
            total[...] += jnp.dot(left, right, preferred_element_type=jnp.float32)
            return carry

        lax.fori_loop(0, steps, body, 0)
        for k in range(embed_count):
            columns = slice(k * width, (k + 1) * width)
            piece = total[pl.ds(k, samples, stride=embed_count), :]
            out_ref[:, columns] = piece.astype(out_ref.dtype)

    return pl.pallas_call(
        kernel,
        out_shape=jax.ShapeDtypeStruct((samples, embed_count * width), kind),
        in_specs=[whole(), whole()],
        out_specs=whole(),
        scratch_shapes=[pltpu.VMEM((lines, width), jnp.float32)],
        compiler_params=params(),
        name="compress",
    )(spread, fetched)


def expand(spread, lead_grad, embed_count, near=None):
    owners, lines, cap = spread.shape
    samples = lines // embed_count
    width = lead_grad.shape[1] // embed_count
    part = tiles_of(owners, 8)
    extra = [] if near is None else [near]

    def kernel(spread_ref, grad_ref, *refs):
        near_refs, (out_ref, tall, turned) = refs[: len(extra)], refs[len(extra) :]
        for k in range(embed_count):
            piece = grad_ref[:, k * width : (k + 1) * width].astype(jnp.float32)
            tall[pl.ds(k, samples, stride=embed_count), :] = piece
        turned[...] = tall[...].T.astype(jnp.bfloat16)

        def body(step, carry):
            first = step * part
            right = jnp.concatenate([spread_ref[first + o] for o in range(part)], axis=1)
            term = jnp.dot(turned[...], right, preferred_element_type=jnp.float32)
            piece = term.T.astype(out_ref.dtype).reshape(part, cap, width)
            if near_refs:
                for o in range(part):
                    out_ref[first + o, 0] = near_refs[0][first + o]
                    out_ref[first + o, 1] = piece[o]
            else:
                out_ref[tile_at(step, part)] = piece
            return carry

        lax.fori_loop(0, owners // part, body, 0)

    views = () if near is None else (2,)
    return pl.pallas_call(
        kernel,
        out_shape=jax.ShapeDtypeStruct((owners,) + views + (cap, width), jnp.bfloat16),
        in_specs=[whole()] * (2 + len(extra)),
        out_specs=whole(),
        scratch_shapes=[
            pltpu.VMEM((lines, width), jnp.float32),
            pltpu.VMEM((width, lines), jnp.bfloat16),
        ],
        compiler_params=params(),
        name="expand",
    )(spread, lead_grad, *extra)


def add_rows(targets, returned, outgoing, rows, cap):
    count, width = returned.shape
    pair = 2 * cap

    def kernel(targets_ref, back_ref, sent_ref, out_ref, total, second, terms, sem):
        total[...] = jnp.zeros_like(total)
        second[...] = jnp.zeros_like(second)

        def body(step, carry):
            base = pl.multiple_of(step * pair, pair)
            lines = pl.ds(base, pair)
            terms[...] = back_ref[lines, :].astype(jnp.float32) + DECAY_WEIGHT * sent_ref[
                lines, :
            ].astype(jnp.float32)
            for first in range(0, cap, UNROLL):
                lanes = range(first, first + UNROLL)
                places = [targets_ref[base + lane] for lane in lanes]
                others = [targets_ref[base + cap + lane] for lane in lanes]
                sums = [
                    total[pl.ds(place, 1), :] + terms[lane : lane + 1, :]
                    for place, lane in zip(places, lanes)
                ]
                other_sums = [
                    second[pl.ds(place, 1), :] + terms[cap + lane : cap + lane + 1, :]
                    for place, lane in zip(others, lanes)
                ]
                for place, value in zip(places, sums):
                    total[pl.ds(place, 1), :] = value
                for place, value in zip(others, other_sums):
                    second[pl.ds(place, 1), :] = value
            return carry

        lax.fori_loop(0, count // pair, body, 0)
        part = rows // 4
        copies = []
        for piece in range(4):
            cut = pl.ds(piece * part, part)
            total[cut, :] = total[cut, :] + second[cut, :]
            copies.append(pltpu.make_async_copy(total.at[cut, :], out_ref.at[cut, :], sem.at[piece]))
            copies[-1].start()
        for copy in copies:
            copy.wait()

    return pl.pallas_call(
        kernel,
        out_shape=jax.ShapeDtypeStruct((rows, width), jnp.float32),
        in_specs=[whole(pltpu.SMEM), whole(), whole()],
        out_specs=whole(pl.ANY),
        scratch_shapes=[
            pltpu.VMEM((rows + 8, width), jnp.float32),
            pltpu.VMEM((rows + 8, width), jnp.float32),
            pltpu.VMEM((pair, width), jnp.float32),
            pltpu.SemaphoreType.DMA((4,)),
        ],
        compiler_params=params(),
        name="add_rows",
    )(targets, returned, outgoing)


GROUP = 16
TABLE_AXES = ("section", "table")
STAGE_LIMIT = 44 * 1024 * 1024
NT = (((1,), (1,)), ((), ()))


def dot_nt(left, right):
    return lax.dot_general(left, right, NT, preferred_element_type=jnp.float32)


def dot(left, right):
    return jnp.dot(left, right, preferred_element_type=jnp.float32)


def halves(value):
    high = value.astype(jnp.bfloat16)
    low = (value - high.astype(jnp.float32)).astype(jnp.bfloat16)
    return jnp.concatenate([high, low], axis=1)


def same_sample(count):
    first = lax.broadcasted_iota(jnp.int32, (count * GROUP, count * GROUP), 0)
    second = lax.broadcasted_iota(jnp.int32, (count * GROUP, count * GROUP), 1)
    return (first & (GROUP - 1)) == (second & (GROUP - 1))


def stacked(ref, rows, count, width):
    return jnp.concatenate([ref[rows, k * width : (k + 1) * width] for k in range(count)], axis=0)


def repeated(proj):
    count, width = proj.shape
    lines = [jnp.broadcast_to(proj[k : k + 1, :], (GROUP, width)) for k in range(count)]
    return jnp.concatenate(lines, axis=0).astype(jnp.bfloat16)


def mix_forward(small, layer, acts, inter, scale, normed, grams, count):
    batch, model_width = acts.shape
    width = model_width // count
    both = small[layer].astype(jnp.float32)
    proj = repeated(both[:count])
    keep = same_sample(count)
    size = GROUP * count
    for group in range(batch // GROUP):
        block = stacked(acts, pl.ds(group * GROUP, GROUP), count, width)
        gram = jnp.where(keep, dot_nt(block, block), 0.0)
        grams[group * size : (group + 1) * size, :] = halves(gram)
    mixed = dot(grams[...], jnp.concatenate([proj, proj], axis=0))
    for group in range(batch // GROUP):
        rows = pl.ds(group * GROUP, GROUP)
        start = group * size
        parts = [mixed[start + k * GROUP : start + (k + 1) * GROUP] for k in range(count)]
        squares = sum(part * part for part in parts)
        mean = jnp.sum(squares, axis=1, keepdims=True) * (1.0 / model_width)
        inv = lax.rsqrt(mean + EPSILON)
        scale[rows, :] = jnp.broadcast_to(inv, (GROUP, width))
        for k in range(count):
            columns = slice(k * width, (k + 1) * width)
            inter[rows, columns] = parts[k]
            gain = both[count + k : count + k + 1]
            normed[rows, columns] = (parts[k] * inv * gain).astype(jnp.bfloat16)


def gram_scratch(batch, count):
    return pltpu.VMEM((batch * count, 2 * GROUP * count), jnp.bfloat16)


def hidden_tile(hidden_width):
    return min(hidden_width, 1024)


def model_tile(model_width):
    return min(model_width, 512)


def tile_at(step, size):
    return pl.ds(pl.multiple_of(step * size, size), size)


class Stream:
    def __init__(self, mine, own, other, held, sems, axis, size):
        self.mine, self.own, self.other, self.held, self.sems = mine, own, other, held, sems
        self.axis, self.size = axis, size
        self.tiles = own.shape[axis] // size

    def copy(self, source, step):
        cut = tile_at(step, self.size)
        index = (slice(None), cut) if self.axis == 1 else (cut, slice(None))
        return pltpu.make_async_copy(source.at[index], self.held.at[index], self.sems.at[step])

    def start(self):
        @pl.when(self.mine)
        def _():
            for step in range(self.tiles):
                self.copy(self.own, step).start()

        @pl.when(jnp.logical_not(self.mine))
        def _():
            for step in range(self.tiles):
                self.copy(self.other, step).start()

    def wait(self, step):
        self.copy(self.own, step).wait()


def no_wait(step):
    return None


def over_tiles(total, tile, many, wait, work):
    many = min(many, total // tile)

    def body(step, carry):
        for inner in range(many):
            wait(step * many + inner)
        work(tile_at(step, many * tile))
        return carry

    lax.fori_loop(0, total // (many * tile), body, 0)


def up_product(normed, w_up, hidden, turned, wait, many=1):
    def work(columns):
        opened = jnp.maximum(dot(normed[...], w_up[:, columns]), 0.0).astype(jnp.bfloat16)
        hidden[:, columns] = opened
        turned[columns, :] = opened.T

    width = hidden.shape[1]
    over_tiles(width, hidden_tile(width), many, wait, work)


def down_product(hidden, w_down, acts, out, wait, many=1):
    def work(columns):
        term = dot(hidden[...], w_down[:, columns])
        out[:, columns] = (acts[:, columns].astype(jnp.float32) + term).astype(jnp.bfloat16)

    width = out.shape[1]
    over_tiles(width, model_tile(width), many, wait, work)


def turn(rows, turned):
    turned[...] = rows[...].T


def opened_only(hidden, grad):
    return jnp.where(hidden.astype(jnp.float32) > 0.0, grad, 0.0).astype(jnp.bfloat16)


def down_back(grad, w_down, hidden, out, wait, many=1):
    def work(lines):
        g_hidden = dot(w_down[lines, :], grad[...])
        if hidden is not None:
            out[lines, :] = opened_only(hidden[lines, :], g_hidden)
        else:
            out[lines, :] = g_hidden.astype(jnp.bfloat16)

    width = out.shape[0]
    over_tiles(width, hidden_tile(width), many, wait, work)


def up_back(g_before, w_up, weighted, wait, many=1):
    def work(columns):
        weighted[:, columns] = dot(w_up[columns, :], g_before[...]).T

    width = weighted.shape[1]
    over_tiles(width, model_tile(width), many, wait, work)


def mix_backward(small, layer, grad, acts, inter, scale, weighted, out, count):
    batch, model_width = acts.shape
    width = model_width // count
    both = small[layer].astype(jnp.float32)
    proj = repeated(both[:count])
    keep = same_sample(count)
    for start in range(0, batch, GROUP):
        rows = pl.ds(start, GROUP)
        columns = [slice(k * width, (k + 1) * width) for k in range(count)]
        gained = [weighted[rows, columns[k]] * both[count + k : count + k + 1] for k in range(count)]
        shared = sum(gained[k] * inter[rows, columns[k]] for k in range(count))
        mean = jnp.sum(shared, axis=1, keepdims=True) * (1.0 / model_width)
        inv = scale[rows, 0:1]
        pull = inv * inv * mean
        parts = [
            (inv * (gained[k] - inter[rows, columns[k]] * pull)).astype(jnp.bfloat16)
            for k in range(count)
        ]
        block = stacked(acts, rows, count, width)
        g_inter = jnp.concatenate(parts, axis=0)
        left = jnp.concatenate([g_inter, proj], axis=1)
        right = jnp.concatenate([proj, g_inter], axis=1)
        links = jnp.where(keep, dot_nt(left, right), 0.0)
        g_acts = dot(halves(links), jnp.concatenate([block, block], axis=0))
        for k in range(count):
            piece = g_acts[k * GROUP : (k + 1) * GROUP] + grad[rows, columns[k]].astype(jnp.float32)
            out[rows, columns[k]] = piece.astype(jnp.bfloat16)


def saved_shapes(batch, model_width, hidden_width, width):
    return [
        jax.ShapeDtypeStruct((2, hidden_width, batch), jnp.bfloat16),
        jax.ShapeDtypeStruct((2, batch, model_width), jnp.float32),
        jax.ShapeDtypeStruct((2, batch, width), jnp.float32),
        jax.ShapeDtypeStruct((2, batch, model_width), jnp.bfloat16),
    ]


def weight_specs():
    return [whole()] + [whole(pltpu.HBM)] * 4


def weight_scratch(model_width, hidden_width):
    tiles = max(hidden_width // hidden_tile(hidden_width), model_width // model_tile(model_width))
    return [
        pltpu.VMEM((2, model_width, hidden_width), jnp.bfloat16),
        pltpu.VMEM((2, hidden_width, model_width), jnp.bfloat16),
        pltpu.SemaphoreType.DMA((4, tiles)),
    ]


def streams_of(core, weights, held, forward):
    own_up, other_up, own_down, other_down = weights
    held_up, held_down, sems = held
    model_width, hidden_width = own_up.shape
    wide, narrow = hidden_tile(hidden_width), model_tile(model_width)
    made = []
    for layer in (0, 1):
        mine = core == layer
        up_forward, down_forward = forward[layer]
        up_cut = (1, wide) if up_forward else (0, narrow)
        down_cut = (1, narrow) if down_forward else (0, wide)
        made.append(
            (
                Stream(mine, own_up, other_up, held_up.at[layer], sems.at[2 * layer], *up_cut),
                Stream(mine, own_down, other_down, held_down.at[layer], sems.at[2 * layer + 1], *down_cut),
            )
        )
    return made


def stage_cost(products, batch, model_width, hidden_width):
    return pl.CostEstimate(
        flops=2 * products * batch * model_width * hidden_width, bytes_accessed=1 << 20, transcendentals=0
    )


def stage_params():
    return pltpu.CompilerParams(vmem_limit_bytes=STAGE_LIMIT)


def forward_stage(place, pieces, top, weights, count):
    batch, model_width = top.shape
    hidden_width = weights[1].shape[1]
    width = model_width // count

    def kernel(place_ref, *refs):
        piece_refs, (top_ref, small_ref), refs = refs[: len(pieces)], refs[len(pieces) :][:2], refs[len(pieces) + 2 :]
        matrices, refs = refs[:4], refs[4:]
        out_ref, hid, inter, scale, kept, g_hidden = refs[:6]
        held, (normed, hidden, top_turned, grams) = refs[6:9], refs[9:]
        core = place_ref[0]

        @pl.when(place_ref[1] == 1)
        def _():
            layers = streams_of(core, matrices, held, [(True, True), (True, True)])
            for up, down in layers:
                up.start()
                down.start()
            start = 0
            for piece in piece_refs:
                kept[0, start : start + piece.shape[0], :] = piece[...]
                start += piece.shape[0]
            for layer, (up, down) in enumerate(layers):
                mix_forward(
                    small_ref, layer, kept.at[layer], inter.at[layer], scale.at[layer], normed, grams, count
                )
                up_product(normed, up.held, hidden, hid.at[layer], up.wait)
                to = kept.at[1] if layer == 0 else out_ref
                down_product(hidden, down.held, kept.at[layer], to, down.wait)

        @pl.when(place_ref[2] == 1)
        def _():
            layers = streams_of(core, matrices, held, [(True, True), (True, False)])
            down = layers[1][1]
            down.start()
            turn(top_ref, top_turned)
            down_back(top_turned, down.held, None, g_hidden, down.wait)

    out = pl.pallas_call(
        kernel,
        out_shape=[jax.ShapeDtypeStruct(top.shape, jnp.bfloat16)]
        + saved_shapes(batch, model_width, hidden_width, width)
        + [jax.ShapeDtypeStruct((hidden_width, batch), jnp.bfloat16)],
        in_specs=[whole(pltpu.SMEM)] + [whole()] * (len(pieces) + 1) + weight_specs(),
        out_specs=[whole()] * 6,
        scratch_shapes=weight_scratch(model_width, hidden_width)
        + [
            pltpu.VMEM((batch, model_width), jnp.bfloat16),
            pltpu.VMEM((batch, hidden_width), jnp.bfloat16),
            pltpu.VMEM((model_width, batch), jnp.bfloat16),
            gram_scratch(batch, count),
        ],
        compiler_params=stage_params(),
        cost_estimate=stage_cost(4, batch, model_width, hidden_width),
        name="forward_stage",
    )(place, *pieces, top, weights[0], *map(in_hbm, weights[1:]))
    return out[0], out[1:5], out[5]


def turn_stage(place, acts, top, g_hidden, weights, count):
    batch, model_width = acts.shape
    hidden_width = weights[1].shape[1]
    width = model_width // count

    def kernel(place_ref, acts_ref, top_ref, ghid_ref, small_ref, *refs):
        matrices, refs = refs[:4], refs[4:]
        out_ref, held = refs[0], refs[1:4]
        hid, hidden, inter, scale, upper, grad, turned, normed, weighted, g_before, grams = refs[4:]

        @pl.when(place_ref[1] == 1)
        def _():
            layers = streams_of(place_ref[0], matrices, held, [(True, True), (True, True)])
            (up0, down0), (up1, down1) = layers
            for stream in (up0, down0, up1):
                stream.start()
            mix_forward(small_ref, 0, acts_ref, inter.at[0], scale.at[0], normed, grams, count)
            up_product(normed, up0.held, hidden, hid, up0.wait)
            down_product(hidden, down0.held, acts_ref, upper, down0.wait)
            mix_forward(small_ref, 1, upper, inter.at[1], scale.at[1], normed, grams, count)

            def masked(columns):
                before = dot(normed[...], up1.held[:, columns])
                opened = jnp.maximum(before, 0.0).astype(jnp.bfloat16).T
                g_before[columns, :] = opened_only(opened, ghid_ref[columns, :].astype(jnp.float32))

            over_tiles(hidden_width, hidden_tile(hidden_width), 1, up1.wait, masked)
            up_back(g_before, up1.held, weighted, no_wait)
            mix_backward(small_ref, 1, top_ref, upper, inter.at[1], scale.at[1], weighted, grad, count)
            turn(grad, turned)
            down_back(turned, down0.held, hid, g_before, no_wait)
            up_back(g_before, up0.held, weighted, no_wait)
            mix_backward(small_ref, 0, grad, acts_ref, inter.at[0], scale.at[0], weighted, out_ref, count)

    return pl.pallas_call(
        kernel,
        out_shape=jax.ShapeDtypeStruct(acts.shape, jnp.bfloat16),
        in_specs=[whole(pltpu.SMEM)] + [whole()] * 3 + weight_specs(),
        out_specs=whole(),
        scratch_shapes=weight_scratch(model_width, hidden_width)
        + [
            pltpu.VMEM((hidden_width, batch), jnp.bfloat16),
            pltpu.VMEM((batch, hidden_width), jnp.bfloat16),
            pltpu.VMEM((2, batch, model_width), jnp.float32),
            pltpu.VMEM((2, batch, width), jnp.float32),
            pltpu.VMEM((batch, model_width), jnp.bfloat16),
            pltpu.VMEM((batch, model_width), jnp.bfloat16),
            pltpu.VMEM((model_width, batch), jnp.bfloat16),
            pltpu.VMEM((batch, model_width), jnp.bfloat16),
            pltpu.VMEM((batch, model_width), jnp.float32),
            pltpu.VMEM((hidden_width, batch), jnp.bfloat16),
            gram_scratch(batch, count),
        ],
        compiler_params=stage_params(),
        cost_estimate=stage_cost(6, batch, model_width, hidden_width),
        name="turn_stage",
    )(place, acts, top, g_hidden, weights[0], *map(in_hbm, weights[1:]))


def backward_stage(place, grad, saved, weights, count):
    batch, model_width = grad.shape
    hidden_width = weights[1].shape[1]

    def kernel(place_ref, grad_ref, hid, inter, scale, kept, small_ref, *refs):
        matrices, refs = refs[:4], refs[4:]
        out_ref, held = refs[0], refs[1:4]
        middle, turned, weighted, g_before = refs[4:]

        @pl.when(place_ref[1] == 1)
        def _():
            layers = streams_of(place_ref[0], matrices, held, [(False, False), (False, False)])
            for up, down in reversed(layers):
                down.start()
                up.start()
            for layer, given, to in ((1, grad_ref, middle), (0, middle, out_ref)):
                up, down = layers[layer]
                turn(given, turned)
                down_back(turned, down.held, hid.at[layer], g_before, down.wait)
                up_back(g_before, up.held, weighted, up.wait)
                mix_backward(
                    small_ref, layer, given, kept.at[layer], inter.at[layer], scale.at[layer],
                    weighted, to, count,
                )

    return pl.pallas_call(
        kernel,
        out_shape=jax.ShapeDtypeStruct(grad.shape, jnp.bfloat16),
        in_specs=[whole(pltpu.SMEM)] + [whole()] * 5 + weight_specs(),
        out_specs=whole(),
        scratch_shapes=weight_scratch(model_width, hidden_width)
        + [
            pltpu.VMEM((batch, model_width), jnp.bfloat16),
            pltpu.VMEM((model_width, batch), jnp.bfloat16),
            pltpu.VMEM((batch, model_width), jnp.float32),
            pltpu.VMEM((hidden_width, batch), jnp.bfloat16),
        ],
        compiler_params=stage_params(),
        cost_estimate=stage_cost(4, batch, model_width, hidden_width),
        name="backward_stage",
    )(place, grad, *saved, weights[0], *map(in_hbm, weights[1:]))


def swapped(value, section_count):
    return lax.ppermute(value, "section", [(s, s ^ 1) for s in range(section_count)])


def moved(value, from_stage, to_stage):
    pairs = [(2 * from_stage + core, 2 * to_stage + core) for core in (0, 1)]
    return lax.ppermute(value, "section", pairs)


def mirror(value):
    along = lax.axis_size("table")
    return lax.ppermute(value, "table", [(t, (t + along // 2) % along) for t in range(along)])


def swap_in_half(value):
    along = lax.axis_size("table")
    half = along // 2
    groups = [
        [s * along + h * half + t for s in range(lax.axis_size("section")) for t in range(half)]
        for h in (0, 1)
    ]
    return lax.all_to_all(
        value, TABLE_AXES, split_axis=0, concat_axis=0, axis_index_groups=groups, tiled=True
    )


def near_first(per_asker, my_half):
    sections = lax.axis_size("section")
    half = lax.axis_size("table") // 2
    split = per_asker.reshape((sections, 2, half) + per_asker.shape[1:])
    near = lax.dynamic_index_in_dim(split, my_half, 1, keepdims=False)
    far = lax.dynamic_index_in_dim(split, 1 - my_half, 1, keepdims=False)
    return jnp.stack([near, far], axis=2).reshape((sections * half, 2) + per_asker.shape[1:])


def after(value, earlier):
    return lax.optimization_barrier((value, earlier))[0]


def per_device(
    emb_table,
    lcb_weight,
    fm_proj,
    norm_gain,
    w_up,
    w_down,
    top_grad,
    lookup_slot,
    wanted_rows,
    row_counts,
):
    section_count = lax.axis_size("section")
    along = lax.axis_size("table")
    half = along // 2
    near_owners = section_count * half
    stages = section_count // 2
    stage = lax.axis_index("section") // 2
    core = lax.axis_index("section") % 2
    my_half = lax.axis_index("table") // half
    cap = wanted_rows.shape[2]
    rows, embed_width = emb_table.shape
    embed_count = lcb_weight.shape[0]
    look_dev = lookup_slot.shape[1]
    model_width = top_grad.shape[3]

    own_slots = lookup_slot[0]
    mirror_slots = mirror(own_slots)
    small = jnp.concatenate([fm_proj[0], norm_gain[0].reshape(embed_count, -1)], axis=0)
    other_up = swapped(w_up[0], section_count)
    other_down = swapped(w_down[0], section_count)
    other_small = swapped(small, section_count)

    picked = near_first(wanted_rows[0], my_half)
    outgoing = pick_rows(emb_table, wanted_rows[0], my_half)
    sent = after(outgoing, mirror_slots).reshape(near_owners, 2, cap, embed_width)
    fetched = swap_in_half(sent)

    def spread_of(slots):
        owner, column = slots // cap, slots % cap
        place = owner % along
        near = jnp.where(place // half == my_half, owner // along * half + place % half, near_owners)
        return spread_weights(near * cap + column, lcb_weight, near_owners, cap)

    spread_far, kept_far = spread_of(mirror_slots)
    spread_near, kept_near = spread_of(own_slots)
    smalls = jnp.stack(
        [jnp.where(core == 0, small, other_small), jnp.where(core == 0, other_small, small)]
    )
    weights = [smalls, w_up[0], other_up, w_down[0], other_down]
    spread_far, spread_near = lax.optimization_barrier((spread_far, spread_near))
    far_part = mirror(compress(spread_far, fetched, 1, embed_count, jnp.bfloat16))
    near_part = compress(spread_near, fetched, 0, embed_count, jnp.float32)
    lead = (near_part + far_part.astype(jnp.float32)).astype(jnp.bfloat16)
    pieces = [lead] + [moved(lead, s, 0) for s in range(1, stages)]
    top = top_grad.reshape(stages, 2, look_dev, model_width)
    top = lax.dynamic_index_in_dim(top, core, 1, keepdims=False).reshape(-1, model_width)

    def at(tick):
        is_last = (stage == stages - 1) & (tick == 0)
        return jnp.stack([core, stage == tick, is_last]).astype(jnp.int32)

    saved = None
    for tick in range(stages - 1):
        out, fresh, product = forward_stage(at(tick), pieces, top, weights, embed_count)
        if saved is None:
            saved, g_hidden = fresh, product
        else:
            saved = [jnp.where(stage == tick, new, old) for new, old in zip(fresh, saved)]
        pieces = [moved(out, tick, tick + 1)]
    grad = turn_stage(at(stages - 1), pieces[0], top, g_hidden, weights, embed_count)
    for tick in reversed(range(stages - 1)):
        grad = moved(grad, tick + 1, tick)
        grad = backward_stage(at(tick), grad, saved, weights, embed_count)

    own_grad = grad[:look_dev]
    for s in range(1, stages):
        piece = grad[s * look_dev : (s + 1) * look_dev]
        own_grad = jnp.where(stage == s, moved(piece, 0, s), own_grad)
    mirror_grad = mirror(own_grad)

    near_grad = expand(kept_near, own_grad, embed_count)
    slot_grad = expand(kept_far, mirror_grad, embed_count, near_grad)
    returned = swap_in_half(slot_grad)
    live_slots = jnp.arange(cap) < near_first(row_counts[0], my_half)[..., None]
    targets = jnp.where(live_slots, picked, rows).reshape(-1)
    return add_rows(targets, returned.reshape(-1, embed_width), outgoing, rows, cap)


def solution(mesh):
    in_specs = (
        P(("section", "table"), None),
        P(),
        P("section", None, None),
        P("section", None),
        P("section", None, None),
        P("section", None, None),
        P("table", None, None, None),
        P("table", "section", None),
        P(("section", "table"), None, None),
        P(("section", "table"), None),
    )
    out_specs = P(("section", "table"), None)
    return jax.shard_map(
        per_device, mesh=mesh, in_specs=in_specs, out_specs=out_specs, check_vma=False
    )
```

```python
import jax
import jax.numpy as jnp
from jax import lax
from jax.experimental import pallas as pl
from jax.experimental.pallas import tpu as pltpu
from jax.sharding import PartitionSpec as P

EPSILON = 1e-05
DECAY_WEIGHT = 0.5
VMEM_LIMIT = 28 * 1024 * 1024
UNROLL = 32


def whole(memory_space=pltpu.VMEM):
    return pl.BlockSpec(memory_space=memory_space)


def in_hbm(value):
    return pltpu.with_memory_space_constraint(value, pltpu.HBM)


def params():
    return pltpu.CompilerParams(vmem_limit_bytes=VMEM_LIMIT)


def tiles_of(count, most):
    return max(step for step in range(1, most + 1) if count % step == 0)


def pick_rows(emb_table, wanted, my_half):
    rows, width = emb_table.shape
    askers, cap = wanted.shape
    half = lax.axis_size("table") // 2
    together = tiles_of(askers, 8)
    pieces = 4

    def kernel(half_ref, wanted_ref, table_ref, out_ref, narrow, wide, lines, sems):
        copies = []
        for piece in range(pieces):
            cut = pl.ds(piece * (rows // pieces), rows // pieces)
            copies.append(pltpu.make_async_copy(table_ref.at[cut], narrow.at[cut], sems.at[piece]))
            copies[-1].start()
        for piece in range(pieces):
            cut = pl.ds(piece * (rows // pieces), rows // pieces)
            copies[piece].wait()
            wide[cut, :] = narrow[cut, :].astype(jnp.float32)

        def fill(part, carry):
            def one(line, inner):
                at = part * together + line
                device, is_mirror = at // 2, at % 2
                side = jnp.where(is_mirror == 0, half_ref[0], 1 - half_ref[0])
                asker = (device // half * 2 + side) * half + device % half
                first = pl.multiple_of(line * cap, cap)
                for lane in range(cap):
                    row = wanted_ref[asker * cap + lane]
                    lines[pl.ds(first + lane, 1), :] = wide[pl.ds(row, 1), :]
                return inner

            lax.fori_loop(0, together, one, 0)
            base = pl.multiple_of(part * (together * cap), together * cap)
            out_ref[pl.ds(base, together * cap), :] = lines[...].astype(out_ref.dtype)
            return carry

        lax.fori_loop(0, askers // together, fill, 0)

    return pl.pallas_call(
        kernel,
        out_shape=jax.ShapeDtypeStruct((askers * cap, width), emb_table.dtype),
        in_specs=[whole(pltpu.SMEM), whole(pltpu.SMEM), whole(pltpu.HBM)],
        out_specs=whole(),
        scratch_shapes=[
            pltpu.VMEM((rows, width), emb_table.dtype),
            pltpu.VMEM((rows, width), jnp.float32),
            pltpu.VMEM((together * cap, width), jnp.float32),
            pltpu.SemaphoreType.DMA((pieces,)),
        ],
        compiler_params=params(),
        name="pick_rows",
    )(my_half.astype(jnp.int32).reshape(1), wanted.reshape(-1), in_hbm(emb_table))


def spread_weights(codes, lcb_weight, owners, cap):
    samples, feature_count = codes.shape
    embed_count = lcb_weight.shape[0]
    group = tiles_of(samples, 16)

    def kernel(codes_ref, lcb_ref, out_ref, kept_ref):
        lcb = lcb_ref[...].astype(jnp.float32)
        owner_of = lax.broadcasted_iota(jnp.int32, (owners, embed_count, feature_count), 0)
        column_of = lax.broadcasted_iota(jnp.int32, (cap, feature_count), 0)
        for pair in range(0, group, 2):
            made = []
            for sample in (pair, pair + 1):
                slots = codes_ref[sample : sample + 1, :]
                owner = lax.div(slots, cap)
                column = slots - owner * cap
                left = jnp.where(owner_of == owner[None], lcb[None], 0.0)
                left = left.reshape(owners * embed_count, feature_count).astype(jnp.bfloat16)
                right = jnp.where(column_of == column, 1.0, 0.0).astype(jnp.bfloat16)
                both = lax.dot_general(
                    left, right, (((1,), (1,)), ((), ())), preferred_element_type=jnp.float32
                )
                made.append(both.reshape(owners, embed_count, cap))
            rows = pl.ds(pair * embed_count, 2 * embed_count)
            joined = jnp.concatenate(made, axis=1).astype(out_ref.dtype)
            out_ref[:, rows, :] = joined
            kept_ref[:, rows, :] = joined

    return pl.pallas_call(
        kernel,
        out_shape=[
            pltpu.VMEM((owners, samples * embed_count, cap), jnp.bfloat16),
            pltpu.HBM((owners, samples * embed_count, cap), jnp.bfloat16),
        ],
        grid=(samples // group,),
        in_specs=[
            pl.BlockSpec((group, feature_count), lambda i: (i, 0)),
            pl.BlockSpec((embed_count, feature_count), lambda i: (0, 0)),
        ],
        out_specs=[pl.BlockSpec((owners, group * embed_count, cap), lambda i: (0, i, 0))] * 2,
        compiler_params=params(),
        cost_estimate=pl.CostEstimate(
            flops=2 * samples * owners * embed_count * feature_count * cap,
            bytes_accessed=2 * owners * samples * embed_count * cap,
            transcendentals=0,
        ),
        name="spread_weights",
    )(codes, lcb_weight)


def compress(spread, fetched, view, embed_count, kind):
    owners, lines, cap = spread.shape
    width = fetched.shape[3]
    samples = lines // embed_count
    part = tiles_of(owners, 8)
    steps = owners // part

    def kernel(spread_ref, rows_ref, out_ref, total):
        total[...] = jnp.zeros_like(total)

        def body(step, carry):
            first = step * part
            left = jnp.concatenate([spread_ref[first + o] for o in range(part)], axis=1)
            right = jnp.concatenate([rows_ref[first + o, view] for o in range(part)], axis=0)
            total[...] += jnp.dot(left, right, preferred_element_type=jnp.float32)
            return carry

        lax.fori_loop(0, steps, body, 0)
        for k in range(embed_count):
            columns = slice(k * width, (k + 1) * width)
            piece = total[pl.ds(k, samples, stride=embed_count), :]
            out_ref[:, columns] = piece.astype(out_ref.dtype)

    return pl.pallas_call(
        kernel,
        out_shape=jax.ShapeDtypeStruct((samples, embed_count * width), kind),
        in_specs=[whole(), whole()],
        out_specs=whole(),
        scratch_shapes=[pltpu.VMEM((lines, width), jnp.float32)],
        compiler_params=params(),
        name="compress",
    )(spread, fetched)


def expand(spread, lead_grad, embed_count, near=None):
    owners, lines, cap = spread.shape
    samples = lines // embed_count
    width = lead_grad.shape[1] // embed_count
    part = tiles_of(owners, 8)
    extra = [] if near is None else [near]

    def kernel(spread_ref, grad_ref, *refs):
        near_refs, (out_ref, tall, turned) = refs[: len(extra)], refs[len(extra) :]
        for k in range(embed_count):
            piece = grad_ref[:, k * width : (k + 1) * width].astype(jnp.float32)
            tall[pl.ds(k, samples, stride=embed_count), :] = piece
        turned[...] = tall[...].T.astype(jnp.bfloat16)

        def body(step, carry):
            first = step * part
            right = jnp.concatenate([spread_ref[first + o] for o in range(part)], axis=1)
            term = jnp.dot(turned[...], right, preferred_element_type=jnp.float32)
            piece = term.T.astype(out_ref.dtype).reshape(part, cap, width)
            if near_refs:
                for o in range(part):
                    out_ref[first + o, 0] = near_refs[0][first + o]
                    out_ref[first + o, 1] = piece[o]
            else:
                out_ref[tile_at(step, part)] = piece
            return carry

        lax.fori_loop(0, owners // part, body, 0)

    views = () if near is None else (2,)
    return pl.pallas_call(
        kernel,
        out_shape=jax.ShapeDtypeStruct((owners,) + views + (cap, width), jnp.bfloat16),
        in_specs=[whole()] * (2 + len(extra)),
        out_specs=whole(),
        scratch_shapes=[
            pltpu.VMEM((lines, width), jnp.float32),
            pltpu.VMEM((width, lines), jnp.bfloat16),
        ],
        compiler_params=params(),
        name="expand",
    )(spread, lead_grad, *extra)


def add_rows(targets, returned, outgoing, rows, cap):
    count, width = returned.shape
    pair = 2 * cap

    def kernel(targets_ref, back_ref, sent_ref, out_ref, total, second, terms, sem):
        total[...] = jnp.zeros_like(total)
        second[...] = jnp.zeros_like(second)

        def body(step, carry):
            base = pl.multiple_of(step * pair, pair)
            lines = pl.ds(base, pair)
            terms[...] = back_ref[lines, :].astype(jnp.float32) + DECAY_WEIGHT * sent_ref[
                lines, :
            ].astype(jnp.float32)
            for first in range(0, cap, UNROLL):
                lanes = range(first, first + UNROLL)
                places = [targets_ref[base + lane] for lane in lanes]
                others = [targets_ref[base + cap + lane] for lane in lanes]
                sums = [
                    total[pl.ds(place, 1), :] + terms[lane : lane + 1, :]
                    for place, lane in zip(places, lanes)
                ]
                other_sums = [
                    second[pl.ds(place, 1), :] + terms[cap + lane : cap + lane + 1, :]
                    for place, lane in zip(others, lanes)
                ]
                for place, value in zip(places, sums):
                    total[pl.ds(place, 1), :] = value
                for place, value in zip(others, other_sums):
                    second[pl.ds(place, 1), :] = value
            return carry

        lax.fori_loop(0, count // pair, body, 0)
        part = rows // 4
        copies = []
        for piece in range(4):
            cut = pl.ds(piece * part, part)
            total[cut, :] = total[cut, :] + second[cut, :]
            copies.append(pltpu.make_async_copy(total.at[cut, :], out_ref.at[cut, :], sem.at[piece]))
            copies[-1].start()
        for copy in copies:
            copy.wait()

    return pl.pallas_call(
        kernel,
        out_shape=jax.ShapeDtypeStruct((rows, width), jnp.float32),
        in_specs=[whole(pltpu.SMEM), whole(), whole()],
        out_specs=whole(pl.ANY),
        scratch_shapes=[
            pltpu.VMEM((rows + 8, width), jnp.float32),
            pltpu.VMEM((rows + 8, width), jnp.float32),
            pltpu.VMEM((pair, width), jnp.float32),
            pltpu.SemaphoreType.DMA((4,)),
        ],
        compiler_params=params(),
        name="add_rows",
    )(targets, returned, outgoing)


GROUP = 16
TABLE_AXES = ("section", "table")
STAGE_LIMIT = 28 * 1024 * 1024
NT = (((1,), (1,)), ((), ()))


def dot_nt(left, right):
    return lax.dot_general(left, right, NT, preferred_element_type=jnp.float32)


def dot(left, right):
    return jnp.dot(left, right, preferred_element_type=jnp.float32)


def halves(value):
    high = value.astype(jnp.bfloat16)
    low = (value - high.astype(jnp.float32)).astype(jnp.bfloat16)
    return jnp.concatenate([high, low], axis=1)


def same_sample(count):
    first = lax.broadcasted_iota(jnp.int32, (count * GROUP, count * GROUP), 0)
    second = lax.broadcasted_iota(jnp.int32, (count * GROUP, count * GROUP), 1)
    return (first & (GROUP - 1)) == (second & (GROUP - 1))


def stacked(ref, rows, count, width):
    return jnp.concatenate([ref[rows, k * width : (k + 1) * width] for k in range(count)], axis=0)


def repeated(proj):
    count, width = proj.shape
    lines = [jnp.broadcast_to(proj[k : k + 1, :], (GROUP, width)) for k in range(count)]
    return jnp.concatenate(lines, axis=0).astype(jnp.bfloat16)


def mix_forward(small, layer, acts, inter, scale, normed, grams, count):
    batch, model_width = acts.shape
    width = model_width // count
    both = small[layer].astype(jnp.float32)
    proj = repeated(both[:count])
    keep = same_sample(count)
    size = GROUP * count
    for group in range(batch // GROUP):
        block = stacked(acts, pl.ds(group * GROUP, GROUP), count, width)
        gram = jnp.where(keep, dot_nt(block, block), 0.0)
        grams[group * size : (group + 1) * size, :] = halves(gram)
    mixed = dot(grams[...], jnp.concatenate([proj, proj], axis=0))
    for group in range(batch // GROUP):
        rows = pl.ds(group * GROUP, GROUP)
        start = group * size
        parts = [mixed[start + k * GROUP : start + (k + 1) * GROUP] for k in range(count)]
        squares = sum(part * part for part in parts)
        mean = jnp.sum(squares, axis=1, keepdims=True) * (1.0 / model_width)
        inv = lax.rsqrt(mean + EPSILON)
        scale[rows, :] = jnp.broadcast_to(inv, (GROUP, width))
        for k in range(count):
            columns = slice(k * width, (k + 1) * width)
            inter[rows, columns] = parts[k]
            gain = both[count + k : count + k + 1]
            normed[rows, columns] = (parts[k] * inv * gain).astype(jnp.bfloat16)


def gram_scratch(batch, count):
    return pltpu.VMEM((batch * count, 2 * GROUP * count), jnp.bfloat16)


def hidden_tile(hidden_width):
    return min(hidden_width, 1024)


def model_tile(model_width):
    return min(model_width, 512)


def tile_at(step, size):
    return pl.ds(pl.multiple_of(step * size, size), size)


class Stream:
    def __init__(self, mine, own, other, held, sems, axis, size):
        self.mine, self.own, self.other, self.held, self.sems = mine, own, other, held, sems
        self.axis, self.size = axis, size
        self.tiles = own.shape[axis] // size

    def copy(self, source, step):
        cut = tile_at(step, self.size)
        index = (slice(None), cut) if self.axis == 1 else (cut, slice(None))
        return pltpu.make_async_copy(source.at[index], self.held.at[index], self.sems.at[step])

    def start(self):
        @pl.when(self.mine)
        def _():
            for step in range(self.tiles):
                self.copy(self.own, step).start()

        @pl.when(jnp.logical_not(self.mine))
        def _():
            for step in range(self.tiles):
                self.copy(self.other, step).start()

    def wait(self, step):
        self.copy(self.own, step).wait()


def no_wait(step):
    return None


class Held:
    def __init__(self, held):
        self.held = held
        self.wait = no_wait

    def start(self):
        return None


def over_tiles(total, tile, many, wait, work):
    many = min(many, total // tile)

    def body(step, carry):
        for inner in range(many):
            wait(step * many + inner)
        work(tile_at(step, many * tile))
        return carry

    lax.fori_loop(0, total // (many * tile), body, 0)


def up_product(normed, w_up, hidden, turned, wait, many=1):
    def work(columns):
        opened = jnp.maximum(dot(normed[...], w_up[:, columns]), 0.0).astype(jnp.bfloat16)
        hidden[:, columns] = opened
        turned[columns, :] = opened.T

    width = hidden.shape[1]
    over_tiles(width, hidden_tile(width), many, wait, work)


def down_product(hidden, w_down, acts, out, wait, many=1):
    def work(columns):
        term = dot(hidden[...], w_down[:, columns])
        out[:, columns] = (acts[:, columns].astype(jnp.float32) + term).astype(jnp.bfloat16)

    width = out.shape[1]
    over_tiles(width, model_tile(width), many, wait, work)


def turn(rows, turned):
    turned[...] = rows[...].T


def opened_only(hidden, grad):
    return jnp.where(hidden.astype(jnp.float32) > 0.0, grad, 0.0).astype(jnp.bfloat16)


def down_back(grad, w_down, hidden, out, wait, many=1):
    def work(lines):
        g_hidden = dot(w_down[lines, :], grad[...])
        if hidden is not None:
            out[lines, :] = opened_only(hidden[lines, :], g_hidden)
        else:
            out[lines, :] = g_hidden.astype(jnp.bfloat16)

    width = out.shape[0]
    over_tiles(width, hidden_tile(width), many, wait, work)


def up_back(g_before, w_up, weighted, wait, many=1):
    def work(columns):
        weighted[:, columns] = dot(w_up[columns, :], g_before[...]).T

    width = weighted.shape[1]
    over_tiles(width, model_tile(width), many, wait, work)


def mix_backward(small, layer, grad, acts, inter, scale, weighted, out, count):
    batch, model_width = acts.shape
    width = model_width // count
    both = small[layer].astype(jnp.float32)
    proj = repeated(both[:count])
    keep = same_sample(count)
    for start in range(0, batch, GROUP):
        rows = pl.ds(start, GROUP)
        columns = [slice(k * width, (k + 1) * width) for k in range(count)]
        gained = [weighted[rows, columns[k]] * both[count + k : count + k + 1] for k in range(count)]
        shared = sum(gained[k] * inter[rows, columns[k]] for k in range(count))
        mean = jnp.sum(shared, axis=1, keepdims=True) * (1.0 / model_width)
        inv = scale[rows, 0:1]
        pull = inv * inv * mean
        parts = [
            (inv * (gained[k] - inter[rows, columns[k]] * pull)).astype(jnp.bfloat16)
            for k in range(count)
        ]
        block = stacked(acts, rows, count, width)
        g_inter = jnp.concatenate(parts, axis=0)
        left = jnp.concatenate([g_inter, proj], axis=1)
        right = jnp.concatenate([proj, g_inter], axis=1)
        links = jnp.where(keep, dot_nt(left, right), 0.0)
        g_acts = dot(halves(links), jnp.concatenate([block, block], axis=0))
        for k in range(count):
            piece = g_acts[k * GROUP : (k + 1) * GROUP] + grad[rows, columns[k]].astype(jnp.float32)
            out[rows, columns[k]] = piece.astype(jnp.bfloat16)


def saved_shapes(batch, model_width, hidden_width, width):
    return [
        jax.ShapeDtypeStruct((2, hidden_width, batch), jnp.bfloat16),
        jax.ShapeDtypeStruct((2, batch, model_width), jnp.float32),
        jax.ShapeDtypeStruct((2, batch, width), jnp.float32),
        jax.ShapeDtypeStruct((2, batch, model_width), jnp.bfloat16),
    ]


def weight_specs():
    return [whole()] + [whole(pltpu.HBM)] * 4 + [whole()] * 2


def weight_scratch(model_width, hidden_width):
    tiles = max(hidden_width // hidden_tile(hidden_width), model_width // model_tile(model_width))
    return [
        pltpu.VMEM((model_width, hidden_width), jnp.bfloat16),
        pltpu.VMEM((hidden_width, model_width), jnp.bfloat16),
        pltpu.SemaphoreType.DMA((2, tiles)),
    ]


def streams_of(core, weights, held, forward, ready):
    own_up, other_up, own_down, other_down, ready_up, ready_down = weights
    held_up, held_down, sems = held
    model_width, hidden_width = own_up.shape
    wide, narrow = hidden_tile(hidden_width), model_tile(model_width)
    made = []
    for layer in (0, 1):
        if layer == ready:
            made.append((Held(ready_up), Held(ready_down)))
            continue
        mine = core == layer
        up_forward, down_forward = forward[layer]
        up_cut = (1, wide) if up_forward else (0, narrow)
        down_cut = (1, narrow) if down_forward else (0, wide)
        made.append(
            (
                Stream(mine, own_up, other_up, held_up, sems.at[0], *up_cut),
                Stream(mine, own_down, other_down, held_down, sems.at[1], *down_cut),
            )
        )
    return made


def hold_layer(place, layer, weights):
    small, own_up, other_up, own_down, other_down = weights

    def kernel(place_ref, own_up_ref, other_up_ref, own_down_ref, other_down_ref, up_out, down_out, sems):
        def load(up_ref, down_ref):
            up = pltpu.make_async_copy(up_ref, up_out, sems.at[0])
            down = pltpu.make_async_copy(down_ref, down_out, sems.at[1])
            up.start()
            down.start()
            up.wait()
            down.wait()

        @pl.when((place_ref[1] == 1) & (place_ref[0] == layer))
        def _():
            load(own_up_ref, own_down_ref)

        @pl.when((place_ref[1] == 1) & (place_ref[0] != layer))
        def _():
            load(other_up_ref, other_down_ref)

    return pl.pallas_call(
        kernel,
        out_shape=[pltpu.VMEM(own_up.shape, own_up.dtype), pltpu.VMEM(own_down.shape, own_down.dtype)],
        in_specs=[whole(pltpu.SMEM)] + [whole(pltpu.HBM)] * 4,
        out_specs=[whole(), whole()],
        scratch_shapes=[pltpu.SemaphoreType.DMA((2,))],
        compiler_params=pltpu.CompilerParams(vmem_limit_bytes=4 * 1024 * 1024),
        name="hold_layer",
    )(place, *map(in_hbm, weights[1:]))


def stage_cost(products, batch, model_width, hidden_width):
    return pl.CostEstimate(
        flops=2 * products * batch * model_width * hidden_width, bytes_accessed=1 << 20, transcendentals=0
    )


def stage_params():
    return pltpu.CompilerParams(vmem_limit_bytes=STAGE_LIMIT)


def forward_stage(place, pieces, top, weights, ready, count):
    batch, model_width = top.shape
    hidden_width = weights[1].shape[1]
    width = model_width // count

    def kernel(place_ref, *refs):
        piece_refs, (top_ref, small_ref), refs = refs[: len(pieces)], refs[len(pieces) :][:2], refs[len(pieces) + 2 :]
        matrices, refs = refs[:6], refs[6:]
        out_ref, hid, inter, scale, kept, g_hidden = refs[:6]
        held, (normed, hidden, top_turned, grams) = refs[6:9], refs[9:]
        core = place_ref[0]

        @pl.when(place_ref[1] == 1)
        def _():
            layers = streams_of(core, matrices, held, [(True, True), (True, True)], 0)
            for up, down in layers:
                up.start()
                down.start()
            start = 0
            for piece in piece_refs:
                kept[0, start : start + piece.shape[0], :] = piece[...]
                start += piece.shape[0]
            for layer, (up, down) in enumerate(layers):
                mix_forward(
                    small_ref, layer, kept.at[layer], inter.at[layer], scale.at[layer], normed, grams, count
                )
                up_product(normed, up.held, hidden, hid.at[layer], up.wait)
                to = kept.at[1] if layer == 0 else out_ref
                down_product(hidden, down.held, kept.at[layer], to, down.wait)

        @pl.when(place_ref[2] == 1)
        def _():
            layers = streams_of(core, matrices, held, [(True, True), (True, False)], 0)
            down = layers[1][1]
            down.start()
            turn(top_ref, top_turned)
            down_back(top_turned, down.held, None, g_hidden, down.wait)

    out = pl.pallas_call(
        kernel,
        out_shape=[jax.ShapeDtypeStruct(top.shape, jnp.bfloat16)]
        + saved_shapes(batch, model_width, hidden_width, width)
        + [jax.ShapeDtypeStruct((hidden_width, batch), jnp.bfloat16)],
        in_specs=[whole(pltpu.SMEM)] + [whole()] * (len(pieces) + 1) + weight_specs(),
        out_specs=[whole()] * 6,
        scratch_shapes=weight_scratch(model_width, hidden_width)
        + [
            pltpu.VMEM((batch, model_width), jnp.bfloat16),
            pltpu.VMEM((batch, hidden_width), jnp.bfloat16),
            pltpu.VMEM((model_width, batch), jnp.bfloat16),
            gram_scratch(batch, count),
        ],
        compiler_params=stage_params(),
        cost_estimate=stage_cost(4, batch, model_width, hidden_width),
        name="forward_stage",
    )(place, *pieces, top, weights[0], *map(in_hbm, weights[1:]), *ready)
    return out[0], out[1:5], out[5]


def turn_stage(place, acts, top, g_hidden, weights, ready, count):
    batch, model_width = acts.shape
    hidden_width = weights[1].shape[1]
    width = model_width // count

    def kernel(place_ref, acts_ref, top_ref, ghid_ref, small_ref, *refs):
        matrices, refs = refs[:6], refs[6:]
        out_ref, held = refs[0], refs[1:4]
        hid, hidden, inter, scale, upper, grad, turned, normed, weighted, g_before, grams = refs[4:]

        @pl.when(place_ref[1] == 1)
        def _():
            layers = streams_of(place_ref[0], matrices, held, [(True, True), (True, True)], 0)
            (up0, down0), (up1, down1) = layers
            for stream in (up0, down0, up1):
                stream.start()
            mix_forward(small_ref, 0, acts_ref, inter.at[0], scale.at[0], normed, grams, count)
            up_product(normed, up0.held, hidden, hid, up0.wait)
            down_product(hidden, down0.held, acts_ref, upper, down0.wait)
            mix_forward(small_ref, 1, upper, inter.at[1], scale.at[1], normed, grams, count)

            def masked(columns):
                before = dot(normed[...], up1.held[:, columns])
                opened = jnp.maximum(before, 0.0).astype(jnp.bfloat16).T
                g_before[columns, :] = opened_only(opened, ghid_ref[columns, :].astype(jnp.float32))

            over_tiles(hidden_width, hidden_tile(hidden_width), 1, up1.wait, masked)
            up_back(g_before, up1.held, weighted, no_wait)
            mix_backward(small_ref, 1, top_ref, upper, inter.at[1], scale.at[1], weighted, grad, count)
            turn(grad, turned)
            down_back(turned, down0.held, hid, g_before, no_wait)
            up_back(g_before, up0.held, weighted, no_wait)
            mix_backward(small_ref, 0, grad, acts_ref, inter.at[0], scale.at[0], weighted, out_ref, count)

    return pl.pallas_call(
        kernel,
        out_shape=jax.ShapeDtypeStruct(acts.shape, jnp.bfloat16),
        in_specs=[whole(pltpu.SMEM)] + [whole()] * 3 + weight_specs(),
        out_specs=whole(),
        scratch_shapes=weight_scratch(model_width, hidden_width)
        + [
            pltpu.VMEM((hidden_width, batch), jnp.bfloat16),
            pltpu.VMEM((batch, hidden_width), jnp.bfloat16),
            pltpu.VMEM((2, batch, model_width), jnp.float32),
            pltpu.VMEM((2, batch, width), jnp.float32),
            pltpu.VMEM((batch, model_width), jnp.bfloat16),
            pltpu.VMEM((batch, model_width), jnp.bfloat16),
            pltpu.VMEM((model_width, batch), jnp.bfloat16),
            pltpu.VMEM((batch, model_width), jnp.bfloat16),
            pltpu.VMEM((batch, model_width), jnp.float32),
            pltpu.VMEM((hidden_width, batch), jnp.bfloat16),
            gram_scratch(batch, count),
        ],
        compiler_params=stage_params(),
        cost_estimate=stage_cost(6, batch, model_width, hidden_width),
        name="turn_stage",
    )(place, acts, top, g_hidden, weights[0], *map(in_hbm, weights[1:]), *ready)


def backward_stage(place, grad, saved, weights, ready, count):
    batch, model_width = grad.shape
    hidden_width = weights[1].shape[1]

    def kernel(place_ref, grad_ref, hid, inter, scale, kept, small_ref, *refs):
        matrices, refs = refs[:6], refs[6:]
        out_ref, held = refs[0], refs[1:4]
        middle, turned, weighted, g_before = refs[4:]

        @pl.when(place_ref[1] == 1)
        def _():
            layers = streams_of(place_ref[0], matrices, held, [(False, False), (False, False)], 1)
            for up, down in reversed(layers):
                down.start()
                up.start()
            for layer, given, to in ((1, grad_ref, middle), (0, middle, out_ref)):
                up, down = layers[layer]
                turn(given, turned)
                down_back(turned, down.held, hid.at[layer], g_before, down.wait)
                up_back(g_before, up.held, weighted, up.wait)
                mix_backward(
                    small_ref, layer, given, kept.at[layer], inter.at[layer], scale.at[layer],
                    weighted, to, count,
                )

    return pl.pallas_call(
        kernel,
        out_shape=jax.ShapeDtypeStruct(grad.shape, jnp.bfloat16),
        in_specs=[whole(pltpu.SMEM)] + [whole()] * 5 + weight_specs(),
        out_specs=whole(),
        scratch_shapes=weight_scratch(model_width, hidden_width)
        + [
            pltpu.VMEM((batch, model_width), jnp.bfloat16),
            pltpu.VMEM((model_width, batch), jnp.bfloat16),
            pltpu.VMEM((batch, model_width), jnp.float32),
            pltpu.VMEM((hidden_width, batch), jnp.bfloat16),
        ],
        compiler_params=stage_params(),
        cost_estimate=stage_cost(4, batch, model_width, hidden_width),
        name="backward_stage",
    )(place, grad, *saved, weights[0], *map(in_hbm, weights[1:]), *ready)


def swapped(value, section_count):
    return lax.ppermute(value, "section", [(s, s ^ 1) for s in range(section_count)])


def moved(value, from_stage, to_stage):
    pairs = [(2 * from_stage + core, 2 * to_stage + core) for core in (0, 1)]
    return lax.ppermute(value, "section", pairs)


def mirror(value):
    along = lax.axis_size("table")
    return lax.ppermute(value, "table", [(t, (t + along // 2) % along) for t in range(along)])


def swap_in_half(value):
    along = lax.axis_size("table")
    half = along // 2
    groups = [
        [s * along + h * half + t for s in range(lax.axis_size("section")) for t in range(half)]
        for h in (0, 1)
    ]
    return lax.all_to_all(
        value, TABLE_AXES, split_axis=0, concat_axis=0, axis_index_groups=groups, tiled=True
    )


def near_first(per_asker, my_half):
    sections = lax.axis_size("section")
    half = lax.axis_size("table") // 2
    split = per_asker.reshape((sections, 2, half) + per_asker.shape[1:])
    near = lax.dynamic_index_in_dim(split, my_half, 1, keepdims=False)
    far = lax.dynamic_index_in_dim(split, 1 - my_half, 1, keepdims=False)
    return jnp.stack([near, far], axis=2).reshape((sections * half, 2) + per_asker.shape[1:])


def after(value, earlier):
    return lax.optimization_barrier((value, earlier))[0]


def per_device(
    emb_table,
    lcb_weight,
    fm_proj,
    norm_gain,
    w_up,
    w_down,
    top_grad,
    lookup_slot,
    wanted_rows,
    row_counts,
):
    section_count = lax.axis_size("section")
    along = lax.axis_size("table")
    half = along // 2
    near_owners = section_count * half
    stages = section_count // 2
    stage = lax.axis_index("section") // 2
    core = lax.axis_index("section") % 2
    my_half = lax.axis_index("table") // half
    cap = wanted_rows.shape[2]
    rows, embed_width = emb_table.shape
    embed_count = lcb_weight.shape[0]
    look_dev = lookup_slot.shape[1]
    model_width = top_grad.shape[3]

    own_slots = lookup_slot[0]
    mirror_slots = mirror(own_slots)
    small = jnp.concatenate([fm_proj[0], norm_gain[0].reshape(embed_count, -1)], axis=0)
    other_up = swapped(w_up[0], section_count)
    other_down = swapped(w_down[0], section_count)
    other_small = swapped(small, section_count)

    picked = near_first(wanted_rows[0], my_half)
    outgoing = pick_rows(emb_table, wanted_rows[0], my_half)
    sent = after(outgoing, mirror_slots).reshape(near_owners, 2, cap, embed_width)
    fetched = swap_in_half(sent)

    def spread_of(slots):
        owner, column = slots // cap, slots % cap
        place = owner % along
        near = jnp.where(place // half == my_half, owner // along * half + place % half, near_owners)
        return spread_weights(near * cap + column, lcb_weight, near_owners, cap)

    spread_far, kept_far = spread_of(mirror_slots)
    spread_near, kept_near = spread_of(own_slots)
    smalls = jnp.stack(
        [jnp.where(core == 0, small, other_small), jnp.where(core == 0, other_small, small)]
    )
    weights = [smalls, w_up[0], other_up, w_down[0], other_down]
    spread_far, spread_near = lax.optimization_barrier((spread_far, spread_near))
    far_part = mirror(compress(spread_far, fetched, 1, embed_count, jnp.bfloat16))
    near_part = compress(spread_near, fetched, 0, embed_count, jnp.float32)
    lead = (near_part + far_part.astype(jnp.float32)).astype(jnp.bfloat16)
    pieces = [lead] + [moved(lead, s, 0) for s in range(1, stages)]
    top = top_grad.reshape(stages, 2, look_dev, model_width)
    top = lax.dynamic_index_in_dim(top, core, 1, keepdims=False).reshape(-1, model_width)

    def at(tick):
        is_last = (stage == stages - 1) & (tick == 0)
        return jnp.stack([core, stage == tick, is_last]).astype(jnp.int32)

    saved = None
    for tick in range(stages - 1):
        place = at(tick)
        ready = hold_layer(after(place, lead if tick == 0 else out), 0, weights)
        out, fresh, product = forward_stage(place, pieces, top, weights, ready, embed_count)
        if saved is None:
            saved, g_hidden = fresh, product
        else:
            saved = [jnp.where(stage == tick, new, old) for new, old in zip(fresh, saved)]
        pieces = [moved(out, tick, tick + 1)]
    place = at(stages - 1)
    ready = hold_layer(after(place, out), 0, weights)
    grad = turn_stage(place, pieces[0], top, g_hidden, weights, ready, embed_count)
    for tick in reversed(range(stages - 1)):
        place = at(tick)
        ready = hold_layer(after(place, grad), 1, weights)
        grad = moved(grad, tick + 1, tick)
        grad = backward_stage(place, grad, saved, weights, ready, embed_count)

    own_grad = grad[:look_dev]
    for s in range(1, stages):
        piece = grad[s * look_dev : (s + 1) * look_dev]
        own_grad = jnp.where(stage == s, moved(piece, 0, s), own_grad)
    mirror_grad = mirror(own_grad)

    near_grad = expand(kept_near, own_grad, embed_count)
    slot_grad = expand(kept_far, mirror_grad, embed_count, near_grad)
    returned = swap_in_half(slot_grad)
    live_slots = jnp.arange(cap) < near_first(row_counts[0], my_half)[..., None]
    targets = jnp.where(live_slots, picked, rows).reshape(-1)
    return add_rows(targets, returned.reshape(-1, embed_width), outgoing, rows, cap)


def solution(mesh):
    in_specs = (
        P(("section", "table"), None),
        P(),
        P("section", None, None),
        P("section", None),
        P("section", None, None),
        P("section", None, None),
        P("table", None, None, None),
        P("table", "section", None),
        P(("section", "table"), None, None),
        P(("section", "table"), None),
    )
    out_specs = P(("section", "table"), None)
    return jax.shard_map(
        per_device, mesh=mesh, in_specs=in_specs, out_specs=out_specs, check_vma=False
    )
```

```python
import jax
import jax.numpy as jnp
from jax import lax
from jax.experimental import pallas as pl
from jax.experimental.pallas import tpu as pltpu
from jax.sharding import PartitionSpec as P

EPSILON = 1e-05
DECAY_WEIGHT = 0.5
VMEM_LIMIT = 28 * 1024 * 1024
UNROLL = 32


def whole(memory_space=pltpu.VMEM):
    return pl.BlockSpec(memory_space=memory_space)


def in_hbm(value):
    return pltpu.with_memory_space_constraint(value, pltpu.HBM)


def params():
    return pltpu.CompilerParams(vmem_limit_bytes=VMEM_LIMIT)


def tiles_of(count, most):
    return max(step for step in range(1, most + 1) if count % step == 0)


def pick_rows(emb_table, wanted, my_half):
    rows, width = emb_table.shape
    askers, cap = wanted.shape
    half = lax.axis_size("table") // 2
    together = tiles_of(askers, 8)
    pieces = 4

    def kernel(half_ref, wanted_ref, table_ref, out_ref, narrow, wide, lines, sems):
        copies = []
        for piece in range(pieces):
            cut = pl.ds(piece * (rows // pieces), rows // pieces)
            copies.append(pltpu.make_async_copy(table_ref.at[cut], narrow.at[cut], sems.at[piece]))
            copies[-1].start()
        for piece in range(pieces):
            cut = pl.ds(piece * (rows // pieces), rows // pieces)
            copies[piece].wait()
            wide[cut, :] = narrow[cut, :].astype(jnp.float32)

        def fill(part, carry):
            def one(line, inner):
                at = part * together + line
                device, is_mirror = at // 2, at % 2
                side = jnp.where(is_mirror == 0, half_ref[0], 1 - half_ref[0])
                asker = (device // half * 2 + side) * half + device % half
                first = pl.multiple_of(line * cap, cap)
                for lane in range(cap):
                    row = wanted_ref[asker * cap + lane]
                    lines[pl.ds(first + lane, 1), :] = wide[pl.ds(row, 1), :]
                return inner

            lax.fori_loop(0, together, one, 0)
            base = pl.multiple_of(part * (together * cap), together * cap)
            out_ref[pl.ds(base, together * cap), :] = lines[...].astype(out_ref.dtype)
            return carry

        lax.fori_loop(0, askers // together, fill, 0)

    return pl.pallas_call(
        kernel,
        out_shape=jax.ShapeDtypeStruct((askers * cap, width), emb_table.dtype),
        in_specs=[whole(pltpu.SMEM), whole(pltpu.SMEM), whole(pltpu.HBM)],
        out_specs=whole(),
        scratch_shapes=[
            pltpu.VMEM((rows, width), emb_table.dtype),
            pltpu.VMEM((rows, width), jnp.float32),
            pltpu.VMEM((together * cap, width), jnp.float32),
            pltpu.SemaphoreType.DMA((pieces,)),
        ],
        compiler_params=params(),
        name="pick_rows",
    )(my_half.astype(jnp.int32).reshape(1), wanted.reshape(-1), in_hbm(emb_table))


def spread_weights(codes, lcb_weight, owners, cap):
    samples, feature_count = codes.shape
    embed_count = lcb_weight.shape[0]
    group = tiles_of(samples, 16)

    def kernel(codes_ref, lcb_ref, out_ref, kept_ref):
        lcb = lcb_ref[...].astype(jnp.float32)
        owner_of = lax.broadcasted_iota(jnp.int32, (owners, embed_count, feature_count), 0)
        column_of = lax.broadcasted_iota(jnp.int32, (cap, feature_count), 0)
        for pair in range(0, group, 2):
            made = []
            for sample in (pair, pair + 1):
                slots = codes_ref[sample : sample + 1, :]
                owner = lax.div(slots, cap)
                column = slots - owner * cap
                left = jnp.where(owner_of == owner[None], lcb[None], 0.0)
                left = left.reshape(owners * embed_count, feature_count).astype(jnp.bfloat16)
                right = jnp.where(column_of == column, 1.0, 0.0).astype(jnp.bfloat16)
                both = lax.dot_general(
                    left, right, (((1,), (1,)), ((), ())), preferred_element_type=jnp.float32
                )
                made.append(both.reshape(owners, embed_count, cap))
            rows = pl.ds(pair * embed_count, 2 * embed_count)
            joined = jnp.concatenate(made, axis=1).astype(out_ref.dtype)
            out_ref[:, rows, :] = joined
            kept_ref[:, rows, :] = joined

    return pl.pallas_call(
        kernel,
        out_shape=[
            pltpu.VMEM((owners, samples * embed_count, cap), jnp.bfloat16),
            pltpu.HBM((owners, samples * embed_count, cap), jnp.bfloat16),
        ],
        grid=(samples // group,),
        in_specs=[
            pl.BlockSpec((group, feature_count), lambda i: (i, 0)),
            pl.BlockSpec((embed_count, feature_count), lambda i: (0, 0)),
        ],
        out_specs=[pl.BlockSpec((owners, group * embed_count, cap), lambda i: (0, i, 0))] * 2,
        compiler_params=params(),
        cost_estimate=pl.CostEstimate(
            flops=2 * samples * owners * embed_count * feature_count * cap,
            bytes_accessed=2 * owners * samples * embed_count * cap,
            transcendentals=0,
        ),
        name="spread_weights",
    )(codes, lcb_weight)


def compress(spread, fetched, view, embed_count, kind):
    owners, lines, cap = spread.shape
    width = fetched.shape[3]
    samples = lines // embed_count
    part = tiles_of(owners, 8)
    steps = owners // part

    def kernel(spread_ref, rows_ref, out_ref, total):
        total[...] = jnp.zeros_like(total)

        def body(step, carry):
            first = step * part
            left = jnp.concatenate([spread_ref[first + o] for o in range(part)], axis=1)
            right = jnp.concatenate([rows_ref[first + o, view] for o in range(part)], axis=0)
            total[...] += jnp.dot(left, right, preferred_element_type=jnp.float32)
            return carry

        lax.fori_loop(0, steps, body, 0)
        for k in range(embed_count):
            columns = slice(k * width, (k + 1) * width)
            piece = total[pl.ds(k, samples, stride=embed_count), :]
            out_ref[:, columns] = piece.astype(out_ref.dtype)

    return pl.pallas_call(
        kernel,
        out_shape=jax.ShapeDtypeStruct((samples, embed_count * width), kind),
        in_specs=[whole(), whole()],
        out_specs=whole(),
        scratch_shapes=[pltpu.VMEM((lines, width), jnp.float32)],
        compiler_params=params(),
        name="compress",
    )(spread, fetched)


def expand(spread, lead_grad, embed_count, near=None):
    owners, lines, cap = spread.shape
    samples = lines // embed_count
    width = lead_grad.shape[1] // embed_count
    part = tiles_of(owners, 8)
    extra = [] if near is None else [near]

    def kernel(spread_ref, grad_ref, *refs):
        near_refs, (out_ref, tall, turned) = refs[: len(extra)], refs[len(extra) :]
        for k in range(embed_count):
            piece = grad_ref[:, k * width : (k + 1) * width].astype(jnp.float32)
            tall[pl.ds(k, samples, stride=embed_count), :] = piece
        turned[...] = tall[...].T.astype(jnp.bfloat16)

        def body(step, carry):
            first = step * part
            right = jnp.concatenate([spread_ref[first + o] for o in range(part)], axis=1)
            term = jnp.dot(turned[...], right, preferred_element_type=jnp.float32)
            piece = term.T.astype(out_ref.dtype).reshape(part, cap, width)
            if near_refs:
                for o in range(part):
                    out_ref[first + o, 0] = near_refs[0][first + o]
                    out_ref[first + o, 1] = piece[o]
            else:
                out_ref[tile_at(step, part)] = piece
            return carry

        lax.fori_loop(0, owners // part, body, 0)

    views = () if near is None else (2,)
    return pl.pallas_call(
        kernel,
        out_shape=jax.ShapeDtypeStruct((owners,) + views + (cap, width), jnp.bfloat16),
        in_specs=[whole()] * (2 + len(extra)),
        out_specs=whole(),
        scratch_shapes=[
            pltpu.VMEM((lines, width), jnp.float32),
            pltpu.VMEM((width, lines), jnp.bfloat16),
        ],
        compiler_params=params(),
        name="expand",
    )(spread, lead_grad, *extra)


def add_rows(targets, returned, outgoing, rows, cap):
    count, width = returned.shape
    pair = 2 * cap

    def kernel(targets_ref, back_ref, sent_ref, out_ref, total, second, terms, sem):
        total[...] = jnp.zeros_like(total)
        second[...] = jnp.zeros_like(second)

        def body(step, carry):
            base = pl.multiple_of(step * pair, pair)
            lines = pl.ds(base, pair)
            terms[...] = back_ref[lines, :].astype(jnp.float32) + DECAY_WEIGHT * sent_ref[
                lines, :
            ].astype(jnp.float32)
            for first in range(0, cap, UNROLL):
                lanes = range(first, first + UNROLL)
                places = [targets_ref[base + lane] for lane in lanes]
                others = [targets_ref[base + cap + lane] for lane in lanes]
                sums = [
                    total[pl.ds(place, 1), :] + terms[lane : lane + 1, :]
                    for place, lane in zip(places, lanes)
                ]
                other_sums = [
                    second[pl.ds(place, 1), :] + terms[cap + lane : cap + lane + 1, :]
                    for place, lane in zip(others, lanes)
                ]
                for place, value in zip(places, sums):
                    total[pl.ds(place, 1), :] = value
                for place, value in zip(others, other_sums):
                    second[pl.ds(place, 1), :] = value
            return carry

        lax.fori_loop(0, count // pair, body, 0)
        part = rows // 4
        copies = []
        for piece in range(4):
            cut = pl.ds(piece * part, part)
            total[cut, :] = total[cut, :] + second[cut, :]
            copies.append(pltpu.make_async_copy(total.at[cut, :], out_ref.at[cut, :], sem.at[piece]))
            copies[-1].start()
        for copy in copies:
            copy.wait()

    return pl.pallas_call(
        kernel,
        out_shape=jax.ShapeDtypeStruct((rows, width), jnp.float32),
        in_specs=[whole(pltpu.SMEM), whole(), whole()],
        out_specs=whole(pl.ANY),
        scratch_shapes=[
            pltpu.VMEM((rows + 8, width), jnp.float32),
            pltpu.VMEM((rows + 8, width), jnp.float32),
            pltpu.VMEM((pair, width), jnp.float32),
            pltpu.SemaphoreType.DMA((4,)),
        ],
        compiler_params=params(),
        name="add_rows",
    )(targets, returned, outgoing)


GROUP = 16
TABLE_AXES = ("section", "table")
STAGE_LIMIT = 28 * 1024 * 1024
NT = (((1,), (1,)), ((), ()))


def dot_nt(left, right):
    return lax.dot_general(left, right, NT, preferred_element_type=jnp.float32)


def dot(left, right):
    return jnp.dot(left, right, preferred_element_type=jnp.float32)


def halves(value):
    high = value.astype(jnp.bfloat16)
    low = (value - high.astype(jnp.float32)).astype(jnp.bfloat16)
    return jnp.concatenate([high, low], axis=1)


def same_sample(count):
    first = lax.broadcasted_iota(jnp.int32, (count * GROUP, count * GROUP), 0)
    second = lax.broadcasted_iota(jnp.int32, (count * GROUP, count * GROUP), 1)
    return (first & (GROUP - 1)) == (second & (GROUP - 1))


def stacked(ref, rows, count, width):
    return jnp.concatenate([ref[rows, k * width : (k + 1) * width] for k in range(count)], axis=0)


def repeated(proj):
    count, width = proj.shape
    lines = [jnp.broadcast_to(proj[k : k + 1, :], (GROUP, width)) for k in range(count)]
    return jnp.concatenate(lines, axis=0).astype(jnp.bfloat16)


def mix_forward(small, layer, acts, inter, scale, normed, grams, count):
    batch, model_width = acts.shape
    width = model_width // count
    both = small[layer].astype(jnp.float32)
    proj = repeated(both[:count])
    keep = same_sample(count)
    size = GROUP * count
    for group in range(batch // GROUP):
        block = stacked(acts, pl.ds(group * GROUP, GROUP), count, width)
        gram = jnp.where(keep, dot_nt(block, block), 0.0)
        grams[group * size : (group + 1) * size, :] = halves(gram)
    mixed = dot(grams[...], jnp.concatenate([proj, proj], axis=0))
    for group in range(batch // GROUP):
        rows = pl.ds(group * GROUP, GROUP)
        start = group * size
        parts = [mixed[start + k * GROUP : start + (k + 1) * GROUP] for k in range(count)]
        squares = sum(part * part for part in parts)
        mean = jnp.sum(squares, axis=1, keepdims=True) * (1.0 / model_width)
        inv = lax.rsqrt(mean + EPSILON)
        scale[rows, :] = jnp.broadcast_to(inv, (GROUP, width))
        for k in range(count):
            columns = slice(k * width, (k + 1) * width)
            inter[rows, columns] = parts[k]
            gain = both[count + k : count + k + 1]
            normed[rows, columns] = (parts[k] * inv * gain).astype(jnp.bfloat16)


def gram_scratch(batch, count):
    return pltpu.VMEM((batch * count, 2 * GROUP * count), jnp.bfloat16)


def hidden_tile(hidden_width):
    return min(hidden_width, 1024)


def model_tile(model_width):
    return min(model_width, 512)


def tile_at(step, size):
    return pl.ds(pl.multiple_of(step * size, size), size)


class Stream:
    def __init__(self, mine, own, other, held, sems, axis, size):
        self.mine, self.own, self.other, self.held, self.sems = mine, own, other, held, sems
        self.axis, self.size = axis, size
        self.tiles = own.shape[axis] // size

    def copy(self, source, step):
        cut = tile_at(step, self.size)
        index = (slice(None), cut) if self.axis == 1 else (cut, slice(None))
        return pltpu.make_async_copy(source.at[index], self.held.at[index], self.sems.at[step])

    def start(self):
        @pl.when(self.mine)
        def _():
            for step in range(self.tiles):
                self.copy(self.own, step).start()

        @pl.when(jnp.logical_not(self.mine))
        def _():
            for step in range(self.tiles):
                self.copy(self.other, step).start()

    def wait(self, step):
        self.copy(self.own, step).wait()


def no_wait(step):
    return None


class Held:
    def __init__(self, held):
        self.held = held
        self.wait = no_wait

    def start(self):
        return None


def over_tiles(total, tile, many, wait, work):
    many = min(many, total // tile)

    def body(step, carry):
        for inner in range(many):
            wait(step * many + inner)
        work(tile_at(step, many * tile))
        return carry

    lax.fori_loop(0, total // (many * tile), body, 0)


def up_product(normed, w_up, hidden, turned, wait, many=1):
    def work(columns):
        opened = jnp.maximum(dot(normed[...], w_up[:, columns]), 0.0).astype(jnp.bfloat16)
        hidden[:, columns] = opened
        turned[columns, :] = opened.T

    width = hidden.shape[1]
    over_tiles(width, hidden_tile(width), many, wait, work)


def down_product(hidden, w_down, acts, out, wait, many=1):
    def work(columns):
        term = dot(hidden[...], w_down[:, columns])
        out[:, columns] = (acts[:, columns].astype(jnp.float32) + term).astype(jnp.bfloat16)

    width = out.shape[1]
    over_tiles(width, model_tile(width), many, wait, work)


def turn(rows, turned):
    turned[...] = rows[...].T


def opened_only(hidden, grad):
    return jnp.where(hidden.astype(jnp.float32) > 0.0, grad, 0.0).astype(jnp.bfloat16)


def down_back(grad, w_down, hidden, out, wait, many=1):
    def work(lines):
        g_hidden = dot(w_down[lines, :], grad[...])
        if hidden is not None:
            out[lines, :] = opened_only(hidden[lines, :], g_hidden)
        else:
            out[lines, :] = g_hidden.astype(jnp.bfloat16)

    width = out.shape[0]
    over_tiles(width, hidden_tile(width), many, wait, work)


def up_back(g_before, w_up, weighted, wait, many=1):
    def work(columns):
        weighted[:, columns] = dot(w_up[columns, :], g_before[...]).T

    width = weighted.shape[1]
    over_tiles(width, model_tile(width), many, wait, work)


def mix_backward(small, layer, grad, acts, inter, scale, weighted, out, count):
    batch, model_width = acts.shape
    width = model_width // count
    both = small[layer].astype(jnp.float32)
    proj = repeated(both[:count])
    keep = same_sample(count)
    for start in range(0, batch, GROUP):
        rows = pl.ds(start, GROUP)
        columns = [slice(k * width, (k + 1) * width) for k in range(count)]
        gained = [weighted[rows, columns[k]] * both[count + k : count + k + 1] for k in range(count)]
        shared = sum(gained[k] * inter[rows, columns[k]] for k in range(count))
        mean = jnp.sum(shared, axis=1, keepdims=True) * (1.0 / model_width)
        inv = scale[rows, 0:1]
        pull = inv * inv * mean
        parts = [
            (inv * (gained[k] - inter[rows, columns[k]] * pull)).astype(jnp.bfloat16)
            for k in range(count)
        ]
        block = stacked(acts, rows, count, width)
        g_inter = jnp.concatenate(parts, axis=0)
        left = jnp.concatenate([g_inter, proj], axis=1)
        right = jnp.concatenate([proj, g_inter], axis=1)
        links = jnp.where(keep, dot_nt(left, right), 0.0)
        g_acts = dot(halves(links), jnp.concatenate([block, block], axis=0))
        for k in range(count):
            piece = g_acts[k * GROUP : (k + 1) * GROUP] + grad[rows, columns[k]].astype(jnp.float32)
            out[rows, columns[k]] = piece.astype(jnp.bfloat16)


def saved_shapes(batch, model_width, hidden_width, width):
    return [
        jax.ShapeDtypeStruct((2, hidden_width, batch), jnp.bfloat16),
        jax.ShapeDtypeStruct((2, batch, model_width), jnp.float32),
        jax.ShapeDtypeStruct((2, batch, width), jnp.float32),
        jax.ShapeDtypeStruct((2, batch, model_width), jnp.bfloat16),
    ]


def weight_specs():
    return [whole()] + [whole(pltpu.HBM)] * 4 + [whole()] * 2


def weight_scratch(model_width, hidden_width):
    tiles = max(hidden_width // hidden_tile(hidden_width), model_width // model_tile(model_width))
    return [
        pltpu.VMEM((model_width, hidden_width), jnp.bfloat16),
        pltpu.VMEM((hidden_width, model_width), jnp.bfloat16),
        pltpu.SemaphoreType.DMA((2, tiles)),
    ]


def streams_of(core, weights, held, forward, ready):
    own_up, other_up, own_down, other_down, ready_up, ready_down = weights
    held_up, held_down, sems = held
    model_width, hidden_width = own_up.shape
    wide, narrow = hidden_tile(hidden_width), model_tile(model_width)
    made = []
    for layer in (0, 1):
        if layer == ready:
            made.append((Held(ready_up), Held(ready_down)))
            continue
        mine = core == layer
        up_forward, down_forward = forward[layer]
        up_cut = (1, wide) if up_forward else (0, narrow)
        down_cut = (1, narrow) if down_forward else (0, wide)
        made.append(
            (
                Stream(mine, own_up, other_up, held_up, sems.at[0], *up_cut),
                Stream(mine, own_down, other_down, held_down, sems.at[1], *down_cut),
            )
        )
    return made


def hold_matrix(place, layer, own, other):
    pieces = 8
    part = own.shape[0] // pieces

    def kernel(place_ref, own_ref, other_ref, out_ref, sems):
        def load(source):
            copies = []
            for piece in range(pieces):
                cut = pl.ds(piece * part, part)
                copies.append(pltpu.make_async_copy(source.at[cut], out_ref.at[cut], sems.at[piece]))
                copies[-1].start()
            for copy in copies:
                copy.wait()

        @pl.when((place_ref[1] == 1) & (place_ref[0] == layer))
        def _():
            load(own_ref)

        @pl.when((place_ref[1] == 1) & (place_ref[0] != layer))
        def _():
            load(other_ref)

    return pl.pallas_call(
        kernel,
        out_shape=pltpu.VMEM(own.shape, own.dtype),
        in_specs=[whole(pltpu.SMEM)] + [whole(pltpu.HBM)] * 2,
        out_specs=whole(),
        scratch_shapes=[pltpu.SemaphoreType.DMA((pieces,))],
        compiler_params=pltpu.CompilerParams(vmem_limit_bytes=4 * 1024 * 1024),
        name="hold_matrix",
    )(place, in_hbm(own), in_hbm(other))


def hold_layer(place, layer, weights, earlier):
    small, own_up, other_up, own_down, other_down = weights
    place = after(place, earlier)
    return [
        hold_matrix(place, layer, own_up, other_up),
        hold_matrix(place, layer, own_down, other_down),
    ]


def stage_cost(products, batch, model_width, hidden_width):
    return pl.CostEstimate(
        flops=2 * products * batch * model_width * hidden_width, bytes_accessed=1 << 20, transcendentals=0
    )


def stage_params():
    return pltpu.CompilerParams(vmem_limit_bytes=STAGE_LIMIT)


def forward_stage(place, pieces, top, weights, ready, count):
    batch, model_width = top.shape
    hidden_width = weights[1].shape[1]
    width = model_width // count

    def kernel(place_ref, *refs):
        piece_refs, (top_ref, small_ref), refs = refs[: len(pieces)], refs[len(pieces) :][:2], refs[len(pieces) + 2 :]
        matrices, refs = refs[:6], refs[6:]
        out_ref, hid, inter, scale, kept, g_hidden = refs[:6]
        held, (normed, hidden, top_turned, grams) = refs[6:9], refs[9:]
        core = place_ref[0]

        @pl.when(place_ref[1] == 1)
        def _():
            layers = streams_of(core, matrices, held, [(True, True), (True, True)], 0)
            for up, down in layers:
                up.start()
                down.start()
            start = 0
            for piece in piece_refs:
                kept[0, start : start + piece.shape[0], :] = piece[...]
                start += piece.shape[0]
            for layer, (up, down) in enumerate(layers):
                mix_forward(
                    small_ref, layer, kept.at[layer], inter.at[layer], scale.at[layer], normed, grams, count
                )
                up_product(normed, up.held, hidden, hid.at[layer], up.wait)
                to = kept.at[1] if layer == 0 else out_ref
                down_product(hidden, down.held, kept.at[layer], to, down.wait)

        @pl.when(place_ref[2] == 1)
        def _():
            layers = streams_of(core, matrices, held, [(True, True), (True, False)], 0)
            down = layers[1][1]
            down.start()
            turn(top_ref, top_turned)
            down_back(top_turned, down.held, None, g_hidden, down.wait)

    out = pl.pallas_call(
        kernel,
        out_shape=[jax.ShapeDtypeStruct(top.shape, jnp.bfloat16)]
        + saved_shapes(batch, model_width, hidden_width, width)
        + [jax.ShapeDtypeStruct((hidden_width, batch), jnp.bfloat16)],
        in_specs=[whole(pltpu.SMEM)] + [whole()] * (len(pieces) + 1) + weight_specs(),
        out_specs=[whole()] * 6,
        scratch_shapes=weight_scratch(model_width, hidden_width)
        + [
            pltpu.VMEM((batch, model_width), jnp.bfloat16),
            pltpu.VMEM((batch, hidden_width), jnp.bfloat16),
            pltpu.VMEM((model_width, batch), jnp.bfloat16),
            gram_scratch(batch, count),
        ],
        compiler_params=stage_params(),
        cost_estimate=stage_cost(4, batch, model_width, hidden_width),
        name="forward_stage",
    )(place, *pieces, top, weights[0], *map(in_hbm, weights[1:]), *ready)
    return out[0], out[1:5], out[5]


def turn_stage(place, acts, top, g_hidden, weights, ready, count):
    batch, model_width = acts.shape
    hidden_width = weights[1].shape[1]
    width = model_width // count

    def kernel(place_ref, acts_ref, top_ref, ghid_ref, small_ref, *refs):
        matrices, refs = refs[:6], refs[6:]
        out_ref, held = refs[0], refs[1:4]
        hid, hidden, inter, scale, upper, grad, turned, normed, weighted, g_before, grams = refs[4:]

        @pl.when(place_ref[1] == 1)
        def _():
            layers = streams_of(place_ref[0], matrices, held, [(True, True), (True, True)], 0)
            (up0, down0), (up1, down1) = layers
            for stream in (up0, down0, up1):
                stream.start()
            mix_forward(small_ref, 0, acts_ref, inter.at[0], scale.at[0], normed, grams, count)
            up_product(normed, up0.held, hidden, hid, up0.wait)
            down_product(hidden, down0.held, acts_ref, upper, down0.wait)
            mix_forward(small_ref, 1, upper, inter.at[1], scale.at[1], normed, grams, count)

            def masked(columns):
                before = dot(normed[...], up1.held[:, columns])
                opened = jnp.maximum(before, 0.0).astype(jnp.bfloat16).T
                g_before[columns, :] = opened_only(opened, ghid_ref[columns, :].astype(jnp.float32))

            over_tiles(hidden_width, hidden_tile(hidden_width), 1, up1.wait, masked)
            up_back(g_before, up1.held, weighted, no_wait)
            mix_backward(small_ref, 1, top_ref, upper, inter.at[1], scale.at[1], weighted, grad, count)
            turn(grad, turned)
            down_back(turned, down0.held, hid, g_before, no_wait)
            up_back(g_before, up0.held, weighted, no_wait)
            mix_backward(small_ref, 0, grad, acts_ref, inter.at[0], scale.at[0], weighted, out_ref, count)

    return pl.pallas_call(
        kernel,
        out_shape=jax.ShapeDtypeStruct(acts.shape, jnp.bfloat16),
        in_specs=[whole(pltpu.SMEM)] + [whole()] * 3 + weight_specs(),
        out_specs=whole(),
        scratch_shapes=weight_scratch(model_width, hidden_width)
        + [
            pltpu.VMEM((hidden_width, batch), jnp.bfloat16),
            pltpu.VMEM((batch, hidden_width), jnp.bfloat16),
            pltpu.VMEM((2, batch, model_width), jnp.float32),
            pltpu.VMEM((2, batch, width), jnp.float32),
            pltpu.VMEM((batch, model_width), jnp.bfloat16),
            pltpu.VMEM((batch, model_width), jnp.bfloat16),
            pltpu.VMEM((model_width, batch), jnp.bfloat16),
            pltpu.VMEM((batch, model_width), jnp.bfloat16),
            pltpu.VMEM((batch, model_width), jnp.float32),
            pltpu.VMEM((hidden_width, batch), jnp.bfloat16),
            gram_scratch(batch, count),
        ],
        compiler_params=stage_params(),
        cost_estimate=stage_cost(6, batch, model_width, hidden_width),
        name="turn_stage",
    )(place, acts, top, g_hidden, weights[0], *map(in_hbm, weights[1:]), *ready)


def backward_stage(place, grad, saved, weights, ready, count):
    batch, model_width = grad.shape
    hidden_width = weights[1].shape[1]

    def kernel(place_ref, grad_ref, hid, inter, scale, kept, small_ref, *refs):
        matrices, refs = refs[:6], refs[6:]
        out_ref, held = refs[0], refs[1:4]
        middle, turned, weighted, g_before = refs[4:]

        @pl.when(place_ref[1] == 1)
        def _():
            layers = streams_of(place_ref[0], matrices, held, [(False, False), (False, False)], 1)
            for up, down in reversed(layers):
                down.start()
                up.start()
            for layer, given, to in ((1, grad_ref, middle), (0, middle, out_ref)):
                up, down = layers[layer]
                turn(given, turned)
                down_back(turned, down.held, hid.at[layer], g_before, down.wait)
                up_back(g_before, up.held, weighted, up.wait)
                mix_backward(
                    small_ref, layer, given, kept.at[layer], inter.at[layer], scale.at[layer],
                    weighted, to, count,
                )

    return pl.pallas_call(
        kernel,
        out_shape=jax.ShapeDtypeStruct(grad.shape, jnp.bfloat16),
        in_specs=[whole(pltpu.SMEM)] + [whole()] * 5 + weight_specs(),
        out_specs=whole(),
        scratch_shapes=weight_scratch(model_width, hidden_width)
        + [
            pltpu.VMEM((batch, model_width), jnp.bfloat16),
            pltpu.VMEM((model_width, batch), jnp.bfloat16),
            pltpu.VMEM((batch, model_width), jnp.float32),
            pltpu.VMEM((hidden_width, batch), jnp.bfloat16),
        ],
        compiler_params=stage_params(),
        cost_estimate=stage_cost(4, batch, model_width, hidden_width),
        name="backward_stage",
    )(place, grad, *saved, weights[0], *map(in_hbm, weights[1:]), *ready)


def swapped(value, section_count):
    return lax.ppermute(value, "section", [(s, s ^ 1) for s in range(section_count)])


def moved(value, from_stage, to_stage):
    pairs = [(2 * from_stage + core, 2 * to_stage + core) for core in (0, 1)]
    return lax.ppermute(value, "section", pairs)


def mirror(value):
    along = lax.axis_size("table")
    return lax.ppermute(value, "table", [(t, (t + along // 2) % along) for t in range(along)])


def swap_in_half(value):
    along = lax.axis_size("table")
    half = along // 2
    groups = [
        [s * along + h * half + t for s in range(lax.axis_size("section")) for t in range(half)]
        for h in (0, 1)
    ]
    return lax.all_to_all(
        value, TABLE_AXES, split_axis=0, concat_axis=0, axis_index_groups=groups, tiled=True
    )


def near_first(per_asker, my_half):
    sections = lax.axis_size("section")
    half = lax.axis_size("table") // 2
    split = per_asker.reshape((sections, 2, half) + per_asker.shape[1:])
    near = lax.dynamic_index_in_dim(split, my_half, 1, keepdims=False)
    far = lax.dynamic_index_in_dim(split, 1 - my_half, 1, keepdims=False)
    return jnp.stack([near, far], axis=2).reshape((sections * half, 2) + per_asker.shape[1:])


def after(value, earlier):
    return lax.optimization_barrier((value, earlier))[0]


def per_device(
    emb_table,
    lcb_weight,
    fm_proj,
    norm_gain,
    w_up,
    w_down,
    top_grad,
    lookup_slot,
    wanted_rows,
    row_counts,
):
    section_count = lax.axis_size("section")
    along = lax.axis_size("table")
    half = along // 2
    near_owners = section_count * half
    stages = section_count // 2
    stage = lax.axis_index("section") // 2
    core = lax.axis_index("section") % 2
    my_half = lax.axis_index("table") // half
    cap = wanted_rows.shape[2]
    rows, embed_width = emb_table.shape
    embed_count = lcb_weight.shape[0]
    look_dev = lookup_slot.shape[1]
    model_width = top_grad.shape[3]

    own_slots = lookup_slot[0]
    mirror_slots = mirror(own_slots)
    small = jnp.concatenate([fm_proj[0], norm_gain[0].reshape(embed_count, -1)], axis=0)
    other_up = swapped(w_up[0], section_count)
    other_down = swapped(w_down[0], section_count)
    other_small = swapped(small, section_count)

    picked = near_first(wanted_rows[0], my_half)
    outgoing = pick_rows(emb_table, wanted_rows[0], my_half)
    sent = after(outgoing, mirror_slots).reshape(near_owners, 2, cap, embed_width)
    fetched = swap_in_half(sent)

    def spread_of(slots):
        owner, column = slots // cap, slots % cap
        place = owner % along
        near = jnp.where(place // half == my_half, owner // along * half + place % half, near_owners)
        return spread_weights(near * cap + column, lcb_weight, near_owners, cap)

    spread_far, kept_far = spread_of(mirror_slots)
    spread_near, kept_near = spread_of(own_slots)
    smalls = jnp.stack(
        [jnp.where(core == 0, small, other_small), jnp.where(core == 0, other_small, small)]
    )
    weights = [smalls, w_up[0], other_up, w_down[0], other_down]
    spread_far, spread_near = lax.optimization_barrier((spread_far, spread_near))
    far_part = mirror(compress(spread_far, fetched, 1, embed_count, jnp.bfloat16))
    near_part = compress(spread_near, fetched, 0, embed_count, jnp.float32)

    def at(tick):
        is_last = (stage == stages - 1) & (tick == 0)
        return jnp.stack([core, stage == tick, is_last]).astype(jnp.int32)

    first_up = hold_matrix(after(at(0), near_part), 0, weights[1], weights[2])
    far_part = after(far_part, first_up)
    lead = (near_part + far_part.astype(jnp.float32)).astype(jnp.bfloat16)
    first_down = hold_matrix(after(at(0), lead), 0, weights[3], weights[4])
    pieces = [lead] + [moved(lead, s, 0) for s in range(1, stages)]
    top = top_grad.reshape(stages, 2, look_dev, model_width)
    top = lax.dynamic_index_in_dim(top, core, 1, keepdims=False).reshape(-1, model_width)

    saved = None
    for tick in range(stages - 1):
        place = at(tick)
        ready = [first_up, first_down] if tick == 0 else hold_layer(place, 0, weights, out)
        out, fresh, product = forward_stage(place, pieces, top, weights, ready, embed_count)
        if saved is None:
            saved, g_hidden = fresh, product
        else:
            saved = [jnp.where(stage == tick, new, old) for new, old in zip(fresh, saved)]
        pieces = [moved(out, tick, tick + 1)]
    place = at(stages - 1)
    ready = hold_layer(place, 0, weights, out)
    grad = turn_stage(place, pieces[0], top, g_hidden, weights, ready, embed_count)
    for tick in reversed(range(stages - 1)):
        place = at(tick)
        ready = hold_layer(place, 1, weights, grad)
        grad = moved(grad, tick + 1, tick)
        grad = backward_stage(place, grad, saved, weights, ready, embed_count)

    own_grad = grad[:look_dev]
    for s in range(1, stages):
        piece = grad[s * look_dev : (s + 1) * look_dev]
        own_grad = jnp.where(stage == s, moved(piece, 0, s), own_grad)
    mirror_grad = mirror(own_grad)

    near_grad = expand(kept_near, own_grad, embed_count)
    slot_grad = expand(kept_far, mirror_grad, embed_count, near_grad)
    returned = swap_in_half(slot_grad)
    live_slots = jnp.arange(cap) < near_first(row_counts[0], my_half)[..., None]
    targets = jnp.where(live_slots, picked, rows).reshape(-1)
    return add_rows(targets, returned.reshape(-1, embed_width), outgoing, rows, cap)


def solution(mesh):
    in_specs = (
        P(("section", "table"), None),
        P(),
        P("section", None, None),
        P("section", None),
        P("section", None, None),
        P("section", None, None),
        P("table", None, None, None),
        P("table", "section", None),
        P(("section", "table"), None, None),
        P(("section", "table"), None),
    )
    out_specs = P(("section", "table"), None)
    return jax.shard_map(
        per_device, mesh=mesh, in_specs=in_specs, out_specs=out_specs, check_vma=False
    )
```

```python
import jax
import jax.numpy as jnp
from jax import lax
from jax.experimental import pallas as pl
from jax.experimental.pallas import tpu as pltpu
from jax.sharding import PartitionSpec as P

EPSILON = 1e-05
DECAY_WEIGHT = 0.5
VMEM_LIMIT = 28 * 1024 * 1024
UNROLL = 32


def whole(memory_space=pltpu.VMEM):
    return pl.BlockSpec(memory_space=memory_space)


def in_hbm(value):
    return pltpu.with_memory_space_constraint(value, pltpu.HBM)


def params():
    return pltpu.CompilerParams(vmem_limit_bytes=VMEM_LIMIT)


def tiles_of(count, most):
    return max(step for step in range(1, most + 1) if count % step == 0)


def pick_rows(emb_table, wanted, my_half):
    rows, width = emb_table.shape
    askers, cap = wanted.shape
    half = lax.axis_size("table") // 2
    together = tiles_of(askers, 8)
    pieces = 4

    def kernel(half_ref, wanted_ref, table_ref, out_ref, narrow, wide, lines, sems):
        copies = []
        for piece in range(pieces):
            cut = pl.ds(piece * (rows // pieces), rows // pieces)
            copies.append(pltpu.make_async_copy(table_ref.at[cut], narrow.at[cut], sems.at[piece]))
            copies[-1].start()
        for piece in range(pieces):
            cut = pl.ds(piece * (rows // pieces), rows // pieces)
            copies[piece].wait()
            wide[cut, :] = narrow[cut, :].astype(jnp.float32)

        def fill(part, carry):
            def one(line, inner):
                at = part * together + line
                device, is_mirror = at // 2, at % 2
                side = jnp.where(is_mirror == 0, half_ref[0], 1 - half_ref[0])
                asker = (device // half * 2 + side) * half + device % half
                first = pl.multiple_of(line * cap, cap)
                for lane in range(cap):
                    row = wanted_ref[asker * cap + lane]
                    lines[pl.ds(first + lane, 1), :] = wide[pl.ds(row, 1), :]
                return inner

            lax.fori_loop(0, together, one, 0)
            base = pl.multiple_of(part * (together * cap), together * cap)
            out_ref[pl.ds(base, together * cap), :] = lines[...].astype(out_ref.dtype)
            return carry

        lax.fori_loop(0, askers // together, fill, 0)

    return pl.pallas_call(
        kernel,
        out_shape=jax.ShapeDtypeStruct((askers * cap, width), emb_table.dtype),
        in_specs=[whole(pltpu.SMEM), whole(pltpu.SMEM), whole(pltpu.HBM)],
        out_specs=whole(),
        scratch_shapes=[
            pltpu.VMEM((rows, width), emb_table.dtype),
            pltpu.VMEM((rows, width), jnp.float32),
            pltpu.VMEM((together * cap, width), jnp.float32),
            pltpu.SemaphoreType.DMA((pieces,)),
        ],
        compiler_params=params(),
        name="pick_rows",
    )(my_half.astype(jnp.int32).reshape(1), wanted.reshape(-1), in_hbm(emb_table))


def spread_weights(codes, lcb_weight, owners, cap):
    samples, feature_count = codes.shape
    embed_count = lcb_weight.shape[0]
    group = tiles_of(samples, 16)

    def kernel(codes_ref, lcb_ref, out_ref, kept_ref):
        lcb = lcb_ref[...].astype(jnp.float32)
        owner_of = lax.broadcasted_iota(jnp.int32, (owners, embed_count, feature_count), 0)
        column_of = lax.broadcasted_iota(jnp.int32, (cap, feature_count), 0)
        for pair in range(0, group, 2):
            made = []
            for sample in (pair, pair + 1):
                slots = codes_ref[sample : sample + 1, :]
                owner = lax.div(slots, cap)
                column = slots - owner * cap
                left = jnp.where(owner_of == owner[None], lcb[None], 0.0)
                left = left.reshape(owners * embed_count, feature_count).astype(jnp.bfloat16)
                right = jnp.where(column_of == column, 1.0, 0.0).astype(jnp.bfloat16)
                both = lax.dot_general(
                    left, right, (((1,), (1,)), ((), ())), preferred_element_type=jnp.float32
                )
                made.append(both.reshape(owners, embed_count, cap))
            rows = pl.ds(pair * embed_count, 2 * embed_count)
            joined = jnp.concatenate(made, axis=1).astype(out_ref.dtype)
            out_ref[:, rows, :] = joined
            kept_ref[:, rows, :] = joined

    return pl.pallas_call(
        kernel,
        out_shape=[
            pltpu.VMEM((owners, samples * embed_count, cap), jnp.bfloat16),
            pltpu.HBM((owners, samples * embed_count, cap), jnp.bfloat16),
        ],
        grid=(samples // group,),
        in_specs=[
            pl.BlockSpec((group, feature_count), lambda i: (i, 0)),
            pl.BlockSpec((embed_count, feature_count), lambda i: (0, 0)),
        ],
        out_specs=[pl.BlockSpec((owners, group * embed_count, cap), lambda i: (0, i, 0))] * 2,
        compiler_params=params(),
        cost_estimate=pl.CostEstimate(
            flops=2 * samples * owners * embed_count * feature_count * cap,
            bytes_accessed=2 * owners * samples * embed_count * cap,
            transcendentals=0,
        ),
        name="spread_weights",
    )(codes, lcb_weight)


def compress(spread, fetched, view, embed_count, kind):
    owners, lines, cap = spread.shape
    width = fetched.shape[3]
    samples = lines // embed_count
    part = tiles_of(owners, 8)
    steps = owners // part

    def kernel(spread_ref, rows_ref, out_ref, total):
        total[...] = jnp.zeros_like(total)

        def body(step, carry):
            first = step * part
            left = jnp.concatenate([spread_ref[first + o] for o in range(part)], axis=1)
            right = jnp.concatenate([rows_ref[first + o, view] for o in range(part)], axis=0)
            total[...] += jnp.dot(left, right, preferred_element_type=jnp.float32)
            return carry

        lax.fori_loop(0, steps, body, 0)
        for k in range(embed_count):
            columns = slice(k * width, (k + 1) * width)
            piece = total[pl.ds(k, samples, stride=embed_count), :]
            out_ref[:, columns] = piece.astype(out_ref.dtype)

    return pl.pallas_call(
        kernel,
        out_shape=jax.ShapeDtypeStruct((samples, embed_count * width), kind),
        in_specs=[whole(), whole()],
        out_specs=whole(),
        scratch_shapes=[pltpu.VMEM((lines, width), jnp.float32)],
        compiler_params=params(),
        name="compress",
    )(spread, fetched)


def expand(spread, lead_grad, embed_count, near=None):
    owners, lines, cap = spread.shape
    samples = lines // embed_count
    width = lead_grad.shape[1] // embed_count
    part = tiles_of(owners, 8)
    extra = [] if near is None else [near]

    def kernel(spread_ref, grad_ref, *refs):
        near_refs, (out_ref, tall, turned) = refs[: len(extra)], refs[len(extra) :]
        for k in range(embed_count):
            piece = grad_ref[:, k * width : (k + 1) * width].astype(jnp.float32)
            tall[pl.ds(k, samples, stride=embed_count), :] = piece
        turned[...] = tall[...].T.astype(jnp.bfloat16)

        def body(step, carry):
            first = step * part
            right = jnp.concatenate([spread_ref[first + o] for o in range(part)], axis=1)
            term = jnp.dot(turned[...], right, preferred_element_type=jnp.float32)
            piece = term.T.astype(out_ref.dtype).reshape(part, cap, width)
            if near_refs:
                for o in range(part):
                    out_ref[first + o, 0] = near_refs[0][first + o]
                    out_ref[first + o, 1] = piece[o]
            else:
                out_ref[tile_at(step, part)] = piece
            return carry

        lax.fori_loop(0, owners // part, body, 0)

    views = () if near is None else (2,)
    return pl.pallas_call(
        kernel,
        out_shape=jax.ShapeDtypeStruct((owners,) + views + (cap, width), jnp.bfloat16),
        in_specs=[whole()] * (2 + len(extra)),
        out_specs=whole(),
        scratch_shapes=[
            pltpu.VMEM((lines, width), jnp.float32),
            pltpu.VMEM((width, lines), jnp.bfloat16),
        ],
        compiler_params=params(),
        name="expand",
    )(spread, lead_grad, *extra)


def add_rows(targets, returned, outgoing, rows, cap):
    count, width = returned.shape
    pair = 2 * cap

    def kernel(targets_ref, back_ref, sent_ref, out_ref, total, second, terms, sem):
        total[...] = jnp.zeros_like(total)
        second[...] = jnp.zeros_like(second)

        def body(step, carry):
            base = pl.multiple_of(step * pair, pair)
            lines = pl.ds(base, pair)
            terms[...] = back_ref[lines, :].astype(jnp.float32) + DECAY_WEIGHT * sent_ref[
                lines, :
            ].astype(jnp.float32)
            for first in range(0, cap, UNROLL):
                lanes = range(first, first + UNROLL)
                places = [targets_ref[base + lane] for lane in lanes]
                others = [targets_ref[base + cap + lane] for lane in lanes]
                sums = [
                    total[pl.ds(place, 1), :] + terms[lane : lane + 1, :]
                    for place, lane in zip(places, lanes)
                ]
                other_sums = [
                    second[pl.ds(place, 1), :] + terms[cap + lane : cap + lane + 1, :]
                    for place, lane in zip(others, lanes)
                ]
                for place, value in zip(places, sums):
                    total[pl.ds(place, 1), :] = value
                for place, value in zip(others, other_sums):
                    second[pl.ds(place, 1), :] = value
            return carry

        lax.fori_loop(0, count // pair, body, 0)
        part = rows // 4
        copies = []
        for piece in range(4):
            cut = pl.ds(piece * part, part)
            total[cut, :] = total[cut, :] + second[cut, :]
            copies.append(pltpu.make_async_copy(total.at[cut, :], out_ref.at[cut, :], sem.at[piece]))
            copies[-1].start()
        for copy in copies:
            copy.wait()

    return pl.pallas_call(
        kernel,
        out_shape=jax.ShapeDtypeStruct((rows, width), jnp.float32),
        in_specs=[whole(pltpu.SMEM), whole(), whole()],
        out_specs=whole(pl.ANY),
        scratch_shapes=[
            pltpu.VMEM((rows + 8, width), jnp.float32),
            pltpu.VMEM((rows + 8, width), jnp.float32),
            pltpu.VMEM((pair, width), jnp.float32),
            pltpu.SemaphoreType.DMA((4,)),
        ],
        compiler_params=params(),
        name="add_rows",
    )(targets, returned, outgoing)


GROUP = 16
TABLE_AXES = ("section", "table")
STAGE_LIMIT = 28 * 1024 * 1024
NT = (((1,), (1,)), ((), ()))


def dot_nt(left, right):
    return lax.dot_general(left, right, NT, preferred_element_type=jnp.float32)


def dot(left, right):
    return jnp.dot(left, right, preferred_element_type=jnp.float32)


def halves(value):
    high = value.astype(jnp.bfloat16)
    low = (value - high.astype(jnp.float32)).astype(jnp.bfloat16)
    return jnp.concatenate([high, low], axis=1)


def same_sample(count):
    first = lax.broadcasted_iota(jnp.int32, (count * GROUP, count * GROUP), 0)
    second = lax.broadcasted_iota(jnp.int32, (count * GROUP, count * GROUP), 1)
    return (first & (GROUP - 1)) == (second & (GROUP - 1))


def stacked(ref, rows, count, width):
    return jnp.concatenate([ref[rows, k * width : (k + 1) * width] for k in range(count)], axis=0)


def repeated(proj):
    count, width = proj.shape
    lines = [jnp.broadcast_to(proj[k : k + 1, :], (GROUP, width)) for k in range(count)]
    return jnp.concatenate(lines, axis=0).astype(jnp.bfloat16)


def mix_forward(small, layer, acts, inter, scale, normed, grams, count):
    batch, model_width = acts.shape
    width = model_width // count
    both = small[layer].astype(jnp.float32)
    proj = repeated(both[:count])
    keep = same_sample(count)
    size = GROUP * count
    for group in range(batch // GROUP):
        block = stacked(acts, pl.ds(group * GROUP, GROUP), count, width)
        gram = jnp.where(keep, dot_nt(block, block), 0.0)
        grams[group * size : (group + 1) * size, :] = halves(gram)
    mixed = dot(grams[...], jnp.concatenate([proj, proj], axis=0))
    for group in range(batch // GROUP):
        rows = pl.ds(group * GROUP, GROUP)
        start = group * size
        parts = [mixed[start + k * GROUP : start + (k + 1) * GROUP] for k in range(count)]
        squares = sum(part * part for part in parts)
        mean = jnp.sum(squares, axis=1, keepdims=True) * (1.0 / model_width)
        inv = lax.rsqrt(mean + EPSILON)
        scale[rows, :] = jnp.broadcast_to(inv, (GROUP, width))
        for k in range(count):
            columns = slice(k * width, (k + 1) * width)
            inter[rows, columns] = parts[k]
            gain = both[count + k : count + k + 1]
            normed[rows, columns] = (parts[k] * inv * gain).astype(jnp.bfloat16)


def gram_scratch(batch, count):
    return pltpu.VMEM((batch * count, 2 * GROUP * count), jnp.bfloat16)


def hidden_tile(hidden_width):
    return min(hidden_width, 1024)


def model_tile(model_width):
    return min(model_width, 512)


def tile_at(step, size):
    return pl.ds(pl.multiple_of(step * size, size), size)


class Stream:
    def __init__(self, mine, own, other, held, sems, axis, size):
        self.mine, self.own, self.other, self.held, self.sems = mine, own, other, held, sems
        self.axis, self.size = axis, size
        self.tiles = own.shape[axis] // size

    def copy(self, source, step):
        cut = tile_at(step, self.size)
        index = (slice(None), cut) if self.axis == 1 else (cut, slice(None))
        return pltpu.make_async_copy(source.at[index], self.held.at[index], self.sems.at[step])

    def start(self):
        @pl.when(self.mine)
        def _():
            for step in range(self.tiles):
                self.copy(self.own, step).start()

        @pl.when(jnp.logical_not(self.mine))
        def _():
            for step in range(self.tiles):
                self.copy(self.other, step).start()

    def wait(self, step):
        self.copy(self.own, step).wait()


def no_wait(step):
    return None


class Held:
    def __init__(self, held):
        self.held = held
        self.wait = no_wait

    def start(self):
        return None


def over_tiles(total, tile, many, wait, work):
    many = min(many, total // tile)

    def body(step, carry):
        for inner in range(many):
            wait(step * many + inner)
        work(tile_at(step, many * tile))
        return carry

    lax.fori_loop(0, total // (many * tile), body, 0)


def up_product(normed, w_up, hidden, turned, wait, many=1):
    def work(columns):
        opened = jnp.maximum(dot(normed[...], w_up[:, columns]), 0.0).astype(jnp.bfloat16)
        hidden[:, columns] = opened
        if turned is not None:
            turned[columns, :] = opened.T

    width = hidden.shape[1]
    over_tiles(width, hidden_tile(width), many, wait, work)


def down_product(hidden, w_down, acts, out, wait, many=1):
    def work(columns):
        term = dot(hidden[...], w_down[:, columns])
        out[:, columns] = (acts[:, columns].astype(jnp.float32) + term).astype(jnp.bfloat16)

    width = out.shape[1]
    over_tiles(width, model_tile(width), many, wait, work)


def turn(rows, turned):
    turned[...] = rows[...].T


def opened_only(hidden, grad):
    return jnp.where(hidden.astype(jnp.float32) > 0.0, grad, 0.0).astype(jnp.bfloat16)


def down_back(grad, w_down, hidden, out, wait, many=1):
    def work(lines):
        g_hidden = dot(w_down[lines, :], grad[...])
        if hidden is not None:
            out[lines, :] = opened_only(hidden[lines, :], g_hidden)
        else:
            out[lines, :] = g_hidden.astype(jnp.bfloat16)

    width = out.shape[0]
    over_tiles(width, hidden_tile(width), many, wait, work)


def up_back(g_before, w_up, weighted, wait, many=1):
    def work(columns):
        weighted[:, columns] = dot(w_up[columns, :], g_before[...]).T

    width = weighted.shape[1]
    over_tiles(width, model_tile(width), many, wait, work)


def mix_backward(small, layer, grad, acts, inter, scale, weighted, out, count):
    batch, model_width = acts.shape
    width = model_width // count
    both = small[layer].astype(jnp.float32)
    proj = repeated(both[:count])
    keep = same_sample(count)
    for start in range(0, batch, GROUP):
        rows = pl.ds(start, GROUP)
        columns = [slice(k * width, (k + 1) * width) for k in range(count)]
        gained = [weighted[rows, columns[k]] * both[count + k : count + k + 1] for k in range(count)]
        shared = sum(gained[k] * inter[rows, columns[k]] for k in range(count))
        mean = jnp.sum(shared, axis=1, keepdims=True) * (1.0 / model_width)
        inv = scale[rows, 0:1]
        pull = inv * inv * mean
        parts = [
            (inv * (gained[k] - inter[rows, columns[k]] * pull)).astype(jnp.bfloat16)
            for k in range(count)
        ]
        block = stacked(acts, rows, count, width)
        g_inter = jnp.concatenate(parts, axis=0)
        left = jnp.concatenate([g_inter, proj], axis=1)
        right = jnp.concatenate([proj, g_inter], axis=1)
        links = jnp.where(keep, dot_nt(left, right), 0.0)
        g_acts = dot(halves(links), jnp.concatenate([block, block], axis=0))
        for k in range(count):
            piece = g_acts[k * GROUP : (k + 1) * GROUP] + grad[rows, columns[k]].astype(jnp.float32)
            out[rows, columns[k]] = piece.astype(jnp.bfloat16)


def saved_shapes(batch, model_width, hidden_width, width):
    return [
        jax.ShapeDtypeStruct((2, batch, hidden_width), jnp.bfloat16),
        jax.ShapeDtypeStruct((2, batch, model_width), jnp.float32),
        jax.ShapeDtypeStruct((2, batch, width), jnp.float32),
        jax.ShapeDtypeStruct((2, batch, model_width), jnp.bfloat16),
    ]


def weight_specs():
    return [whole()] + [whole(pltpu.HBM)] * 4 + [whole()] * 2


def weight_scratch(model_width, hidden_width):
    tiles = max(hidden_width // hidden_tile(hidden_width), model_width // model_tile(model_width))
    return [
        pltpu.VMEM((model_width, hidden_width), jnp.bfloat16),
        pltpu.VMEM((hidden_width, model_width), jnp.bfloat16),
        pltpu.SemaphoreType.DMA((2, tiles)),
    ]


def streams_of(core, weights, held, forward, ready):
    own_up, other_up, own_down, other_down, ready_up, ready_down = weights
    held_up, held_down, sems = held
    model_width, hidden_width = own_up.shape
    wide, narrow = hidden_tile(hidden_width), model_tile(model_width)
    made = []
    for layer in (0, 1):
        if layer == ready:
            made.append((Held(ready_up), Held(ready_down)))
            continue
        mine = core == layer
        up_forward, down_forward = forward[layer]
        up_cut = (1, wide) if up_forward else (0, narrow)
        down_cut = (1, narrow) if down_forward else (0, wide)
        made.append(
            (
                Stream(mine, own_up, other_up, held_up, sems.at[0], *up_cut),
                Stream(mine, own_down, other_down, held_down, sems.at[1], *down_cut),
            )
        )
    return made


def hold_matrix(place, layer, own, other):
    pieces = 8
    part = own.shape[0] // pieces

    def kernel(place_ref, own_ref, other_ref, out_ref, sems):
        def load(source):
            copies = []
            for piece in range(pieces):
                cut = pl.ds(piece * part, part)
                copies.append(pltpu.make_async_copy(source.at[cut], out_ref.at[cut], sems.at[piece]))
                copies[-1].start()
            for copy in copies:
                copy.wait()

        @pl.when((place_ref[1] == 1) & (place_ref[0] == layer))
        def _():
            load(own_ref)

        @pl.when((place_ref[1] == 1) & (place_ref[0] != layer))
        def _():
            load(other_ref)

    return pl.pallas_call(
        kernel,
        out_shape=pltpu.VMEM(own.shape, own.dtype),
        in_specs=[whole(pltpu.SMEM)] + [whole(pltpu.HBM)] * 2,
        out_specs=whole(),
        scratch_shapes=[pltpu.SemaphoreType.DMA((pieces,))],
        compiler_params=pltpu.CompilerParams(vmem_limit_bytes=4 * 1024 * 1024),
        name="hold_matrix",
    )(place, in_hbm(own), in_hbm(other))


def hold_layer(place, layer, weights, earlier):
    small, own_up, other_up, own_down, other_down = weights
    place = after(place, earlier)
    return [
        hold_matrix(place, layer, own_up, other_up),
        hold_matrix(place, layer, own_down, other_down),
    ]


def stage_cost(products, batch, model_width, hidden_width):
    return pl.CostEstimate(
        flops=2 * products * batch * model_width * hidden_width, bytes_accessed=1 << 20, transcendentals=0
    )


def stage_params():
    return pltpu.CompilerParams(vmem_limit_bytes=STAGE_LIMIT)


def forward_stage(place, pieces, top, weights, ready, count):
    batch, model_width = top.shape
    hidden_width = weights[1].shape[1]
    width = model_width // count

    def kernel(place_ref, *refs):
        piece_refs, (top_ref, small_ref), refs = refs[: len(pieces)], refs[len(pieces) :][:2], refs[len(pieces) + 2 :]
        matrices, refs = refs[:6], refs[6:]
        out_ref, hid, inter, scale, kept, g_hidden = refs[:6]
        held, (normed, top_turned, grams) = refs[6:9], refs[9:]
        core = place_ref[0]

        @pl.when(place_ref[1] == 1)
        def _():
            layers = streams_of(core, matrices, held, [(True, True), (True, True)], 0)
            for up, down in layers:
                up.start()
                down.start()
            start = 0
            for piece in piece_refs:
                kept[0, start : start + piece.shape[0], :] = piece[...]
                start += piece.shape[0]
            for layer, (up, down) in enumerate(layers):
                mix_forward(
                    small_ref, layer, kept.at[layer], inter.at[layer], scale.at[layer], normed, grams, count
                )
                up_product(normed, up.held, hid.at[layer], None, up.wait)
                to = kept.at[1] if layer == 0 else out_ref
                down_product(hid.at[layer], down.held, kept.at[layer], to, down.wait)

        @pl.when(place_ref[2] == 1)
        def _():
            layers = streams_of(core, matrices, held, [(True, True), (True, False)], 0)
            down = layers[1][1]
            down.start()
            turn(top_ref, top_turned)
            down_back(top_turned, down.held, None, g_hidden, down.wait)

    out = pl.pallas_call(
        kernel,
        out_shape=[jax.ShapeDtypeStruct(top.shape, jnp.bfloat16)]
        + saved_shapes(batch, model_width, hidden_width, width)
        + [jax.ShapeDtypeStruct((hidden_width, batch), jnp.bfloat16)],
        in_specs=[whole(pltpu.SMEM)] + [whole()] * (len(pieces) + 1) + weight_specs(),
        out_specs=[whole()] * 6,
        scratch_shapes=weight_scratch(model_width, hidden_width)
        + [
            pltpu.VMEM((batch, model_width), jnp.bfloat16),
            pltpu.VMEM((model_width, batch), jnp.bfloat16),
            gram_scratch(batch, count),
        ],
        compiler_params=stage_params(),
        cost_estimate=stage_cost(4, batch, model_width, hidden_width),
        name="forward_stage",
    )(place, *pieces, top, weights[0], *map(in_hbm, weights[1:]), *ready)
    return out[0], out[1:5], out[5]


def turn_hidden(active, hidden):
    layers, batch, hidden_width = hidden.shape

    def kernel(active_ref, hidden_ref, out_ref):
        @pl.when(active_ref[0] == 1)
        def _():
            tile = hidden_tile(hidden_width)

            def body(step, carry):
                for layer in range(layers):
                    out_ref[layer, tile_at(step, tile), :] = hidden_ref[layer, :, tile_at(step, tile)].T
                return carry

            lax.fori_loop(0, hidden_width // tile, body, 0)

    return pl.pallas_call(
        kernel,
        out_shape=jax.ShapeDtypeStruct((layers, hidden_width, batch), hidden.dtype),
        in_specs=[whole(pltpu.SMEM), whole()],
        out_specs=whole(),
        compiler_params=pltpu.CompilerParams(vmem_limit_bytes=8 * 1024 * 1024),
        name="turn_hidden",
    )(active, hidden)


def turn_stage(place, acts, top, g_hidden, weights, ready, count):
    batch, model_width = acts.shape
    hidden_width = weights[1].shape[1]
    width = model_width // count

    def kernel(place_ref, acts_ref, top_ref, ghid_ref, small_ref, *refs):
        matrices, refs = refs[:6], refs[6:]
        out_ref, held = refs[0], refs[1:4]
        hid, hidden, inter, scale, upper, grad, turned, normed, weighted, g_before, grams = refs[4:]

        @pl.when(place_ref[1] == 1)
        def _():
            layers = streams_of(place_ref[0], matrices, held, [(True, True), (True, True)], 0)
            (up0, down0), (up1, down1) = layers
            for stream in (up0, down0, up1):
                stream.start()
            mix_forward(small_ref, 0, acts_ref, inter.at[0], scale.at[0], normed, grams, count)
            up_product(normed, up0.held, hidden, hid, up0.wait)
            down_product(hidden, down0.held, acts_ref, upper, down0.wait)
            mix_forward(small_ref, 1, upper, inter.at[1], scale.at[1], normed, grams, count)

            def masked(columns):
                before = dot(normed[...], up1.held[:, columns])
                opened = jnp.maximum(before, 0.0).astype(jnp.bfloat16).T
                g_before[columns, :] = opened_only(opened, ghid_ref[columns, :].astype(jnp.float32))

            over_tiles(hidden_width, hidden_tile(hidden_width), 1, up1.wait, masked)
            up_back(g_before, up1.held, weighted, no_wait)
            mix_backward(small_ref, 1, top_ref, upper, inter.at[1], scale.at[1], weighted, grad, count)
            turn(grad, turned)
            down_back(turned, down0.held, hid, g_before, no_wait)
            up_back(g_before, up0.held, weighted, no_wait)
            mix_backward(small_ref, 0, grad, acts_ref, inter.at[0], scale.at[0], weighted, out_ref, count)

    return pl.pallas_call(
        kernel,
        out_shape=jax.ShapeDtypeStruct(acts.shape, jnp.bfloat16),
        in_specs=[whole(pltpu.SMEM)] + [whole()] * 3 + weight_specs(),
        out_specs=whole(),
        scratch_shapes=weight_scratch(model_width, hidden_width)
        + [
            pltpu.VMEM((hidden_width, batch), jnp.bfloat16),
            pltpu.VMEM((batch, hidden_width), jnp.bfloat16),
            pltpu.VMEM((2, batch, model_width), jnp.float32),
            pltpu.VMEM((2, batch, width), jnp.float32),
            pltpu.VMEM((batch, model_width), jnp.bfloat16),
            pltpu.VMEM((batch, model_width), jnp.bfloat16),
            pltpu.VMEM((model_width, batch), jnp.bfloat16),
            pltpu.VMEM((batch, model_width), jnp.bfloat16),
            pltpu.VMEM((batch, model_width), jnp.float32),
            pltpu.VMEM((hidden_width, batch), jnp.bfloat16),
            gram_scratch(batch, count),
        ],
        compiler_params=stage_params(),
        cost_estimate=stage_cost(6, batch, model_width, hidden_width),
        name="turn_stage",
    )(place, acts, top, g_hidden, weights[0], *map(in_hbm, weights[1:]), *ready)


def backward_stage(place, grad, saved, weights, ready, count):
    batch, model_width = grad.shape
    hidden_width = weights[1].shape[1]

    def kernel(place_ref, grad_ref, hid, inter, scale, kept, small_ref, *refs):
        matrices, refs = refs[:6], refs[6:]
        out_ref, held = refs[0], refs[1:4]
        middle, turned, weighted, g_before = refs[4:]

        @pl.when(place_ref[1] == 1)
        def _():
            layers = streams_of(place_ref[0], matrices, held, [(False, False), (False, False)], 1)
            for up, down in reversed(layers):
                down.start()
                up.start()
            for layer, given, to in ((1, grad_ref, middle), (0, middle, out_ref)):
                up, down = layers[layer]
                turn(given, turned)
                down_back(turned, down.held, hid.at[layer], g_before, down.wait)
                up_back(g_before, up.held, weighted, up.wait)
                mix_backward(
                    small_ref, layer, given, kept.at[layer], inter.at[layer], scale.at[layer],
                    weighted, to, count,
                )

    return pl.pallas_call(
        kernel,
        out_shape=jax.ShapeDtypeStruct(grad.shape, jnp.bfloat16),
        in_specs=[whole(pltpu.SMEM)] + [whole()] * 5 + weight_specs(),
        out_specs=whole(),
        scratch_shapes=weight_scratch(model_width, hidden_width)
        + [
            pltpu.VMEM((batch, model_width), jnp.bfloat16),
            pltpu.VMEM((model_width, batch), jnp.bfloat16),
            pltpu.VMEM((batch, model_width), jnp.float32),
            pltpu.VMEM((hidden_width, batch), jnp.bfloat16),
        ],
        compiler_params=stage_params(),
        cost_estimate=stage_cost(4, batch, model_width, hidden_width),
        name="backward_stage",
    )(place, grad, *saved, weights[0], *map(in_hbm, weights[1:]), *ready)


def swapped(value, section_count):
    return lax.ppermute(value, "section", [(s, s ^ 1) for s in range(section_count)])


def moved(value, from_stage, to_stage):
    pairs = [(2 * from_stage + core, 2 * to_stage + core) for core in (0, 1)]
    return lax.ppermute(value, "section", pairs)


def mirror(value):
    along = lax.axis_size("table")
    return lax.ppermute(value, "table", [(t, (t + along // 2) % along) for t in range(along)])


def swap_in_half(value):
    along = lax.axis_size("table")
    half = along // 2
    groups = [
        [s * along + h * half + t for s in range(lax.axis_size("section")) for t in range(half)]
        for h in (0, 1)
    ]
    return lax.all_to_all(
        value, TABLE_AXES, split_axis=0, concat_axis=0, axis_index_groups=groups, tiled=True
    )


def near_first(per_asker, my_half):
    sections = lax.axis_size("section")
    half = lax.axis_size("table") // 2
    split = per_asker.reshape((sections, 2, half) + per_asker.shape[1:])
    near = lax.dynamic_index_in_dim(split, my_half, 1, keepdims=False)
    far = lax.dynamic_index_in_dim(split, 1 - my_half, 1, keepdims=False)
    return jnp.stack([near, far], axis=2).reshape((sections * half, 2) + per_asker.shape[1:])


def after(value, earlier):
    return lax.optimization_barrier((value, earlier))[0]


def per_device(
    emb_table,
    lcb_weight,
    fm_proj,
    norm_gain,
    w_up,
    w_down,
    top_grad,
    lookup_slot,
    wanted_rows,
    row_counts,
):
    section_count = lax.axis_size("section")
    along = lax.axis_size("table")
    half = along // 2
    near_owners = section_count * half
    stages = section_count // 2
    stage = lax.axis_index("section") // 2
    core = lax.axis_index("section") % 2
    my_half = lax.axis_index("table") // half
    cap = wanted_rows.shape[2]
    rows, embed_width = emb_table.shape
    embed_count = lcb_weight.shape[0]
    look_dev = lookup_slot.shape[1]
    model_width = top_grad.shape[3]

    own_slots = lookup_slot[0]
    mirror_slots = mirror(own_slots)
    small = jnp.concatenate([fm_proj[0], norm_gain[0].reshape(embed_count, -1)], axis=0)
    other_up = swapped(w_up[0], section_count)
    other_down = swapped(w_down[0], section_count)
    other_small = swapped(small, section_count)

    picked = near_first(wanted_rows[0], my_half)
    outgoing = pick_rows(emb_table, wanted_rows[0], my_half)
    sent = after(outgoing, mirror_slots).reshape(near_owners, 2, cap, embed_width)
    fetched = swap_in_half(sent)

    def spread_of(slots):
        owner, column = slots // cap, slots % cap
        place = owner % along
        near = jnp.where(place // half == my_half, owner // along * half + place % half, near_owners)
        return spread_weights(near * cap + column, lcb_weight, near_owners, cap)

    spread_far, kept_far = spread_of(mirror_slots)
    spread_near, kept_near = spread_of(own_slots)
    smalls = jnp.stack(
        [jnp.where(core == 0, small, other_small), jnp.where(core == 0, other_small, small)]
    )
    weights = [smalls, w_up[0], other_up, w_down[0], other_down]
    spread_far, spread_near = lax.optimization_barrier((spread_far, spread_near))
    far_part = mirror(compress(spread_far, fetched, 1, embed_count, jnp.bfloat16))
    near_part = compress(spread_near, fetched, 0, embed_count, jnp.float32)

    def at(tick):
        is_last = (stage == stages - 1) & (tick == 0)
        return jnp.stack([core, stage == tick, is_last]).astype(jnp.int32)

    first_up = hold_matrix(after(at(0), near_part), 0, weights[1], weights[2])
    far_part = after(far_part, first_up)
    lead = (near_part + far_part.astype(jnp.float32)).astype(jnp.bfloat16)
    first_down = hold_matrix(after(at(0), lead), 0, weights[3], weights[4])
    pieces = [lead] + [moved(lead, s, 0) for s in range(1, stages)]
    top = top_grad.reshape(stages, 2, look_dev, model_width)
    top = lax.dynamic_index_in_dim(top, core, 1, keepdims=False).reshape(-1, model_width)

    saved = None
    for tick in range(stages - 1):
        place = at(tick)
        ready = [first_up, first_down] if tick == 0 else hold_layer(place, 0, weights, out)
        out, fresh, product = forward_stage(place, pieces, top, weights, ready, embed_count)
        if saved is None:
            saved, g_hidden = fresh, product
        else:
            saved = [jnp.where(stage == tick, new, old) for new, old in zip(fresh, saved)]
        pieces = [moved(out, tick, tick + 1)]
    place = at(stages - 1)
    ready = hold_layer(place, 0, weights, out)
    grad = turn_stage(place, pieces[0], top, g_hidden, weights, ready, embed_count)
    was_forward = (stage < stages - 1).astype(jnp.int32).reshape(1)
    saved = [turn_hidden(after(was_forward, grad), saved[0])] + list(saved[1:])
    for tick in reversed(range(stages - 1)):
        place = at(tick)
        ready = hold_layer(place, 1, weights, grad)
        grad = moved(grad, tick + 1, tick)
        grad = backward_stage(place, grad, saved, weights, ready, embed_count)

    own_grad = grad[:look_dev]
    for s in range(1, stages):
        piece = grad[s * look_dev : (s + 1) * look_dev]
        own_grad = jnp.where(stage == s, moved(piece, 0, s), own_grad)
    mirror_grad = mirror(own_grad)

    near_grad = expand(kept_near, own_grad, embed_count)
    slot_grad = expand(kept_far, mirror_grad, embed_count, near_grad)
    returned = swap_in_half(slot_grad)
    live_slots = jnp.arange(cap) < near_first(row_counts[0], my_half)[..., None]
    targets = jnp.where(live_slots, picked, rows).reshape(-1)
    return add_rows(targets, returned.reshape(-1, embed_width), outgoing, rows, cap)


def solution(mesh):
    in_specs = (
        P(("section", "table"), None),
        P(),
        P("section", None, None),
        P("section", None),
        P("section", None, None),
        P("section", None, None),
        P("table", None, None, None),
        P("table", "section", None),
        P(("section", "table"), None, None),
        P(("section", "table"), None),
    )
    out_specs = P(("section", "table"), None)
    return jax.shard_map(
        per_device, mesh=mesh, in_specs=in_specs, out_specs=out_specs, check_vma=False
    )
```
